32 devices in a mesh: crop: 4 (over x, core), row: 8 (over z, y).
Axes of the slice: x: 2, y: 2, z: 4, core: 2. Of those that a mesh axis runs over, the one named last changes fastest.
Arguments:
- node: bfloat16 [4, 256, 256], P('crop', 'row'), may hold values from -6 to 6
- pair: bfloat16 [4, 256, 256, 128], P('crop', 'row'), may hold values from -6 to 6
- recycle: int32 [4], P('crop'), may hold values from 0 to 3
- mask: int32 [4, 256], P('crop'), may hold values 0 or 1
- node_cot: bfloat16 [4, 256, 256], P('crop', 'row'), may hold values from -6 to 6
- pair_cot: bfloat16 [4, 256, 256, 128], P('crop', 'row'), may hold values from -6 to 6
- master: float32 [1199616], P(('crop', 'row')), may hold values from -4 to 4, as said below
- first: float32 [1199616], P(('crop', 'row')), may hold values from -0.0014648438 to 0.0014648438
- second: float32 [1199616], P(('crop', 'row')), may hold values from 1e-08 to 1e-07
Outputs:
- node_out: bfloat16 [4, 256, 256], P('crop', 'row')
- pair_out: bfloat16 [4, 256, 256, 128], P('crop', 'row')
- node_grad: bfloat16 [4, 256, 256], P('crop', 'row')
- pair_grad: bfloat16 [4, 256, 256, 128], P('crop', 'row')
- weight_grad: float32 [1199616], P(('crop', 'row'))
- bias_grad: float32 [128], replicated
- grad_norm: float32 [], replicated
- new_master: float32 [1199616], P(('crop', 'row'))
- new_first: float32 [1199616], P(('crop', 'row'))
- new_second: float32 [1199616], P(('crop', 'row'))
- new_weights: bfloat16 [1199616], P(('crop', 'row'))
The draws below stay inside these ranges and needn't reach their ends.
Inputs may be any that keep to these rules, and one draw needn't show every extreme that they name: `master`: the parameters packed end to end in the order that the first step lists.
All inputs are finite; a program needn't handle non-finite values. No bound on the sum of `mask` on one device may be relied on, other than what follows from the above.
Results may differ from the reference program's by a relative error of at most 0.022.
Values may be sent and summed in bfloat16 or wider, within the bound.
No kernel may reach another device: no remote copies, remote signals or barrier semaphores. Data moves between devices by JAX's collectives and lax.ppermute only.
A program may use at most 384 MiB of HBM per device.

```python
import math
import jax
import jax.numpy as jnp
from jax import lax

NODE_DIM = 256
PAIR_DIM = 128
HEADS = 8
HEAD_DIM = 32
OUTER = 32
TRI_DIM = 128
FFN_NODE = 1024
FFN_PAIR = 512
RECYCLES = 4
RESIDUES = 256
ADAM_STEP = 3
CROPS = 4
PARAMS = 1199616


def segment_scales():
    heads_width = HEADS * HEAD_DIM
    table = [(RECYCLES * NODE_DIM, 0.0, 0.5), (NODE_DIM, 1.0, 0.1), (3 * NODE_DIM * heads_width, 0.0, NODE_DIM ** (-0.5)), (PAIR_DIM * HEADS, 0.0, PAIR_DIM ** (-0.5)), (heads_width * NODE_DIM, 0.0, 6.4 * heads_width ** (-0.5)), (NODE_DIM, 1.0, 0.1), (NODE_DIM * FFN_NODE, 0.0, NODE_DIM ** (-0.5)), (FFN_NODE * NODE_DIM, 0.0, FFN_NODE ** (-0.5)), (NODE_DIM, 1.0, 0.1), (2 * NODE_DIM * OUTER, 0.0, NODE_DIM ** (-0.5)), (OUTER * OUTER * PAIR_DIM, 0.0, (OUTER * OUTER) ** (-0.5))]
    for repeat in range(2):
        table += [(PAIR_DIM, 1.0, 0.1), (2 * PAIR_DIM * TRI_DIM + PAIR_DIM * PAIR_DIM, 0.0, PAIR_DIM ** (-0.5)), (TRI_DIM, 1.0, 0.1), (TRI_DIM * PAIR_DIM, 0.0, TRI_DIM ** (-0.5))]
    table += [(PAIR_DIM, 1.0, 0.1), (PAIR_DIM * FFN_PAIR, 0.0, PAIR_DIM ** (-0.5)), (FFN_PAIR * PAIR_DIM, 0.0, FFN_PAIR ** (-0.5)), (PAIR_DIM, 0.0, 0.5)]
    return table


def draw_master(key, part):
    table = segment_scales()
    centers = jnp.concatenate([jnp.full((extent,), center, jnp.float32) for extent, center, spread in table])
    spreads = jnp.concatenate([jnp.full((extent,), spread, jnp.float32) for extent, center, spread in table])
    noise = jnp.clip(jax.random.normal(key, (PARAMS,), jnp.float32), -4.0, 4.0)
    return centers + spreads * noise


def touch_ends(values, rng, low, high):
    longest = values.shape.index(max(values.shape))
    spots = []
    for shift in (0, 1):
        where = [jax.random.randint(jax.random.fold_in(rng, axis), (), 0, length) for axis, length in enumerate(values.shape)]
        where[longest] = (where[longest] + shift) % values.shape[longest]
        spots.append(tuple(where))
    return values.at[spots[0]].set(low).at[spots[1]].set(high)


def block_levels(rng, dims, shards, smallest, largest):
    loudness = 1.0
    for axis_at, parts in shards:
        steps = jax.random.uniform(jax.random.fold_in(jax.random.fold_in(rng, 6), axis_at), (parts,), jnp.float32, smallest / len(shards), largest / len(shards))
        loudness = loudness * jnp.repeat(jnp.exp(steps), dims[axis_at] // parts).reshape((-1,) + (1,) * (len(dims) - 1 - axis_at))
    return loudness


def normal_values(rng, dims, width, reach, shards=(), kind=jnp.bfloat16):
    level = block_levels(rng, dims, shards, -0.22, 0.18) if shards else 1.0
    result = jax.random.normal(rng, dims, jnp.float32) * width * level
    return jnp.minimum(jnp.maximum(result, -reach), reach).astype(kind)


def setup_inputs(seed: int = 0) -> dict:
    streams_of = jax.random.split(jax.random.key(seed), 10)
    node = normal_values(streams_of[0], (CROPS, RESIDUES, NODE_DIM), 1.0, 6.0, ((0, 4), (1, 8)))
    pair = normal_values(streams_of[1], (CROPS, RESIDUES, RESIDUES, PAIR_DIM), 1.0, 6.0, ((0, 4), (1, 8)))
    recycle = touch_ends(jax.random.randint(streams_of[2], (CROPS,), 0, 4), jax.random.fold_in(streams_of[2], 1), 0, 3).astype(jnp.int32)
    mask = touch_ends((jax.random.randint(streams_of[3], (CROPS, RESIDUES), 0, 8) < 7).astype(jnp.int32), jax.random.fold_in(streams_of[3], 1), 0, 1)
    node_cot = normal_values(streams_of[4], (CROPS, RESIDUES, NODE_DIM), 1.0, 6.0, ((0, 4), (1, 8)))
    pair_cot = normal_values(streams_of[5], (CROPS, RESIDUES, RESIDUES, PAIR_DIM), 1.0, 6.0, ((0, 4), (1, 8)))
    master = draw_master(jax.random.fold_in(streams_of[9], 71), 0)
    first = normal_values(streams_of[7], (PARAMS,), 0.0001, 0.0014648438, ((0, 32),), jnp.float32)
    second = jnp.clip(jnp.exp(math.log(1.0000000116860974e-07) - 2.3025851 * jax.random.uniform(streams_of[8], (PARAMS,), jnp.float32) ** block_levels(streams_of[8], (PARAMS,), ((0, 32),), -0.2, 0.2)), 9.99999993922529e-09, 1.0000000116860974e-07)
    return dict(node=node, pair=pair, recycle=recycle, mask=mask, node_cot=node_cot, pair_cot=pair_cot, master=master, first=first, second=second)


@jax.custom_vjp
def low(v):
    return lax.optimization_barrier(v.astype(jnp.bfloat16)).astype(jnp.float32)

@jax.custom_vjp
def low_back(v):
    return v

def low_keep(v):
    return (low(v), None)

def low_pass(kept, grad):
    return (grad,)

def back_keep(v):
    return (v, None)

def back_low(kept, grad):
    return (low(grad),)
low.defvjp(low_keep, low_pass)
low_back.defvjp(back_keep, back_low)
EPS_NORM = 1e-05
ADAM_EPS = 1e-08
BETA_ONE = 0.9
BETA_TWO = 0.95
LEARN_RATE = 0.06
WEIGHT_DECAY = 0.1
CLIP_NORM = 1.0
MASK_FILL = 1000000000.0
HIGHEST = lax.Precision.HIGHEST

def segment_list():
    heads_width = HEADS * HEAD_DIM
    entries = [('embed', (RECYCLES, NODE_DIM)), ('gain_one', (NODE_DIM,)), ('w_query', (NODE_DIM, heads_width)), ('w_key', (NODE_DIM, heads_width)), ('w_value', (NODE_DIM, heads_width)), ('w_bias', (PAIR_DIM, HEADS)), ('w_attn_out', (heads_width, NODE_DIM)), ('gain_two', (NODE_DIM,)), ('w_node_up', (NODE_DIM, FFN_NODE)), ('w_node_down', (FFN_NODE, NODE_DIM)), ('gain_three', (NODE_DIM,)), ('w_left_node', (NODE_DIM, OUTER)), ('w_right_node', (NODE_DIM, OUTER)), ('w_outer', (OUTER * OUTER, PAIR_DIM))]
    for prefix in ('out_', 'in_'):
        entries += [(prefix + 'gain_in', (PAIR_DIM,)), (prefix + 'w_left', (PAIR_DIM, TRI_DIM)), (prefix + 'w_right', (PAIR_DIM, TRI_DIM)), (prefix + 'w_gate', (PAIR_DIM, PAIR_DIM)), (prefix + 'gain_tri', (TRI_DIM,)), (prefix + 'w_tri_out', (TRI_DIM, PAIR_DIM))]
    entries += [('gain_pair', (PAIR_DIM,)), ('w_pair_up', (PAIR_DIM, FFN_PAIR)), ('w_pair_down', (FFN_PAIR, PAIR_DIM)), ('bias_pair', (PAIR_DIM,))]
    return entries

def unpack(flat):
    params = {}
    offset = 0
    for entry_name, entry_shape in segment_list():
        extent = math.prod(entry_shape)
        params[entry_name] = flat[offset:offset + extent].reshape(entry_shape)
        offset += extent
    return params

def layer_norm(values, gain):
    centered = values - lax.optimization_barrier(jnp.mean(values, axis=-1, keepdims=True))
    spread = lax.optimization_barrier(jnp.mean(centered * centered, axis=-1, keepdims=True))
    return centered * lax.rsqrt(spread + EPS_NORM) * gain

def both_round(values):
    return low(low_back(values))

def product(left_arg, right_arg):
    return jnp.matmul(left_arg, right_arg, precision=HIGHEST)

def triangle(pair_in, params, prefix, pair_mask, incoming):
    normed = low(layer_norm(pair_in, params[prefix + 'gain_in']))
    left_proj = both_round(product(normed, params[prefix + 'w_left']) * pair_mask[:, :, None])
    right_proj = both_round(product(normed, params[prefix + 'w_right']) * pair_mask[:, :, None])
    gate_pre = low_back(product(normed, params[prefix + 'w_gate']))
    if incoming:
        tri_mixed = jnp.einsum('kid,kjd->ijd', left_proj, right_proj, precision=HIGHEST)
    else:
        tri_mixed = jnp.einsum('ikd,jkd->ijd', left_proj, right_proj, precision=HIGHEST)
    tri_mixed = low_back(tri_mixed)
    update = low_back(product(low(layer_norm(tri_mixed, params[prefix + 'gain_tri'])), params[prefix + 'w_tri_out']))
    return pair_in + jax.nn.sigmoid(gate_pre) * update

def crop_forward(master, node_row, pair_row, crop_count, mask_row):
    params = unpack(low(master))
    one_hot = (jnp.arange(RECYCLES, dtype=jnp.int32) == crop_count).astype(jnp.float32)
    key_keep = mask_row.astype(jnp.float32)
    start_node = node_row + product(one_hot, params['embed'])[None, :]
    normed = low(layer_norm(start_node, params['gain_one']))
    query = both_round(product(normed, params['w_query'])).reshape(RESIDUES, HEADS, HEAD_DIM)
    key_proj = both_round(product(normed, params['w_key'])).reshape(RESIDUES, HEADS, HEAD_DIM)
    value_proj = both_round(product(normed, params['w_value'])).reshape(RESIDUES, HEADS, HEAD_DIM)
    pair_bias = jnp.einsum('ijd,dh->hij', pair_row, params['w_bias'], precision=HIGHEST)
    scores = jnp.einsum('ihd,jhd->hij', query, key_proj, precision=HIGHEST) * HEAD_DIM ** (-0.5)
    scores = low_back(scores + pair_bias + ((key_keep - 1.0) * MASK_FILL)[None, None, :])
    soft = low(jax.nn.softmax(scores, axis=-1))
    attended = both_round(jnp.einsum('hij,jhd->ihd', soft, value_proj, precision=HIGHEST).reshape(RESIDUES, HEADS * HEAD_DIM))
    after_attn = start_node + low_back(product(attended, params['w_attn_out']))
    normed = low(layer_norm(after_attn, params['gain_two']))
    hidden = low_back(product(normed, params['w_node_up']))
    activated = low(jax.nn.gelu(hidden, approximate=False))
    node_final = after_attn + low_back(product(activated, params['w_node_down']))
    normed = low(layer_norm(node_final, params['gain_three']))
    left_node = both_round(product(normed, params['w_left_node']))
    right_node = both_round(product(normed, params['w_right_node']))
    table = both_round(jnp.einsum('ip,pqe->iqe', left_node, params['w_outer'].reshape(OUTER, OUTER, PAIR_DIM), precision=HIGHEST))
    outer = low_back(jnp.einsum('iqe,jq->ije', table, right_node, precision=HIGHEST))
    pair_mask = key_keep[:, None] * key_keep[None, :]
    pair_state = pair_row + outer
    pair_state = triangle(pair_state, params, 'out_', pair_mask, False)
    pair_state = triangle(pair_state, params, 'in_', pair_mask, True)
    normed = low(layer_norm(pair_state, params['gain_pair']))
    hidden = low_back(product(normed, params['w_pair_up']))
    activated = low(jax.nn.gelu(hidden, approximate=False))
    pair_final = pair_state + low_back(product(activated, params['w_pair_down']) + params['bias_pair'])
    return (node_final, pair_final)

def reference(node, pair, recycle, mask, node_cot, pair_cot, master, first, second):

    def crop_step(grad_total, crop_items):
        node_row, pair_row, crop_count, mask_row, node_cot_row, pair_cot_row = crop_items

        def forward(master_arg, node_arg, pair_arg):
            return crop_forward(master_arg, node_arg, pair_arg, crop_count, mask_row)
        outputs, pullback = jax.vjp(forward, master, node_row.astype(jnp.float32), pair_row.astype(jnp.float32))
        grad_master, grad_node, grad_pair = pullback((node_cot_row.astype(jnp.float32), pair_cot_row.astype(jnp.float32)))
        return (grad_total + grad_master, (outputs[0].astype(jnp.bfloat16), outputs[1].astype(jnp.bfloat16), grad_node.astype(jnp.bfloat16), grad_pair.astype(jnp.bfloat16)))
    grad_total, stacked = lax.scan(crop_step, jnp.zeros((PARAMS,), jnp.float32), (node, pair, recycle, mask, node_cot, pair_cot))
    bias_grad = grad_total[PARAMS - PAIR_DIM:]
    grad_norm = jnp.sqrt(jnp.sum(grad_total * grad_total))
    clipped = grad_total * (CLIP_NORM / jnp.maximum(grad_norm, CLIP_NORM))
    new_first = BETA_ONE * first + (1.0 - BETA_ONE) * clipped
    new_second = BETA_TWO * second + (1.0 - BETA_TWO) * clipped * clipped
    first_hat = new_first / (1.0 - BETA_ONE ** ADAM_STEP)
    second_hat = new_second / (1.0 - BETA_TWO ** ADAM_STEP)
    new_master = master - LEARN_RATE * (first_hat / (jnp.sqrt(second_hat) + ADAM_EPS) + WEIGHT_DECAY * master)
    return (stacked[0], stacked[1], stacked[2], stacked[3], grad_total, bias_grad, grad_norm, new_master, new_first, new_second, new_master.astype(jnp.bfloat16))
```

```python
import math

import jax
import jax.numpy as jnp
import numpy as np
from jax import lax
from jax.experimental import pallas as pl
from jax.experimental.pallas import tpu as pltpu
from jax.sharding import PartitionSpec as P

NODE_DIM = 256
PAIR_DIM = 128
HEADS = 8
HEAD_DIM = 32
OUTER = 32
TRI_DIM = 128
FFN_NODE = 1024
FFN_PAIR = 512
RECYCLES = 4
ADAM_STEP = 3


EPS_NORM = 1e-05
ADAM_EPS = 1e-08
BETA_ONE = 0.9
BETA_TWO = 0.95
LEARN_RATE = 0.06
WEIGHT_DECAY = 0.1
CLIP_NORM = 1.0
MASK_FILL = 1000000000.0
HIGHEST = lax.Precision.HIGHEST


def segment_list():
    heads_width = HEADS * HEAD_DIM
    entries = [
        ("embed", (RECYCLES, NODE_DIM)),
        ("gain_one", (NODE_DIM,)),
        ("w_query", (NODE_DIM, heads_width)),
        ("w_key", (NODE_DIM, heads_width)),
        ("w_value", (NODE_DIM, heads_width)),
        ("w_bias", (PAIR_DIM, HEADS)),
        ("w_attn_out", (heads_width, NODE_DIM)),
        ("gain_two", (NODE_DIM,)),
        ("w_node_up", (NODE_DIM, FFN_NODE)),
        ("w_node_down", (FFN_NODE, NODE_DIM)),
        ("gain_three", (NODE_DIM,)),
        ("w_left_node", (NODE_DIM, OUTER)),
        ("w_right_node", (NODE_DIM, OUTER)),
        ("w_outer", (OUTER * OUTER, PAIR_DIM)),
    ]
    for prefix in ("out_", "in_"):
        entries += [
            (prefix + "gain_in", (PAIR_DIM,)),
            (prefix + "w_left", (PAIR_DIM, TRI_DIM)),
            (prefix + "w_right", (PAIR_DIM, TRI_DIM)),
            (prefix + "w_gate", (PAIR_DIM, PAIR_DIM)),
            (prefix + "gain_tri", (TRI_DIM,)),
            (prefix + "w_tri_out", (TRI_DIM, PAIR_DIM)),
        ]
    entries += [
        ("gain_pair", (PAIR_DIM,)),
        ("w_pair_up", (PAIR_DIM, FFN_PAIR)),
        ("w_pair_down", (FFN_PAIR, PAIR_DIM)),
        ("bias_pair", (PAIR_DIM,)),
    ]
    return entries


def unpack(flat):
    params = {}
    offset = 0
    for entry_name, entry_shape in segment_list():
        extent = math.prod(entry_shape)
        params[entry_name] = flat[offset : offset + extent].reshape(entry_shape)
        offset += extent
    return params


LOW = jnp.bfloat16
WIDE = jnp.float32
BOTH = ("crop", "row")
TILE = 16
VMEM_LIMIT = 56 * 2**20
INV_SQRT2 = 1.0 / math.sqrt(2.0)
INV_SQRT2PI = 1.0 / math.sqrt(2.0 * math.pi)


class Layout:
    def __init__(self, crops, rows):
        self.crops, self.rows, self.wide = crops, rows, rows // crops
        self.planes = (0, 2, 1, 3) if crops == 4 else tuple(range(crops))
        self.slots = (0, 2, 1, 3) if crops == 4 else tuple(range(crops))
        self.crop_of = tuple(self.planes.index(k) for k in range(crops))
        self.high_of = tuple(self.slots.index(k) for k in range(crops))
        ident = lambda c, z, y: (c * crops + z) * self.wide + y
        spots = [
            (c, z, y) for c in range(crops) for z in range(crops) for y in range(self.wide)
        ]
        self.outward = [
            (ident(c, z, y), ident(self.slots[z], self.planes[c], y)) for c, z, y in spots
        ]
        self.homeward = [(there, here) for here, there in self.outward]
        self.groups = [
            [
                ident(self.slots[z], plane, y)
                for z in range(crops)
                for y in range(self.wide)
            ]
            for plane in range(crops)
        ]
        half = crops // 2
        self.cores = [
            [(2 * x + k) * rows + r for k in range(2)] for x in range(half) for r in range(rows)
        ]
        self.chips = [
            [(2 * x + k) * rows + r for x in range(half)] for k in range(2) for r in range(rows)
        ]


def exchange(blocks, axes, groups=None):
    return lax.all_to_all(blocks, axes, 0, 0, axis_index_groups=groups, tiled=True)


def spread(part, count, axes, groups=None):
    return exchange(jnp.broadcast_to(part[None], (count,) + part.shape), axes, groups)


def dot_nn(a, b):
    return lax.dot_general(a, b, (((1,), (0,)), ((), ())), preferred_element_type=WIDE)


def dot_nt(a, b):
    return lax.dot_general(a, b, (((1,), (1,)), ((), ())), preferred_element_type=WIDE)


def dot_tn(a, b):
    return lax.dot_general(a, b, (((0,), (0,)), ((), ())), preferred_element_type=WIDE)


def norm_parts(x):
    centered = x - jnp.mean(x, axis=0, keepdims=True)
    scale = lax.rsqrt(jnp.mean(centered * centered, axis=0, keepdims=True) + EPS_NORM)
    return centered * scale, scale


def norm_back(grad, hat, scale, gain):
    grad_gain = jnp.sum(grad * hat, axis=1, keepdims=True)
    wide = grad * gain
    inner = jnp.mean(wide * hat, axis=0, keepdims=True)
    return scale * (wide - jnp.mean(wide, axis=0, keepdims=True) - hat * inner), grad_gain


def sigmoid(x):
    return 0.5 * jnp.tanh(0.5 * x) + 0.5


def cat(ref, start, count):
    return jnp.concatenate([ref[start + t] for t in range(count)], axis=1)


def put(ref, start, count, value):
    width = value.shape[1] // count
    for t in range(count):
        ref[start + t] = value[:, t * width : (t + 1) * width]


def swapped(value):
    if value.shape[0] % TILE or value.shape[1] % TILE:
        return jnp.swapaxes(value.astype(WIDE), 0, 1).astype(LOW)
    return jnp.swapaxes(value, 0, 1)


def cell_mask(mask_ref, start, count):
    return jnp.concatenate([mask_ref[start + t] for t in range(count)], axis=1)


def send_pair(scratch, out_ref):
    parts, share = out_ref.shape[0], out_ref.shape[1] // 2
    channels = parts * share
    for side in range(2):
        value = swapped(scratch[:, side * channels : (side + 1) * channels, :])
        out_ref[:, side * share : (side + 1) * share] = value.reshape(
            (parts, share) + value.shape[1:]
        )


def take_pair(in_ref, scratch):
    parts, share = in_ref.shape[0], in_ref.shape[1] // 2
    channels = parts * share
    for side in range(2):
        value = in_ref[:, side * share : (side + 1) * share]
        value = value.reshape((channels,) + value.shape[2:])
        scratch[:, side * channels : (side + 1) * channels, :] = swapped(value)


def front(x, gain, w_sides, mask):
    hat, _ = norm_parts(x)
    normed = (hat * gain).astype(LOW)
    return (dot_nn(w_sides, normed) * mask).astype(LOW)


def gate_of(x, gain, w_gate):
    hat, _ = norm_parts(x)
    return sigmoid(dot_nn(w_gate, (hat * gain).astype(LOW)))


def post(x, mixed, gain_in, w_gate, gain_tri, w_out):
    hat, _ = norm_parts(mixed)
    update = dot_nn(w_out, (hat * gain_tri).astype(LOW))
    return x + gate_of(x, gain_in, w_gate) * update


def post_back(grad, x, mixed, gain_in, w_gate, gain_tri, w_out, w_out_back):
    hat, scale = norm_parts(mixed)
    normed = (hat * gain_tri).astype(LOW)
    update = dot_nn(w_out, normed)
    gate = gate_of(x, gain_in, w_gate)
    update_grad = (grad * gate).astype(LOW)
    gate_grad = (grad * update * (gate * (1.0 - gate))).astype(LOW)
    grad_out = dot_nt(normed, update_grad)
    mixed_grad, grad_gain = norm_back(dot_nn(w_out_back, update_grad), hat, scale, gain_tri)
    return mixed_grad.astype(LOW), gate_grad, grad_out, grad_gain


def front_back(grad, x, sides_grad, gate_grad, mask, gain, w_all_back):
    hat, scale = norm_parts(x)
    normed = (hat * gain).astype(LOW)
    sides = jnp.concatenate([sides_grad * mask.astype(LOW), gate_grad], axis=0)
    grad_w = dot_nt(normed, sides)
    x_grad, grad_gain = norm_back(dot_nn(w_all_back, sides), hat, scale, gain)
    return grad + x_grad, grad_w, grad_gain


def gelu_parts(x):
    cumulative = 0.5 * lax.erf(x * INV_SQRT2) + 0.5
    density = INV_SQRT2PI * jnp.exp(-0.5 * x * x)
    return x * cumulative, cumulative + x * density


def zero_first(*refs):
    @pl.when(pl.program_id(0) == 0)
    def _():
        for ref in refs:
            ref[...] = jnp.zeros_like(ref)


def run(body, step_rows, rows, in_arrays, in_kinds, outs, scratch, flops):
    def spec(kind, shape):
        if kind == "r":
            return pl.BlockSpec((step_rows,) + shape[1:], lambda i: (i,) + (0,) * (len(shape) - 1))
        if kind == "s":
            return pl.BlockSpec(
                shape[:-2] + (step_rows, shape[-1]),
                lambda i: (0,) * (len(shape) - 2) + (i, 0),
            )
        return pl.BlockSpec(shape, lambda i: (0,) * len(shape))

    moved = sum(a.size * a.dtype.itemsize for a in in_arrays)
    return pl.pallas_call(
        body,
        grid=(rows // step_rows,),
        in_specs=[spec(kind, a.shape) for kind, a in zip(in_kinds, in_arrays)],
        out_specs=[spec(kind, shape) for kind, shape, _ in outs],
        out_shape=[jax.ShapeDtypeStruct(shape, dtype) for _, shape, dtype in outs],
        scratch_shapes=scratch,
        compiler_params=pltpu.CompilerParams(vmem_limit_bytes=VMEM_LIMIT),
        cost_estimate=pl.CostEstimate(flops=flops, bytes_accessed=moved, transcendentals=0),
    )(*in_arrays)


def loop(count, body):
    def step(t, carry):
        body(t)
        return carry

    lax.fori_loop(0, count, step, 0)


GROUP = 2


def kernel_open(pair, table, right, mask, gain, w_sides, x_out, sides_out, scratch):
    rows = pair.shape[0]
    group = min(GROUP, rows)
    w_low = w_sides[...].T
    right_low = right[...]

    def step(t):
        at = t * group
        x = jnp.concatenate(
            [
                pair[at + k].T.astype(WIDE) + dot_nn(table[at + k], right_low)
                for k in range(group)
            ],
            axis=1,
        )
        put(x_out, at, group, x)
        put(scratch, at, group, front(x, gain[...], w_low, cell_mask(mask, at, group)))

    loop(rows // group, step)
    send_pair(scratch, sides_out)


def kernel_middle(
    mixed, x_in, mask, gain_in, w_gate, gain_tri, w_out, gain_next, w_sides, x_out, sides_out,
    arrived, scratch,
):
    rows = x_in.shape[0]
    group = min(GROUP, rows)
    arrived[...] = swapped(mixed[...])
    w_low, gate_low, out_low = w_sides[...].T, w_gate[...].T, w_out[...].T

    def step(t):
        at = t * group
        x = post(
            cat(x_in, at, group), cat(arrived, at, group).astype(WIDE),
            gain_in[...], gate_low, gain_tri[...], out_low,
        )
        put(x_out, at, group, x)
        put(scratch, at, group, front(x, gain_next[...], w_low, cell_mask(mask, at, group)))

    loop(rows // group, step)
    send_pair(scratch, sides_out)


def kernel_turn(
    mixed, x_in, cot, gain_in, w_gate, gain_tri, w_out, gain_pair, w_up, w_down, bias,
    pair_out, x_grad, gate_grad, mixed_grad, g_out, g_tri, g_up, g_down, g_pair, g_bias,
    arrived, leaving,
):
    rows = x_in.shape[0]
    group = min(GROUP, rows)
    arrived[...] = swapped(mixed[...])
    gate_low, out_low, out_back = w_gate[...].T, w_out[...].T, w_out[...]
    up_low, up_back = w_up[...].T, w_up[...]
    down_low, down_back = w_down[...].T, w_down[...]
    zero_first(g_out, g_tri, g_up, g_down, g_pair, g_bias)
    chunk = PAIR_DIM

    def step(t):
        at = t * group
        x_two = cat(x_in, at, group)
        mix = cat(arrived, at, group).astype(WIDE)
        x = post(x_two, mix, gain_in[...], gate_low, gain_tri[...], out_low)
        hat, scale = norm_parts(x)
        normed = (hat * gain_pair[...]).astype(LOW)
        cot_low = jnp.concatenate([cot[at + k].T for k in range(group)], axis=1)
        total = x + bias[...]
        normed_grad = jnp.zeros_like(x)
        for c in range(FFN_PAIR // chunk):
            part = slice(c * chunk, (c + 1) * chunk)
            act, slope = gelu_parts(dot_nn(up_low[part], normed))
            act_low = act.astype(LOW)
            total = total + dot_nn(down_low[:, part], act_low)
            hidden_grad = (dot_nn(down_back[part], cot_low) * slope).astype(LOW)
            normed_grad = normed_grad + dot_nn(up_back[:, part], hidden_grad)
            g_up[:, part] += dot_nt(normed, hidden_grad)
            g_down[part] += dot_nt(act_low, cot_low)
        total_low = total.astype(LOW)
        width = total.shape[1] // group
        for k in range(group):
            pair_out[at + k] = total_low[:, k * width : (k + 1) * width].T
        cot_wide = cot_low.astype(WIDE)
        g_bias[...] += jnp.sum(cot_wide, axis=1, keepdims=True)
        back, grad_gain = norm_back(normed_grad, hat, scale, gain_pair[...])
        g_pair[...] += grad_gain
        grad = cot_wide + back
        put(x_grad, at, group, grad)
        mix_grad, gates, grad_out, grad_tri = post_back(
            grad, x_two, mix, gain_in[...], gate_low, gain_tri[...], out_low, out_back
        )
        put(leaving, at, group, mix_grad)
        put(gate_grad, at, group, gates)
        g_out[...] += grad_out
        g_tri[...] += grad_tri

    loop(rows // group, step)
    mixed_grad[...] = swapped(leaving[...])


def kernel_return(
    sides_grad, x_after, gate_after, grad_in, mask, gain_after, w_after, mixed, x_before,
    gain_in, w_gate, gain_tri, w_out,
    x_grad, gate_grad, mixed_grad, g_after, g_gain, g_out, g_tri,
    sides, arrived, leaving,
):
    rows = x_after.shape[0]
    group = min(GROUP, rows)
    take_pair(sides_grad, sides)
    arrived[...] = swapped(mixed[...])
    gate_low, out_low, out_back = w_gate[...].T, w_out[...].T, w_out[...]
    zero_first(g_after, g_gain, g_out, g_tri)

    def step(t):
        at = t * group
        grad, grad_w, grad_gain = front_back(
            cat(grad_in, at, group), cat(x_after, at, group), cat(sides, at, group),
            cat(gate_after, at, group), cell_mask(mask, at, group), gain_after[...], w_after[...],
        )
        g_after[...] += grad_w
        g_gain[...] += grad_gain
        put(x_grad, at, group, grad)
        mix_grad, gates, grad_out, grad_tri = post_back(
            grad, cat(x_before, at, group), cat(arrived, at, group).astype(WIDE),
            gain_in[...], gate_low, gain_tri[...], out_low, out_back,
        )
        put(leaving, at, group, mix_grad)
        put(gate_grad, at, group, gates)
        g_out[...] += grad_out
        g_tri[...] += grad_tri

    loop(rows // group, step)
    mixed_grad[...] = swapped(leaving[...])


def kernel_close(
    sides_grad, x_after, gate_after, grad_in, mask, gain_after, w_after, table, right,
    pair_grad, table_grad, right_grad, g_after, g_gain, sides,
):
    rows = x_after.shape[0]
    group = min(GROUP, rows)
    take_pair(sides_grad, sides)
    zero_first(g_after, g_gain, right_grad)

    def step(t):
        at = t * group
        grad, grad_w, grad_gain = front_back(
            cat(grad_in, at, group), cat(x_after, at, group), cat(sides, at, group),
            cat(gate_after, at, group), cell_mask(mask, at, group), gain_after[...], w_after[...],
        )
        g_after[...] += grad_w
        g_gain[...] += grad_gain
        low = grad.astype(LOW)
        width = low.shape[1] // group
        for k in range(group):
            own = low[:, k * width : (k + 1) * width]
            pair_grad[at + k] = own.T
            table_grad[at + k] = dot_nn(own, right[...]).astype(LOW)
            right_grad[...] += dot_tn(table[at + k], own)

    loop(rows // group, step)


def kernel_mix(incoming, left, right, out):
    length = left.shape[-1]
    a = left[...].reshape(length, length)
    b = right[...].reshape(length, length)
    mixed = dot_tn(a, b) if incoming else dot_nt(a, b)
    out[...] = mixed.astype(LOW).reshape(out.shape)


def kernel_mix_back(incoming, grad, left, right, out):
    length = left.shape[-1]
    g = grad[...].reshape(length, length)
    a = left[...].reshape(length, length)
    b = right[...].reshape(length, length)
    block = (out.shape[0], out.shape[3], out.shape[4])
    a_grad = dot_nt(b, g) if incoming else dot_nn(g, b)
    b_grad = dot_nn(a, g) if incoming else dot_tn(g, a)
    out[:, 0, 0] = a_grad.astype(LOW).reshape(block)
    out[:, 1, 0] = b_grad.astype(LOW).reshape(block)


def mix(sides, incoming):
    parts, double, rows, length = sides.shape
    share = double // 2
    block = (parts, 1, rows, length)
    return pl.pallas_call(
        lambda *refs: kernel_mix(incoming, *refs),
        grid=(share,),
        in_specs=[
            pl.BlockSpec(block, lambda c: (0, c, 0, 0)),
            pl.BlockSpec(block, lambda c: (0, c + share, 0, 0)),
        ],
        out_specs=pl.BlockSpec(block, lambda c: (0, c, 0, 0)),
        out_shape=jax.ShapeDtypeStruct((parts, share, rows, length), LOW),
        compiler_params=pltpu.CompilerParams(vmem_limit_bytes=VMEM_LIMIT),
        cost_estimate=pl.CostEstimate(
            flops=2 * share * length**3, bytes_accessed=3 * share * length * length * 2,
            transcendentals=0,
        ),
    )(sides, sides)


def mix_back(grad, sides, incoming):
    parts, double, rows, length = sides.shape
    share = double // 2
    block = (parts, 1, rows, length)
    out = pl.pallas_call(
        lambda *refs: kernel_mix_back(incoming, *refs),
        grid=(share,),
        in_specs=[
            pl.BlockSpec(block, lambda c: (0, c, 0, 0)),
            pl.BlockSpec(block, lambda c: (0, c, 0, 0)),
            pl.BlockSpec(block, lambda c: (0, c + share, 0, 0)),
        ],
        out_specs=pl.BlockSpec((parts, 2, 1, rows, length), lambda c: (0, 0, c, 0, 0)),
        out_shape=jax.ShapeDtypeStruct((parts, 2, share, rows, length), LOW),
        compiler_params=pltpu.CompilerParams(vmem_limit_bytes=VMEM_LIMIT),
        cost_estimate=pl.CostEstimate(
            flops=4 * share * length**3, bytes_accessed=5 * share * length * length * 2,
            transcendentals=0,
        ),
    )(grad, sides, sides)
    return out.reshape(sides.shape)


def row_norm(x):
    centered = x - jnp.mean(x, axis=-1, keepdims=True)
    scale = lax.rsqrt(jnp.mean(centered * centered, axis=-1, keepdims=True) + EPS_NORM)
    return centered * scale, scale


def row_norm_back(grad, hat, scale, gain):
    grad_gain = jnp.sum(grad * hat, axis=0)
    wide = grad * gain
    inner = jnp.mean(wide * hat, axis=-1, keepdims=True)
    return scale * (wide - jnp.mean(wide, axis=-1, keepdims=True) - hat * inner), grad_gain


def low_of(x):
    return x.astype(LOW)


def local(layout, node, pair, recycle, mask, node_cot, pair_cot, master, first, second):
    crops, ranks = layout.crops, layout.rows
    devices = crops * ranks
    local_rows, length = node.shape[1], pair.shape[2]
    share = TRI_DIM // ranks
    heads_width = HEADS * HEAD_DIM
    scale_factor = HEAD_DIM ** (-0.5)
    node, pair, node_cot, pair_cot = node[0], pair[0], node_cot[0], pair_cot[0]

    crop_at, row_at = lax.axis_index("crop"), lax.axis_index("row")
    high_at, wide_at = row_at // layout.wide, row_at % layout.wide
    pick = lambda table, index: jnp.asarray(np.array(table, np.int32))[index]
    plane_crop = pick(layout.crop_of, high_at)
    plane_slot = pick(layout.high_of, crop_at) * layout.wide + wide_at

    padded = -(-master.shape[0] // 1024) * 1024
    shard = jnp.pad(low_of(master), (0, padded - master.shape[0])).reshape(-1, 128)
    shards = spread(shard, ranks, "row")
    shards = spread(shards, crops // 2, BOTH, layout.chips)
    shards = spread(shards, 2, BOTH, layout.cores)
    shards = jnp.swapaxes(shards, 0, 1).reshape(devices, padded)
    params = unpack(shards[:, : master.shape[0]].reshape(-1))
    wide = {entry_name: entry.astype(WIDE) for entry_name, entry in params.items()}
    node_all = spread(node, ranks, "row").reshape(length, NODE_DIM)
    pair_plane = lax.ppermute(pair, BOTH, layout.outward)
    cot_plane = lax.ppermute(pair_cot, BOTH, layout.outward)
    keep = mask.astype(WIDE)
    keep_plane = lax.ppermute(keep, BOTH, layout.outward)
    keep_rows = lax.dynamic_slice_in_dim(keep_plane[0], plane_slot * local_rows, local_rows, 0)
    mask_plane = (keep_rows[:, None] * keep_plane)[:, None, :]

    one_hot = (recycle[:, None] == jnp.arange(RECYCLES, dtype=jnp.int32)[None, :]).astype(WIDE)
    start_all = node_all.astype(WIDE) + jnp.matmul(one_hot, wide["embed"], precision=HIGHEST)
    hat_all, scale_all = row_norm(start_all)
    normed_all = low_of(hat_all * wide["gain_one"])
    own = lambda a: lax.dynamic_slice_in_dim(a, row_at * local_rows, local_rows, 0)
    start_node, hat_one, scale_one, normed_one = (
        own(a) for a in (start_all, hat_all, scale_all, normed_all)
    )
    query = low_of(dot_nn(normed_one, params["w_query"])).reshape(local_rows, HEADS, HEAD_DIM)
    key = low_of(dot_nn(normed_all, params["w_key"])).reshape(length, HEADS, HEAD_DIM)
    value = low_of(dot_nn(normed_all, params["w_value"])).reshape(length, HEADS, HEAD_DIM)
    pair_bias = jnp.einsum("ijd,dh->hij", pair, params["w_bias"], preferred_element_type=WIDE)
    scores = jnp.einsum("ihd,jhd->hij", query, key, preferred_element_type=WIDE) * scale_factor
    scores = scores + pair_bias + ((keep - 1.0) * MASK_FILL)[:, None, :]
    soft = jax.nn.softmax(scores, axis=-1)
    soft_low = low_of(soft)
    attended = jnp.einsum("hij,jhd->ihd", soft_low, value, preferred_element_type=WIDE)
    attended = low_of(attended.reshape(local_rows, heads_width))
    after_attn = start_node + dot_nn(attended, params["w_attn_out"])
    hat_two, scale_two = row_norm(after_attn)
    normed_two = low_of(hat_two * wide["gain_two"])
    act, slope = gelu_parts(dot_nn(normed_two, params["w_node_up"]))
    act_low = low_of(act)
    node_final = after_attn + dot_nn(act_low, params["w_node_down"])
    hat_three, scale_three = row_norm(node_final)
    normed_three = low_of(hat_three * wide["gain_three"])
    w_factors = jnp.concatenate([params["w_left_node"], params["w_right_node"]], axis=1)
    factors = low_of(dot_nn(normed_three, w_factors))

    factors_all = spread(factors, devices, BOTH)
    factors_all = lax.dynamic_slice_in_dim(factors_all, plane_crop * ranks, ranks, 0)
    left = lax.dynamic_index_in_dim(factors_all, plane_slot, 0, keepdims=False)[:, :OUTER]
    right = factors_all[:, :, OUTER:].reshape(length, OUTER)
    w_outer = params["w_outer"].reshape(OUTER, OUTER, PAIR_DIM)
    table = low_of(jnp.einsum("ip,pqe->ieq", left, w_outer, preferred_element_type=WIDE))

    column = lambda name: wide[name].reshape(-1, 1)
    sides_of = lambda prefix: jnp.concatenate(
        [params[prefix + "w_left"], params[prefix + "w_right"]], axis=1
    )
    all_of = lambda prefix: jnp.concatenate(
        [params[prefix + "w_left"], params[prefix + "w_right"], params[prefix + "w_gate"]], axis=1
    )
    tri_of = lambda prefix: (
        column(prefix + "gain_in"), params[prefix + "w_gate"], column(prefix + "gain_tri"),
        params[prefix + "w_tri_out"],
    )
    step_rows = min(TILE, local_rows)
    state = (local_rows, TRI_DIM, length)
    sides_shape = (ranks, 2 * share, local_rows, length)
    mixed_shape = (TRI_DIM, local_rows, length)
    natural = (local_rows, length, PAIR_DIM)
    buffer = lambda channels: pltpu.VMEM((step_rows, channels, length), LOW)
    trade = lambda blocks: exchange(blocks, BOTH, layout.groups)
    merge = lambda blocks: blocks.reshape(mixed_shape)
    split = lambda blocks: blocks.reshape(ranks, share, local_rows, length)
    unit = 2 * local_rows * length * PAIR_DIM * PAIR_DIM

    x_one, sides = run(
        kernel_open, step_rows, local_rows,
        (pair_plane, table, right.T, mask_plane, column("out_gain_in"), sides_of("out_")), "rrwrww",
        (("r", state, WIDE), ("s", sides_shape, LOW)), [buffer(2 * TRI_DIM)], 3 * unit,
    )
    sides_out = trade(sides)
    mixed_out = merge(trade(mix(sides_out, False)))
    x_two, sides = run(
        kernel_middle, step_rows, local_rows,
        (mixed_out, x_one, mask_plane, *tri_of("out_"), column("in_gain_in"), sides_of("in_")),
        "srr" + "wwww" + "ww",
        (("r", state, WIDE), ("s", sides_shape, LOW)),
        [buffer(TRI_DIM), buffer(2 * TRI_DIM)], 4 * unit,
    )
    sides_in = trade(sides)
    mixed_in = merge(trade(mix(sides_in, True)))
    square = (TRI_DIM, PAIR_DIM)
    gain_shape = (PAIR_DIM, 1)
    pair_final, x_grad, gate_grad, mixed_grad, g_in_out, g_in_tri, g_up, g_down, g_pair, g_bias = run(
        kernel_turn, step_rows, local_rows,
        (mixed_in, x_two, cot_plane, *tri_of("in_"), column("gain_pair"), params["w_pair_up"],
         params["w_pair_down"], column("bias_pair")),
        "srr" + "wwww" + "wwww",
        (("r", natural, LOW), ("r", state, WIDE), ("r", state, LOW), ("s", mixed_shape, LOW),
         ("a", square, WIDE), ("a", gain_shape, WIDE), ("a", (PAIR_DIM, FFN_PAIR), WIDE),
         ("a", (FFN_PAIR, PAIR_DIM), WIDE), ("a", gain_shape, WIDE), ("a", gain_shape, WIDE)),
        [buffer(TRI_DIM), buffer(TRI_DIM)], 32 * unit,
    )
    pair_out = lax.ppermute(pair_final, BOTH, layout.homeward)
    sides_grad = trade(mix_back(trade(split(mixed_grad)), sides_in, True))
    after_shape = (PAIR_DIM, 2 * TRI_DIM + PAIR_DIM)
    x_grad, gate_grad, mixed_grad, g_in_all, g_in_gain, g_out_out, g_out_tri = run(
        kernel_return, step_rows, local_rows,
        (sides_grad, x_two, gate_grad, x_grad, mask_plane, column("in_gain_in"), all_of("in_"),
         mixed_out, x_one, *tri_of("out_")),
        "srrrr" + "ww" + "sr" + "wwww",
        (("r", state, WIDE), ("r", state, LOW), ("s", mixed_shape, LOW), ("a", after_shape, WIDE),
         ("a", gain_shape, WIDE), ("a", square, WIDE), ("a", gain_shape, WIDE)),
        [buffer(2 * TRI_DIM), buffer(TRI_DIM), buffer(TRI_DIM)], 12 * unit,
    )
    sides_grad = trade(mix_back(trade(split(mixed_grad)), sides_out, False))
    pair_one_grad, table_grad, right_part, g_out_all, g_out_gain = run(
        kernel_close, step_rows, local_rows,
        (sides_grad, x_one, gate_grad, x_grad, mask_plane, column("out_gain_in"), all_of("out_"),
         table, right),
        "srrrr" + "ww" + "rw",
        (("r", natural, LOW), ("r", (local_rows, PAIR_DIM, OUTER), LOW), ("a", (OUTER, length), WIDE),
         ("a", after_shape, WIDE), ("a", gain_shape, WIDE)),
        [buffer(2 * TRI_DIM)], 8 * unit,
    )
    pair_one_home = lax.ppermute(pair_one_grad, BOTH, layout.homeward)

    left_grad = low_of(jnp.einsum("ieq,pqe->ip", table_grad, w_outer, preferred_element_type=WIDE))
    g_outer = jnp.einsum("ip,ieq->pqe", left, table_grad, preferred_element_type=WIDE)
    right_blocks = low_of(right_part.T).reshape(ranks, local_rows, OUTER)
    factor_blocks = jnp.concatenate(
        [jnp.broadcast_to(left_grad[None], right_blocks.shape), right_blocks], axis=2
    )
    factor_grads = exchange(jnp.tile(factor_blocks, (crops, 1, 1)), BOTH)
    factor_grads = factor_grads.reshape(crops, crops, layout.wide, local_rows, 2 * OUTER)
    factor_grads = lax.dynamic_index_in_dim(
        factor_grads, pick(layout.planes, crop_at), 1, keepdims=False
    ).reshape(ranks, local_rows, 2 * OUTER)
    left_rows = lax.dynamic_index_in_dim(
        factor_grads, pick(layout.slots, high_at) * layout.wide + wide_at, 0, keepdims=False
    )[:, :OUTER]
    right_rows = low_of(jnp.sum(factor_grads[:, :, OUTER:].astype(WIDE), axis=0))
    factor_rows = jnp.concatenate([left_rows, right_rows], axis=1)

    g_factors = dot_tn(normed_three, factor_rows)
    final_part, g_three = row_norm_back(
        dot_nt(factor_rows, w_factors), hat_three, scale_three, wide["gain_three"]
    )
    final_grad = node_cot.astype(WIDE) + final_part
    final_low = low_of(final_grad)
    g_node_down = dot_tn(act_low, final_low)
    hidden_grad = low_of(dot_nt(final_low, params["w_node_down"]) * slope)
    g_node_up = dot_tn(normed_two, hidden_grad)
    after_part, g_two = row_norm_back(
        dot_nt(hidden_grad, params["w_node_up"]), hat_two, scale_two, wide["gain_two"]
    )
    after_grad = final_grad + after_part
    after_low = low_of(after_grad)
    g_attn_out = dot_tn(attended, after_low)
    attended_grad = low_of(dot_nt(after_low, params["w_attn_out"]))
    attended_grad = attended_grad.reshape(local_rows, HEADS, HEAD_DIM)
    soft_grad = jnp.einsum("ihd,jhd->hij", attended_grad, value, preferred_element_type=WIDE)
    score_low = low_of(soft * (soft_grad - jnp.sum(soft_grad * soft, axis=-1, keepdims=True)))
    query_grad = jnp.einsum("hij,jhd->ihd", score_low, key, preferred_element_type=WIDE)
    key_part = jnp.einsum("hij,ihd->jhd", score_low, query, preferred_element_type=WIDE)
    value_part = jnp.einsum("hij,ihd->jhd", soft_low, attended_grad, preferred_element_type=WIDE)
    key_value = jnp.concatenate(
        [
            low_of(key_part.reshape(length, heads_width) * scale_factor),
            low_of(value_part.reshape(length, heads_width)),
        ],
        axis=1,
    )
    key_value = exchange(key_value.reshape(ranks, local_rows, 2 * heads_width), "row")
    key_value = low_of(jnp.sum(key_value.astype(WIDE), axis=0))
    query_low = low_of(query_grad.reshape(local_rows, heads_width) * scale_factor)
    g_bias_head = jnp.einsum("ijd,hij->dh", pair, score_low, preferred_element_type=WIDE)
    pair_grad = pair_one_home.astype(WIDE) + jnp.einsum(
        "hij,dh->ijd", score_low, params["w_bias"], preferred_element_type=WIDE
    )
    projections = jnp.concatenate([query_low, key_value], axis=1)
    g_projections = dot_tn(normed_one, projections)
    w_projections = jnp.concatenate([params["w_query"], params["w_key"], params["w_value"]], axis=1)
    start_part, g_one = row_norm_back(
        dot_nt(projections, w_projections), hat_one, scale_one, wide["gain_one"]
    )
    node_grad = after_grad + start_part
    g_embed = one_hot[0][:, None] * jnp.sum(node_grad, axis=0)[None, :]

    grads = {
        "embed": g_embed,
        "gain_one": g_one,
        "w_query": g_projections[:, :heads_width],
        "w_key": g_projections[:, heads_width : 2 * heads_width],
        "w_value": g_projections[:, 2 * heads_width :],
        "w_bias": g_bias_head,
        "w_attn_out": g_attn_out,
        "gain_two": g_two,
        "w_node_up": g_node_up,
        "w_node_down": g_node_down,
        "gain_three": g_three,
        "w_left_node": g_factors[:, :OUTER],
        "w_right_node": g_factors[:, OUTER:],
        "w_outer": g_outer,
        "gain_pair": g_pair,
        "w_pair_up": g_up,
        "w_pair_down": g_down,
        "bias_pair": g_bias,
    }
    for prefix, g_all, g_gain, g_tri, g_out in (
        ("out_", g_out_all, g_out_gain, g_out_tri, g_out_out),
        ("in_", g_in_all, g_in_gain, g_in_tri, g_in_out),
    ):
        grads[prefix + "gain_in"] = g_gain
        grads[prefix + "w_left"] = g_all[:, :TRI_DIM]
        grads[prefix + "w_right"] = g_all[:, TRI_DIM : 2 * TRI_DIM]
        grads[prefix + "w_gate"] = g_all[:, 2 * TRI_DIM :]
        grads[prefix + "gain_tri"] = g_tri
        grads[prefix + "w_tri_out"] = g_out
    flat_grad = jnp.concatenate(
        [low_of(grads[entry_name]).reshape(-1) for entry_name, entry_shape in segment_list()]
    )

    blocks = jnp.pad(flat_grad.reshape(devices, -1), ((0, 0), (0, padded - master.shape[0])))
    blocks = blocks.reshape(crops // 2, 2, ranks, padded // 128, 128)
    total = lambda got: low_of(jnp.sum(got.astype(WIDE), axis=0))
    blocks = total(exchange(jnp.swapaxes(blocks, 0, 1), BOTH, layout.cores))
    blocks = total(exchange(blocks, BOTH, layout.chips))
    blocks = jnp.sum(exchange(blocks, "row").astype(WIDE), axis=0)
    grad_own = blocks.reshape(-1)[: master.shape[0]]
    bias_total = jnp.sum(spread(g_bias.reshape(1, PAIR_DIM), devices, BOTH), axis=(0, 1))
    square = jnp.sum(grad_own * grad_own)
    squares = spread(jnp.full((1, 128), square), devices, BOTH)
    grad_norm = jnp.sqrt(jnp.sum(squares[:, 0, 0]))
    clipped = grad_own * (CLIP_NORM / jnp.maximum(grad_norm, CLIP_NORM))
    new_first = BETA_ONE * first + (1.0 - BETA_ONE) * clipped
    new_second = BETA_TWO * second + (1.0 - BETA_TWO) * clipped * clipped
    first_hat = new_first / (1.0 - BETA_ONE**ADAM_STEP)
    second_hat = new_second / (1.0 - BETA_TWO**ADAM_STEP)
    new_master = master - LEARN_RATE * (
        first_hat / (jnp.sqrt(second_hat) + ADAM_EPS) + WEIGHT_DECAY * master
    )
    return (
        low_of(node_final)[None],
        pair_out[None],
        low_of(node_grad)[None],
        low_of(pair_grad)[None],
        grad_own,
        bias_total,
        grad_norm,
        new_master,
        new_first,
        new_second,
        low_of(new_master),
    )


def solution(mesh):
    layout = Layout(mesh.shape["crop"], mesh.shape["row"])
    return jax.shard_map(
        lambda *arrays: local(layout, *arrays),
        mesh=mesh,
        in_specs=(
            P("crop", "row", None),
            P("crop", "row", None, None),
            P("crop"),
            P("crop", None),
            P("crop", "row", None),
            P("crop", "row", None, None),
            P(("crop", "row")),
            P(("crop", "row")),
            P(("crop", "row")),
        ),
        out_specs=(
            P("crop", "row", None),
            P("crop", "row", None, None),
            P("crop", "row", None),
            P("crop", "row", None, None),
            P(("crop", "row")),
            P(),
            P(),
            P(("crop", "row")),
            P(("crop", "row")),
            P(("crop", "row")),
            P(("crop", "row")),
        ),
        check_vma=False,
    )
```

```python
import math
from typing import Any, NamedTuple

import jax
import jax.numpy as jnp
import numpy as np
from jax import lax
from jax.experimental import pallas as pl
from jax.experimental.pallas import tpu as pltpu
from jax.sharding import PartitionSpec as P

NODE_DIM = 256
PAIR_DIM = 128
HEADS = 8
HEAD_DIM = 32
OUTER = 32
TRI_DIM = 128
FFN_NODE = 1024
FFN_PAIR = 512
RECYCLES = 4
ADAM_STEP = 3


EPS_NORM = 1e-05
ADAM_EPS = 1e-08
BETA_ONE = 0.9
BETA_TWO = 0.95
LEARN_RATE = 0.06
WEIGHT_DECAY = 0.1
CLIP_NORM = 1.0
MASK_FILL = 1000000000.0
HIGHEST = lax.Precision.HIGHEST


class Triangle(NamedTuple):
    gain_in: Any
    w_left: Any
    w_right: Any
    w_gate: Any
    gain_tri: Any
    w_tri_out: Any


class Params(NamedTuple):
    embed: Any
    gain_one: Any
    w_query: Any
    w_key: Any
    w_value: Any
    w_bias: Any
    w_attn_out: Any
    gain_two: Any
    w_node_up: Any
    w_node_down: Any
    gain_three: Any
    w_left_node: Any
    w_right_node: Any
    w_outer: Any
    outgoing: Triangle
    incoming: Triangle
    gain_pair: Any
    w_pair_up: Any
    w_pair_down: Any
    bias_pair: Any


LANES = 128
HEADS_WIDTH = HEADS * HEAD_DIM


def first_rows():
    square = PAIR_DIM * TRI_DIM
    triangle = Triangle(PAIR_DIM, square, square, PAIR_DIM * PAIR_DIM, TRI_DIM, square)
    sizes = Params(
        embed=RECYCLES * NODE_DIM,
        gain_one=NODE_DIM,
        w_query=NODE_DIM * HEADS_WIDTH,
        w_key=NODE_DIM * HEADS_WIDTH,
        w_value=NODE_DIM * HEADS_WIDTH,
        w_bias=PAIR_DIM * HEADS,
        w_attn_out=HEADS_WIDTH * NODE_DIM,
        gain_two=NODE_DIM,
        w_node_up=NODE_DIM * FFN_NODE,
        w_node_down=FFN_NODE * NODE_DIM,
        gain_three=NODE_DIM,
        w_left_node=NODE_DIM * OUTER,
        w_right_node=NODE_DIM * OUTER,
        w_outer=OUTER * OUTER * PAIR_DIM,
        outgoing=triangle,
        incoming=triangle,
        gain_pair=PAIR_DIM,
        w_pair_up=PAIR_DIM * FFN_PAIR,
        w_pair_down=FFN_PAIR * PAIR_DIM,
        bias_pair=PAIR_DIM,
    )
    leaves, tree = jax.tree.flatten(sizes)
    ends = np.cumsum(leaves) // LANES
    starts = [0] + [int(end) for end in ends[:-1]]
    return jax.tree.unflatten(tree, starts), int(ends[-1])


LOW = jnp.bfloat16
WIDE = jnp.float32
BOTH = ("crop", "row")
TILE = 16
VMEM_LIMIT = 56 * 2**20
INV_SQRT2 = 1.0 / math.sqrt(2.0)
INV_SQRT2PI = 1.0 / math.sqrt(2.0 * math.pi)


class Layout:
    def __init__(self, crops, rows):
        self.crops, self.rows = crops, rows
        self.devices = crops * rows
        self.wide = 2 ** (int(math.log2(rows)) // 2)
        self.high = rows // self.wide
        half = crops // 2
        self.moves = [
            (here, self.work_place(here))
            for here in range(self.devices)
            if here != self.work_place(here)
        ]
        self.groups = [
            [self.work_place(c * rows + r) for r in range(rows)] for c in range(crops)
        ]
        self.cores = [
            [(2 * x + k) * rows + r for k in range(2)] for x in range(half) for r in range(rows)
        ]
        self.chips = [
            [(2 * x + k) * rows + r for x in range(half)] for k in range(2) for r in range(rows)
        ]

    def work_place(self, here):
        crop, row = here // self.rows, here % self.rows
        high, wide = row // self.wide, row % self.wide
        core = crop % 2
        away = (high // (self.high // 2) + core) % 2
        crop = crop + away * (1 - 2 * core)
        high = high + away * (self.high - 1 - 2 * high)
        return crop * self.rows + high * self.wide + wide


def exchange(blocks, axes, groups=None):
    return lax.all_to_all(blocks, axes, 0, 0, axis_index_groups=groups, tiled=True)


def spread(part, count, axes, groups=None):
    return exchange(jnp.broadcast_to(part[None], (count,) + part.shape), axes, groups)


def dot_nn(a, b):
    return lax.dot_general(a, b, (((1,), (0,)), ((), ())), preferred_element_type=WIDE)


def dot_nt(a, b):
    return lax.dot_general(a, b, (((1,), (1,)), ((), ())), preferred_element_type=WIDE)


def dot_tn(a, b):
    return lax.dot_general(a, b, (((0,), (0,)), ((), ())), preferred_element_type=WIDE)


def norm_parts(x):
    centered = x - jnp.mean(x, axis=0, keepdims=True)
    scale = lax.rsqrt(jnp.mean(centered * centered, axis=0, keepdims=True) + EPS_NORM)
    return centered * scale, scale


def norm_back(grad, hat, scale, gain):
    grad_gain = jnp.sum(grad * hat, axis=1, keepdims=True)
    wide = grad * gain
    inner = jnp.mean(wide * hat, axis=0, keepdims=True)
    return scale * (wide - jnp.mean(wide, axis=0, keepdims=True) - hat * inner), grad_gain


def sigmoid(x):
    return 0.5 * jnp.tanh(0.5 * x) + 0.5


def column(row):
    return jnp.broadcast_to(row, (LANES, row.shape[1])).T[:, :1]


def row_of(values):
    return jnp.broadcast_to(values, (values.shape[0], LANES)).T[:1]


def cat(ref, start, count):
    return jnp.concatenate([ref[start + t] for t in range(count)], axis=1)


def put(ref, start, count, value):
    width = value.shape[1] // count
    for t in range(count):
        ref[start + t] = value[:, t * width : (t + 1) * width]


def swapped(value):
    if value.shape[0] % TILE or value.shape[1] % TILE:
        return jnp.swapaxes(value.astype(WIDE), 0, 1).astype(LOW)
    return jnp.swapaxes(value, 0, 1)


def cell_mask(mask_ref, start, count):
    return jnp.concatenate([mask_ref[start + t] for t in range(count)], axis=1)


def send_pair(scratch, out_ref):
    parts, share = out_ref.shape[0], out_ref.shape[1] // 2
    channels = parts * share
    for side in range(2):
        value = swapped(scratch[:, side * channels : (side + 1) * channels, :])
        out_ref[:, side * share : (side + 1) * share] = value.reshape(
            (parts, share) + value.shape[1:]
        )


def take_pair(in_ref, scratch):
    parts, share = in_ref.shape[0], in_ref.shape[1] // 2
    channels = parts * share
    for side in range(2):
        value = in_ref[:, side * share : (side + 1) * share]
        value = value.reshape((channels,) + value.shape[2:])
        scratch[:, side * channels : (side + 1) * channels, :] = swapped(value)


def front(x, gain, w_sides, mask):
    hat, _ = norm_parts(x)
    normed = (hat * gain).astype(LOW)
    return (dot_nn(w_sides, normed) * mask).astype(LOW)


def gate_of(x, gain, w_gate):
    hat, _ = norm_parts(x)
    return sigmoid(dot_nn(w_gate, (hat * gain).astype(LOW)))


def post(x, mixed, gain_in, w_gate, gain_tri, w_out):
    hat, _ = norm_parts(mixed)
    update = dot_nn(w_out, (hat * gain_tri).astype(LOW))
    return x + gate_of(x, gain_in, w_gate) * update


def post_back(grad, x, mixed, gain_in, w_gate, gain_tri, w_out, w_out_back):
    hat, scale = norm_parts(mixed)
    normed = (hat * gain_tri).astype(LOW)
    update = dot_nn(w_out, normed)
    gate = gate_of(x, gain_in, w_gate)
    update_grad = (grad * gate).astype(LOW)
    gate_grad = (grad * update * (gate * (1.0 - gate))).astype(LOW)
    grad_out = dot_nt(normed, update_grad)
    mixed_grad, grad_gain = norm_back(dot_nn(w_out_back, update_grad), hat, scale, gain_tri)
    return mixed_grad.astype(LOW), gate_grad, grad_out, grad_gain


def front_back(grad, x, sides_grad, gate_grad, mask, gain, w_all_back):
    hat, scale = norm_parts(x)
    normed = (hat * gain).astype(LOW)
    sides = jnp.concatenate([sides_grad * mask.astype(LOW), gate_grad], axis=0)
    grad_w = dot_nt(normed, sides)
    x_grad, grad_gain = norm_back(dot_nn(w_all_back, sides), hat, scale, gain)
    return grad + x_grad, grad_w, grad_gain


def gelu_parts(x):
    cumulative = 0.5 * lax.erf(x * INV_SQRT2) + 0.5
    density = INV_SQRT2PI * jnp.exp(-0.5 * x * x)
    return x * cumulative, cumulative + x * density


def zero_first(*refs):
    @pl.when(pl.program_id(0) == 0)
    def _():
        for ref in refs:
            ref[...] = jnp.zeros_like(ref)


def run(body, step_rows, rows, in_arrays, in_kinds, outs, scratch, flops):
    def spec(kind, shape):
        if kind == "r":
            return pl.BlockSpec((step_rows,) + shape[1:], lambda i: (i,) + (0,) * (len(shape) - 1))
        if kind == "s":
            return pl.BlockSpec(
                shape[:-2] + (step_rows, shape[-1]),
                lambda i: (0,) * (len(shape) - 2) + (i, 0),
            )
        return pl.BlockSpec(shape, lambda i: (0,) * len(shape))

    moved = sum(a.size * a.dtype.itemsize for a in in_arrays)
    return pl.pallas_call(
        body,
        grid=(rows // step_rows,),
        in_specs=[spec(kind, a.shape) for kind, a in zip(in_kinds, in_arrays)],
        out_specs=[spec(kind, shape) for kind, shape, _ in outs],
        out_shape=[jax.ShapeDtypeStruct(shape, dtype) for _, shape, dtype in outs],
        scratch_shapes=scratch,
        compiler_params=pltpu.CompilerParams(vmem_limit_bytes=VMEM_LIMIT),
        cost_estimate=pl.CostEstimate(flops=flops, bytes_accessed=moved, transcendentals=0),
    )(*in_arrays)


def loop(count, body):
    def step(t, carry):
        body(t)
        return carry

    lax.fori_loop(0, count, step, 0)


GROUP = 2


def sides_low(w):
    return jnp.concatenate([w[:PAIR_DIM].T, w[PAIR_DIM : 2 * PAIR_DIM].T], axis=0)


def all_back(w):
    return jnp.concatenate([w[k * PAIR_DIM : (k + 1) * PAIR_DIM] for k in range(3)], axis=1)


def kernel_open(pair, table, right, mask, gain, w_sides, x_out, sides_out, scratch):
    rows = pair.shape[0]
    group = min(GROUP, rows)
    w_low = sides_low(w_sides)
    right_low = right[...]
    gain_low = column(gain[...])

    def step(t):
        at = t * group
        x = jnp.concatenate(
            [
                pair[at + k].T.astype(WIDE) + dot_nn(table[at + k], right_low)
                for k in range(group)
            ],
            axis=1,
        )
        put(x_out, at, group, x)
        put(scratch, at, group, front(x, gain_low, w_low, cell_mask(mask, at, group)))

    loop(rows // group, step)
    send_pair(scratch, sides_out)


def kernel_middle(
    mixed, x_in, mask, gain_in, w_gate, gain_tri, w_out, gain_next, w_sides, x_out, sides_out,
    arrived, scratch,
):
    rows = x_in.shape[0]
    group = min(GROUP, rows)
    arrived[...] = swapped(mixed[...])
    w_low, gate_low, out_low = sides_low(w_sides), w_gate[...].T, w_out[...].T
    in_col, tri_col, next_col = column(gain_in[...]), column(gain_tri[...]), column(gain_next[...])

    def step(t):
        at = t * group
        x = post(
            cat(x_in, at, group), cat(arrived, at, group).astype(WIDE),
            in_col, gate_low, tri_col, out_low,
        )
        put(x_out, at, group, x)
        put(scratch, at, group, front(x, next_col, w_low, cell_mask(mask, at, group)))

    loop(rows // group, step)
    send_pair(scratch, sides_out)


def kernel_turn(
    mixed, x_in, cot, gain_in, w_gate, gain_tri, w_out, gain_pair, w_up, w_down, bias,
    pair_out, x_grad, gate_grad, mixed_grad, g_out, g_tri, g_up, g_down, g_pair, g_bias,
    arrived, leaving,
):
    rows = x_in.shape[0]
    group = min(GROUP, rows)
    arrived[...] = swapped(mixed[...])
    gate_low, out_low, out_back = w_gate[...].T, w_out[...].T, w_out[...]
    up_low, up_back = w_up[...].T, w_up[...]
    down_low, down_back = w_down[...].T, w_down[...]
    in_col, tri_col = column(gain_in[...]), column(gain_tri[...])
    pair_col, bias_col = column(gain_pair[...]), column(bias[...])
    zero_first(g_out, g_tri, g_up, g_down, g_pair, g_bias)
    chunk = PAIR_DIM

    def step(t):
        at = t * group
        x_two = cat(x_in, at, group)
        mix = cat(arrived, at, group).astype(WIDE)
        x = post(x_two, mix, in_col, gate_low, tri_col, out_low)
        hat, scale = norm_parts(x)
        normed = (hat * pair_col).astype(LOW)
        cot_low = jnp.concatenate([cot[at + k].T for k in range(group)], axis=1)
        total = x + bias_col
        normed_grad = jnp.zeros_like(x)
        for c in range(FFN_PAIR // chunk):
            part = slice(c * chunk, (c + 1) * chunk)
            act, slope = gelu_parts(dot_nn(up_low[part], normed))
            act_low = act.astype(LOW)
            total = total + dot_nn(down_low[:, part], act_low)
            hidden_grad = (dot_nn(down_back[part], cot_low) * slope).astype(LOW)
            normed_grad = normed_grad + dot_nn(up_back[:, part], hidden_grad)
            g_up[:, part] += dot_nt(normed, hidden_grad)
            g_down[part] += dot_nt(act_low, cot_low)
        total_low = total.astype(LOW)
        width = total.shape[1] // group
        for k in range(group):
            pair_out[at + k] = total_low[:, k * width : (k + 1) * width].T
        cot_wide = cot_low.astype(WIDE)
        g_bias[...] += jnp.sum(cot_wide, axis=1, keepdims=True)
        back, grad_gain = norm_back(normed_grad, hat, scale, pair_col)
        g_pair[...] += grad_gain
        grad = cot_wide + back
        put(x_grad, at, group, grad)
        mix_grad, gates, grad_out, grad_tri = post_back(
            grad, x_two, mix, in_col, gate_low, tri_col, out_low, out_back
        )
        put(leaving, at, group, mix_grad)
        put(gate_grad, at, group, gates)
        g_out[...] += grad_out
        g_tri[...] += grad_tri

    loop(rows // group, step)
    mixed_grad[...] = swapped(leaving[...])


def kernel_return(
    sides_grad, x_after, gate_after, grad_in, mask, gain_after, w_after, mixed, x_before,
    gain_in, w_gate, gain_tri, w_out,
    x_grad, gate_grad, mixed_grad, g_after, g_gain, g_out, g_tri,
    sides, arrived, leaving,
):
    rows = x_after.shape[0]
    group = min(GROUP, rows)
    take_pair(sides_grad, sides)
    arrived[...] = swapped(mixed[...])
    gate_low, out_low, out_back = w_gate[...].T, w_out[...].T, w_out[...]
    in_col, tri_col, after_col = column(gain_in[...]), column(gain_tri[...]), column(gain_after[...])
    after_back = all_back(w_after)
    zero_first(g_after, g_gain, g_out, g_tri)

    def step(t):
        at = t * group
        grad, grad_w, grad_gain = front_back(
            cat(grad_in, at, group), cat(x_after, at, group), cat(sides, at, group),
            cat(gate_after, at, group), cell_mask(mask, at, group), after_col, after_back,
        )
        g_after[...] += grad_w
        g_gain[...] += grad_gain
        put(x_grad, at, group, grad)
        mix_grad, gates, grad_out, grad_tri = post_back(
            grad, cat(x_before, at, group), cat(arrived, at, group).astype(WIDE),
            in_col, gate_low, tri_col, out_low, out_back,
        )
        put(leaving, at, group, mix_grad)
        put(gate_grad, at, group, gates)
        g_out[...] += grad_out
        g_tri[...] += grad_tri

    loop(rows // group, step)
    mixed_grad[...] = swapped(leaving[...])


def kernel_close(
    sides_grad, x_after, gate_after, grad_in, mask, gain_after, w_after, table, right,
    pair_grad, table_grad, right_grad, g_after, g_gain, sides,
):
    rows = x_after.shape[0]
    group = min(GROUP, rows)
    take_pair(sides_grad, sides)
    after_col, after_back = column(gain_after[...]), all_back(w_after)
    zero_first(g_after, g_gain, right_grad)

    def step(t):
        at = t * group
        grad, grad_w, grad_gain = front_back(
            cat(grad_in, at, group), cat(x_after, at, group), cat(sides, at, group),
            cat(gate_after, at, group), cell_mask(mask, at, group), after_col, after_back,
        )
        g_after[...] += grad_w
        g_gain[...] += grad_gain
        low = grad.astype(LOW)
        width = low.shape[1] // group
        for k in range(group):
            own = low[:, k * width : (k + 1) * width]
            pair_grad[at + k] = own.T
            table_grad[at + k] = dot_nn(own, right[...]).astype(LOW)
            right_grad[...] += dot_tn(table[at + k], own)

    loop(rows // group, step)


CHANNELS = 4


def kernel_mix(incoming, left, right, out):
    parts, count, rows, length = out.shape
    for c in range(count):
        a = left[:, c].reshape(length, length)
        b = right[:, c].reshape(length, length)
        mixed = dot_tn(a, b) if incoming else dot_nt(a, b)
        out[:, c] = mixed.astype(LOW).reshape(parts, rows, length)


def kernel_mix_back(incoming, grad, left, right, out):
    parts, count, rows, length = grad.shape
    for c in range(count):
        g = grad[:, c].reshape(length, length)
        a = left[:, c].reshape(length, length)
        b = right[:, c].reshape(length, length)
        a_grad = dot_nt(b, g) if incoming else dot_nn(g, b)
        b_grad = dot_nn(a, g) if incoming else dot_tn(g, a)
        out[:, 0, c] = a_grad.astype(LOW).reshape(parts, rows, length)
        out[:, 1, c] = b_grad.astype(LOW).reshape(parts, rows, length)


def mix(sides, incoming):
    parts, double, rows, length = sides.shape
    share = double // 2
    count = min(CHANNELS, share)
    steps = share // count
    block = (parts, count, rows, length)
    return pl.pallas_call(
        lambda *refs: kernel_mix(incoming, *refs),
        grid=(steps,),
        in_specs=[
            pl.BlockSpec(block, lambda c: (0, c, 0, 0)),
            pl.BlockSpec(block, lambda c: (0, c + steps, 0, 0)),
        ],
        out_specs=pl.BlockSpec(block, lambda c: (0, c, 0, 0)),
        out_shape=jax.ShapeDtypeStruct((parts, share, rows, length), LOW),
        compiler_params=pltpu.CompilerParams(vmem_limit_bytes=VMEM_LIMIT),
        cost_estimate=pl.CostEstimate(
            flops=2 * share * length**3, bytes_accessed=3 * share * length * length * 2,
            transcendentals=0,
        ),
    )(sides, sides)


def mix_back(grad, sides, incoming):
    parts, double, rows, length = sides.shape
    share = double // 2
    count = min(CHANNELS, share)
    steps = share // count
    block = (parts, count, rows, length)
    out = pl.pallas_call(
        lambda *refs: kernel_mix_back(incoming, *refs),
        grid=(steps,),
        in_specs=[
            pl.BlockSpec(block, lambda c: (0, c, 0, 0)),
            pl.BlockSpec(block, lambda c: (0, c, 0, 0)),
            pl.BlockSpec(block, lambda c: (0, c + steps, 0, 0)),
        ],
        out_specs=pl.BlockSpec((parts, 2, count, rows, length), lambda c: (0, 0, c, 0, 0)),
        out_shape=jax.ShapeDtypeStruct((parts, 2, share, rows, length), LOW),
        compiler_params=pltpu.CompilerParams(vmem_limit_bytes=VMEM_LIMIT),
        cost_estimate=pl.CostEstimate(
            flops=4 * share * length**3, bytes_accessed=5 * share * length * length * 2,
            transcendentals=0,
        ),
    )(grad, sides, sides)
    return out.reshape(sides.shape)


def share_rows(share):
    return -(-(share + 2 * LANES) // (TILE * LANES)) * TILE


def whole(shape):
    return pl.BlockSpec(shape, lambda *_: (0,) * len(shape))


def one_call(body, in_arrays, outs, scratch):
    return pl.pallas_call(
        body,
        in_specs=[whole(a.shape) for a in in_arrays],
        out_specs=[whole(shape) for shape, _ in outs],
        out_shape=[jax.ShapeDtypeStruct(shape, dtype) for shape, dtype in outs],
        scratch_shapes=scratch,
        grid=(1,),
        compiler_params=pltpu.CompilerParams(vmem_limit_bytes=VMEM_LIMIT),
    )(*in_arrays)


def share_order(layout):
    return [((d // layout.rows) % 2, d // (2 * layout.rows), d % layout.rows) for d in range(layout.devices)]


def unpack(layout, shares, share):
    at, total = first_rows()
    height = shares.shape[3]
    first = [share * d // LANES for d in range(layout.devices)]
    order = share_order(layout)
    matrices = [
        (NODE_DIM, 3, 3 * HEADS_WIDTH), (HEADS_WIDTH, 1, NODE_DIM), (NODE_DIM, 1, FFN_NODE),
        (FFN_NODE, 1, NODE_DIM), (PAIR_DIM, 1, FFN_PAIR),
    ]
    places = [at.w_query, at.w_attn_out, at.w_node_up, at.w_node_down, at.w_pair_up]

    def body(shares_ref, flat_out, *rest):
        outs, flat = rest[:-1], rest[-1]
        for d, place in enumerate(order):
            block = shares_ref[place].astype(WIDE)
            if d:
                tail = flat[first[d] : first[d] + 1]
                flat[first[d] : first[d] + height] = block
                flat[first[d] : first[d] + 1] = block[:1] + tail
            else:
                flat[:height] = block
        flat_out[...] = flat[: flat_out.shape[0]].astype(LOW)
        for out, place, (rows, count, width) in zip(outs, places, matrices):
            pieces = width // count // LANES
            for m in range(count):
                for a in range(pieces):
                    start = place + m * rows * pieces + a
                    value = flat[pl.ds(start, rows, stride=pieces), :] if pieces > 1 else flat[start : start + rows]
                    lane = (m * pieces + a) * LANES
                    out[:, lane : lane + LANES] = value.astype(LOW)

    flat_rows = -(-total // TILE) * TILE
    return one_call(
        body,
        (shares,),
        [((flat_rows, LANES), LOW)] + [((rows, width), LOW) for rows, _, width in matrices],
        [pltpu.VMEM((first[-1] + height + TILE, LANES), WIDE)],
    )


def pack(layout, grads, share):
    _, total = first_rows()
    height = share_rows(share)
    first = [share * d // LANES for d in range(layout.devices)]
    order = share_order(layout)

    def body(*refs):
        ins, out, flat = refs[:-2], refs[-2], refs[-1]
        flat[total:] = jnp.zeros((flat.shape[0] - total, LANES), WIDE)
        for ref, (place, count, _) in zip(ins, grads):
            if ref.shape[1] == 1:
                flat[place : place + 1] = row_of(ref[...])
                continue
            rows, pieces = ref.shape[0], ref.shape[1] // count // LANES
            for m in range(count):
                for a in range(pieces):
                    lane = (m * pieces + a) * LANES
                    value = ref[:, lane : lane + LANES]
                    start = place + m * rows * pieces + a
                    if pieces > 1 and rows > 1:
                        flat[pl.ds(start, rows, stride=pieces), :] = value
                    else:
                        flat[start : start + rows] = value
        for d, where in enumerate(order):
            out[where] = flat[first[d] : first[d] + height].astype(LOW)

    shape = (2, layout.crops // 2, layout.rows, height, LANES)
    return one_call(
        body,
        tuple(array for _, _, array in grads),
        [(shape, LOW)],
        [pltpu.VMEM((first[-1] + height + TILE, LANES), WIDE)],
    )[0]


def row_norm(x):
    centered = x - jnp.mean(x, axis=-1, keepdims=True)
    scale = lax.rsqrt(jnp.mean(centered * centered, axis=-1, keepdims=True) + EPS_NORM)
    return centered * scale, scale


def row_norm_back(grad, hat, scale, gain):
    grad_gain = jnp.sum(grad * hat, axis=0)
    wide = grad * gain
    inner = jnp.mean(wide * hat, axis=-1, keepdims=True)
    return scale * (wide - jnp.mean(wide, axis=-1, keepdims=True) - hat * inner), grad_gain


def low_of(x):
    return x.astype(LOW)


def local(layout, node, pair, recycle, mask, node_cot, pair_cot, master, first, second):
    crops, ranks = layout.crops, layout.rows
    devices = crops * ranks
    local_rows, length = node.shape[1], pair.shape[2]
    share = TRI_DIM // ranks
    heads_width = HEADS * HEAD_DIM
    scale_factor = HEAD_DIM ** (-0.5)
    node, pair, node_cot, pair_cot = node[0], pair[0], node_cot[0], pair_cot[0]

    crop_at, row_at = lax.axis_index("crop"), lax.axis_index("row")
    here = crop_at * ranks + row_at
    partner = layout.work_place(here)
    stays = partner == here
    work_crop, work_row = partner // ranks, partner % ranks
    moved = lambda array: jnp.where(stays, array, lax.ppermute(array, BOTH, layout.moves))

    amount = master.shape[0]
    height = share_rows(amount)
    offset = (here * (amount % LANES)) % LANES
    shard = lax.dynamic_update_slice(jnp.zeros(height * LANES, LOW), low_of(master), (offset,))
    shards = spread(shard.reshape(height, LANES), ranks, "row")
    shards = spread(shards, crops // 2, BOTH, layout.chips)
    shards = spread(shards, 2, BOTH, layout.cores)
    shards = shards.reshape(2, crops // 2, ranks, height, LANES)
    flat, w_projections, w_attn_out, w_node_up, w_node_down, w_pair_up = unpack(
        layout, shards, amount
    )
    at, _ = first_rows()
    rows_from = lambda start, count: lax.slice_in_dim(flat, start, start + count, axis=0)
    wide_row = lambda start, count=1: rows_from(start, count).astype(WIDE).reshape(1, -1)
    narrow = lambda start, count, width: lax.optimization_barrier(rows_from(start, count)).reshape(-1, width)
    w_bias = narrow(at.w_bias, HEADS, HEADS)
    w_factors = narrow(at.w_left_node, 2 * NODE_DIM * OUTER // LANES, OUTER)
    w_factors = jnp.concatenate([w_factors[:NODE_DIM], w_factors[NODE_DIM:]], axis=1)
    embed = rows_from(at.embed, 2 * RECYCLES).astype(WIDE).reshape(RECYCLES, NODE_DIM)
    gain_one, gain_two, gain_three = (
        wide_row(start, NODE_DIM // LANES) for start in (at.gain_one, at.gain_two, at.gain_three)
    )
    node_all = spread(node, ranks, "row").reshape(length, NODE_DIM)
    pair_plane, cot_plane = moved(pair), moved(pair_cot)
    keep = mask.astype(WIDE)
    keep_plane = moved(keep)
    keep_rows = lax.dynamic_slice_in_dim(keep_plane[0], work_row * local_rows, local_rows, 0)
    mask_plane = (keep_rows[:, None] * keep_plane)[:, None, :]

    one_hot = (recycle[:, None] == jnp.arange(RECYCLES, dtype=jnp.int32)[None, :]).astype(WIDE)
    start_all = node_all.astype(WIDE) + jnp.matmul(one_hot, embed, precision=HIGHEST)
    hat_all, scale_all = row_norm(start_all)
    normed_all = low_of(hat_all * gain_one)
    own = lambda a: lax.dynamic_slice_in_dim(a, row_at * local_rows, local_rows, 0)
    start_node, hat_one, scale_one, normed_one = (
        own(a) for a in (start_all, hat_all, scale_all, normed_all)
    )
    query = low_of(dot_nn(normed_one, w_projections[:, :heads_width]))
    query = query.reshape(local_rows, HEADS, HEAD_DIM)
    key_value = low_of(dot_nn(normed_all, w_projections[:, heads_width:]))
    key = key_value[:, :heads_width].reshape(length, HEADS, HEAD_DIM)
    value = key_value[:, heads_width:].reshape(length, HEADS, HEAD_DIM)
    pair_bias = jnp.einsum("ijd,dh->hij", pair, w_bias, preferred_element_type=WIDE)
    scores = jnp.einsum("ihd,jhd->hij", query, key, preferred_element_type=WIDE) * scale_factor
    scores = scores + pair_bias + ((keep - 1.0) * MASK_FILL)[:, None, :]
    soft = jax.nn.softmax(scores, axis=-1)
    soft_low = low_of(soft)
    attended = jnp.einsum("hij,jhd->ihd", soft_low, value, preferred_element_type=WIDE)
    attended = low_of(attended.reshape(local_rows, heads_width))
    after_attn = start_node + dot_nn(attended, w_attn_out)
    hat_two, scale_two = row_norm(after_attn)
    normed_two = low_of(hat_two * gain_two)
    act, slope = gelu_parts(dot_nn(normed_two, w_node_up))
    act_low = low_of(act)
    node_final = after_attn + dot_nn(act_low, w_node_down)
    hat_three, scale_three = row_norm(node_final)
    normed_three = low_of(hat_three * gain_three)
    factors = low_of(dot_nn(normed_three, w_factors))

    factors_all = spread(factors, devices, BOTH)
    factors_all = lax.dynamic_slice_in_dim(factors_all, work_crop * ranks, ranks, 0)
    left = lax.dynamic_index_in_dim(factors_all, work_row, 0, keepdims=False)[:, :OUTER]
    right = factors_all[:, :, OUTER:].reshape(length, OUTER)
    w_outer = rows_from(at.w_outer, OUTER * OUTER).reshape(OUTER, OUTER, PAIR_DIM)
    table = low_of(jnp.einsum("ip,pqe->ieq", left, w_outer, preferred_element_type=WIDE))

    gain_row = lambda start: wide_row(start)
    matrix = lambda start, rows=PAIR_DIM: rows_from(start, rows)
    sides_of = lambda tri: matrix(tri.w_left, 2 * PAIR_DIM)
    all_of = lambda tri: matrix(tri.w_left, 3 * PAIR_DIM)
    tri_of = lambda tri: (
        gain_row(tri.gain_in), matrix(tri.w_gate), gain_row(tri.gain_tri), matrix(tri.w_tri_out)
    )
    step_rows = min(TILE, local_rows)
    state = (local_rows, TRI_DIM, length)
    sides_shape = (ranks, 2 * share, local_rows, length)
    mixed_shape = (TRI_DIM, local_rows, length)
    natural = (local_rows, length, PAIR_DIM)
    buffer = lambda channels: pltpu.VMEM((step_rows, channels, length), LOW)
    trade = lambda blocks: exchange(blocks, BOTH, layout.groups)
    merge = lambda blocks: blocks.reshape(mixed_shape)
    split = lambda blocks: blocks.reshape(ranks, share, local_rows, length)
    unit = 2 * local_rows * length * PAIR_DIM * PAIR_DIM

    x_one, sides = run(
        kernel_open, step_rows, local_rows,
        (pair_plane, table, right.T, mask_plane, gain_row(at.outgoing.gain_in), sides_of(at.outgoing)), "rrwrww",
        (("r", state, WIDE), ("s", sides_shape, LOW)), [buffer(2 * TRI_DIM)], 3 * unit,
    )
    sides_out = trade(sides)
    mixed_out = merge(trade(mix(sides_out, False)))
    x_two, sides = run(
        kernel_middle, step_rows, local_rows,
        (mixed_out, x_one, mask_plane, *tri_of(at.outgoing), gain_row(at.incoming.gain_in), sides_of(at.incoming)),
        "srr" + "wwww" + "ww",
        (("r", state, WIDE), ("s", sides_shape, LOW)),
        [buffer(TRI_DIM), buffer(2 * TRI_DIM)], 4 * unit,
    )
    sides_in = trade(sides)
    mixed_in = merge(trade(mix(sides_in, True)))
    square = (TRI_DIM, PAIR_DIM)
    gain_shape = (PAIR_DIM, 1)
    pair_final, x_grad, gate_grad, mixed_grad, g_in_out, g_in_tri, g_up, g_down, g_pair, g_bias = run(
        kernel_turn, step_rows, local_rows,
        (mixed_in, x_two, cot_plane, *tri_of(at.incoming), gain_row(at.gain_pair), w_pair_up,
         matrix(at.w_pair_down, FFN_PAIR), gain_row(at.bias_pair)),
        "srr" + "wwww" + "wwww",
        (("r", natural, LOW), ("r", state, WIDE), ("r", state, LOW), ("s", mixed_shape, LOW),
         ("a", square, WIDE), ("a", gain_shape, WIDE), ("a", (PAIR_DIM, FFN_PAIR), WIDE),
         ("a", (FFN_PAIR, PAIR_DIM), WIDE), ("a", gain_shape, WIDE), ("a", gain_shape, WIDE)),
        [buffer(TRI_DIM), buffer(TRI_DIM)], 32 * unit,
    )
    pair_out = moved(pair_final)
    sides_grad = trade(mix_back(trade(split(mixed_grad)), sides_in, True))
    after_shape = (PAIR_DIM, 2 * TRI_DIM + PAIR_DIM)
    x_grad, gate_grad, mixed_grad, g_in_all, g_in_gain, g_out_out, g_out_tri = run(
        kernel_return, step_rows, local_rows,
        (sides_grad, x_two, gate_grad, x_grad, mask_plane, gain_row(at.incoming.gain_in), all_of(at.incoming),
         mixed_out, x_one, *tri_of(at.outgoing)),
        "srrrr" + "ww" + "sr" + "wwww",
        (("r", state, WIDE), ("r", state, LOW), ("s", mixed_shape, LOW), ("a", after_shape, WIDE),
         ("a", gain_shape, WIDE), ("a", square, WIDE), ("a", gain_shape, WIDE)),
        [buffer(2 * TRI_DIM), buffer(TRI_DIM), buffer(TRI_DIM)], 12 * unit,
    )
    sides_grad = trade(mix_back(trade(split(mixed_grad)), sides_out, False))
    pair_one_grad, table_grad, right_part, g_out_all, g_out_gain = run(
        kernel_close, step_rows, local_rows,
        (sides_grad, x_one, gate_grad, x_grad, mask_plane, gain_row(at.outgoing.gain_in), all_of(at.outgoing),
         table, right),
        "srrrr" + "ww" + "rw",
        (("r", natural, LOW), ("r", (local_rows, PAIR_DIM, OUTER), LOW), ("a", (OUTER, length), WIDE),
         ("a", after_shape, WIDE), ("a", gain_shape, WIDE)),
        [buffer(2 * TRI_DIM)], 8 * unit,
    )
    pair_one_home = moved(pair_one_grad)

    left_grad = low_of(jnp.einsum("ieq,pqe->ip", table_grad, w_outer, preferred_element_type=WIDE))
    g_outer = jnp.einsum("ip,ieq->pqe", left, table_grad, preferred_element_type=WIDE)
    right_blocks = low_of(right_part.T).reshape(ranks, local_rows, OUTER)
    factor_blocks = jnp.concatenate(
        [jnp.broadcast_to(left_grad[None], right_blocks.shape), right_blocks], axis=2
    )
    factor_grads = exchange(jnp.tile(factor_blocks, (crops, 1, 1)), BOTH)
    left_rows = lax.dynamic_index_in_dim(factor_grads, partner, 0, keepdims=False)[:, :OUTER]
    factor_grads = lax.dynamic_slice_in_dim(factor_grads, (crop_at // 2) * 2 * ranks, 2 * ranks, 0)
    factor_grads = factor_grads.reshape(2, 2, ranks // 2, local_rows, 2 * OUTER)
    factor_grads = lax.dynamic_index_in_dim(factor_grads, crop_at % 2, 1, keepdims=False)
    factor_grads = factor_grads.reshape(ranks, local_rows, 2 * OUTER)
    right_rows = low_of(jnp.sum(factor_grads[:, :, OUTER:].astype(WIDE), axis=0))
    factor_rows = jnp.concatenate([left_rows, right_rows], axis=1)

    g_factors = dot_tn(normed_three, factor_rows)
    final_part, g_three = row_norm_back(
        dot_nt(factor_rows, w_factors), hat_three, scale_three, gain_three
    )
    final_grad = node_cot.astype(WIDE) + final_part
    final_low = low_of(final_grad)
    g_node_down = dot_tn(act_low, final_low)
    hidden_grad = low_of(dot_nt(final_low, w_node_down) * slope)
    g_node_up = dot_tn(normed_two, hidden_grad)
    after_part, g_two = row_norm_back(
        dot_nt(hidden_grad, w_node_up), hat_two, scale_two, gain_two
    )
    after_grad = final_grad + after_part
    after_low = low_of(after_grad)
    g_attn_out = dot_tn(attended, after_low)
    attended_grad = low_of(dot_nt(after_low, w_attn_out))
    attended_grad = attended_grad.reshape(local_rows, HEADS, HEAD_DIM)
    soft_grad = jnp.einsum("ihd,jhd->hij", attended_grad, value, preferred_element_type=WIDE)
    score_low = low_of(soft * (soft_grad - jnp.sum(soft_grad * soft, axis=-1, keepdims=True)))
    query_grad = jnp.einsum("hij,jhd->ihd", score_low, key, preferred_element_type=WIDE)
    key_part = jnp.einsum("hij,ihd->jhd", score_low, query, preferred_element_type=WIDE)
    value_part = jnp.einsum("hij,ihd->jhd", soft_low, attended_grad, preferred_element_type=WIDE)
    key_value = jnp.concatenate(
        [
            low_of(key_part.reshape(length, heads_width) * scale_factor),
            low_of(value_part.reshape(length, heads_width)),
        ],
        axis=1,
    )
    key_value = exchange(key_value.reshape(ranks, local_rows, 2 * heads_width), "row")
    key_value = low_of(jnp.sum(key_value.astype(WIDE), axis=0))
    query_low = low_of(query_grad.reshape(local_rows, heads_width) * scale_factor)
    g_bias_head = jnp.einsum("ijd,hij->dh", pair, score_low, preferred_element_type=WIDE)
    pair_grad = pair_one_home.astype(WIDE) + jnp.einsum(
        "hij,dh->ijd", score_low, w_bias, preferred_element_type=WIDE
    )
    projections = jnp.concatenate([query_low, key_value], axis=1)
    g_projections = dot_tn(normed_one, projections)
    start_part, g_one = row_norm_back(
        dot_nt(projections, w_projections), hat_one, scale_one, gain_one
    )
    node_grad = after_grad + start_part
    g_embed = one_hot[0][:, None] * jnp.sum(node_grad, axis=0)[None, :]

    as_rows = lambda array: lax.optimization_barrier(array).reshape(-1, LANES)
    grads = [
        (at.embed, 1, g_embed),
        (at.gain_one, 1, g_one[None]),
        (at.w_query, 3, g_projections),
        (at.w_bias, 1, as_rows(g_bias_head)),
        (at.w_attn_out, 1, g_attn_out),
        (at.gain_two, 1, g_two[None]),
        (at.w_node_up, 1, g_node_up),
        (at.w_node_down, 1, g_node_down),
        (at.gain_three, 1, g_three[None]),
        (at.w_left_node, 1, as_rows(g_factors[:, :OUTER])),
        (at.w_right_node, 1, as_rows(g_factors[:, OUTER:])),
        (at.w_outer, 1, g_outer.reshape(OUTER * OUTER, PAIR_DIM)),
        (at.gain_pair, 1, g_pair),
        (at.w_pair_up, 1, g_up),
        (at.w_pair_down, 1, g_down),
        (at.bias_pair, 1, g_bias),
    ]
    for tri, g_all, g_gain, g_tri, g_out in (
        (at.outgoing, g_out_all, g_out_gain, g_out_tri, g_out_out),
        (at.incoming, g_in_all, g_in_gain, g_in_tri, g_in_out),
    ):
        grads += [
            (tri.gain_in, 1, g_gain),
            (tri.w_left, 3, g_all),
            (tri.gain_tri, 1, g_tri),
            (tri.w_tri_out, 1, g_out),
        ]

    blocks = pack(layout, grads, amount)
    total = lambda got: low_of(jnp.sum(got.astype(WIDE), axis=0))
    blocks = total(exchange(blocks, BOTH, layout.cores))
    blocks = total(exchange(blocks, BOTH, layout.chips))
    blocks = jnp.sum(exchange(blocks, "row").astype(WIDE), axis=0)
    grad_own = lax.dynamic_slice(blocks.reshape(-1), (offset,), (amount,))
    bias_total = jnp.sum(spread(g_bias.reshape(1, PAIR_DIM), devices, BOTH), axis=(0, 1))
    square_own = jnp.sum(grad_own * grad_own)
    squares = spread(jnp.full((1, LANES), square_own), devices, BOTH)
    grad_norm = jnp.sqrt(jnp.sum(squares[:, 0, 0]))
    clipped = grad_own * (CLIP_NORM / jnp.maximum(grad_norm, CLIP_NORM))
    new_first = BETA_ONE * first + (1.0 - BETA_ONE) * clipped
    new_second = BETA_TWO * second + (1.0 - BETA_TWO) * clipped * clipped
    first_hat = new_first / (1.0 - BETA_ONE**ADAM_STEP)
    second_hat = new_second / (1.0 - BETA_TWO**ADAM_STEP)
    new_master = master - LEARN_RATE * (
        first_hat / (jnp.sqrt(second_hat) + ADAM_EPS) + WEIGHT_DECAY * master
    )
    return (
        low_of(node_final)[None],
        pair_out[None],
        low_of(node_grad)[None],
        low_of(pair_grad)[None],
        grad_own,
        bias_total,
        grad_norm,
        new_master,
        new_first,
        new_second,
        low_of(new_master),
    )


def solution(mesh):
    layout = Layout(mesh.shape["crop"], mesh.shape["row"])
    return jax.shard_map(
        lambda *arrays: local(layout, *arrays),
        mesh=mesh,
        in_specs=(
            P("crop", "row", None),
            P("crop", "row", None, None),
            P("crop"),
            P("crop", None),
            P("crop", "row", None),
            P("crop", "row", None, None),
            P(("crop", "row")),
            P(("crop", "row")),
            P(("crop", "row")),
        ),
        out_specs=(
            P("crop", "row", None),
            P("crop", "row", None, None),
            P("crop", "row", None),
            P("crop", "row", None, None),
            P(("crop", "row")),
            P(),
            P(),
            P(("crop", "row")),
            P(("crop", "row")),
            P(("crop", "row")),
            P(("crop", "row")),
        ),
        check_vma=False,
    )
```

```python
import math
from typing import Any, NamedTuple

import jax
import jax.numpy as jnp
import numpy as np
from jax import lax
from jax.experimental import pallas as pl
from jax.experimental.pallas import tpu as pltpu
from jax.sharding import PartitionSpec as P

NODE_DIM = 256
PAIR_DIM = 128
HEADS = 8
HEAD_DIM = 32
OUTER = 32
TRI_DIM = 128
FFN_NODE = 1024
FFN_PAIR = 512
RECYCLES = 4
ADAM_STEP = 3


EPS_NORM = 1e-05
ADAM_EPS = 1e-08
BETA_ONE = 0.9
BETA_TWO = 0.95
LEARN_RATE = 0.06
WEIGHT_DECAY = 0.1
CLIP_NORM = 1.0
MASK_FILL = 1000000000.0
HIGHEST = lax.Precision.HIGHEST


class Triangle(NamedTuple):
    gain_in: Any
    w_left: Any
    w_right: Any
    w_gate: Any
    gain_tri: Any
    w_tri_out: Any


class Params(NamedTuple):
    embed: Any
    gain_one: Any
    w_query: Any
    w_key: Any
    w_value: Any
    w_bias: Any
    w_attn_out: Any
    gain_two: Any
    w_node_up: Any
    w_node_down: Any
    gain_three: Any
    w_left_node: Any
    w_right_node: Any
    w_outer: Any
    outgoing: Triangle
    incoming: Triangle
    gain_pair: Any
    w_pair_up: Any
    w_pair_down: Any
    bias_pair: Any


LANES = 128
HEADS_WIDTH = HEADS * HEAD_DIM


def first_rows():
    square = PAIR_DIM * TRI_DIM
    triangle = Triangle(PAIR_DIM, square, square, PAIR_DIM * PAIR_DIM, TRI_DIM, square)
    sizes = Params(
        embed=RECYCLES * NODE_DIM,
        gain_one=NODE_DIM,
        w_query=NODE_DIM * HEADS_WIDTH,
        w_key=NODE_DIM * HEADS_WIDTH,
        w_value=NODE_DIM * HEADS_WIDTH,
        w_bias=PAIR_DIM * HEADS,
        w_attn_out=HEADS_WIDTH * NODE_DIM,
        gain_two=NODE_DIM,
        w_node_up=NODE_DIM * FFN_NODE,
        w_node_down=FFN_NODE * NODE_DIM,
        gain_three=NODE_DIM,
        w_left_node=NODE_DIM * OUTER,
        w_right_node=NODE_DIM * OUTER,
        w_outer=OUTER * OUTER * PAIR_DIM,
        outgoing=triangle,
        incoming=triangle,
        gain_pair=PAIR_DIM,
        w_pair_up=PAIR_DIM * FFN_PAIR,
        w_pair_down=FFN_PAIR * PAIR_DIM,
        bias_pair=PAIR_DIM,
    )
    leaves, tree = jax.tree.flatten(sizes)
    ends = np.cumsum(leaves) // LANES
    starts = [0] + [int(end) for end in ends[:-1]]
    return jax.tree.unflatten(tree, starts), int(ends[-1])


LOW = jnp.bfloat16
WIDE = jnp.float32
BOTH = ("crop", "row")
TILE = 16
VMEM_LIMIT = 56 * 2**20
INV_SQRT2 = 1.0 / math.sqrt(2.0)
INV_SQRT2PI = 1.0 / math.sqrt(2.0 * math.pi)


class Layout:
    def __init__(self, crops, rows):
        self.crops, self.rows = crops, rows
        self.devices = crops * rows
        self.wide = 2 ** (int(math.log2(rows)) // 2)
        self.high = rows // self.wide
        half = crops // 2
        self.moves = [
            (here, self.work_place(here))
            for here in range(self.devices)
            if here != self.work_place(here)
        ]
        self.groups = [
            [self.work_place(c * rows + r) for r in range(rows)] for c in range(crops)
        ]
        self.cores = [
            [(2 * x + k) * rows + r for k in range(2)] for x in range(half) for r in range(rows)
        ]
        self.chips = [
            [(2 * x + k) * rows + r for x in range(half)] for k in range(2) for r in range(rows)
        ]

    def work_place(self, here):
        crop, row = here // self.rows, here % self.rows
        high, wide = row // self.wide, row % self.wide
        core = crop % 2
        away = (high // (self.high // 2) + core) % 2
        crop = crop + away * (1 - 2 * core)
        high = high + away * (self.high - 1 - 2 * high)
        return crop * self.rows + high * self.wide + wide


def exchange(blocks, axes, groups=None):
    return lax.all_to_all(blocks, axes, 0, 0, axis_index_groups=groups, tiled=True)


def spread(part, count, axes, groups=None):
    return exchange(jnp.broadcast_to(part[None], (count,) + part.shape), axes, groups)


def dot_nn(a, b):
    return lax.dot_general(a, b, (((1,), (0,)), ((), ())), preferred_element_type=WIDE)


def dot_nt(a, b):
    return lax.dot_general(a, b, (((1,), (1,)), ((), ())), preferred_element_type=WIDE)


def dot_tn(a, b):
    return lax.dot_general(a, b, (((0,), (0,)), ((), ())), preferred_element_type=WIDE)


def norm_parts(x):
    centered = x - jnp.mean(x, axis=0, keepdims=True)
    scale = lax.rsqrt(jnp.mean(centered * centered, axis=0, keepdims=True) + EPS_NORM)
    return centered * scale, scale


def norm_back(grad, hat, scale, gain):
    grad_gain = jnp.sum(grad * hat, axis=1, keepdims=True)
    wide = grad * gain
    inner = jnp.mean(wide * hat, axis=0, keepdims=True)
    return scale * (wide - jnp.mean(wide, axis=0, keepdims=True) - hat * inner), grad_gain


def sigmoid(x):
    return 0.5 * jnp.tanh(0.5 * x) + 0.5


EMBED = slice(0, 8)
GAIN_ONE, GAIN_TWO, GAIN_THREE = slice(8, 10), slice(10, 12), slice(12, 14)
OUT_GAIN, OUT_TRI, IN_GAIN, IN_TRI = (slice(k, k + 1) for k in range(14, 18))
PAIR_GAIN, PAIR_BIAS = slice(18, 19), slice(19, 20)


def column(row):
    return jnp.broadcast_to(row, (LANES, row.shape[1])).T[:, :1]


def row_of(values):
    return jnp.broadcast_to(values, (values.shape[0], LANES)).T[:1]


def cat(ref):
    return jnp.concatenate([ref[t] for t in range(ref.shape[0])], axis=1)


def put(ref, value):
    count = ref.shape[0]
    width = value.shape[1] // count
    for t in range(count):
        ref[t] = value[:, t * width : (t + 1) * width].astype(ref.dtype)


def swapped(value):
    if value.shape[0] % TILE or value.shape[1] % TILE:
        return jnp.swapaxes(value.astype(WIDE), 0, 1).astype(LOW)
    return jnp.swapaxes(value, 0, 1)


def send_pair(scratch, out_ref):
    parts, share = out_ref.shape[0], out_ref.shape[1] // 2
    channels = parts * share
    for side in range(2):
        value = swapped(scratch[:, side * channels : (side + 1) * channels, :])
        out_ref[:, side * share : (side + 1) * share] = value.reshape(
            (parts, share) + value.shape[1:]
        )


def take_pair(in_ref, scratch):
    parts, share = in_ref.shape[0], in_ref.shape[1] // 2
    channels = parts * share
    for side in range(2):
        value = in_ref[:, side * share : (side + 1) * share]
        value = value.reshape((channels,) + value.shape[2:])
        scratch[:, side * channels : (side + 1) * channels, :] = swapped(value)


def front(x, gain, w_all, mask, x_out, hat_out, scale_out, gate_out, sides):
    hat, scale = norm_parts(x)
    all_three = dot_nn(w_all, (hat * gain).astype(LOW))
    channels = 2 * TRI_DIM
    put(sides, all_three[:channels] * mask)
    put(x_out, x)
    put(hat_out, hat)
    put(scale_out, scale)
    put(gate_out, sigmoid(all_three[channels:]))


def triangle_update(mixed, gain, w_out):
    hat, scale = norm_parts(mixed)
    normed = (hat * gain).astype(LOW)
    return hat, scale, normed, dot_nn(w_out, normed)


def post_back(grad, gate, hat, scale, normed, update, gain, w_out_back):
    update_grad = (grad * gate).astype(LOW)
    gate_grad = (grad * update * (gate * (1.0 - gate))).astype(LOW)
    grad_out = dot_nt(normed, update_grad)
    mixed_grad, grad_gain = norm_back(dot_nn(w_out_back, update_grad), hat, scale, gain)
    return mixed_grad, gate_grad, grad_out, grad_gain


def front_back(grad, hat, scale, sides_grad, gate_grad, mask, gain, w_all_back):
    normed = (hat * gain).astype(LOW)
    sides = jnp.concatenate([sides_grad * mask.astype(LOW), gate_grad], axis=0)
    grad_w = dot_nt(normed, sides)
    x_grad, grad_gain = norm_back(dot_nn(w_all_back, sides), hat, scale, gain)
    return grad + x_grad, grad_w, grad_gain


def gelu_parts(x):
    cumulative = 0.5 * lax.erf(x * INV_SQRT2) + 0.5
    density = INV_SQRT2PI * jnp.exp(-0.5 * x * x)
    return x * cumulative, cumulative + x * density


def zero_first(*refs):
    @pl.when((pl.program_id(0) == 0) & (pl.program_id(1) == 0))
    def _():
        for ref in refs:
            ref[...] = jnp.zeros_like(ref)


def run(body, step, extent, in_arrays, in_kinds, outs, scratch, flops):
    def spec(kind, shape):
        lead = (0,) * len(shape)
        block, at = {
            "r": (step[:1] + shape[1:-1] + step[1:], lambda c, r: (r,) + lead[2:] + (c,)),
            "n": (step + shape[2:], lambda c, r: (r, c) + lead[2:]),
            "s": (shape[:-2] + step, lambda c, r: lead[2:] + (r, c)),
            "c": (shape[:-1] + step[1:], lambda c, r: lead[1:] + (c,)),
            "t": (step[:1] + shape[1:], lambda c, r: (r,) + lead[1:]),
            "p": ((1,) + step[:1] + shape[2:], lambda c, r: (c, r) + lead[2:]),
            "q": (step[1:] + shape[1:], lambda c, r: (c,) + lead[1:]),
            "w": (shape, lambda c, r: lead),
        }[kind]
        return pl.BlockSpec(block, at)

    moved = sum(a.size * a.dtype.itemsize for a in in_arrays)
    return pl.pallas_call(
        body,
        grid=(extent[1] // step[1], extent[0] // step[0]),
        in_specs=[spec(kind, a.shape) for kind, a in zip(in_kinds, in_arrays)],
        out_specs=[spec(kind, shape) for kind, shape, _ in outs],
        out_shape=[jax.ShapeDtypeStruct(shape, dtype) for _, shape, dtype in outs],
        scratch_shapes=scratch,
        compiler_params=pltpu.CompilerParams(vmem_limit_bytes=VMEM_LIMIT),
        cost_estimate=pl.CostEstimate(flops=flops, bytes_accessed=moved, transcendentals=0),
    )(*in_arrays)


def all_low(w):
    return jnp.concatenate([w[k * PAIR_DIM : (k + 1) * PAIR_DIM].T for k in range(3)], axis=0)


def all_back(w):
    return jnp.concatenate([w[k * PAIR_DIM : (k + 1) * PAIR_DIM] for k in range(3)], axis=1)


def kernel_open(
    pair, table, right, mask, vectors, w_all, x_out, hat_out, scale_out, gate_out, sides_out, sides
):
    right_low = right[...]
    x = jnp.concatenate(
        [pair[t].T.astype(WIDE) + dot_tn(table[t], right_low) for t in range(pair.shape[0])],
        axis=1,
    )
    front(
        x, column(vectors[OUT_GAIN]), all_low(w_all), cat(mask), x_out, hat_out, scale_out, gate_out, sides
    )
    send_pair(sides, sides_out)


def kernel_middle(
    mixed, x_in, gate_in, mask, vectors, w_out, w_all,
    x_out, hat_out, scale_out, gate_out, sides_out, arrived, sides,
):
    arrived[...] = swapped(mixed[...])
    *_, update = triangle_update(cat(arrived).astype(WIDE), column(vectors[OUT_TRI]), w_out[...].T)
    x = cat(x_in) + cat(gate_in).astype(WIDE) * update
    front(
        x, column(vectors[IN_GAIN]), all_low(w_all), cat(mask),
        x_out, hat_out, scale_out, gate_out, sides,
    )
    send_pair(sides, sides_out)


def kernel_turn(
    mixed, x_in, gate_in, cot, vectors, w_out, w_up, w_down,
    pair_out, x_grad, gate_grad, mixed_grad, g_out, g_tri, g_up, g_down, g_pair, g_bias,
    arrived, leaving,
):
    rows = x_in.shape[0]
    arrived[...] = swapped(mixed[...])
    up_low, up_back = w_up[...].T, w_up[...]
    down_low, down_back = w_down[...].T, w_down[...]
    tri_col, pair_col = column(vectors[IN_TRI]), column(vectors[PAIR_GAIN])
    zero_first(g_out, g_tri, g_up, g_down, g_pair, g_bias)
    chunk = PAIR_DIM

    gate = cat(gate_in).astype(WIDE)
    mix_parts = triangle_update(cat(arrived).astype(WIDE), tri_col, w_out[...].T)
    x = cat(x_in) + gate * mix_parts[-1]
    hat, scale = norm_parts(x)
    normed = (hat * pair_col).astype(LOW)
    cot_low = jnp.concatenate([cot[t].T for t in range(rows)], axis=1)
    total = x + column(vectors[PAIR_BIAS])
    normed_grad = jnp.zeros_like(x)
    for c in range(FFN_PAIR // chunk):
        part = slice(c * chunk, (c + 1) * chunk)
        act, slope = gelu_parts(dot_nn(up_low[part], normed))
        act_low = act.astype(LOW)
        total = total + dot_nn(down_low[:, part], act_low)
        hidden_grad = (dot_nn(down_back[part], cot_low) * slope).astype(LOW)
        normed_grad = normed_grad + dot_nn(up_back[:, part], hidden_grad)
        g_up[:, part] += dot_nt(normed, hidden_grad)
        g_down[part] += dot_nt(act_low, cot_low)
    total_low = total.astype(LOW)
    width = total.shape[1] // rows
    for t in range(rows):
        pair_out[t] = total_low[:, t * width : (t + 1) * width].T
    cot_wide = cot_low.astype(WIDE)
    g_bias[...] += jnp.sum(cot_wide, axis=1, keepdims=True)
    back, grad_gain = norm_back(normed_grad, hat, scale, pair_col)
    g_pair[...] += grad_gain
    grad = cot_wide + back
    put(x_grad, grad)
    mix_grad, gates, grad_out, grad_tri = post_back(grad, gate, *mix_parts, tri_col, w_out[...])
    put(leaving, mix_grad)
    put(gate_grad, gates)
    g_out[...] += grad_out
    g_tri[...] += grad_tri
    mixed_grad[...] = swapped(leaving[...])


def kernel_return(
    sides_grad, hat_after, scale_after, gate_after, grad_in, mask, vectors, w_after,
    mixed, gate_in, w_out,
    x_grad, gate_grad, mixed_grad, g_after, g_gain, g_out, g_tri,
    sides, arrived, leaving,
):
    take_pair(sides_grad, sides)
    arrived[...] = swapped(mixed[...])
    tri_col = column(vectors[OUT_TRI])
    zero_first(g_after, g_gain, g_out, g_tri)
    grad, grad_w, grad_gain = front_back(
        cat(grad_in), cat(hat_after).astype(WIDE), cat(scale_after), cat(sides), cat(gate_after),
        cat(mask), column(vectors[IN_GAIN]), all_back(w_after),
    )
    g_after[...] += grad_w
    g_gain[...] += grad_gain
    put(x_grad, grad)
    mix_parts = triangle_update(cat(arrived).astype(WIDE), tri_col, w_out[...].T)
    mix_grad, gates, grad_out, grad_tri = post_back(
        grad, cat(gate_in).astype(WIDE), *mix_parts, tri_col, w_out[...]
    )
    put(leaving, mix_grad)
    put(gate_grad, gates)
    g_out[...] += grad_out
    g_tri[...] += grad_tri
    mixed_grad[...] = swapped(leaving[...])


def kernel_close(
    sides_grad, hat_after, scale_after, gate_after, grad_in, mask, vectors, w_after,
    table, right,
    pair_grad, table_grad, right_grad, g_after, g_gain, sides,
):
    take_pair(sides_grad, sides)
    zero_first(g_after, g_gain)

    @pl.when(pl.program_id(1) == 0)
    def _():
        right_grad[...] = jnp.zeros_like(right_grad)

    grad, grad_w, grad_gain = front_back(
        cat(grad_in), cat(hat_after).astype(WIDE), cat(scale_after), cat(sides), cat(gate_after),
        cat(mask), column(vectors[OUT_GAIN]), all_back(w_after),
    )
    g_after[...] += grad_w
    g_gain[...] += grad_gain
    low = grad.astype(LOW)
    rows = table.shape[0]
    width = low.shape[1] // rows
    for t in range(rows):
        own = low[:, t * width : (t + 1) * width]
        pair_grad[t] = own.T
        table_grad[0, t] = dot_nt(right[...], own)
        right_grad[...] += dot_nn(table[t], own)


CHANNELS = 4


def kernel_mix(incoming, left, right, out):
    parts, count, rows, length = out.shape
    for c in range(count):
        a = left[:, c].reshape(length, length)
        b = right[:, c].reshape(length, length)
        mixed = dot_tn(a, b) if incoming else dot_nt(a, b)
        out[:, c] = mixed.astype(LOW).reshape(parts, rows, length)


def kernel_mix_back(incoming, grad, left, right, out):
    parts, count, rows, length = grad.shape
    for c in range(count):
        g = grad[:, c].reshape(length, length)
        a = left[:, c].reshape(length, length)
        b = right[:, c].reshape(length, length)
        a_grad = dot_nt(b, g) if incoming else dot_nn(g, b)
        b_grad = dot_nn(a, g) if incoming else dot_tn(g, a)
        out[:, 0, c] = a_grad.astype(LOW).reshape(parts, rows, length)
        out[:, 1, c] = b_grad.astype(LOW).reshape(parts, rows, length)


def mix(sides, incoming):
    parts, double, rows, length = sides.shape
    share = double // 2
    count = min(CHANNELS, share)
    steps = share // count
    block = (parts, count, rows, length)
    return pl.pallas_call(
        lambda *refs: kernel_mix(incoming, *refs),
        grid=(steps,),
        in_specs=[
            pl.BlockSpec(block, lambda c: (0, c, 0, 0)),
            pl.BlockSpec(block, lambda c: (0, c + steps, 0, 0)),
        ],
        out_specs=pl.BlockSpec(block, lambda c: (0, c, 0, 0)),
        out_shape=jax.ShapeDtypeStruct((parts, share, rows, length), LOW),
        compiler_params=pltpu.CompilerParams(vmem_limit_bytes=VMEM_LIMIT),
        cost_estimate=pl.CostEstimate(
            flops=2 * share * length**3, bytes_accessed=3 * share * length * length * 2,
            transcendentals=0,
        ),
    )(sides, sides)


def mix_back(grad, sides, incoming):
    parts, double, rows, length = sides.shape
    share = double // 2
    count = min(CHANNELS, share)
    steps = share // count
    block = (parts, count, rows, length)
    out = pl.pallas_call(
        lambda *refs: kernel_mix_back(incoming, *refs),
        grid=(steps,),
        in_specs=[
            pl.BlockSpec(block, lambda c: (0, c, 0, 0)),
            pl.BlockSpec(block, lambda c: (0, c, 0, 0)),
            pl.BlockSpec(block, lambda c: (0, c + steps, 0, 0)),
        ],
        out_specs=pl.BlockSpec((parts, 2, count, rows, length), lambda c: (0, 0, c, 0, 0)),
        out_shape=jax.ShapeDtypeStruct((parts, 2, share, rows, length), LOW),
        compiler_params=pltpu.CompilerParams(vmem_limit_bytes=VMEM_LIMIT),
        cost_estimate=pl.CostEstimate(
            flops=4 * share * length**3, bytes_accessed=5 * share * length * length * 2,
            transcendentals=0,
        ),
    )(grad, sides, sides)
    return out.reshape(sides.shape)


def share_rows(share):
    return -(-(share + 2 * LANES) // (TILE * LANES)) * TILE


def whole(shape):
    return pl.BlockSpec(shape, lambda *_: (0,) * len(shape))


def one_call(body, scalars, in_arrays, outs, scratch=()):
    return pl.pallas_call(
        body,
        in_specs=[pl.BlockSpec(memory_space=pltpu.SMEM)] * len(scalars)
        + [whole(a.shape) for a in in_arrays],
        out_specs=[whole(shape) for shape, _ in outs],
        out_shape=[jax.ShapeDtypeStruct(shape, dtype) for shape, dtype in outs],
        scratch_shapes=list(scratch),
        grid=(1,),
        compiler_params=pltpu.CompilerParams(vmem_limit_bytes=VMEM_LIMIT),
    )(*scalars, *in_arrays)


def lane_in(shape, start, width):
    lane = lax.broadcasted_iota(jnp.int32, shape, 1)
    return (lane >= start) & (lane < start + width)


def rolled(value, shift):
    shift %= LANES
    return pltpu.roll(value, shift, 1) if shift else value


def share_order(layout):
    return [((d // layout.rows) % 2, d // (2 * layout.rows), d % layout.rows) for d in range(layout.devices)]


def unpack(layout, shares, share):
    at, _ = first_rows()
    height = shares.shape[3]
    first = [share * d // LANES for d in range(layout.devices)]
    order = share_order(layout)
    matrices = [
        (at.w_query, NODE_DIM, 3, 3 * HEADS_WIDTH),
        (at.w_attn_out, HEADS_WIDTH, 1, NODE_DIM),
        (at.w_node_up, NODE_DIM, 1, FFN_NODE),
        (at.w_node_down, FFN_NODE, 1, NODE_DIM),
        (at.w_outer, OUTER * OUTER, 1, PAIR_DIM),
        (at.outgoing.w_left, 3 * PAIR_DIM, 1, TRI_DIM),
        (at.outgoing.w_tri_out, TRI_DIM, 1, PAIR_DIM),
        (at.incoming.w_left, 3 * PAIR_DIM, 1, TRI_DIM),
        (at.incoming.w_tri_out, TRI_DIM, 1, PAIR_DIM),
        (at.w_pair_up, PAIR_DIM, 1, FFN_PAIR),
        (at.w_pair_down, FFN_PAIR, 1, PAIR_DIM),
    ]
    small = [(at.embed, 8), (at.gain_one, 2), (at.gain_two, 2), (at.gain_three, 2)]
    small += [
        (start, 1)
        for start in (
            at.outgoing.gain_in, at.outgoing.gain_tri, at.incoming.gain_in, at.incoming.gain_tri,
            at.gain_pair, at.bias_pair,
        )
    ]

    def body(shares_ref, vectors, bias_out, factors_out, *rest):
        outs, flat, narrow = rest[:-2], rest[-2], rest[-1]
        for d, place in enumerate(order):
            block = shares_ref[place].astype(WIDE)
            if d:
                tail = flat[first[d] : first[d] + 1]
                flat[first[d] : first[d] + height] = block
                flat[first[d] : first[d] + 1] = block[:1] + tail
            else:
                flat[:height] = block
        row = 0
        vectors[...] = jnp.zeros_like(vectors)
        for start, count in small:
            vectors[row : row + count] = flat[start : start + count]
            row += count
        for out, (place, rows, count, width) in zip(outs, matrices):
            pieces = width // count // LANES
            for m in range(count):
                for a in range(pieces):
                    start = place + m * rows * pieces + a
                    value = (
                        flat[pl.ds(start, rows, stride=pieces), :]
                        if pieces > 1
                        else flat[start : start + rows]
                    )
                    lane = (m * pieces + a) * LANES
                    out[:, lane : lane + LANES] = value.astype(LOW)
        per_row = LANES // HEADS
        shape = (HEADS, LANES)
        value = flat[at.w_bias : at.w_bias + HEADS]
        for a in range(per_row):
            kept = jnp.where(lane_in(shape, 0, HEADS), rolled(value, -HEADS * a), 0.0)
            narrow[pl.ds(a, HEADS, stride=per_row), :] = kept
        bias_out[...] = narrow[:PAIR_DIM].astype(LOW)
        per_row = LANES // OUTER
        count = NODE_DIM // per_row
        shape = (count, LANES)
        left, right = (flat[start : start + count] for start in (at.w_left_node, at.w_right_node))
        for a in range(per_row):
            kept = jnp.where(lane_in(shape, 0, OUTER), rolled(left, -OUTER * a), 0.0)
            kept += jnp.where(lane_in(shape, OUTER, OUTER), rolled(right, OUTER - OUTER * a), 0.0)
            narrow[pl.ds(a, count, stride=per_row), :] = kept
        factors_out[...] = narrow[...].astype(LOW)

    return one_call(
        body,
        (),
        (shares,),
        [((24, LANES), WIDE), ((PAIR_DIM, LANES), LOW), ((NODE_DIM, LANES), LOW)]
        + [((rows, width), LOW) for _, rows, _, width in matrices],
        [pltpu.VMEM((first[-1] + height + TILE, LANES), WIDE), pltpu.VMEM((NODE_DIM, LANES), WIDE)],
    )


def pack(layout, share, recycle, grads, node_parts):
    at, total = first_rows()
    height = share_rows(share)
    first = [share * d // LANES for d in range(layout.devices)]
    order = share_order(layout)
    many = len(grads)

    def body(recycle_ref, *refs):
        ins, rest = refs[:many], refs[many:]
        (
            arrived, query_low, start, normed_one, after_grad, vectors, w_projections,
            act_low, final_low, normed_two, hidden_grad, attended, after_low, g_factors,
            out, node_grad_out, flat, narrow,
        ) = rest

        def store(place, count, value):
            rows, pieces = value.shape[0], value.shape[1] // count // LANES
            for m in range(count):
                for a in range(pieces):
                    lane = (m * pieces + a) * LANES
                    begin = place + m * rows * pieces + a
                    part = value[:, lane : lane + LANES]
                    if pieces > 1 and rows > 1:
                        flat[pl.ds(begin, rows, stride=pieces), :] = part
                    else:
                        flat[begin : begin + rows] = part

        flat[total:] = jnp.zeros((flat.shape[0] - total, LANES), WIDE)
        for ref, (place, count, _) in zip(ins, grads):
            store(place, count, row_of(ref[...]) if ref.shape[1] == 1 else ref[...])
        store(at.w_node_down, 1, dot_tn(act_low[...], final_low[...]))
        store(at.w_node_up, 1, dot_tn(normed_two[...], hidden_grad[...]))
        store(at.w_attn_out, 1, dot_tn(attended[...], after_low[...]))
        per_row = LANES // OUTER
        count = NODE_DIM // per_row
        narrow[...] = g_factors[...]
        left = jnp.zeros((count, LANES), WIDE)
        right = left
        for a in range(per_row):
            piece = narrow[pl.ds(a, count, stride=per_row), :]
            inside = lane_in(piece.shape, OUTER * a, OUTER)
            left = jnp.where(inside, rolled(piece, OUTER * a), left)
            right = jnp.where(inside, rolled(piece, OUTER * a - OUTER), right)
        store(at.w_left_node, 1, left)
        store(at.w_right_node, 1, right)

        key_value = jnp.sum(arrived[...].astype(WIDE), axis=0).astype(LOW)
        projections = jnp.concatenate([query_low[...], key_value], axis=1)
        store(at.w_query, 3, dot_tn(normed_one[...], projections))
        hat, scale = row_norm(start[...])
        part, grad_gain = row_norm_back(
            dot_nt(projections, w_projections[...]), hat, scale, vector(vectors, GAIN_ONE)
        )
        node_grad = after_grad[...] + part
        node_grad_out[...] = node_grad.astype(LOW)
        store(at.gain_one, 1, grad_gain)
        flat[at.embed : at.embed + 2 * RECYCLES] = jnp.zeros((2 * RECYCLES, LANES), WIDE)
        column_sum = jnp.sum(node_grad, axis=0, keepdims=True)
        for a in range(NODE_DIM // LANES):
            place = at.embed + (NODE_DIM // LANES) * recycle_ref[0] + a
            flat[pl.ds(place, 1), :] = column_sum[:, a * LANES : (a + 1) * LANES]
        for d, where in enumerate(order):
            out[where] = flat[first[d] : first[d] + height].astype(LOW)

    shape = (2, layout.crops // 2, layout.rows, height, LANES)
    return one_call(
        body,
        (recycle,),
        tuple(array for _, _, array in grads) + tuple(node_parts),
        [(shape, LOW), (node_parts[2].shape, LOW)],
        [pltpu.VMEM((first[-1] + height + TILE, LANES), WIDE), pltpu.VMEM((NODE_DIM, LANES), WIDE)],
    )


def row_norm(x):
    centered = x - jnp.mean(x, axis=-1, keepdims=True)
    scale = lax.rsqrt(jnp.mean(centered * centered, axis=-1, keepdims=True) + EPS_NORM)
    return centered * scale, scale


def row_norm_back(grad, hat, scale, gain):
    grad_gain = jnp.sum(grad * hat, axis=0, keepdims=True)
    wide = grad * gain
    inner = jnp.mean(wide * hat, axis=-1, keepdims=True)
    return scale * (wide - jnp.mean(wide, axis=-1, keepdims=True) - hat * inner), grad_gain


def vector(ref, rows):
    return jnp.concatenate([ref[r : r + 1] for r in range(rows.start, rows.stop)], axis=1)


def by_head(value):
    return jnp.concatenate(
        [
            jnp.where(lane_in(value.shape, h * HEAD_DIM, HEAD_DIM), value, 0.0)
            for h in range(HEADS)
        ],
        axis=0,
    )


def head_sum(value):
    rows = value.shape[0] // HEADS
    parts = [value[h * rows : (h + 1) * rows] for h in range(HEADS)]
    return sum(
        jnp.where(lane_in(part.shape, h * HEAD_DIM, HEAD_DIM), part, 0.0)
        for h, part in enumerate(parts)
    )


SCORE_SCALE = HEAD_DIM ** (-0.5)
KEEP_LANE = 2 * OUTER


def node_forward(
    recycle, node_ref, all_ref, bias_ref, keep, keep_rows, vectors, w_projections, w_attn_out, w_up, w_down,
    w_factors,
    node_out, factors_out, start_out, normed_one, soft_out, heads_out, key_out, value_out,
    attended_out, after_out, act_out, slope_out, final_out, flat,
):
    pieces = NODE_DIM // LANES
    length = all_ref.shape[0] // pieces
    embed = jnp.concatenate(
        [vectors[pl.ds(pieces * recycle[0] + a, 1), :] for a in range(pieces)], axis=1
    )
    flat[...] = all_ref[...].astype(WIDE)
    all_rows = jnp.concatenate(
        [flat[pl.ds(a, length, stride=pieces), :] for a in range(pieces)], axis=1
    )
    gain = vector(vectors, GAIN_ONE)
    normed_all = (row_norm(all_rows + embed)[0] * gain).astype(LOW)
    start = node_ref[...].astype(WIDE) + embed
    normed = (row_norm(start)[0] * gain).astype(LOW)
    start_out[...] = start
    normed_one[...] = normed
    query = dot_nn(normed, w_projections[:, :HEADS_WIDTH]).astype(LOW).astype(WIDE)
    heads = by_head(query).astype(LOW)
    key_value = dot_nn(normed_all, w_projections[:, HEADS_WIDTH:]).astype(LOW)
    key, value = key_value[:, :HEADS_WIDTH], key_value[:, HEADS_WIDTH:]
    heads_out[...] = heads
    key_out[...] = key
    value_out[...] = value
    scores = dot_nt(heads, key) * SCORE_SCALE + bias_ref[...] + (keep[...] - 1.0) * MASK_FILL
    powers = jnp.exp(scores - jnp.max(scores, axis=-1, keepdims=True))
    soft = powers / jnp.sum(powers, axis=-1, keepdims=True)
    soft_out[...] = soft
    attended = head_sum(dot_nn(soft.astype(LOW), value)).astype(LOW)
    attended_out[...] = attended
    after = start + dot_nn(attended, w_attn_out[...])
    after_out[...] = after
    normed = (row_norm(after)[0] * vector(vectors, GAIN_TWO)).astype(LOW)
    act, slope = gelu_parts(dot_nn(normed, w_up[...]))
    act_out[...] = act.astype(LOW)
    slope_out[...] = slope
    final = after + dot_nn(act.astype(LOW), w_down[...])
    final_out[...] = final
    node_out[...] = final.astype(LOW)
    normed = (row_norm(final)[0] * vector(vectors, GAIN_THREE)).astype(LOW)
    factors = dot_nn(normed, w_factors[...])
    factors = jnp.where(lane_in(factors.shape, KEEP_LANE, 1), keep_rows[...], factors).astype(LOW)
    factors_out[...] = jnp.broadcast_to(factors[None], factors_out.shape)


def node_backward(
    sources, factor_ref, cot, vectors, soft_ref, heads, key, value, after_ref, slope, final_ref,
    w_attn_out, w_up, w_down, w_factors,
    key_value_out, query_out, score_out, after_grad_out, final_low_out, normed_two_out,
    hidden_out, after_low_out, g_factors, g_two, g_three,
):
    ranks = key_value_out.shape[0]
    left = factor_ref[sources[0]].astype(WIDE)
    right = sum(factor_ref[sources[1 + r]].astype(WIDE) for r in range(ranks))
    rows = jnp.where(lane_in(left.shape, 0, OUTER), left, right).astype(LOW)
    hat, scale = row_norm(final_ref[...])
    gain = vector(vectors, GAIN_THREE)
    g_factors[...] = dot_tn((hat * gain).astype(LOW), rows)
    part, g_three[...] = row_norm_back(dot_nt(rows, w_factors[...]), hat, scale, gain)
    final_grad = cot[...].astype(WIDE) + part
    final_low = final_grad.astype(LOW)
    final_low_out[...] = final_low
    hidden_grad = (dot_nt(final_low, w_down[...]) * slope[...]).astype(LOW)
    hidden_out[...] = hidden_grad
    hat, scale = row_norm(after_ref[...])
    gain = vector(vectors, GAIN_TWO)
    normed_two_out[...] = (hat * gain).astype(LOW)
    part, g_two[...] = row_norm_back(dot_nt(hidden_grad, w_up[...]), hat, scale, gain)
    after_grad = final_grad + part
    after_grad_out[...] = after_grad
    after_low = after_grad.astype(LOW)
    after_low_out[...] = after_low
    attended_grad = dot_nt(after_low, w_attn_out[...]).astype(LOW).astype(WIDE)
    grad_heads = by_head(attended_grad).astype(LOW)
    soft = soft_ref[...]
    soft_grad = dot_nt(grad_heads, value[...])
    score_grad = soft * (soft_grad - jnp.sum(soft_grad * soft, axis=-1, keepdims=True))
    score_low = score_grad.astype(LOW)
    score_out[...] = score_low
    key_part = (dot_tn(score_low, heads[...]) * SCORE_SCALE).astype(LOW)
    value_part = dot_tn(soft.astype(LOW), grad_heads).astype(LOW)
    local_rows = cot.shape[0]
    for r in range(ranks):
        span = slice(r * local_rows, (r + 1) * local_rows)
        key_value_out[r, :, :HEADS_WIDTH] = key_part[span]
        key_value_out[r, :, HEADS_WIDTH:] = value_part[span]
    query_out[...] = (head_sum(dot_nn(score_low, key[...])) * SCORE_SCALE).astype(LOW)


def outer_tables(
    sources, factors, w_outer, table_out, right_out, left_out, mask_out, w_wide, steps
):
    local_rows = left_out.shape[0]
    ranks = right_out.shape[1] // local_rows
    left_low = factors[sources[0]][:, :OUTER]
    left_out[...] = left_low
    right = jnp.concatenate([factors[sources[1 + r]].astype(WIDE) for r in range(ranks)], axis=0)
    turned = right.T
    right_out[...] = turned[OUTER : 2 * OUTER].astype(LOW)
    own_keep = factors[sources[0]][:, KEEP_LANE : KEEP_LANE + 1].astype(WIDE)
    mask_out[:, 0, :] = own_keep * turned[KEEP_LANE : KEEP_LANE + 1]
    w_wide[...] = w_outer[...].astype(WIDE)
    for q in range(OUTER):
        w_q = w_wide[pl.ds(q, OUTER, stride=OUTER), :].astype(LOW)
        steps[q] = dot_nn(left_low, w_q)
    table_out[...] = jnp.swapaxes(steps[...], 0, 1).astype(LOW)


def outer_backward(table_grad, right_grad, left, w_outer, factors_out, g_outer, w_wide, steps):
    crops, ranks, local_rows, _ = factors_out.shape
    steps[...] = jnp.swapaxes(jnp.sum(table_grad[...], axis=0), 0, 1)
    w_wide[...] = w_outer[...].astype(WIDE)
    left_grad = jnp.zeros((local_rows, OUTER), WIDE)
    for q in range(OUTER):
        grad_q = steps[q].astype(LOW)
        w_q = w_wide[pl.ds(q, OUTER, stride=OUTER), :].astype(LOW)
        left_grad = left_grad + dot_nt(grad_q, w_q)
        g_outer[pl.ds(q, OUTER, stride=OUTER), :] = dot_tn(left[...], grad_q)
    right_rows = right_grad[...].T
    for r in range(ranks):
        block = jnp.concatenate(
            [
                left_grad,
                right_rows[r * local_rows : (r + 1) * local_rows],
                jnp.zeros((local_rows, LANES - 2 * OUTER), WIDE),
            ],
            axis=1,
        ).astype(LOW)
        for c in range(crops):
            factors_out[c, r] = block


def low_of(x):
    return x.astype(LOW)


def local(layout, node, pair, recycle, mask, node_cot, pair_cot, master, first, second):
    crops, ranks = layout.crops, layout.rows
    devices = crops * ranks
    local_rows, length = node.shape[1], pair.shape[2]
    share = TRI_DIM // ranks
    node, pair, node_cot, pair_cot = node[0], pair[0], node_cot[0], pair_cot[0]

    crop_at, row_at = lax.axis_index("crop"), lax.axis_index("row")
    here = crop_at * ranks + row_at
    partner = layout.work_place(here)
    stays = partner == here
    work_crop, work_row = partner // ranks, partner % ranks
    moved = lambda array: jnp.where(stays, array, lax.ppermute(array, BOTH, layout.moves))

    at, _ = first_rows()

    amount = master.shape[0]
    height = share_rows(amount)
    offset = (here * (amount % LANES)) % LANES
    shard = lax.dynamic_update_slice(jnp.zeros(height * LANES, LOW), low_of(master), (offset,))
    node_rows = local_rows * NODE_DIM // LANES
    shards = jnp.concatenate([shard.reshape(height, LANES), node.reshape(-1, LANES)], axis=0)
    shards = spread(shards, ranks, "row").reshape(ranks, -1, LANES)
    shards, pair = lax.optimization_barrier((shards, pair))
    node_all = shards[:, height:].reshape(-1, LANES)
    shards = shards[:, :height].reshape(-1, LANES)
    shards = spread(shards, crops // 2, BOTH, layout.chips)
    shards = spread(shards, 2, BOTH, layout.cores)
    shards = shards.reshape(2, crops // 2, ranks, height, LANES)
    (
        vectors, w_bias, w_factors, w_projections, w_attn_out, w_node_up, w_node_down, w_outer,
        w_out_all, w_out_end, w_in_all, w_in_end, w_pair_up, w_pair_down,
    ) = unpack(layout, shards, amount)
    pair_plane = moved(pair)
    keep = mask.astype(WIDE)
    keep_rows = lax.dynamic_slice_in_dim(keep[0], row_at * local_rows, local_rows, 0)[:, None]

    pair_bias = jnp.einsum("ijd,dh->hij", pair, w_bias[:, :HEADS], preferred_element_type=WIDE)
    rows_low = lambda width: ((local_rows, width), LOW)
    rows_wide = lambda width: ((local_rows, width), WIDE)
    by_heads = (HEADS * local_rows, length)
    (
        node_out, factors, start, normed_one, soft, heads, key, value, attended, after, act_low,
        slope, node_final,
    ) = one_call(
        node_forward,
        (recycle,),
        (node, node_all, pair_bias.reshape(by_heads), keep, keep_rows, vectors, w_projections, w_attn_out,
         w_node_up, w_node_down, w_factors),
        [rows_low(NODE_DIM), ((devices, local_rows, LANES), LOW), rows_wide(NODE_DIM),
         rows_low(NODE_DIM), (by_heads, WIDE), (by_heads[:1] + (HEADS_WIDTH,), LOW),
         ((length, HEADS_WIDTH), LOW), ((length, HEADS_WIDTH), LOW), rows_low(HEADS_WIDTH),
         rows_wide(NODE_DIM), rows_low(FFN_NODE), rows_wide(FFN_NODE), rows_wide(NODE_DIM)],
        [pltpu.VMEM(node_all.shape, WIDE)],
    )

    factors = exchange(factors, BOTH)
    factors, pair_cot = lax.optimization_barrier((factors, pair_cot))
    everyone = jnp.arange(ranks, dtype=jnp.int32)
    sources = jnp.concatenate([partner[None], work_crop * ranks + everyone]).astype(jnp.int32)
    table, right, left, mask_plane = one_call(
        outer_tables,
        (sources,),
        (factors, w_outer),
        [((local_rows, OUTER, PAIR_DIM), LOW), ((OUTER, length), LOW), ((local_rows, OUTER), LOW),
         ((local_rows, 1, length), WIDE)],
        [pltpu.VMEM((OUTER * OUTER, PAIR_DIM), WIDE), pltpu.VMEM((OUTER, local_rows, PAIR_DIM), WIDE)],
    )

    step = (min(TILE, local_rows), min(LANES, length))
    extent = (local_rows, length)
    pieces = length // step[1]
    state = (local_rows, TRI_DIM, length)
    line = (local_rows, 1, length)
    sides_shape = (ranks, 2 * share, local_rows, length)
    mixed_shape = (TRI_DIM, local_rows, length)
    natural = (local_rows, length, PAIR_DIM)
    buffer = lambda channels: pltpu.VMEM((step[0], channels, step[1]), LOW)
    trade = lambda blocks: exchange(blocks, BOTH, layout.groups)
    merge = lambda blocks: blocks.reshape(mixed_shape)
    split = lambda blocks: blocks.reshape(ranks, share, local_rows, length)
    unit = 2 * local_rows * length * PAIR_DIM * PAIR_DIM
    front_outs = (
        ("r", state, WIDE), ("r", state, LOW), ("r", line, WIDE), ("r", state, LOW),
        ("s", sides_shape, LOW),
    )
    square = (TRI_DIM, PAIR_DIM)
    gain_shape = (PAIR_DIM, 1)
    after_shape = (PAIR_DIM, 2 * TRI_DIM + PAIR_DIM)

    x_one, hat_tri_out, scale_tri_out, gate_tri_out, sides = run(
        kernel_open, step, extent,
        (pair_plane, table, right, mask_plane, vectors, w_out_all),
        "ntcrww", front_outs, [buffer(2 * TRI_DIM)], 4 * unit,
    )
    sides_out, cot_plane = lax.optimization_barrier((trade(sides), moved(pair_cot)))
    mixed_out = merge(trade(mix(sides_out, False)))
    x_two, hat_tri_in, scale_tri_in, gate_tri_in, sides = run(
        kernel_middle, step, extent,
        (mixed_out, x_one, gate_tri_out, mask_plane, vectors, w_out_end, w_in_all), "srrrwww", front_outs, [buffer(TRI_DIM), buffer(2 * TRI_DIM)], 5 * unit,
    )
    sides_in = trade(sides)
    mixed_in = merge(trade(mix(sides_in, True)))
    pair_final, x_grad, gate_grad, mixed_grad, g_in_out, g_in_tri, g_up, g_down, g_pair, g_bias = run(
        kernel_turn, step, extent,
        (mixed_in, x_two, gate_tri_in, cot_plane, vectors, w_in_end, w_pair_up, w_pair_down),
        "srrnwwww",
        (("n", natural, LOW), ("r", state, WIDE), ("r", state, LOW), ("s", mixed_shape, LOW),
         ("w", square, WIDE), ("w", gain_shape, WIDE), ("w", (PAIR_DIM, FFN_PAIR), WIDE),
         ("w", (FFN_PAIR, PAIR_DIM), WIDE), ("w", gain_shape, WIDE), ("w", gain_shape, WIDE)),
        [buffer(TRI_DIM), buffer(TRI_DIM)], 32 * unit,
    )
    sides_grad = trade(mix_back(trade(split(mixed_grad)), sides_in, True))
    sides_grad, pair_out = lax.optimization_barrier((sides_grad, moved(pair_final)))
    x_grad, gate_grad, mixed_grad, g_in_all, g_in_gain, g_out_out, g_out_tri = run(
        kernel_return, step, extent,
        (sides_grad, hat_tri_in, scale_tri_in, gate_grad, x_grad, mask_plane,
         vectors, w_in_all, mixed_out, gate_tri_out, w_out_end),
        "srrrrrwwsrw",
        (("r", state, WIDE), ("r", state, LOW), ("s", mixed_shape, LOW), ("w", after_shape, WIDE),
         ("w", gain_shape, WIDE), ("w", square, WIDE), ("w", gain_shape, WIDE)),
        [buffer(2 * TRI_DIM), buffer(TRI_DIM), buffer(TRI_DIM)], 12 * unit,
    )
    sides_grad = trade(mix_back(trade(split(mixed_grad)), sides_out, False))
    pair_one_grad, table_grad, right_part, g_out_all, g_out_gain = run(
        kernel_close, step, extent,
        (sides_grad, hat_tri_out, scale_tri_out, gate_grad, x_grad, mask_plane,
         vectors, w_out_all, table, right),
        "srrrrrwwtc",
        (("n", natural, LOW), ("p", (pieces, local_rows, OUTER, PAIR_DIM), WIDE),
         ("c", (OUTER, length), WIDE), ("w", after_shape, WIDE), ("w", gain_shape, WIDE)),
        [buffer(2 * TRI_DIM)], 8 * unit,
    )

    factor_grads, g_outer = one_call(
        outer_backward,
        (),
        (table_grad, right_part, left, w_outer),
        [((crops, ranks, local_rows, LANES), LOW), ((OUTER * OUTER, PAIR_DIM), WIDE)],
        [pltpu.VMEM((OUTER * OUTER, PAIR_DIM), WIDE), pltpu.VMEM((OUTER, local_rows, PAIR_DIM), WIDE)],
    )
    factor_grads = exchange(factor_grads.reshape(devices, local_rows, LANES), BOTH)

    workers = layout.work_place(crop_at * ranks + everyone)
    sources = jnp.concatenate([partner[None], workers]).astype(jnp.int32)
    (
        key_value, query_low, score_low, after_grad, final_low, normed_two, hidden_grad, after_low,
        g_factors, g_two, g_three,
    ) = one_call(
        node_backward,
        (sources,),
        (factor_grads, node_cot, vectors, soft, heads, key, value, after, slope, node_final,
         w_attn_out, w_node_up, w_node_down, w_factors),
        [((ranks, local_rows, 2 * HEADS_WIDTH), LOW), rows_low(HEADS_WIDTH), (by_heads, LOW),
         rows_wide(NODE_DIM), rows_low(NODE_DIM), rows_low(NODE_DIM), rows_low(FFN_NODE),
         rows_low(NODE_DIM), ((NODE_DIM, LANES), WIDE), ((1, NODE_DIM), WIDE), ((1, NODE_DIM), WIDE)],
    )
    key_value = exchange(key_value, "row")
    key_value, pair_one_grad = lax.optimization_barrier((key_value, pair_one_grad))
    pair_one_home = moved(pair_one_grad)
    score_low = score_low.reshape(HEADS, local_rows, length)
    g_bias_head = jnp.einsum("ijd,hij->dh", pair, score_low, preferred_element_type=WIDE)
    grads = [
        (at.w_bias, 1, lax.optimization_barrier(g_bias_head).reshape(-1, LANES)),
        (at.gain_two, 1, g_two),
        (at.gain_three, 1, g_three),
        (at.w_outer, 1, g_outer),
        (at.gain_pair, 1, g_pair),
        (at.w_pair_up, 1, g_up),
        (at.w_pair_down, 1, g_down),
        (at.bias_pair, 1, g_bias),
    ]
    for tri, g_all, g_gain, g_tri, g_out in (
        (at.outgoing, g_out_all, g_out_gain, g_out_tri, g_out_out),
        (at.incoming, g_in_all, g_in_gain, g_in_tri, g_in_out),
    ):
        grads += [
            (tri.gain_in, 1, g_gain),
            (tri.w_left, 3, g_all),
            (tri.gain_tri, 1, g_tri),
            (tri.w_tri_out, 1, g_out),
        ]

    blocks, node_grad = pack(
        layout, amount, recycle, grads,
        (key_value, query_low, start, normed_one, after_grad, vectors, w_projections, act_low,
         final_low, normed_two, hidden_grad, attended, after_low, g_factors),
    )
    total = lambda got: low_of(jnp.sum(got.astype(WIDE), axis=0))
    blocks = total(exchange(blocks, BOTH, layout.cores))
    blocks = total(exchange(blocks, BOTH, layout.chips))
    blocks = jnp.sum(exchange(blocks, "row").astype(WIDE), axis=0)
    blocks, pair_one_home = lax.optimization_barrier((blocks, pair_one_home))
    grad_own = lax.dynamic_slice(blocks.reshape(-1), (offset,), (amount,))
    pair_grad = pair_one_home.astype(WIDE) + jnp.einsum(
        "hij,dh->ijd", score_low, w_bias[:, :HEADS], preferred_element_type=WIDE
    )
    square_own = jnp.broadcast_to(jnp.sum(grad_own * grad_own), (1, LANES))
    last = jnp.concatenate([g_bias.reshape(1, LANES), square_own], axis=0)
    last = jnp.sum(spread(last, devices, BOTH).reshape(devices, 2, LANES), axis=0)
    bias_total = last[0]
    grad_norm = jnp.sqrt(last[1, 0])
    clipped = grad_own * (CLIP_NORM / jnp.maximum(grad_norm, CLIP_NORM))
    new_first = BETA_ONE * first + (1.0 - BETA_ONE) * clipped
    new_second = BETA_TWO * second + (1.0 - BETA_TWO) * clipped * clipped
    first_hat = new_first / (1.0 - BETA_ONE**ADAM_STEP)
    second_hat = new_second / (1.0 - BETA_TWO**ADAM_STEP)
    new_master = master - LEARN_RATE * (
        first_hat / (jnp.sqrt(second_hat) + ADAM_EPS) + WEIGHT_DECAY * master
    )
    return (
        node_out[None],
        pair_out[None],
        node_grad[None],
        low_of(pair_grad)[None],
        grad_own,
        bias_total,
        grad_norm,
        new_master,
        new_first,
        new_second,
        low_of(new_master),
    )


def solution(mesh):
    layout = Layout(mesh.shape["crop"], mesh.shape["row"])
    return jax.shard_map(
        lambda *arrays: local(layout, *arrays),
        mesh=mesh,
        in_specs=(
            P("crop", "row", None),
            P("crop", "row", None, None),
            P("crop"),
            P("crop", None),
            P("crop", "row", None),
            P("crop", "row", None, None),
            P(("crop", "row")),
            P(("crop", "row")),
            P(("crop", "row")),
        ),
        out_specs=(
            P("crop", "row", None),
            P("crop", "row", None, None),
            P("crop", "row", None),
            P("crop", "row", None, None),
            P(("crop", "row")),
            P(),
            P(),
            P(("crop", "row")),
            P(("crop", "row")),
            P(("crop", "row")),
            P(("crop", "row")),
        ),
        check_vma=False,
    )
```

```python
import math
from typing import Any, NamedTuple

import jax
import jax.numpy as jnp
import numpy as np
from jax import lax
from jax.experimental import pallas as pl
from jax.experimental.pallas import tpu as pltpu
from jax.sharding import PartitionSpec as P

NODE_DIM = 256
PAIR_DIM = 128
HEADS = 8
HEAD_DIM = 32
OUTER = 32
TRI_DIM = 128
FFN_NODE = 1024
FFN_PAIR = 512
RECYCLES = 4
ADAM_STEP = 3


EPS_NORM = 1e-05
ADAM_EPS = 1e-08
BETA_ONE = 0.9
BETA_TWO = 0.95
LEARN_RATE = 0.06
WEIGHT_DECAY = 0.1
CLIP_NORM = 1.0
MASK_FILL = 1000000000.0
HIGHEST = lax.Precision.HIGHEST


class Triangle(NamedTuple):
    gain_in: Any
    w_left: Any
    w_right: Any
    w_gate: Any
    gain_tri: Any
    w_tri_out: Any


class Params(NamedTuple):
    embed: Any
    gain_one: Any
    w_query: Any
    w_key: Any
    w_value: Any
    w_bias: Any
    w_attn_out: Any
    gain_two: Any
    w_node_up: Any
    w_node_down: Any
    gain_three: Any
    w_left_node: Any
    w_right_node: Any
    w_outer: Any
    outgoing: Triangle
    incoming: Triangle
    gain_pair: Any
    w_pair_up: Any
    w_pair_down: Any
    bias_pair: Any


LANES = 128
HEADS_WIDTH = HEADS * HEAD_DIM


def first_rows():
    square = PAIR_DIM * TRI_DIM
    triangle = Triangle(PAIR_DIM, square, square, PAIR_DIM * PAIR_DIM, TRI_DIM, square)
    sizes = Params(
        embed=RECYCLES * NODE_DIM,
        gain_one=NODE_DIM,
        w_query=NODE_DIM * HEADS_WIDTH,
        w_key=NODE_DIM * HEADS_WIDTH,
        w_value=NODE_DIM * HEADS_WIDTH,
        w_bias=PAIR_DIM * HEADS,
        w_attn_out=HEADS_WIDTH * NODE_DIM,
        gain_two=NODE_DIM,
        w_node_up=NODE_DIM * FFN_NODE,
        w_node_down=FFN_NODE * NODE_DIM,
        gain_three=NODE_DIM,
        w_left_node=NODE_DIM * OUTER,
        w_right_node=NODE_DIM * OUTER,
        w_outer=OUTER * OUTER * PAIR_DIM,
        outgoing=triangle,
        incoming=triangle,
        gain_pair=PAIR_DIM,
        w_pair_up=PAIR_DIM * FFN_PAIR,
        w_pair_down=FFN_PAIR * PAIR_DIM,
        bias_pair=PAIR_DIM,
    )
    leaves, tree = jax.tree.flatten(sizes)
    ends = np.cumsum(leaves) // LANES
    starts = [0] + [int(end) for end in ends[:-1]]
    return jax.tree.unflatten(tree, starts), int(ends[-1])


LOW = jnp.bfloat16
WIDE = jnp.float32
BOTH = ("crop", "row")
TILE = 16
VMEM_LIMIT = 56 * 2**20
INV_SQRT2 = 1.0 / math.sqrt(2.0)
INV_SQRT2PI = 1.0 / math.sqrt(2.0 * math.pi)


class Layout:
    def __init__(self, crops, rows):
        self.crops, self.rows = crops, rows
        self.devices = crops * rows
        self.wide = 2 ** (int(math.log2(rows)) // 2)
        self.high = rows // self.wide
        half = crops // 2
        self.moves = [
            (here, self.work_place(here))
            for here in range(self.devices)
            if here != self.work_place(here)
        ]
        self.groups = [
            [self.work_place(c * rows + r) for r in range(rows)] for c in range(crops)
        ]
        self.cores = [
            [(2 * x + k) * rows + r for k in range(2)] for x in range(half) for r in range(rows)
        ]
        self.slabs = [[2 * x * rows + k for k in range(2 * rows)] for x in range(half)]
        self.chips = [
            [(2 * x + k) * rows + r for x in range(half)] for k in range(2) for r in range(rows)
        ]

    def work_place(self, here):
        crop, row = here // self.rows, here % self.rows
        high, wide = row // self.wide, row % self.wide
        core = crop % 2
        away = (high // (self.high // 2) + core) % 2
        crop = crop + away * (1 - 2 * core)
        high = high + away * (self.high - 1 - 2 * high)
        return crop * self.rows + high * self.wide + wide


def exchange(blocks, axes, groups=None):
    return lax.all_to_all(blocks, axes, 0, 0, axis_index_groups=groups, tiled=True)


def spread(part, count, axes, groups=None):
    return exchange(jnp.broadcast_to(part[None], (count,) + part.shape), axes, groups)


def dot_nn(a, b):
    return lax.dot_general(a, b, (((1,), (0,)), ((), ())), preferred_element_type=WIDE)


def dot_nt(a, b):
    return lax.dot_general(a, b, (((1,), (1,)), ((), ())), preferred_element_type=WIDE)


def dot_tn(a, b):
    return lax.dot_general(a, b, (((0,), (0,)), ((), ())), preferred_element_type=WIDE)


def norm_parts(x):
    hat, _, scale = norm_all(x)
    return hat, scale


def norm_all(x):
    mean = jnp.mean(x, axis=0, keepdims=True)
    centered = x - mean
    scale = lax.rsqrt(jnp.mean(centered * centered, axis=0, keepdims=True) + EPS_NORM)
    return centered * scale, mean, scale


def norm_back(grad, hat, scale, gain):
    grad_gain = jnp.sum(grad * hat, axis=1, keepdims=True)
    wide = grad * gain
    inner = jnp.mean(wide * hat, axis=0, keepdims=True)
    return scale * (wide - jnp.mean(wide, axis=0, keepdims=True) - hat * inner), grad_gain


def sigmoid(x):
    return 0.5 * jnp.tanh(0.5 * x) + 0.5


EMBED = slice(0, 8)
GAIN_ONE, GAIN_TWO, GAIN_THREE = slice(8, 10), slice(10, 12), slice(12, 14)
OUT_GAIN, OUT_TRI, IN_GAIN, IN_TRI = (slice(k, k + 1) for k in range(14, 18))
PAIR_GAIN, PAIR_BIAS = slice(18, 19), slice(19, 20)


def column(row):
    return jnp.broadcast_to(row, (LANES, row.shape[1])).T[:, :1]


def row_of(values):
    return jnp.broadcast_to(values, (values.shape[0], LANES)).T[:1]


def cat(ref):
    return jnp.concatenate([ref[t] for t in range(ref.shape[0])], axis=1)


def put(ref, value):
    count = ref.shape[0]
    width = value.shape[1] // count
    for t in range(count):
        ref[t] = value[:, t * width : (t + 1) * width].astype(ref.dtype)


def swapped(value):
    if value.shape[0] % TILE or value.shape[1] % TILE:
        return jnp.swapaxes(value.astype(WIDE), 0, 1).astype(LOW)
    return jnp.swapaxes(value, 0, 1)


def send_pair(scratch, out_ref):
    parts, share = out_ref.shape[0], out_ref.shape[1] // 2
    channels = parts * share
    for side in range(2):
        value = swapped(scratch[:, side * channels : (side + 1) * channels, :])
        out_ref[:, side * share : (side + 1) * share] = value.reshape(
            (parts, share) + value.shape[1:]
        )


def take_pair(in_ref, scratch):
    parts, share = in_ref.shape[0], in_ref.shape[1] // 2
    channels = parts * share
    for side in range(2):
        value = in_ref[:, side * share : (side + 1) * share]
        value = value.reshape((channels,) + value.shape[2:])
        scratch[:, side * channels : (side + 1) * channels, :] = swapped(value)


def front(x, gain, w_all, mask, x_out, mean_out, scale_out, gate_out, sides):
    hat, mean, scale = norm_all(x)
    all_three = dot_nn(w_all, (hat * gain).astype(LOW))
    channels = 2 * TRI_DIM
    put(sides, all_three[:channels] * mask)
    put(x_out, x)
    put(mean_out, mean)
    put(scale_out, scale)
    put(gate_out, sigmoid(all_three[channels:]))


def triangle_update(mixed, gain, w_out):
    hat, scale = norm_parts(mixed)
    normed = (hat * gain).astype(LOW)
    return hat, scale, normed, dot_nn(w_out, normed)


def post_back(grad, gate, hat, scale, normed, update, gain, w_out_back):
    update_grad = (grad * gate).astype(LOW)
    gate_grad = (grad * update * (gate * (1.0 - gate))).astype(LOW)
    grad_out = dot_nt(normed, update_grad)
    mixed_grad, grad_gain = norm_back(dot_nn(w_out_back, update_grad), hat, scale, gain)
    return mixed_grad, gate_grad, grad_out, grad_gain


def front_back(grad, x, mean, scale, sides_grad, gate_grad, mask, gain, w_all_back):
    hat = (x - mean) * scale
    normed = (hat * gain).astype(LOW)
    sides = jnp.concatenate([sides_grad * mask.astype(LOW), gate_grad], axis=0)
    grad_w = dot_nt(normed, sides)
    x_grad, grad_gain = norm_back(dot_nn(w_all_back, sides), hat, scale, gain)
    return grad + x_grad, grad_w, grad_gain


def gelu_parts(x):
    cumulative = 0.5 * lax.erf(x * INV_SQRT2) + 0.5
    density = INV_SQRT2PI * jnp.exp(-0.5 * x * x)
    return x * cumulative, cumulative + x * density


def zero_first(*refs, earlier=()):
    @pl.when((pl.program_id(0) == 0) & (pl.program_id(1) == 0))
    def _():
        for k, ref in enumerate(refs):
            ref[...] = earlier[k][...] if earlier else jnp.zeros_like(ref)


def run(body, step, extent, in_arrays, in_kinds, outs, scratch, flops, skip=0, aliases={}):
    def spec(kind, shape):
        lead = (0,) * len(shape)
        if kind == "m":
            return pl.BlockSpec(memory_space=pltpu.SMEM)
        if kind == "x":
            return pl.BlockSpec(memory_space=pl.ANY)
        block, at = {
            "R": (step[:1] + shape[1:-1] + step[1:], lambda c, r: (r + skip,) + lead[2:] + (c,)),
            "N": (step + shape[2:], lambda c, r: (r + skip, c) + lead[2:]),
            "r": (step[:1] + shape[1:-1] + step[1:], lambda c, r: (r,) + lead[2:] + (c,)),
            "n": (step + shape[2:], lambda c, r: (r, c) + lead[2:]),
            "s": (shape[:-2] + step, lambda c, r: lead[2:] + (r, c)),
            "c": (shape[:-1] + step[1:], lambda c, r: lead[1:] + (c,)),
            "t": (step[:1] + shape[1:], lambda c, r: (r,) + lead[1:]),
            "p": ((1,) + step[:1] + shape[2:], lambda c, r: (c, r) + lead[2:]),
            "q": (step[1:] + shape[1:], lambda c, r: (c,) + lead[1:]),
            "w": (shape, lambda c, r: lead),
        }[kind]
        return pl.BlockSpec(block, at)

    moved = sum(a.size * a.dtype.itemsize for a in in_arrays)
    return pl.pallas_call(
        body,
        grid=(extent[1] // step[1], extent[0] // step[0]),
        in_specs=[spec(kind, a.shape) for kind, a in zip(in_kinds, in_arrays)],
        out_specs=[spec(kind, shape) for kind, shape, _ in outs],
        out_shape=[jax.ShapeDtypeStruct(shape, dtype) for _, shape, dtype in outs],
        scratch_shapes=scratch,
        input_output_aliases=aliases,
        compiler_params=pltpu.CompilerParams(vmem_limit_bytes=VMEM_LIMIT),
        cost_estimate=pl.CostEstimate(flops=flops, bytes_accessed=moved, transcendentals=0),
    )(*in_arrays)


def all_low(w):
    return jnp.concatenate([w[k * PAIR_DIM : (k + 1) * PAIR_DIM].T for k in range(3)], axis=0)


def all_back(w):
    return jnp.concatenate([w[k * PAIR_DIM : (k + 1) * PAIR_DIM] for k in range(3)], axis=1)


def kernel_open(
    stays, pair, pair_home, table, right, mask, vectors, w_all, x_out, mean_out, scale_out, gate_out, sides_out, sides
):
    right_low = right[...]
    at_home = stays[0] == 1
    x = jnp.concatenate(
        [
            jnp.where(at_home, pair_home[t], pair[t]).T.astype(WIDE) + dot_tn(table[t], right_low)
            for t in range(pair.shape[0])
        ],
        axis=1,
    )
    front(
        x, column(vectors[OUT_GAIN]), all_low(w_all), cat(mask), x_out, mean_out, scale_out, gate_out,
        sides,
    )
    send_pair(sides, sides_out)


def kernel_middle(
    mixed, x_in, gate_in, mask, vectors, w_out, w_all,
    x_out, mean_out, scale_out, gate_out, sides_out, arrived, sides,
):
    arrived[...] = swapped(mixed[...])
    *_, update = triangle_update(cat(arrived).astype(WIDE), column(vectors[OUT_TRI]), w_out[...].T)
    x = cat(x_in).astype(WIDE) + cat(gate_in).astype(WIDE) * update
    front(
        x, column(vectors[IN_GAIN]), all_low(w_all), cat(mask),
        x_out, mean_out, scale_out, gate_out, sides,
    )
    send_pair(sides, sides_out)


def kernel_turn(mixed, x_in, gate_in, cot, vectors, w_out, w_up, w_down, *rest):
    (
        pair_out, x_grad, gate_grad, mixed_grad, g_out, g_tri, g_up, g_down, g_pair, g_bias,
        arrived, leaving,
    ) = rest[-12:]
    rows = x_in.shape[0]
    arrived[...] = swapped(mixed[...])
    up_low, up_back = w_up[...].T, w_up[...]
    down_low, down_back = w_down[...].T, w_down[...]
    tri_col, pair_col = column(vectors[IN_TRI]), column(vectors[PAIR_GAIN])
    zero_first(g_out, g_tri, g_up, g_down, g_pair, g_bias, earlier=rest[3:-12])
    chunk = PAIR_DIM

    gate = cat(gate_in).astype(WIDE)
    mix_parts = triangle_update(cat(arrived).astype(WIDE), tri_col, w_out[...].T)
    x = cat(x_in).astype(WIDE) + gate * mix_parts[-1]
    hat, scale = norm_parts(x)
    normed = (hat * pair_col).astype(LOW)
    cot_low = jnp.concatenate([cot[t].T for t in range(rows)], axis=1)
    total = x + column(vectors[PAIR_BIAS])
    normed_grad = jnp.zeros_like(x)
    for c in range(FFN_PAIR // chunk):
        part = slice(c * chunk, (c + 1) * chunk)
        act, slope = gelu_parts(dot_nn(up_low[part], normed))
        act_low = act.astype(LOW)
        total = total + dot_nn(down_low[:, part], act_low)
        hidden_grad = (dot_nn(down_back[part], cot_low) * slope).astype(LOW)
        normed_grad = normed_grad + dot_nn(up_back[:, part], hidden_grad)
        g_up[:, part] += dot_nt(normed, hidden_grad)
        g_down[part] += dot_nt(act_low, cot_low)
    total_low = total.astype(LOW)
    width = total.shape[1] // rows
    for t in range(rows):
        pair_out[t] = total_low[:, t * width : (t + 1) * width].T
    cot_wide = cot_low.astype(WIDE)
    g_bias[...] += jnp.sum(cot_wide, axis=1, keepdims=True)
    back, grad_gain = norm_back(normed_grad, hat, scale, pair_col)
    g_pair[...] += grad_gain
    grad = cot_wide + back
    put(x_grad, grad)
    mix_grad, gates, grad_out, grad_tri = post_back(grad, gate, *mix_parts, tri_col, w_out[...])
    put(leaving, mix_grad)
    put(gate_grad, gates)
    g_out[...] += grad_out
    g_tri[...] += grad_tri
    mixed_grad[...] = swapped(leaving[...])


def kernel_return(
    sides_grad, x_after, mean_after, scale_after, gate_after, grad_in, mask, vectors, w_after,
    mixed, gate_in, w_out,
    x_grad, gate_grad, mixed_grad, g_after, g_gain, g_out, g_tri,
    sides, arrived, leaving,
):
    take_pair(sides_grad, sides)
    arrived[...] = swapped(mixed[...])
    tri_col = column(vectors[OUT_TRI])
    zero_first(g_after, g_gain, g_out, g_tri)
    grad, grad_w, grad_gain = front_back(
        cat(grad_in).astype(WIDE), cat(x_after).astype(WIDE), cat(mean_after), cat(scale_after),
        cat(sides), cat(gate_after),
        cat(mask), column(vectors[IN_GAIN]), all_back(w_after),
    )
    g_after[...] += grad_w
    g_gain[...] += grad_gain
    put(x_grad, grad)
    mix_parts = triangle_update(cat(arrived).astype(WIDE), tri_col, w_out[...].T)
    mix_grad, gates, grad_out, grad_tri = post_back(
        grad, cat(gate_in).astype(WIDE), *mix_parts, tri_col, w_out[...]
    )
    put(leaving, mix_grad)
    put(gate_grad, gates)
    g_out[...] += grad_out
    g_tri[...] += grad_tri
    mixed_grad[...] = swapped(leaving[...])


def kernel_close(
    sides_grad, x_after, mean_after, scale_after, gate_after, grad_in, mask, vectors, w_after,
    table, right,
    pair_grad, table_grad, right_grad, g_after, g_gain, sides,
):
    take_pair(sides_grad, sides)
    zero_first(g_after, g_gain)

    @pl.when(pl.program_id(1) == 0)
    def _():
        right_grad[...] = jnp.zeros_like(right_grad)

    grad, grad_w, grad_gain = front_back(
        cat(grad_in).astype(WIDE), cat(x_after).astype(WIDE), cat(mean_after), cat(scale_after),
        cat(sides), cat(gate_after),
        cat(mask), column(vectors[OUT_GAIN]), all_back(w_after),
    )
    g_after[...] += grad_w
    g_gain[...] += grad_gain
    low = grad.astype(LOW)
    rows = table.shape[0]
    width = low.shape[1] // rows
    for t in range(rows):
        own = low[:, t * width : (t + 1) * width]
        pair_grad[t] = own.T
        table_grad[0, t] = dot_nt(right[...], own)
        right_grad[...] += dot_nn(table[t], own)


CHANNELS = 8


def kernel_mix(incoming, left, right, *outs):
    parts, count, rows, length = left.shape
    part = rows // len(outs)
    for c in range(count):
        a = left[:, c].reshape(length, length)
        b = right[:, c].reshape(length, length)
        mixed = dot_tn(a, b) if incoming else dot_nt(a, b)
        mixed = mixed.astype(LOW).reshape(parts, rows, length)
        for k, out in enumerate(outs):
            out[:, c] = mixed[:, k * part : (k + 1) * part]


def kernel_mix_back(incoming, *refs):
    *grads, left, right, out = refs
    parts, count, rows, length = left.shape
    for c in range(count):
        g = jnp.concatenate([grad[:, c] for grad in grads], axis=1).reshape(length, length)
        a = left[:, c].reshape(length, length)
        b = right[:, c].reshape(length, length)
        a_grad = dot_nt(b, g) if incoming else dot_nn(g, b)
        b_grad = dot_nn(a, g) if incoming else dot_tn(g, a)
        out[:, 0, c] = a_grad.astype(LOW).reshape(parts, rows, length)
        out[:, 1, c] = b_grad.astype(LOW).reshape(parts, rows, length)


def mix(sides, incoming, pieces=1):
    parts, double, rows, length = sides.shape
    share = double // 2
    count = min(CHANNELS, share)
    steps = share // count
    block = (parts, count, rows, length)
    part = (parts, count, rows // pieces, length)
    return pl.pallas_call(
        lambda *refs: kernel_mix(incoming, *refs),
        grid=(steps,),
        in_specs=[
            pl.BlockSpec(block, lambda c: (0, c, 0, 0)),
            pl.BlockSpec(block, lambda c: (0, c + steps, 0, 0)),
        ],
        out_specs=[pl.BlockSpec(part, lambda c: (0, c, 0, 0))] * pieces,
        out_shape=[jax.ShapeDtypeStruct((parts, share) + part[2:], LOW)] * pieces,
        compiler_params=pltpu.CompilerParams(vmem_limit_bytes=VMEM_LIMIT),
        cost_estimate=pl.CostEstimate(
            flops=2 * share * length**3, bytes_accessed=3 * share * length * length * 2,
            transcendentals=0,
        ),
    )(sides, sides)


def mix_back(grads, sides, incoming):
    parts, double, rows, length = sides.shape
    share = double // 2
    count = min(CHANNELS, share)
    steps = share // count
    block = (parts, count, rows, length)
    part = (parts, count, rows // len(grads), length)
    out = pl.pallas_call(
        lambda *refs: kernel_mix_back(incoming, *refs),
        grid=(steps,),
        in_specs=[pl.BlockSpec(part, lambda c: (0, c, 0, 0))] * len(grads)
        + [
            pl.BlockSpec(block, lambda c: (0, c, 0, 0)),
            pl.BlockSpec(block, lambda c: (0, c + steps, 0, 0)),
        ],
        out_specs=pl.BlockSpec((parts, 2, count, rows, length), lambda c: (0, 0, c, 0, 0)),
        out_shape=jax.ShapeDtypeStruct((parts, 2, share, rows, length), LOW),
        compiler_params=pltpu.CompilerParams(vmem_limit_bytes=VMEM_LIMIT),
        cost_estimate=pl.CostEstimate(
            flops=4 * share * length**3, bytes_accessed=5 * share * length * length * 2,
            transcendentals=0,
        ),
    )(*grads, sides, sides)
    return out.reshape(sides.shape)


def share_rows(share):
    return -(-(share + 2 * LANES) // (TILE * LANES)) * TILE


def whole(shape):
    return pl.BlockSpec(shape, lambda *_: (0,) * len(shape))


def one_call(body, scalars, in_arrays, outs, scratch=()):
    return pl.pallas_call(
        body,
        in_specs=[pl.BlockSpec(memory_space=pltpu.SMEM)] * len(scalars)
        + [whole(a.shape) for a in in_arrays],
        out_specs=[whole(shape) for shape, _ in outs],
        out_shape=[jax.ShapeDtypeStruct(shape, dtype) for shape, dtype in outs],
        scratch_shapes=list(scratch),
        grid=(1,),
        compiler_params=pltpu.CompilerParams(vmem_limit_bytes=VMEM_LIMIT),
    )(*scalars, *in_arrays)


def lane_in(shape, start, width):
    lane = lax.broadcasted_iota(jnp.int32, shape, 1)
    return (lane >= start) & (lane < start + width)


def rolled(value, shift):
    shift %= LANES
    return pltpu.roll(value, shift, 1) if shift else value


def share_order(layout):
    return [((d // layout.rows) % 2, d // (2 * layout.rows), d % layout.rows) for d in range(layout.devices)]


def unpack(layout, shares, share):
    at, _ = first_rows()
    height = shares.shape[3]
    first = [share * d // LANES for d in range(layout.devices)]
    order = share_order(layout)
    matrices = [
        (at.w_query, NODE_DIM, 3, 3 * HEADS_WIDTH),
        (at.w_attn_out, HEADS_WIDTH, 1, NODE_DIM),
        (at.w_node_up, NODE_DIM, 1, FFN_NODE),
        (at.w_node_down, FFN_NODE, 1, NODE_DIM),
        (at.w_outer, OUTER * OUTER, 1, PAIR_DIM),
        (at.outgoing.w_left, 3 * PAIR_DIM, 1, TRI_DIM),
        (at.outgoing.w_tri_out, TRI_DIM, 1, PAIR_DIM),
        (at.incoming.w_left, 3 * PAIR_DIM, 1, TRI_DIM),
        (at.incoming.w_tri_out, TRI_DIM, 1, PAIR_DIM),
        (at.w_pair_up, PAIR_DIM, 1, FFN_PAIR),
        (at.w_pair_down, FFN_PAIR, 1, PAIR_DIM),
    ]
    small = [(at.embed, 8), (at.gain_one, 2), (at.gain_two, 2), (at.gain_three, 2)]
    small += [
        (start, 1)
        for start in (
            at.outgoing.gain_in, at.outgoing.gain_tri, at.incoming.gain_in, at.incoming.gain_tri,
            at.gain_pair, at.bias_pair,
        )
    ]

    def body(shares_ref, vectors, bias_out, factors_out, *rest):
        outs, flat, narrow = rest[:-2], rest[-2], rest[-1]
        for d, place in enumerate(order):
            block = shares_ref[place].astype(WIDE)
            if d:
                tail = flat[first[d] : first[d] + 1]
                flat[first[d] : first[d] + height] = block
                flat[first[d] : first[d] + 1] = block[:1] + tail
            else:
                flat[:height] = block
        row = 0
        vectors[...] = jnp.zeros_like(vectors)
        for start, count in small:
            vectors[row : row + count] = flat[start : start + count]
            row += count
        for out, (place, rows, count, width) in zip(outs, matrices):
            pieces = width // count // LANES
            for m in range(count):
                for a in range(pieces):
                    start = place + m * rows * pieces + a
                    value = (
                        flat[pl.ds(start, rows, stride=pieces), :]
                        if pieces > 1
                        else flat[start : start + rows]
                    )
                    lane = (m * pieces + a) * LANES
                    out[:, lane : lane + LANES] = value.astype(LOW)
        per_row = LANES // HEADS
        shape = (HEADS, LANES)
        value = flat[at.w_bias : at.w_bias + HEADS]
        for a in range(per_row):
            kept = jnp.where(lane_in(shape, 0, HEADS), rolled(value, -HEADS * a), 0.0)
            narrow[pl.ds(a, HEADS, stride=per_row), :] = kept
        bias_out[...] = narrow[:PAIR_DIM].astype(LOW)
        per_row = LANES // OUTER
        count = NODE_DIM // per_row
        shape = (count, LANES)
        left, right = (flat[start : start + count] for start in (at.w_left_node, at.w_right_node))
        for a in range(per_row):
            kept = jnp.where(lane_in(shape, 0, OUTER), rolled(left, -OUTER * a), 0.0)
            kept += jnp.where(lane_in(shape, OUTER, OUTER), rolled(right, OUTER - OUTER * a), 0.0)
            narrow[pl.ds(a, count, stride=per_row), :] = kept
        factors_out[...] = narrow[...].astype(LOW)

    return one_call(
        body,
        (),
        (shares,),
        [((24, LANES), WIDE), ((PAIR_DIM, LANES), LOW), ((NODE_DIM, LANES), LOW)]
        + [((rows, width), LOW) for _, rows, _, width in matrices],
        [pltpu.VMEM((first[-1] + height + TILE, LANES), WIDE), pltpu.VMEM((NODE_DIM, LANES), WIDE)],
    )


def pack(layout, share, scalars, grads, node_parts):
    at, total = first_rows()
    height = share_rows(share)
    first = [share * d // LANES for d in range(layout.devices)]
    order = share_order(layout)
    many = len(grads)

    def body(scalar_ref, *refs):
        ins, rest = refs[:many], refs[many:]
        (
            key_value, query_low, start, normed_own, normed_all, after_grad, vectors, w_projections,
            act_low, final_low, normed_two, hidden_grad, attended, after_low, g_factors,
            out, node_parts_out, flat, narrow, steps,
        ) = rest

        def store(place, count, value):
            rows, pieces = value.shape[0], value.shape[1] // count // LANES
            for m in range(count):
                for a in range(pieces):
                    lane = (m * pieces + a) * LANES
                    begin = place + m * rows * pieces + a
                    part = value[:, lane : lane + LANES]
                    if pieces > 1 and rows > 1:
                        flat[pl.ds(begin, rows, stride=pieces), :] = part
                    else:
                        flat[begin : begin + rows] = part

        flat[total:] = jnp.zeros((flat.shape[0] - total, LANES), WIDE)
        for ref, (place, count, _) in zip(ins, grads):
            store(place, count, row_of(ref[...]) if ref.shape[1] == 1 else ref[...])
        store(at.w_node_down, 1, dot_tn(act_low[...], final_low[...]))
        store(at.w_node_up, 1, dot_tn(normed_two[...], hidden_grad[...]))
        store(at.w_attn_out, 1, dot_tn(attended[...], after_low[...]))
        per_row = LANES // OUTER
        count = NODE_DIM // per_row
        narrow[...] = g_factors[...]
        left = jnp.zeros((count, LANES), WIDE)
        right = left
        for a in range(per_row):
            piece = narrow[pl.ds(a, count, stride=per_row), :]
            inside = lane_in(piece.shape, OUTER * a, OUTER)
            left = jnp.where(inside, rolled(piece, OUTER * a), left)
            right = jnp.where(inside, rolled(piece, OUTER * a - OUTER), right)
        store(at.w_left_node, 1, left)
        store(at.w_right_node, 1, right)

        store(at.w_query, 1, dot_tn(normed_own[...], query_low[...]))
        store(at.w_key, 2, dot_tn(normed_all[...], key_value[...]))
        steps[...] = dot_nt(key_value[...], w_projections[:, HEADS_WIDTH:])
        local_rows = query_low.shape[0]
        own = pl.ds(pl.multiple_of(scalar_ref[1] * local_rows, local_rows), local_rows)
        steps[own, :] += dot_nt(query_low[...], w_projections[:, :HEADS_WIDTH])
        hat, scale = row_norm(start[...])
        part, grad_gain = row_norm_back(steps[...], hat, scale, vector(vectors, GAIN_ONE))
        for r in range(node_parts_out.shape[0]):
            for a in range(NODE_DIM // LANES):
                piece = part[r * local_rows : (r + 1) * local_rows, a * LANES : (a + 1) * LANES]
                node_parts_out[r, a * local_rows : (a + 1) * local_rows] = piece.astype(LOW)
        store(at.gain_one, 1, grad_gain)
        flat[at.embed : at.embed + 2 * RECYCLES] = jnp.zeros((2 * RECYCLES, LANES), WIDE)
        column_sum = jnp.sum(after_grad[...], axis=0, keepdims=True)
        column_sum += jnp.sum(part, axis=0, keepdims=True)
        for a in range(NODE_DIM // LANES):
            place = at.embed + (NODE_DIM // LANES) * scalar_ref[0] + a
            flat[pl.ds(place, 1), :] = column_sum[:, a * LANES : (a + 1) * LANES]
        for d, where in enumerate(order):
            out[where] = flat[first[d] : first[d] + height].astype(LOW)

    shape = (2, layout.crops // 2, layout.rows, height, LANES)
    return one_call(
        body,
        (scalars,),
        tuple(array for _, _, array in grads) + tuple(node_parts),
        [(shape, LOW), ((layout.rows, node_parts[1].shape[0] * NODE_DIM // LANES, LANES), LOW)],
        [
            pltpu.VMEM((first[-1] + height + TILE, LANES), WIDE),
            pltpu.VMEM((NODE_DIM, LANES), WIDE),
            pltpu.VMEM(node_parts[2].shape, WIDE),
        ],
    )


def row_norm(x):
    centered = x - jnp.mean(x, axis=-1, keepdims=True)
    scale = lax.rsqrt(jnp.mean(centered * centered, axis=-1, keepdims=True) + EPS_NORM)
    return centered * scale, scale


def row_norm_back(grad, hat, scale, gain):
    grad_gain = jnp.sum(grad * hat, axis=0, keepdims=True)
    wide = grad * gain
    inner = jnp.mean(wide * hat, axis=-1, keepdims=True)
    return scale * (wide - jnp.mean(wide, axis=-1, keepdims=True) - hat * inner), grad_gain


def vector(ref, rows):
    return jnp.concatenate([ref[r : r + 1] for r in range(rows.start, rows.stop)], axis=1)


def by_head(value):
    return jnp.concatenate(
        [
            jnp.where(lane_in(value.shape, h * HEAD_DIM, HEAD_DIM), value, 0.0)
            for h in range(HEADS)
        ],
        axis=0,
    )


def head_sum(value):
    rows = value.shape[0] // HEADS
    parts = [value[h * rows : (h + 1) * rows] for h in range(HEADS)]
    return sum(
        jnp.where(lane_in(part.shape, h * HEAD_DIM, HEAD_DIM), part, 0.0)
        for h, part in enumerate(parts)
    )


SCORE_SCALE = HEAD_DIM ** (-0.5)
KEEP_LANE = 2 * OUTER


def node_forward(
    recycle, node_ref, all_ref, bias_ref, keep, keep_rows, vectors, w_projections, w_attn_out, w_up, w_down,
    w_factors,
    node_out, factors_out, start_out, normed_own, normed_out, soft_out, heads_out, key_out, value_out,
    attended_out, after_out, act_out, slope_out, final_out, flat,
):
    pieces = NODE_DIM // LANES
    length = all_ref.shape[0] // pieces
    embed = jnp.concatenate(
        [vectors[pl.ds(pieces * recycle[0] + a, 1), :] for a in range(pieces)], axis=1
    )
    flat[...] = all_ref[...].astype(WIDE)
    all_rows = jnp.concatenate(
        [flat[pl.ds(a, length, stride=pieces), :] for a in range(pieces)], axis=1
    )
    gain = vector(vectors, GAIN_ONE)
    start_all = all_rows + embed
    normed_all = (row_norm(start_all)[0] * gain).astype(LOW)
    start_out[...] = start_all
    normed_out[...] = normed_all
    start = node_ref[...].astype(WIDE) + embed
    normed = (row_norm(start)[0] * gain).astype(LOW)
    normed_own[...] = normed
    query = dot_nn(normed, w_projections[:, :HEADS_WIDTH]).astype(LOW).astype(WIDE)
    heads = by_head(query).astype(LOW)
    key_value = dot_nn(normed_all, w_projections[:, HEADS_WIDTH:]).astype(LOW)
    key, value = key_value[:, :HEADS_WIDTH], key_value[:, HEADS_WIDTH:]
    heads_out[...] = heads
    key_out[...] = key
    value_out[...] = value
    scores = dot_nt(heads, key) * SCORE_SCALE + bias_ref[...] + (keep[...] - 1.0) * MASK_FILL
    powers = jnp.exp(scores - jnp.max(scores, axis=-1, keepdims=True))
    soft = powers / jnp.sum(powers, axis=-1, keepdims=True)
    soft_out[...] = soft
    attended = head_sum(dot_nn(soft.astype(LOW), value)).astype(LOW)
    attended_out[...] = attended
    after = start + dot_nn(attended, w_attn_out[...])
    after_out[...] = after
    normed = (row_norm(after)[0] * vector(vectors, GAIN_TWO)).astype(LOW)
    act, slope = gelu_parts(dot_nn(normed, w_up[...]))
    act_out[...] = act.astype(LOW)
    slope_out[...] = slope
    final = after + dot_nn(act.astype(LOW), w_down[...])
    final_out[...] = final
    node_out[...] = final.astype(LOW)
    normed = (row_norm(final)[0] * vector(vectors, GAIN_THREE)).astype(LOW)
    factors = dot_nn(normed, w_factors[...])
    factors = jnp.where(lane_in(factors.shape, KEEP_LANE, 1), keep_rows[...], factors).astype(LOW)
    factors_out[...] = jnp.broadcast_to(factors[None], factors_out.shape)


def node_backward(
    sources, factor_ref, cot, vectors, soft_ref, heads, key, value, after_ref, slope, final_ref,
    w_attn_out, w_up, w_down, w_factors,
    key_value_out, query_out, score_out, after_grad_out, final_low_out, normed_two_out,
    hidden_out, after_low_out, g_factors, g_two, g_three,
):
    ranks = key_value_out.shape[0] // cot.shape[0]
    left = factor_ref[sources[0]].astype(WIDE)
    right = sum(factor_ref[sources[1 + r]].astype(WIDE) for r in range(ranks))
    rows = jnp.where(lane_in(left.shape, 0, OUTER), left, right).astype(LOW)
    hat, scale = row_norm(final_ref[...])
    gain = vector(vectors, GAIN_THREE)
    g_factors[...] = dot_tn((hat * gain).astype(LOW), rows)
    part, g_three[...] = row_norm_back(dot_nt(rows, w_factors[...]), hat, scale, gain)
    final_grad = cot[...].astype(WIDE) + part
    final_low = final_grad.astype(LOW)
    final_low_out[...] = final_low
    hidden_grad = (dot_nt(final_low, w_down[...]) * slope[...]).astype(LOW)
    hidden_out[...] = hidden_grad
    hat, scale = row_norm(after_ref[...])
    gain = vector(vectors, GAIN_TWO)
    normed_two_out[...] = (hat * gain).astype(LOW)
    part, g_two[...] = row_norm_back(dot_nt(hidden_grad, w_up[...]), hat, scale, gain)
    after_grad = final_grad + part
    after_grad_out[...] = after_grad
    after_low = after_grad.astype(LOW)
    after_low_out[...] = after_low
    attended_grad = dot_nt(after_low, w_attn_out[...]).astype(LOW).astype(WIDE)
    grad_heads = by_head(attended_grad).astype(LOW)
    soft = soft_ref[...]
    soft_grad = dot_nt(grad_heads, value[...])
    score_grad = soft * (soft_grad - jnp.sum(soft_grad * soft, axis=-1, keepdims=True))
    score_low = score_grad.astype(LOW)
    score_out[...] = score_low
    key_part = dot_tn(score_low, heads[...]) * SCORE_SCALE
    key_value_out[:, :HEADS_WIDTH] = key_part.astype(LOW)
    key_value_out[:, HEADS_WIDTH:] = dot_tn(soft.astype(LOW), grad_heads).astype(LOW)
    query_out[...] = (head_sum(dot_nn(score_low, key[...])) * SCORE_SCALE).astype(LOW)


def outer_tables(
    sources, factors, w_outer, table_out, right_out, left_out, mask_out, w_wide, steps
):
    local_rows = left_out.shape[0]
    ranks = right_out.shape[1] // local_rows
    left_low = factors[sources[0]][:, :OUTER]
    left_out[...] = left_low
    right = jnp.concatenate([factors[sources[1 + r]].astype(WIDE) for r in range(ranks)], axis=0)
    turned = right.T
    right_out[...] = turned[OUTER : 2 * OUTER].astype(LOW)
    own_keep = factors[sources[0]][:, KEEP_LANE : KEEP_LANE + 1].astype(WIDE)
    mask_out[:, 0, :] = own_keep * turned[KEEP_LANE : KEEP_LANE + 1]
    w_wide[...] = w_outer[...].astype(WIDE)
    for q in range(OUTER):
        w_q = w_wide[pl.ds(q, OUTER, stride=OUTER), :].astype(LOW)
        steps[q] = dot_nn(left_low, w_q)
    table_out[...] = jnp.swapaxes(steps[...], 0, 1).astype(LOW)


def outer_backward(table_grad, right_grad, left, w_outer, factors_out, g_outer, w_wide, steps):
    crops, ranks, local_rows, _ = factors_out.shape
    steps[...] = jnp.swapaxes(jnp.sum(table_grad[...], axis=0), 0, 1)
    w_wide[...] = w_outer[...].astype(WIDE)
    left_grad = jnp.zeros((local_rows, OUTER), WIDE)
    for q in range(OUTER):
        grad_q = steps[q].astype(LOW)
        w_q = w_wide[pl.ds(q, OUTER, stride=OUTER), :].astype(LOW)
        left_grad = left_grad + dot_nt(grad_q, w_q)
        g_outer[pl.ds(q, OUTER, stride=OUTER), :] = dot_tn(left[...], grad_q)
    right_rows = right_grad[...].T
    for r in range(ranks):
        block = jnp.concatenate(
            [
                left_grad,
                right_rows[r * local_rows : (r + 1) * local_rows],
                jnp.zeros((local_rows, LANES - 2 * OUTER), WIDE),
            ],
            axis=1,
        ).astype(LOW)
        for c in range(crops):
            factors_out[c, r] = block


def low_of(x):
    return x.astype(LOW)


def local(layout, node, pair, recycle, mask, node_cot, pair_cot, master, first, second):
    crops, ranks = layout.crops, layout.rows
    devices = crops * ranks
    local_rows, length = node.shape[1], pair.shape[2]
    share = TRI_DIM // ranks
    node, pair, node_cot, pair_cot = node[0], pair[0], node_cot[0], pair_cot[0]

    crop_at, row_at = lax.axis_index("crop"), lax.axis_index("row")
    here = crop_at * ranks + row_at
    partner = layout.work_place(here)
    stays = partner == here
    work_crop, work_row = partner // ranks, partner % ranks
    moved = lambda array: jnp.where(stays, array, lax.ppermute(array, BOTH, layout.moves))

    at, _ = first_rows()

    amount = master.shape[0]
    height = share_rows(amount)
    offset = (here * (amount % LANES)) % LANES
    shard = lax.dynamic_update_slice(jnp.zeros(height * LANES, LOW), low_of(master), (offset,))
    node_rows = local_rows * NODE_DIM // LANES
    shards = jnp.concatenate([shard.reshape(height, LANES), node.reshape(-1, LANES)], axis=0)
    shards = spread(shards, ranks, "row").reshape(ranks, -1, LANES)
    shards, pair = lax.optimization_barrier((shards, pair))
    node_all = shards[:, height:].reshape(-1, LANES)
    shards = shards[:, :height].reshape(-1, LANES)
    shards = spread(shards, crops // 2, BOTH, layout.chips)
    shards = spread(shards, 2, BOTH, layout.cores)
    shards = shards.reshape(2, crops // 2, ranks, height, LANES)
    (
        vectors, w_bias, w_factors, w_projections, w_attn_out, w_node_up, w_node_down, w_outer,
        w_out_all, w_out_end, w_in_all, w_in_end, w_pair_up, w_pair_down,
    ) = unpack(layout, shards, amount)
    pair_plane = lax.ppermute(pair, BOTH, layout.moves)
    keep = mask.astype(WIDE)
    keep_rows = lax.dynamic_slice_in_dim(keep[0], row_at * local_rows, local_rows, 0)[:, None]

    pair_bias = jnp.einsum("ijd,dh->hij", pair, w_bias[:, :HEADS], preferred_element_type=WIDE)
    rows_low = lambda width: ((local_rows, width), LOW)
    rows_wide = lambda width: ((local_rows, width), WIDE)
    by_heads = (HEADS * local_rows, length)
    (
        node_out, factors, start_all, normed_own, normed_all, soft, heads, key, value, attended, after, act_low,
        slope, node_final,
    ) = one_call(
        node_forward,
        (recycle,),
        (node, node_all, pair_bias.reshape(by_heads), keep, keep_rows, vectors, w_projections, w_attn_out,
         w_node_up, w_node_down, w_factors),
        [rows_low(NODE_DIM), ((2 * ranks, local_rows, LANES), LOW), ((length, NODE_DIM), WIDE),
         rows_low(NODE_DIM), ((length, NODE_DIM), LOW), (by_heads, WIDE), (by_heads[:1] + (HEADS_WIDTH,), LOW),
         ((length, HEADS_WIDTH), LOW), ((length, HEADS_WIDTH), LOW), rows_low(HEADS_WIDTH),
         rows_wide(NODE_DIM), rows_low(FFN_NODE), rows_wide(FFN_NODE), rows_wide(NODE_DIM)],
        [pltpu.VMEM(node_all.shape, WIDE)],
    )

    factors = exchange(factors, BOTH, layout.slabs)
    factors, pair_cot = lax.optimization_barrier((factors, pair_cot))
    everyone = jnp.arange(ranks, dtype=jnp.int32)
    slab = 2 * ranks
    sources = jnp.concatenate([partner[None], work_crop * ranks + everyone]).astype(jnp.int32) % slab
    table, right, left, mask_plane = one_call(
        outer_tables,
        (sources,),
        (factors, w_outer),
        [((local_rows, OUTER, PAIR_DIM), LOW), ((OUTER, length), LOW), ((local_rows, OUTER), LOW),
         ((local_rows, 1, length), WIDE)],
        [pltpu.VMEM((OUTER * OUTER, PAIR_DIM), WIDE), pltpu.VMEM((OUTER, local_rows, PAIR_DIM), WIDE)],
    )

    step = (min(TILE, local_rows), min(LANES, length))
    extent = (local_rows, length)
    pieces = length // step[1]
    state = (local_rows, TRI_DIM, length)
    line = (local_rows, 1, length)
    sides_shape = (ranks, 2 * share, local_rows, length)
    mixed_shape = (TRI_DIM, local_rows, length)
    natural = (local_rows, length, PAIR_DIM)
    buffer = lambda channels: pltpu.VMEM((step[0], channels, step[1]), LOW)
    trade = lambda blocks: exchange(blocks, BOTH, layout.groups)
    merge = lambda blocks: blocks.reshape((TRI_DIM,) + blocks.shape[2:])
    split = lambda blocks: blocks.reshape((ranks, share) + blocks.shape[1:])
    unit = 2 * local_rows * length * PAIR_DIM * PAIR_DIM
    front_outs = (
        ("r", state, LOW), ("r", line, WIDE), ("r", line, WIDE), ("r", state, LOW),
        ("s", sides_shape, LOW),
    )
    square = (TRI_DIM, PAIR_DIM)
    gain_shape = (PAIR_DIM, 1)
    after_shape = (PAIR_DIM, 2 * TRI_DIM + PAIR_DIM)

    x_one, mean_tri_out, scale_tri_out, gate_tri_out, sides = run(
        kernel_open, step, extent,
        (stays.astype(jnp.int32)[None], pair_plane, pair, table, right, mask_plane, vectors, w_out_all),
        "mnntcrww", front_outs, [buffer(2 * TRI_DIM)], 4 * unit,
    )
    sides_out, cot_plane = lax.optimization_barrier((trade(sides), moved(pair_cot)))
    mixed_out = merge(trade(mix(sides_out, False)[0]))
    x_two, mean_tri_in, scale_tri_in, gate_tri_in, sides = run(
        kernel_middle, step, extent,
        (mixed_out, x_one, gate_tri_out, mask_plane, vectors, w_out_end, w_in_all), "srrrwww", front_outs, [buffer(TRI_DIM), buffer(2 * TRI_DIM)], 5 * unit,
    )
    sides_in = trade(sides)
    turns = 2 if local_rows % (2 * TILE) == 0 else 1
    turn_rows = local_rows // turns
    mixed_in = [merge(trade(piece)) for piece in mix(sides_in, True, turns)]
    turned, grads_in = (), []
    for k in range(turns):
        turned = run(
            kernel_turn, step, (turn_rows, length),
            (mixed_in[k], x_two, gate_tri_in, cot_plane, vectors, w_in_end, w_pair_up, w_pair_down,
             *turned),
            "sRRNwwww" + ("xxxwwwwww" if k else ""),
            (("N", natural, LOW), ("R", state, LOW), ("R", state, LOW),
             ("s", (TRI_DIM, turn_rows, length), LOW),
             ("w", square, WIDE), ("w", gain_shape, WIDE), ("w", (PAIR_DIM, FFN_PAIR), WIDE),
             ("w", (FFN_PAIR, PAIR_DIM), WIDE), ("w", gain_shape, WIDE), ("w", gain_shape, WIDE)),
            [buffer(TRI_DIM), buffer(TRI_DIM)], 32 * unit // turns,
            skip=k * turn_rows // step[0], aliases={8: 0, 9: 1, 10: 2} if k else {},
        )
        turned = list(turned)
        grads_in.append(trade(split(turned.pop(3))))
    pair_final, x_grad, gate_grad, g_in_out, g_in_tri, g_up, g_down, g_pair, g_bias = turned
    sides_grad = trade(mix_back(grads_in, sides_in, True))
    sides_grad, pair_out = lax.optimization_barrier((sides_grad, moved(pair_final)))
    x_grad, gate_grad, mixed_grad, g_in_all, g_in_gain, g_out_out, g_out_tri = run(
        kernel_return, step, extent,
        (sides_grad, x_two, mean_tri_in, scale_tri_in, gate_grad, x_grad, mask_plane,
         vectors, w_in_all, mixed_out, gate_tri_out, w_out_end),
        "srrrrrrwwsrw",
        (("r", state, LOW), ("r", state, LOW), ("s", mixed_shape, LOW), ("w", after_shape, WIDE),
         ("w", gain_shape, WIDE), ("w", square, WIDE), ("w", gain_shape, WIDE)),
        [buffer(2 * TRI_DIM), buffer(TRI_DIM), buffer(TRI_DIM)], 12 * unit,
    )
    sides_grad = trade(mix_back([trade(split(mixed_grad))], sides_out, False))
    pair_one_grad, table_grad, right_part, g_out_all, g_out_gain = run(
        kernel_close, step, extent,
        (sides_grad, x_one, mean_tri_out, scale_tri_out, gate_grad, x_grad, mask_plane,
         vectors, w_out_all, table, right),
        "srrrrrrwwtc",
        (("n", natural, LOW), ("p", (pieces, local_rows, OUTER, PAIR_DIM), WIDE),
         ("c", (OUTER, length), WIDE), ("w", after_shape, WIDE), ("w", gain_shape, WIDE)),
        [buffer(2 * TRI_DIM)], 8 * unit,
    )

    factor_grads, g_outer = one_call(
        outer_backward,
        (),
        (table_grad, right_part, left, w_outer),
        [((2, ranks, local_rows, LANES), LOW), ((OUTER * OUTER, PAIR_DIM), WIDE)],
        [pltpu.VMEM((OUTER * OUTER, PAIR_DIM), WIDE), pltpu.VMEM((OUTER, local_rows, PAIR_DIM), WIDE)],
    )
    factor_grads = exchange(factor_grads.reshape(slab, local_rows, LANES), BOTH, layout.slabs)
    factor_grads, pair_one_grad = lax.optimization_barrier((factor_grads, pair_one_grad))

    workers = layout.work_place(crop_at * ranks + everyone)
    sources = jnp.concatenate([partner[None], workers]).astype(jnp.int32) % slab
    (
        key_value, query_low, score_low, after_grad, final_low, normed_two, hidden_grad, after_low,
        g_factors, g_two, g_three,
    ) = one_call(
        node_backward,
        (sources,),
        (factor_grads, node_cot, vectors, soft, heads, key, value, after, slope, node_final,
         w_attn_out, w_node_up, w_node_down, w_factors),
        [((length, 2 * HEADS_WIDTH), LOW), rows_low(HEADS_WIDTH), (by_heads, LOW),
         rows_wide(NODE_DIM), rows_low(NODE_DIM), rows_low(NODE_DIM), rows_low(FFN_NODE),
         rows_low(NODE_DIM), ((NODE_DIM, LANES), WIDE), ((1, NODE_DIM), WIDE), ((1, NODE_DIM), WIDE)],
    )
    score_low = score_low.reshape(HEADS, local_rows, length)
    g_bias_head = jnp.einsum("ijd,hij->dh", pair, score_low, preferred_element_type=WIDE)
    g_bias_head = lax.optimization_barrier(g_bias_head).reshape(-1, LANES)
    pair_one_away = lax.ppermute(pair_one_grad, BOTH, layout.moves)
    grads = [
        (at.w_bias, 1, g_bias_head),
        (at.gain_two, 1, g_two),
        (at.gain_three, 1, g_three),
        (at.w_outer, 1, g_outer),
        (at.gain_pair, 1, g_pair),
        (at.w_pair_up, 1, g_up),
        (at.w_pair_down, 1, g_down),
        (at.bias_pair, 1, g_bias),
    ]
    for tri, g_all, g_gain, g_tri, g_out in (
        (at.outgoing, g_out_all, g_out_gain, g_out_tri, g_out_out),
        (at.incoming, g_in_all, g_in_gain, g_in_tri, g_in_out),
    ):
        grads += [
            (tri.gain_in, 1, g_gain),
            (tri.w_left, 3, g_all),
            (tri.gain_tri, 1, g_tri),
            (tri.w_tri_out, 1, g_out),
        ]

    blocks, node_blocks = pack(
        layout, amount, jnp.concatenate([recycle, row_at.astype(jnp.int32)[None]]), grads,
        (key_value, query_low, start_all, normed_own, normed_all, after_grad, vectors,
         w_projections, act_low, final_low, normed_two, hidden_grad, attended, after_low, g_factors),
    )
    total = lambda got: low_of(jnp.sum(got.astype(WIDE), axis=0))
    blocks = total(exchange(blocks, BOTH, layout.cores))
    blocks = total(exchange(blocks, BOTH, layout.chips))
    blocks = exchange(jnp.concatenate([blocks, node_blocks], axis=1), "row")
    pair_grad = jnp.where(stays, pair_one_grad, pair_one_away).astype(WIDE) + jnp.einsum(
        "hij,dh->ijd", score_low, w_bias[:, :HEADS], preferred_element_type=WIDE
    )
    blocks, pair_grad = lax.optimization_barrier((blocks, low_of(pair_grad)))
    blocks = jnp.sum(blocks.astype(WIDE), axis=0)
    node_parts = jnp.split(blocks[height:], NODE_DIM // LANES)
    node_grad = low_of(after_grad + jnp.concatenate(node_parts, axis=1))
    blocks = blocks[:height]
    grad_own = lax.dynamic_slice(blocks.reshape(-1), (offset,), (amount,))
    square_own = jnp.broadcast_to(jnp.sum(grad_own * grad_own), (1, LANES))
    last = jnp.concatenate([g_bias.reshape(1, LANES), square_own], axis=0)
    last = jnp.sum(spread(last, devices, BOTH).reshape(devices, 2, LANES), axis=0)
    bias_total = last[0]
    grad_norm = jnp.sqrt(last[1, 0])
    clipped = grad_own * (CLIP_NORM / jnp.maximum(grad_norm, CLIP_NORM))
    new_first = BETA_ONE * first + (1.0 - BETA_ONE) * clipped
    new_second = BETA_TWO * second + (1.0 - BETA_TWO) * clipped * clipped
    first_hat = new_first / (1.0 - BETA_ONE**ADAM_STEP)
    second_hat = new_second / (1.0 - BETA_TWO**ADAM_STEP)
    new_master = master - LEARN_RATE * (
        first_hat / (jnp.sqrt(second_hat) + ADAM_EPS) + WEIGHT_DECAY * master
    )
    return (
        node_out[None],
        pair_out[None],
        node_grad[None],
        pair_grad[None],
        grad_own,
        bias_total,
        grad_norm,
        new_master,
        new_first,
        new_second,
        low_of(new_master),
    )


def solution(mesh):
    layout = Layout(mesh.shape["crop"], mesh.shape["row"])
    return jax.shard_map(
        lambda *arrays: local(layout, *arrays),
        mesh=mesh,
        in_specs=(
            P("crop", "row", None),
            P("crop", "row", None, None),
            P("crop"),
            P("crop", None),
            P("crop", "row", None),
            P("crop", "row", None, None),
            P(("crop", "row")),
            P(("crop", "row")),
            P(("crop", "row")),
        ),
        out_specs=(
            P("crop", "row", None),
            P("crop", "row", None, None),
            P("crop", "row", None),
            P("crop", "row", None, None),
            P(("crop", "row")),
            P(),
            P(),
            P(("crop", "row")),
            P(("crop", "row")),
            P(("crop", "row")),
            P(("crop", "row")),
        ),
        check_vma=False,
    )
```

```python
import math
from typing import Any, NamedTuple

import jax
import jax.numpy as jnp
import numpy as np
from jax import lax
from jax.experimental import pallas as pl
from jax.experimental.pallas import tpu as pltpu
from jax.sharding import PartitionSpec as P

NODE_DIM = 256
PAIR_DIM = 128
HEADS = 8
HEAD_DIM = 32
OUTER = 32
TRI_DIM = 128
FFN_NODE = 1024
FFN_PAIR = 512
RECYCLES = 4
ADAM_STEP = 3


EPS_NORM = 1e-05
ADAM_EPS = 1e-08
BETA_ONE = 0.9
BETA_TWO = 0.95
LEARN_RATE = 0.06
WEIGHT_DECAY = 0.1
CLIP_NORM = 1.0
MASK_FILL = 1000000000.0
HIGHEST = lax.Precision.HIGHEST


class Triangle(NamedTuple):
    gain_in: Any
    w_left: Any
    w_right: Any
    w_gate: Any
    gain_tri: Any
    w_tri_out: Any


class Params(NamedTuple):
    embed: Any
    gain_one: Any
    w_query: Any
    w_key: Any
    w_value: Any
    w_bias: Any
    w_attn_out: Any
    gain_two: Any
    w_node_up: Any
    w_node_down: Any
    gain_three: Any
    w_left_node: Any
    w_right_node: Any
    w_outer: Any
    outgoing: Triangle
    incoming: Triangle
    gain_pair: Any
    w_pair_up: Any
    w_pair_down: Any
    bias_pair: Any


LANES = 128
HEADS_WIDTH = HEADS * HEAD_DIM


def first_rows():
    square = PAIR_DIM * TRI_DIM
    triangle = Triangle(PAIR_DIM, square, square, PAIR_DIM * PAIR_DIM, TRI_DIM, square)
    sizes = Params(
        embed=RECYCLES * NODE_DIM,
        gain_one=NODE_DIM,
        w_query=NODE_DIM * HEADS_WIDTH,
        w_key=NODE_DIM * HEADS_WIDTH,
        w_value=NODE_DIM * HEADS_WIDTH,
        w_bias=PAIR_DIM * HEADS,
        w_attn_out=HEADS_WIDTH * NODE_DIM,
        gain_two=NODE_DIM,
        w_node_up=NODE_DIM * FFN_NODE,
        w_node_down=FFN_NODE * NODE_DIM,
        gain_three=NODE_DIM,
        w_left_node=NODE_DIM * OUTER,
        w_right_node=NODE_DIM * OUTER,
        w_outer=OUTER * OUTER * PAIR_DIM,
        outgoing=triangle,
        incoming=triangle,
        gain_pair=PAIR_DIM,
        w_pair_up=PAIR_DIM * FFN_PAIR,
        w_pair_down=FFN_PAIR * PAIR_DIM,
        bias_pair=PAIR_DIM,
    )
    leaves, tree = jax.tree.flatten(sizes)
    ends = np.cumsum(leaves) // LANES
    starts = [0] + [int(end) for end in ends[:-1]]
    return jax.tree.unflatten(tree, starts), int(ends[-1])


LOW = jnp.bfloat16
WIDE = jnp.float32
BOTH = ("crop", "row")
TILE = 16
VMEM_LIMIT = 56 * 2**20
INV_SQRT2 = 1.0 / math.sqrt(2.0)
INV_SQRT2PI = 1.0 / math.sqrt(2.0 * math.pi)


class Layout:
    def __init__(self, crops, rows):
        self.crops, self.rows = crops, rows
        self.devices = crops * rows
        self.wide = 2 ** (int(math.log2(rows)) // 2)
        self.high = rows // self.wide
        half = crops // 2
        self.moves = [
            (here, self.work_place(here))
            for here in range(self.devices)
            if here != self.work_place(here)
        ]
        high_of = lambda here: here % rows // self.wide
        self.near = [
            (here, there) for here, there in self.moves if abs(high_of(here) - high_of(there)) == 1
        ]
        self.far = [move for move in self.moves if move not in self.near]
        self.groups = [
            [self.work_place(c * rows + r) for r in range(rows)] for c in range(crops)
        ]
        self.cores = [
            [(2 * x + k) * rows + r for k in range(2)] for x in range(half) for r in range(rows)
        ]
        self.slabs = [[2 * x * rows + k for k in range(2 * rows)] for x in range(half)]
        self.chips = [
            [(2 * x + k) * rows + r for x in range(half)] for k in range(2) for r in range(rows)
        ]

    def work_place(self, here):
        crop, row = here // self.rows, here % self.rows
        high, wide = row // self.wide, row % self.wide
        core = crop % 2
        away = (high // (self.high // 2) + core) % 2
        crop = crop + away * (1 - 2 * core)
        high = high + away * (self.high - 1 - 2 * high)
        return crop * self.rows + high * self.wide + wide


def exchange(blocks, axes, groups=None):
    return lax.all_to_all(blocks, axes, 0, 0, axis_index_groups=groups, tiled=True)


def spread(part, count, axes, groups=None):
    return exchange(jnp.broadcast_to(part[None], (count,) + part.shape), axes, groups)


def dot_nn(a, b):
    return lax.dot_general(a, b, (((1,), (0,)), ((), ())), preferred_element_type=WIDE)


def dot_nt(a, b):
    return lax.dot_general(a, b, (((1,), (1,)), ((), ())), preferred_element_type=WIDE)


def dot_tn(a, b):
    return lax.dot_general(a, b, (((0,), (0,)), ((), ())), preferred_element_type=WIDE)


def norm_parts(x):
    hat, _, scale = norm_all(x)
    return hat, scale


def norm_all(x):
    mean = jnp.mean(x, axis=0, keepdims=True)
    centered = x - mean
    scale = lax.rsqrt(jnp.mean(centered * centered, axis=0, keepdims=True) + EPS_NORM)
    return centered * scale, mean, scale


def norm_back(grad, hat, scale, gain):
    grad_gain = jnp.sum(grad * hat, axis=1, keepdims=True)
    wide = grad * gain
    inner = jnp.mean(wide * hat, axis=0, keepdims=True)
    return scale * (wide - jnp.mean(wide, axis=0, keepdims=True) - hat * inner), grad_gain


def sigmoid(x):
    return 0.5 * jnp.tanh(0.5 * x) + 0.5


EMBED = slice(0, 8)
GAIN_ONE, GAIN_TWO, GAIN_THREE = slice(8, 10), slice(10, 12), slice(12, 14)
OUT_GAIN, OUT_TRI, IN_GAIN, IN_TRI = (slice(k, k + 1) for k in range(14, 18))
PAIR_GAIN, PAIR_BIAS = slice(18, 19), slice(19, 20)


def column(row):
    return jnp.broadcast_to(row, (LANES, row.shape[1])).T[:, :1]


def row_of(values):
    return jnp.broadcast_to(values, (values.shape[0], LANES)).T[:1]


def cat(ref):
    return jnp.concatenate([ref[t] for t in range(ref.shape[0])], axis=1)


def put(ref, value):
    count = ref.shape[0]
    width = value.shape[1] // count
    for t in range(count):
        ref[t] = value[:, t * width : (t + 1) * width].astype(ref.dtype)


def swapped(value):
    if value.shape[0] % TILE or value.shape[1] % TILE:
        return jnp.swapaxes(value.astype(WIDE), 0, 1).astype(LOW)
    return jnp.swapaxes(value, 0, 1)


def send_pair(scratch, out_ref):
    parts, share = out_ref.shape[0], out_ref.shape[1] // 2
    channels = parts * share
    for side in range(2):
        value = swapped(scratch[:, side * channels : (side + 1) * channels, :])
        out_ref[:, side * share : (side + 1) * share] = value.reshape(
            (parts, share) + value.shape[1:]
        )


def take_pair(in_ref, scratch):
    parts, share = in_ref.shape[0], in_ref.shape[1] // 2
    channels = parts * share
    for side in range(2):
        value = in_ref[:, side * share : (side + 1) * share]
        value = value.reshape((channels,) + value.shape[2:])
        scratch[:, side * channels : (side + 1) * channels, :] = swapped(value)


def front(x, gain, w_all, mask, x_out, mean_out, scale_out, gate_out, sides):
    hat, mean, scale = norm_all(x)
    all_three = dot_nn(w_all, (hat * gain).astype(LOW))
    channels = 2 * TRI_DIM
    put(sides, all_three[:channels] * mask)
    put(x_out, x)
    put(mean_out, mean)
    put(scale_out, scale)
    put(gate_out, sigmoid(all_three[channels:]))


def triangle_update(mixed, gain, w_out):
    hat, scale = norm_parts(mixed)
    normed = (hat * gain).astype(LOW)
    return hat, scale, normed, dot_nn(w_out, normed)


def post_back(grad, gate, hat, scale, normed, update, gain, w_out_back):
    update_grad = (grad * gate).astype(LOW)
    gate_grad = (grad * update * (gate * (1.0 - gate))).astype(LOW)
    grad_out = dot_nt(normed, update_grad)
    mixed_grad, grad_gain = norm_back(dot_nn(w_out_back, update_grad), hat, scale, gain)
    return mixed_grad, gate_grad, grad_out, grad_gain


def front_back(grad, x, mean, scale, sides_grad, gate_grad, mask, gain, w_all_back):
    hat = (x - mean) * scale
    normed = (hat * gain).astype(LOW)
    sides = jnp.concatenate([sides_grad * mask.astype(LOW), gate_grad], axis=0)
    grad_w = dot_nt(normed, sides)
    x_grad, grad_gain = norm_back(dot_nn(w_all_back, sides), hat, scale, gain)
    return grad + x_grad, grad_w, grad_gain


def gelu_parts(x):
    cumulative = 0.5 * lax.erf(x * INV_SQRT2) + 0.5
    density = INV_SQRT2PI * jnp.exp(-0.5 * x * x)
    return x * cumulative, cumulative + x * density


def zero_first(*refs, earlier=()):
    @pl.when((pl.program_id(0) == 0) & (pl.program_id(1) == 0))
    def _():
        for k, ref in enumerate(refs):
            ref[...] = earlier[k][...] if earlier else jnp.zeros_like(ref)


def run(body, step, extent, in_arrays, in_kinds, outs, scratch, flops, skip=0, aliases={}):
    def spec(kind, shape):
        lead = (0,) * len(shape)
        if kind == "m":
            return pl.BlockSpec(memory_space=pltpu.SMEM)
        if kind == "x":
            return pl.BlockSpec(memory_space=pl.ANY)
        block, at = {
            "R": (step[:1] + shape[1:-1] + step[1:], lambda c, r: (r + skip,) + lead[2:] + (c,)),
            "N": (step + shape[2:], lambda c, r: (r + skip, c) + lead[2:]),
            "r": (step[:1] + shape[1:-1] + step[1:], lambda c, r: (r,) + lead[2:] + (c,)),
            "n": (step + shape[2:], lambda c, r: (r, c) + lead[2:]),
            "s": (shape[:-2] + step, lambda c, r: lead[2:] + (r, c)),
            "c": (shape[:-1] + step[1:], lambda c, r: lead[1:] + (c,)),
            "t": (step[:1] + shape[1:], lambda c, r: (r,) + lead[1:]),
            "p": ((1,) + step[:1] + shape[2:], lambda c, r: (c, r) + lead[2:]),
            "q": (step[1:] + shape[1:], lambda c, r: (c,) + lead[1:]),
            "w": (shape, lambda c, r: lead),
        }[kind]
        return pl.BlockSpec(block, at)

    moved = sum(a.size * a.dtype.itemsize for a in in_arrays)
    return pl.pallas_call(
        body,
        grid=(extent[1] // step[1], extent[0] // step[0]),
        in_specs=[spec(kind, a.shape) for kind, a in zip(in_kinds, in_arrays)],
        out_specs=[spec(kind, shape) for kind, shape, _ in outs],
        out_shape=[jax.ShapeDtypeStruct(shape, dtype) for _, shape, dtype in outs],
        scratch_shapes=scratch,
        input_output_aliases=aliases,
        compiler_params=pltpu.CompilerParams(vmem_limit_bytes=VMEM_LIMIT),
        cost_estimate=pl.CostEstimate(flops=flops, bytes_accessed=moved, transcendentals=0),
    )(*in_arrays)


def all_low(w):
    return jnp.concatenate([w[k * PAIR_DIM : (k + 1) * PAIR_DIM].T for k in range(3)], axis=0)


def all_back(w):
    return jnp.concatenate([w[k * PAIR_DIM : (k + 1) * PAIR_DIM] for k in range(3)], axis=1)


def kernel_open(
    stays, pair, pair_home, table, right, mask, vectors, w_all, x_out, mean_out, scale_out, gate_out, sides_out, sides
):
    right_low = right[...]
    at_home = stays[0] == 1
    x = jnp.concatenate(
        [
            jnp.where(at_home, pair_home[t], pair[t]).T.astype(WIDE) + dot_tn(table[t], right_low)
            for t in range(pair.shape[0])
        ],
        axis=1,
    )
    front(
        x, column(vectors[OUT_GAIN]), all_low(w_all), cat(mask), x_out, mean_out, scale_out, gate_out,
        sides,
    )
    send_pair(sides, sides_out)


def kernel_middle(
    mixed, x_in, gate_in, mask, vectors, w_out, w_all,
    x_out, mean_out, scale_out, gate_out, sides_out, arrived, sides,
):
    arrived[...] = swapped(mixed[...])
    *_, update = triangle_update(cat(arrived).astype(WIDE), column(vectors[OUT_TRI]), w_out[...].T)
    x = cat(x_in).astype(WIDE) + cat(gate_in).astype(WIDE) * update
    front(
        x, column(vectors[IN_GAIN]), all_low(w_all), cat(mask),
        x_out, mean_out, scale_out, gate_out, sides,
    )
    send_pair(sides, sides_out)


def kernel_turn(mixed, x_in, gate_in, cot, vectors, w_out, w_up, w_down, *rest):
    (
        pair_out, x_grad, gate_grad, mixed_grad, g_out, g_tri, g_up, g_down, g_pair, g_bias,
        arrived, leaving,
    ) = rest[-12:]
    rows = x_in.shape[0]
    arrived[...] = swapped(mixed[...])
    up_low, up_back = w_up[...].T, w_up[...]
    down_low, down_back = w_down[...].T, w_down[...]
    tri_col, pair_col = column(vectors[IN_TRI]), column(vectors[PAIR_GAIN])
    zero_first(g_out, g_tri, g_up, g_down, g_pair, g_bias, earlier=rest[3:-12])
    chunk = PAIR_DIM

    gate = cat(gate_in).astype(WIDE)
    mix_parts = triangle_update(cat(arrived).astype(WIDE), tri_col, w_out[...].T)
    x = cat(x_in).astype(WIDE) + gate * mix_parts[-1]
    hat, scale = norm_parts(x)
    normed = (hat * pair_col).astype(LOW)
    cot_low = jnp.concatenate([cot[t].T for t in range(rows)], axis=1)
    total = x + column(vectors[PAIR_BIAS])
    normed_grad = jnp.zeros_like(x)
    for c in range(FFN_PAIR // chunk):
        part = slice(c * chunk, (c + 1) * chunk)
        act, slope = gelu_parts(dot_nn(up_low[part], normed))
        act_low = act.astype(LOW)
        total = total + dot_nn(down_low[:, part], act_low)
        hidden_grad = (dot_nn(down_back[part], cot_low) * slope).astype(LOW)
        normed_grad = normed_grad + dot_nn(up_back[:, part], hidden_grad)
        g_up[:, part] += dot_nt(normed, hidden_grad)
        g_down[part] += dot_nt(act_low, cot_low)
    total_low = total.astype(LOW)
    width = total.shape[1] // rows
    for t in range(rows):
        pair_out[t] = total_low[:, t * width : (t + 1) * width].T
    cot_wide = cot_low.astype(WIDE)
    g_bias[...] += jnp.sum(cot_wide, axis=1, keepdims=True)
    back, grad_gain = norm_back(normed_grad, hat, scale, pair_col)
    g_pair[...] += grad_gain
    grad = cot_wide + back
    put(x_grad, grad)
    mix_grad, gates, grad_out, grad_tri = post_back(grad, gate, *mix_parts, tri_col, w_out[...])
    put(leaving, mix_grad)
    put(gate_grad, gates)
    g_out[...] += grad_out
    g_tri[...] += grad_tri
    mixed_grad[...] = swapped(leaving[...])


def kernel_return(
    sides_grad, x_after, mean_after, scale_after, gate_after, grad_in, mask, vectors, w_after,
    mixed, gate_in, w_out,
    x_grad, gate_grad, mixed_grad, g_after, g_gain, g_out, g_tri,
    sides, arrived, leaving,
):
    take_pair(sides_grad, sides)
    arrived[...] = swapped(mixed[...])
    tri_col = column(vectors[OUT_TRI])
    zero_first(g_after, g_gain, g_out, g_tri)
    grad, grad_w, grad_gain = front_back(
        cat(grad_in).astype(WIDE), cat(x_after).astype(WIDE), cat(mean_after), cat(scale_after),
        cat(sides), cat(gate_after),
        cat(mask), column(vectors[IN_GAIN]), all_back(w_after),
    )
    g_after[...] += grad_w
    g_gain[...] += grad_gain
    put(x_grad, grad)
    mix_parts = triangle_update(cat(arrived).astype(WIDE), tri_col, w_out[...].T)
    mix_grad, gates, grad_out, grad_tri = post_back(
        grad, cat(gate_in).astype(WIDE), *mix_parts, tri_col, w_out[...]
    )
    put(leaving, mix_grad)
    put(gate_grad, gates)
    g_out[...] += grad_out
    g_tri[...] += grad_tri
    mixed_grad[...] = swapped(leaving[...])


def kernel_close(
    sides_grad, x_after, mean_after, scale_after, gate_after, grad_in, mask, vectors, w_after,
    table, right,
    pair_grad, table_grad, right_grad, g_after, g_gain, sides,
):
    take_pair(sides_grad, sides)
    zero_first(g_after, g_gain)

    @pl.when(pl.program_id(1) == 0)
    def _():
        right_grad[...] = jnp.zeros_like(right_grad)

    grad, grad_w, grad_gain = front_back(
        cat(grad_in).astype(WIDE), cat(x_after).astype(WIDE), cat(mean_after), cat(scale_after),
        cat(sides), cat(gate_after),
        cat(mask), column(vectors[OUT_GAIN]), all_back(w_after),
    )
    g_after[...] += grad_w
    g_gain[...] += grad_gain
    low = grad.astype(LOW)
    rows = table.shape[0]
    width = low.shape[1] // rows
    for t in range(rows):
        own = low[:, t * width : (t + 1) * width]
        pair_grad[t] = own.T
        table_grad[0, t] = dot_nt(right[...], own)
        right_grad[...] += dot_nn(table[t], own)


CHANNELS = 8


def kernel_mix(incoming, left, right, *outs):
    parts, count, rows, length = left.shape
    part = rows // len(outs)
    for c in range(count):
        a = left[:, c].reshape(length, length)
        b = right[:, c].reshape(length, length)
        mixed = dot_tn(a, b) if incoming else dot_nt(a, b)
        mixed = mixed.astype(LOW).reshape(parts, rows, length)
        for k, out in enumerate(outs):
            out[:, c] = mixed[:, k * part : (k + 1) * part]


def kernel_mix_back(incoming, *refs):
    *grads, left, right, out = refs
    parts, count, rows, length = left.shape
    for c in range(count):
        g = jnp.concatenate([grad[:, c] for grad in grads], axis=1).reshape(length, length)
        a = left[:, c].reshape(length, length)
        b = right[:, c].reshape(length, length)
        a_grad = dot_nt(b, g) if incoming else dot_nn(g, b)
        b_grad = dot_nn(a, g) if incoming else dot_tn(g, a)
        out[:, 0, c] = a_grad.astype(LOW).reshape(parts, rows, length)
        out[:, 1, c] = b_grad.astype(LOW).reshape(parts, rows, length)


def mix(sides, incoming, pieces=1):
    parts, double, rows, length = sides.shape
    share = double // 2
    count = min(CHANNELS, share)
    steps = share // count
    block = (parts, count, rows, length)
    part = (parts, count, rows // pieces, length)
    return pl.pallas_call(
        lambda *refs: kernel_mix(incoming, *refs),
        grid=(steps,),
        in_specs=[
            pl.BlockSpec(block, lambda c: (0, c, 0, 0)),
            pl.BlockSpec(block, lambda c: (0, c + steps, 0, 0)),
        ],
        out_specs=[pl.BlockSpec(part, lambda c: (0, c, 0, 0))] * pieces,
        out_shape=[jax.ShapeDtypeStruct((parts, share) + part[2:], LOW)] * pieces,
        compiler_params=pltpu.CompilerParams(vmem_limit_bytes=VMEM_LIMIT),
        cost_estimate=pl.CostEstimate(
            flops=2 * share * length**3, bytes_accessed=3 * share * length * length * 2,
            transcendentals=0,
        ),
    )(sides, sides)


def mix_back(grads, sides, incoming):
    parts, double, rows, length = sides.shape
    share = double // 2
    count = min(CHANNELS, share)
    steps = share // count
    block = (parts, count, rows, length)
    part = (parts, count, rows // len(grads), length)
    out = pl.pallas_call(
        lambda *refs: kernel_mix_back(incoming, *refs),
        grid=(steps,),
        in_specs=[pl.BlockSpec(part, lambda c: (0, c, 0, 0))] * len(grads)
        + [
            pl.BlockSpec(block, lambda c: (0, c, 0, 0)),
            pl.BlockSpec(block, lambda c: (0, c + steps, 0, 0)),
        ],
        out_specs=pl.BlockSpec((parts, 2, count, rows, length), lambda c: (0, 0, c, 0, 0)),
        out_shape=jax.ShapeDtypeStruct((parts, 2, share, rows, length), LOW),
        compiler_params=pltpu.CompilerParams(vmem_limit_bytes=VMEM_LIMIT),
        cost_estimate=pl.CostEstimate(
            flops=4 * share * length**3, bytes_accessed=5 * share * length * length * 2,
            transcendentals=0,
        ),
    )(*grads, sides, sides)
    return out.reshape(sides.shape)


def share_rows(share):
    return -(-(share + 2 * LANES) // (TILE * LANES)) * TILE


def whole(shape):
    return pl.BlockSpec(shape, lambda *_: (0,) * len(shape))


def one_call(body, scalars, in_arrays, outs, scratch=()):
    return pl.pallas_call(
        body,
        in_specs=[pl.BlockSpec(memory_space=pltpu.SMEM)] * len(scalars)
        + [whole(a.shape) for a in in_arrays],
        out_specs=[whole(shape) for shape, _ in outs],
        out_shape=[jax.ShapeDtypeStruct(shape, dtype) for shape, dtype in outs],
        scratch_shapes=list(scratch),
        grid=(1,),
        compiler_params=pltpu.CompilerParams(vmem_limit_bytes=VMEM_LIMIT),
    )(*scalars, *in_arrays)


def lane_in(shape, start, width):
    lane = lax.broadcasted_iota(jnp.int32, shape, 1)
    return (lane >= start) & (lane < start + width)


def rolled(value, shift):
    shift %= LANES
    return pltpu.roll(value, shift, 1) if shift else value


def share_order(layout):
    return [((d // layout.rows) % 2, d // (2 * layout.rows), d % layout.rows) for d in range(layout.devices)]


def unpack(layout, shares, share):
    at, _ = first_rows()
    height = shares.shape[3]
    first = [share * d // LANES for d in range(layout.devices)]
    order = share_order(layout)
    matrices = [
        (at.w_query, NODE_DIM, 3, 3 * HEADS_WIDTH),
        (at.w_attn_out, HEADS_WIDTH, 1, NODE_DIM),
        (at.w_node_up, NODE_DIM, 1, FFN_NODE),
        (at.w_node_down, FFN_NODE, 1, NODE_DIM),
        (at.w_outer, OUTER * OUTER, 1, PAIR_DIM),
        (at.outgoing.w_left, 3 * PAIR_DIM, 1, TRI_DIM),
        (at.outgoing.w_tri_out, TRI_DIM, 1, PAIR_DIM),
        (at.incoming.w_left, 3 * PAIR_DIM, 1, TRI_DIM),
        (at.incoming.w_tri_out, TRI_DIM, 1, PAIR_DIM),
        (at.w_pair_up, PAIR_DIM, 1, FFN_PAIR),
        (at.w_pair_down, FFN_PAIR, 1, PAIR_DIM),
    ]
    small = [(at.embed, 8), (at.gain_one, 2), (at.gain_two, 2), (at.gain_three, 2)]
    small += [
        (start, 1)
        for start in (
            at.outgoing.gain_in, at.outgoing.gain_tri, at.incoming.gain_in, at.incoming.gain_tri,
            at.gain_pair, at.bias_pair,
        )
    ]

    def body(shares_ref, vectors, bias_out, factors_out, *rest):
        outs, flat, narrow = rest[:-2], rest[-2], rest[-1]
        for d, place in enumerate(order):
            block = shares_ref[place].astype(WIDE)
            if d:
                tail = flat[first[d] : first[d] + 1]
                flat[first[d] : first[d] + height] = block
                flat[first[d] : first[d] + 1] = block[:1] + tail
            else:
                flat[:height] = block
        row = 0
        vectors[...] = jnp.zeros_like(vectors)
        for start, count in small:
            vectors[row : row + count] = flat[start : start + count]
            row += count
        for out, (place, rows, count, width) in zip(outs, matrices):
            pieces = width // count // LANES
            for m in range(count):
                for a in range(pieces):
                    start = place + m * rows * pieces + a
                    value = (
                        flat[pl.ds(start, rows, stride=pieces), :]
                        if pieces > 1
                        else flat[start : start + rows]
                    )
                    lane = (m * pieces + a) * LANES
                    out[:, lane : lane + LANES] = value.astype(LOW)
        per_row = LANES // HEADS
        shape = (HEADS, LANES)
        value = flat[at.w_bias : at.w_bias + HEADS]
        for a in range(per_row):
            kept = jnp.where(lane_in(shape, 0, HEADS), rolled(value, -HEADS * a), 0.0)
            narrow[pl.ds(a, HEADS, stride=per_row), :] = kept
        bias_out[...] = narrow[:PAIR_DIM].astype(LOW)
        per_row = LANES // OUTER
        count = NODE_DIM // per_row
        shape = (count, LANES)
        left, right = (flat[start : start + count] for start in (at.w_left_node, at.w_right_node))
        for a in range(per_row):
            kept = jnp.where(lane_in(shape, 0, OUTER), rolled(left, -OUTER * a), 0.0)
            kept += jnp.where(lane_in(shape, OUTER, OUTER), rolled(right, OUTER - OUTER * a), 0.0)
            narrow[pl.ds(a, count, stride=per_row), :] = kept
        factors_out[...] = narrow[...].astype(LOW)

    return one_call(
        body,
        (),
        (shares,),
        [((24, LANES), WIDE), ((PAIR_DIM, LANES), LOW), ((NODE_DIM, LANES), LOW)]
        + [((rows, width), LOW) for _, rows, _, width in matrices],
        [pltpu.VMEM((first[-1] + height + TILE, LANES), WIDE), pltpu.VMEM((NODE_DIM, LANES), WIDE)],
    )


def pack(layout, share, scalars, grads, node_parts):
    at, total = first_rows()
    height = share_rows(share)
    first = [share * d // LANES for d in range(layout.devices)]
    order = share_order(layout)
    many = len(grads)

    def body(scalar_ref, *refs):
        ins, rest = refs[:many], refs[many:]
        (
            key_value, query_low, start, normed_own, normed_all, after_grad, vectors, w_projections,
            act_low, final_low, normed_two, hidden_grad, attended, after_low, g_factors,
            out, node_parts_out, flat, narrow, steps,
        ) = rest

        def store(place, count, value):
            rows, pieces = value.shape[0], value.shape[1] // count // LANES
            for m in range(count):
                for a in range(pieces):
                    lane = (m * pieces + a) * LANES
                    begin = place + m * rows * pieces + a
                    part = value[:, lane : lane + LANES]
                    if pieces > 1 and rows > 1:
                        flat[pl.ds(begin, rows, stride=pieces), :] = part
                    else:
                        flat[begin : begin + rows] = part

        flat[total:] = jnp.zeros((flat.shape[0] - total, LANES), WIDE)
        for ref, (place, count, _) in zip(ins, grads):
            store(place, count, row_of(ref[...]) if ref.shape[1] == 1 else ref[...])
        store(at.w_node_down, 1, dot_tn(act_low[...], final_low[...]))
        store(at.w_node_up, 1, dot_tn(normed_two[...], hidden_grad[...]))
        store(at.w_attn_out, 1, dot_tn(attended[...], after_low[...]))
        per_row = LANES // OUTER
        count = NODE_DIM // per_row
        narrow[...] = g_factors[...]
        left = jnp.zeros((count, LANES), WIDE)
        right = left
        for a in range(per_row):
            piece = narrow[pl.ds(a, count, stride=per_row), :]
            inside = lane_in(piece.shape, OUTER * a, OUTER)
            left = jnp.where(inside, rolled(piece, OUTER * a), left)
            right = jnp.where(inside, rolled(piece, OUTER * a - OUTER), right)
        store(at.w_left_node, 1, left)
        store(at.w_right_node, 1, right)

        store(at.w_query, 1, dot_tn(normed_own[...], query_low[...]))
        store(at.w_key, 2, dot_tn(normed_all[...], key_value[...]))
        steps[...] = dot_nt(key_value[...], w_projections[:, HEADS_WIDTH:])
        local_rows = query_low.shape[0]
        own = pl.ds(pl.multiple_of(scalar_ref[1] * local_rows, local_rows), local_rows)
        steps[own, :] += dot_nt(query_low[...], w_projections[:, :HEADS_WIDTH])
        hat, scale = row_norm(start[...])
        part, grad_gain = row_norm_back(steps[...], hat, scale, vector(vectors, GAIN_ONE))
        for r in range(node_parts_out.shape[0]):
            for a in range(NODE_DIM // LANES):
                piece = part[r * local_rows : (r + 1) * local_rows, a * LANES : (a + 1) * LANES]
                node_parts_out[r, a * local_rows : (a + 1) * local_rows] = piece.astype(LOW)
        store(at.gain_one, 1, grad_gain)
        flat[at.embed : at.embed + 2 * RECYCLES] = jnp.zeros((2 * RECYCLES, LANES), WIDE)
        column_sum = jnp.sum(after_grad[...], axis=0, keepdims=True)
        column_sum += jnp.sum(part, axis=0, keepdims=True)
        for a in range(NODE_DIM // LANES):
            place = at.embed + (NODE_DIM // LANES) * scalar_ref[0] + a
            flat[pl.ds(place, 1), :] = column_sum[:, a * LANES : (a + 1) * LANES]
        for d, where in enumerate(order):
            out[where] = flat[first[d] : first[d] + height].astype(LOW)

    shape = (2, layout.crops // 2, layout.rows, height, LANES)
    return one_call(
        body,
        (scalars,),
        tuple(array for _, _, array in grads) + tuple(node_parts),
        [(shape, LOW), ((layout.rows, node_parts[1].shape[0] * NODE_DIM // LANES, LANES), LOW)],
        [
            pltpu.VMEM((first[-1] + height + TILE, LANES), WIDE),
            pltpu.VMEM((NODE_DIM, LANES), WIDE),
            pltpu.VMEM(node_parts[2].shape, WIDE),
        ],
    )


def row_norm(x):
    centered = x - jnp.mean(x, axis=-1, keepdims=True)
    scale = lax.rsqrt(jnp.mean(centered * centered, axis=-1, keepdims=True) + EPS_NORM)
    return centered * scale, scale


def row_norm_back(grad, hat, scale, gain):
    grad_gain = jnp.sum(grad * hat, axis=0, keepdims=True)
    wide = grad * gain
    inner = jnp.mean(wide * hat, axis=-1, keepdims=True)
    return scale * (wide - jnp.mean(wide, axis=-1, keepdims=True) - hat * inner), grad_gain


def vector(ref, rows):
    return jnp.concatenate([ref[r : r + 1] for r in range(rows.start, rows.stop)], axis=1)


def by_head(value):
    return jnp.concatenate(
        [
            jnp.where(lane_in(value.shape, h * HEAD_DIM, HEAD_DIM), value, 0.0)
            for h in range(HEADS)
        ],
        axis=0,
    )


def head_sum(value):
    rows = value.shape[0] // HEADS
    parts = [value[h * rows : (h + 1) * rows] for h in range(HEADS)]
    return sum(
        jnp.where(lane_in(part.shape, h * HEAD_DIM, HEAD_DIM), part, 0.0)
        for h, part in enumerate(parts)
    )


SCORE_SCALE = HEAD_DIM ** (-0.5)
KEEP_LANE = 2 * OUTER


def node_forward(
    recycle, node_ref, all_ref, bias_ref, keep, keep_rows, vectors, w_projections, w_attn_out, w_up, w_down,
    w_factors,
    node_out, factors_out, start_out, normed_own, normed_out, soft_out, heads_out, key_out, value_out,
    attended_out, after_out, act_out, slope_out, final_out, flat,
):
    pieces = NODE_DIM // LANES
    length = all_ref.shape[0] // pieces
    embed = jnp.concatenate(
        [vectors[pl.ds(pieces * recycle[0] + a, 1), :] for a in range(pieces)], axis=1
    )
    flat[...] = all_ref[...].astype(WIDE)
    all_rows = jnp.concatenate(
        [flat[pl.ds(a, length, stride=pieces), :] for a in range(pieces)], axis=1
    )
    gain = vector(vectors, GAIN_ONE)
    start_all = all_rows + embed
    normed_all = (row_norm(start_all)[0] * gain).astype(LOW)
    start_out[...] = start_all
    normed_out[...] = normed_all
    start = node_ref[...].astype(WIDE) + embed
    normed = (row_norm(start)[0] * gain).astype(LOW)
    normed_own[...] = normed
    query = dot_nn(normed, w_projections[:, :HEADS_WIDTH]).astype(LOW).astype(WIDE)
    heads = by_head(query).astype(LOW)
    key_value = dot_nn(normed_all, w_projections[:, HEADS_WIDTH:]).astype(LOW)
    key, value = key_value[:, :HEADS_WIDTH], key_value[:, HEADS_WIDTH:]
    heads_out[...] = heads
    key_out[...] = key
    value_out[...] = value
    scores = dot_nt(heads, key) * SCORE_SCALE + bias_ref[...] + (keep[...] - 1.0) * MASK_FILL
    powers = jnp.exp(scores - jnp.max(scores, axis=-1, keepdims=True))
    soft = powers / jnp.sum(powers, axis=-1, keepdims=True)
    soft_out[...] = soft
    attended = head_sum(dot_nn(soft.astype(LOW), value)).astype(LOW)
    attended_out[...] = attended
    after = start + dot_nn(attended, w_attn_out[...])
    after_out[...] = after
    normed = (row_norm(after)[0] * vector(vectors, GAIN_TWO)).astype(LOW)
    act, slope = gelu_parts(dot_nn(normed, w_up[...]))
    act_out[...] = act.astype(LOW)
    slope_out[...] = slope
    final = after + dot_nn(act.astype(LOW), w_down[...])
    final_out[...] = final
    node_out[...] = final.astype(LOW)
    normed = (row_norm(final)[0] * vector(vectors, GAIN_THREE)).astype(LOW)
    factors = dot_nn(normed, w_factors[...])
    factors = jnp.where(lane_in(factors.shape, KEEP_LANE, 1), keep_rows[...], factors).astype(LOW)
    factors_out[...] = jnp.broadcast_to(factors[None], factors_out.shape)


def node_backward(
    sources, factor_ref, cot, vectors, soft_ref, heads, key, value, after_ref, slope, final_ref,
    w_attn_out, w_up, w_down, w_factors,
    key_value_out, query_out, score_out, after_grad_out, final_low_out, normed_two_out,
    hidden_out, after_low_out, g_factors, g_two, g_three,
):
    ranks = key_value_out.shape[0] // cot.shape[0]
    left = factor_ref[sources[0]].astype(WIDE)
    right = sum(factor_ref[sources[1 + r]].astype(WIDE) for r in range(ranks))
    rows = jnp.where(lane_in(left.shape, 0, OUTER), left, right).astype(LOW)
    hat, scale = row_norm(final_ref[...])
    gain = vector(vectors, GAIN_THREE)
    g_factors[...] = dot_tn((hat * gain).astype(LOW), rows)
    part, g_three[...] = row_norm_back(dot_nt(rows, w_factors[...]), hat, scale, gain)
    final_grad = cot[...].astype(WIDE) + part
    final_low = final_grad.astype(LOW)
    final_low_out[...] = final_low
    hidden_grad = (dot_nt(final_low, w_down[...]) * slope[...]).astype(LOW)
    hidden_out[...] = hidden_grad
    hat, scale = row_norm(after_ref[...])
    gain = vector(vectors, GAIN_TWO)
    normed_two_out[...] = (hat * gain).astype(LOW)
    part, g_two[...] = row_norm_back(dot_nt(hidden_grad, w_up[...]), hat, scale, gain)
    after_grad = final_grad + part
    after_grad_out[...] = after_grad
    after_low = after_grad.astype(LOW)
    after_low_out[...] = after_low
    attended_grad = dot_nt(after_low, w_attn_out[...]).astype(LOW).astype(WIDE)
    grad_heads = by_head(attended_grad).astype(LOW)
    soft = soft_ref[...]
    soft_grad = dot_nt(grad_heads, value[...])
    score_grad = soft * (soft_grad - jnp.sum(soft_grad * soft, axis=-1, keepdims=True))
    score_low = score_grad.astype(LOW)
    score_out[...] = score_low
    key_part = dot_tn(score_low, heads[...]) * SCORE_SCALE
    key_value_out[:, :HEADS_WIDTH] = key_part.astype(LOW)
    key_value_out[:, HEADS_WIDTH:] = dot_tn(soft.astype(LOW), grad_heads).astype(LOW)
    query_out[...] = (head_sum(dot_nn(score_low, key[...])) * SCORE_SCALE).astype(LOW)


def outer_tables(
    sources, factors, w_outer, table_out, right_out, left_out, mask_out, w_wide, steps
):
    local_rows = left_out.shape[0]
    ranks = right_out.shape[1] // local_rows
    left_low = factors[sources[0]][:, :OUTER]
    left_out[...] = left_low
    right = jnp.concatenate([factors[sources[1 + r]].astype(WIDE) for r in range(ranks)], axis=0)
    turned = right.T
    right_out[...] = turned[OUTER : 2 * OUTER].astype(LOW)
    own_keep = factors[sources[0]][:, KEEP_LANE : KEEP_LANE + 1].astype(WIDE)
    mask_out[:, 0, :] = own_keep * turned[KEEP_LANE : KEEP_LANE + 1]
    w_wide[...] = w_outer[...].astype(WIDE)
    for q in range(OUTER):
        w_q = w_wide[pl.ds(q, OUTER, stride=OUTER), :].astype(LOW)
        steps[q] = dot_nn(left_low, w_q)
    table_out[...] = jnp.swapaxes(steps[...], 0, 1).astype(LOW)


def outer_backward(table_grad, right_grad, left, w_outer, factors_out, g_outer, w_wide, steps):
    crops, ranks, local_rows, _ = factors_out.shape
    steps[...] = jnp.swapaxes(jnp.sum(table_grad[...], axis=0), 0, 1)
    w_wide[...] = w_outer[...].astype(WIDE)
    left_grad = jnp.zeros((local_rows, OUTER), WIDE)
    for q in range(OUTER):
        grad_q = steps[q].astype(LOW)
        w_q = w_wide[pl.ds(q, OUTER, stride=OUTER), :].astype(LOW)
        left_grad = left_grad + dot_nt(grad_q, w_q)
        g_outer[pl.ds(q, OUTER, stride=OUTER), :] = dot_tn(left[...], grad_q)
    right_rows = right_grad[...].T
    for r in range(ranks):
        block = jnp.concatenate(
            [
                left_grad,
                right_rows[r * local_rows : (r + 1) * local_rows],
                jnp.zeros((local_rows, LANES - 2 * OUTER), WIDE),
            ],
            axis=1,
        ).astype(LOW)
        for c in range(crops):
            factors_out[c, r] = block


def low_of(x):
    return x.astype(LOW)


def local(layout, node, pair, recycle, mask, node_cot, pair_cot, master, first, second):
    crops, ranks = layout.crops, layout.rows
    devices = crops * ranks
    local_rows, length = node.shape[1], pair.shape[2]
    share = TRI_DIM // ranks
    node, pair, node_cot, pair_cot = node[0], pair[0], node_cot[0], pair_cot[0]

    crop_at, row_at = lax.axis_index("crop"), lax.axis_index("row")
    here = crop_at * ranks + row_at
    partner = layout.work_place(here)
    stays = partner == here
    work_crop, work_row = partner // ranks, partner % ranks
    near = lambda array: lax.ppermute(array, BOTH, layout.near)
    far = lambda array: lax.ppermute(array, BOTH, layout.far)
    settled = lambda own, close, *pieces: jnp.where(stays, own, close + jnp.concatenate(pieces))

    at, _ = first_rows()

    amount = master.shape[0]
    height = share_rows(amount)
    offset = (here * (amount % LANES)) % LANES
    shard = lax.dynamic_update_slice(jnp.zeros(height * LANES, LOW), low_of(master), (offset,))
    node_rows = local_rows * NODE_DIM // LANES
    shards = jnp.concatenate([shard.reshape(height, LANES), node.reshape(-1, LANES)], axis=0)
    shards = spread(shards, ranks, "row").reshape(ranks, -1, LANES)
    shards, pair = lax.optimization_barrier((shards, pair))
    node_all = shards[:, height:].reshape(-1, LANES)
    shards = shards[:, :height].reshape(-1, LANES)
    shards = spread(shards, crops // 2, BOTH, layout.chips)
    shards = spread(shards, 2, BOTH, layout.cores)
    shards = shards.reshape(2, crops // 2, ranks, height, LANES)
    (
        vectors, w_bias, w_factors, w_projections, w_attn_out, w_node_up, w_node_down, w_outer,
        w_out_all, w_out_end, w_in_all, w_in_end, w_pair_up, w_pair_down,
    ) = unpack(layout, shards, amount)
    pair_plane = lax.ppermute(pair, BOTH, layout.moves)
    keep = mask.astype(WIDE)
    keep_rows = lax.dynamic_slice_in_dim(keep[0], row_at * local_rows, local_rows, 0)[:, None]

    pair_bias = jnp.einsum("ijd,dh->hij", pair, w_bias[:, :HEADS], preferred_element_type=WIDE)
    rows_low = lambda width: ((local_rows, width), LOW)
    rows_wide = lambda width: ((local_rows, width), WIDE)
    by_heads = (HEADS * local_rows, length)
    (
        node_out, factors, start_all, normed_own, normed_all, soft, heads, key, value, attended, after, act_low,
        slope, node_final,
    ) = one_call(
        node_forward,
        (recycle,),
        (node, node_all, pair_bias.reshape(by_heads), keep, keep_rows, vectors, w_projections, w_attn_out,
         w_node_up, w_node_down, w_factors),
        [rows_low(NODE_DIM), ((2 * ranks, local_rows, LANES), LOW), ((length, NODE_DIM), WIDE),
         rows_low(NODE_DIM), ((length, NODE_DIM), LOW), (by_heads, WIDE), (by_heads[:1] + (HEADS_WIDTH,), LOW),
         ((length, HEADS_WIDTH), LOW), ((length, HEADS_WIDTH), LOW), rows_low(HEADS_WIDTH),
         rows_wide(NODE_DIM), rows_low(FFN_NODE), rows_wide(FFN_NODE), rows_wide(NODE_DIM)],
        [pltpu.VMEM(node_all.shape, WIDE)],
    )

    factors = exchange(factors, BOTH, layout.slabs)
    cot_first, cot_last = jnp.split(pair_cot, 2)
    factors, cot_first, pair_plane = lax.optimization_barrier((factors, cot_first, pair_plane))
    everyone = jnp.arange(ranks, dtype=jnp.int32)
    slab = 2 * ranks
    sources = jnp.concatenate([partner[None], work_crop * ranks + everyone]).astype(jnp.int32) % slab
    table, right, left, mask_plane = one_call(
        outer_tables,
        (sources,),
        (factors, w_outer),
        [((local_rows, OUTER, PAIR_DIM), LOW), ((OUTER, length), LOW), ((local_rows, OUTER), LOW),
         ((local_rows, 1, length), WIDE)],
        [pltpu.VMEM((OUTER * OUTER, PAIR_DIM), WIDE), pltpu.VMEM((OUTER, local_rows, PAIR_DIM), WIDE)],
    )

    step = (min(TILE, local_rows), min(LANES, length))
    extent = (local_rows, length)
    pieces = length // step[1]
    state = (local_rows, TRI_DIM, length)
    line = (local_rows, 1, length)
    sides_shape = (ranks, 2 * share, local_rows, length)
    mixed_shape = (TRI_DIM, local_rows, length)
    natural = (local_rows, length, PAIR_DIM)
    buffer = lambda channels: pltpu.VMEM((step[0], channels, step[1]), LOW)
    trade = lambda blocks: exchange(blocks, BOTH, layout.groups)
    merge = lambda blocks: blocks.reshape((TRI_DIM,) + blocks.shape[2:])
    split = lambda blocks: blocks.reshape((ranks, share) + blocks.shape[1:])
    unit = 2 * local_rows * length * PAIR_DIM * PAIR_DIM
    front_outs = (
        ("r", state, LOW), ("r", line, WIDE), ("r", line, WIDE), ("r", state, LOW),
        ("s", sides_shape, LOW),
    )
    square = (TRI_DIM, PAIR_DIM)
    gain_shape = (PAIR_DIM, 1)
    after_shape = (PAIR_DIM, 2 * TRI_DIM + PAIR_DIM)

    x_one, mean_tri_out, scale_tri_out, gate_tri_out, sides = run(
        kernel_open, step, extent,
        (stays.astype(jnp.int32)[None], pair_plane, pair, table, right, mask_plane, vectors, w_out_all),
        "mnntcrww", front_outs, [buffer(2 * TRI_DIM)], 4 * unit,
    )
    sides, cot_first, pair_cot = lax.optimization_barrier((sides, far(cot_first), pair_cot))
    sides_out, cot_near = lax.optimization_barrier((trade(sides), near(pair_cot)))
    mixed_out = merge(trade(mix(sides_out, False)[0]))
    mixed_out, cot_last = lax.optimization_barrier((mixed_out, cot_last))
    x_two, mean_tri_in, scale_tri_in, gate_tri_in, sides = run(
        kernel_middle, step, extent,
        (mixed_out, x_one, gate_tri_out, mask_plane, vectors, w_out_end, w_in_all), "srrrwww", front_outs, [buffer(TRI_DIM), buffer(2 * TRI_DIM)], 5 * unit,
    )
    sides, cot_last = lax.optimization_barrier((sides, far(cot_last)))
    sides_in, cot_plane = lax.optimization_barrier(
        (trade(sides), settled(pair_cot, cot_near, cot_first, cot_last))
    )
    turns = 2 if local_rows % (2 * TILE) == 0 else 1
    turn_rows = local_rows // turns
    mixed_in = [merge(trade(piece)) for piece in mix(sides_in, True, turns)]
    turned, grads_in = (), []
    for k in range(turns):
        turned = run(
            kernel_turn, step, (turn_rows, length),
            (mixed_in[k], x_two, gate_tri_in, cot_plane, vectors, w_in_end, w_pair_up, w_pair_down,
             *turned),
            "sRRNwwww" + ("xxxwwwwww" if k else ""),
            (("N", natural, LOW), ("R", state, LOW), ("R", state, LOW),
             ("s", (TRI_DIM, turn_rows, length), LOW),
             ("w", square, WIDE), ("w", gain_shape, WIDE), ("w", (PAIR_DIM, FFN_PAIR), WIDE),
             ("w", (FFN_PAIR, PAIR_DIM), WIDE), ("w", gain_shape, WIDE), ("w", gain_shape, WIDE)),
            [buffer(TRI_DIM), buffer(TRI_DIM)], 32 * unit // turns,
            skip=k * turn_rows // step[0], aliases={8: 0, 9: 1, 10: 2} if k else {},
        )
        turned = list(turned)
        mixed_grad = turned.pop(3)
        if k:
            grads_in[-1], mixed_grad = lax.optimization_barrier((grads_in[-1], mixed_grad))
        grads_in.append(trade(split(mixed_grad)))
    pair_final, x_grad, gate_grad, g_in_out, g_in_tri, g_up, g_down, g_pair, g_bias = turned
    sides_grad = trade(mix_back(grads_in, sides_in, True))
    out_first, out_last = jnp.split(pair_final, 2)
    sides_grad, out_near, out_first = lax.optimization_barrier(
        (sides_grad, near(pair_final), out_first)
    )
    x_grad, gate_grad, mixed_grad, g_in_all, g_in_gain, g_out_out, g_out_tri = run(
        kernel_return, step, extent,
        (sides_grad, x_two, mean_tri_in, scale_tri_in, gate_grad, x_grad, mask_plane,
         vectors, w_in_all, mixed_out, gate_tri_out, w_out_end),
        "srrrrrrwwsrw",
        (("r", state, LOW), ("r", state, LOW), ("s", mixed_shape, LOW), ("w", after_shape, WIDE),
         ("w", gain_shape, WIDE), ("w", square, WIDE), ("w", gain_shape, WIDE)),
        [buffer(2 * TRI_DIM), buffer(TRI_DIM), buffer(TRI_DIM)], 12 * unit,
    )
    mixed_grad, out_first = lax.optimization_barrier((mixed_grad, far(out_first)))
    sides_grad = trade(mix_back([trade(split(mixed_grad))], sides_out, False))
    sides_grad, out_last = lax.optimization_barrier((sides_grad, out_last))
    pair_one_grad, table_grad, right_part, g_out_all, g_out_gain = run(
        kernel_close, step, extent,
        (sides_grad, x_one, mean_tri_out, scale_tri_out, gate_grad, x_grad, mask_plane,
         vectors, w_out_all, table, right),
        "srrrrrrwwtc",
        (("n", natural, LOW), ("p", (pieces, local_rows, OUTER, PAIR_DIM), WIDE),
         ("c", (OUTER, length), WIDE), ("w", after_shape, WIDE), ("w", gain_shape, WIDE)),
        [buffer(2 * TRI_DIM)], 8 * unit,
    )

    factor_grads, g_outer = one_call(
        outer_backward,
        (),
        (table_grad, right_part, left, w_outer),
        [((2, ranks, local_rows, LANES), LOW), ((OUTER * OUTER, PAIR_DIM), WIDE)],
        [pltpu.VMEM((OUTER * OUTER, PAIR_DIM), WIDE), pltpu.VMEM((OUTER, local_rows, PAIR_DIM), WIDE)],
    )
    factor_grads, out_last = lax.optimization_barrier((factor_grads, far(out_last)))
    pair_out = settled(pair_final, out_near, out_first, out_last)
    factor_grads = exchange(factor_grads.reshape(slab, local_rows, LANES), BOTH, layout.slabs)
    factor_grads, pair_one_grad = lax.optimization_barrier((factor_grads, pair_one_grad))

    workers = layout.work_place(crop_at * ranks + everyone)
    sources = jnp.concatenate([partner[None], workers]).astype(jnp.int32) % slab
    (
        key_value, query_low, score_low, after_grad, final_low, normed_two, hidden_grad, after_low,
        g_factors, g_two, g_three,
    ) = one_call(
        node_backward,
        (sources,),
        (factor_grads, node_cot, vectors, soft, heads, key, value, after, slope, node_final,
         w_attn_out, w_node_up, w_node_down, w_factors),
        [((length, 2 * HEADS_WIDTH), LOW), rows_low(HEADS_WIDTH), (by_heads, LOW),
         rows_wide(NODE_DIM), rows_low(NODE_DIM), rows_low(NODE_DIM), rows_low(FFN_NODE),
         rows_low(NODE_DIM), ((NODE_DIM, LANES), WIDE), ((1, NODE_DIM), WIDE), ((1, NODE_DIM), WIDE)],
    )
    score_low = score_low.reshape(HEADS, local_rows, length)
    g_bias_head = jnp.einsum("ijd,hij->dh", pair, score_low, preferred_element_type=WIDE)
    g_bias_head = lax.optimization_barrier(g_bias_head).reshape(-1, LANES)
    pair_one_away = lax.ppermute(pair_one_grad, BOTH, layout.moves)
    grads = [
        (at.w_bias, 1, g_bias_head),
        (at.gain_two, 1, g_two),
        (at.gain_three, 1, g_three),
        (at.w_outer, 1, g_outer),
        (at.gain_pair, 1, g_pair),
        (at.w_pair_up, 1, g_up),
        (at.w_pair_down, 1, g_down),
        (at.bias_pair, 1, g_bias),
    ]
    for tri, g_all, g_gain, g_tri, g_out in (
        (at.outgoing, g_out_all, g_out_gain, g_out_tri, g_out_out),
        (at.incoming, g_in_all, g_in_gain, g_in_tri, g_in_out),
    ):
        grads += [
            (tri.gain_in, 1, g_gain),
            (tri.w_left, 3, g_all),
            (tri.gain_tri, 1, g_tri),
            (tri.w_tri_out, 1, g_out),
        ]

    blocks, node_blocks = pack(
        layout, amount, jnp.concatenate([recycle, row_at.astype(jnp.int32)[None]]), grads,
        (key_value, query_low, start_all, normed_own, normed_all, after_grad, vectors,
         w_projections, act_low, final_low, normed_two, hidden_grad, attended, after_low, g_factors),
    )
    total = lambda got: low_of(jnp.sum(got.astype(WIDE), axis=0))
    blocks = total(exchange(blocks, BOTH, layout.cores))
    blocks, pair_out = lax.optimization_barrier((exchange(blocks, BOTH, layout.chips), pair_out))
    blocks = total(blocks)
    blocks = exchange(jnp.concatenate([blocks, node_blocks], axis=1), "row")
    pair_grad = jnp.where(stays, pair_one_grad, pair_one_away).astype(WIDE) + jnp.einsum(
        "hij,dh->ijd", score_low, w_bias[:, :HEADS], preferred_element_type=WIDE
    )
    blocks, pair_grad = lax.optimization_barrier((blocks, low_of(pair_grad)))
    blocks = jnp.sum(blocks.astype(WIDE), axis=0)
    node_parts = jnp.split(blocks[height:], NODE_DIM // LANES)
    node_grad = low_of(after_grad + jnp.concatenate(node_parts, axis=1))
    blocks = blocks[:height]
    grad_own = lax.dynamic_slice(blocks.reshape(-1), (offset,), (amount,))
    square_own = jnp.broadcast_to(jnp.sum(grad_own * grad_own), (1, LANES))
    last = jnp.concatenate([g_bias.reshape(1, LANES), square_own], axis=0)
    last = jnp.sum(spread(last, devices, BOTH).reshape(devices, 2, LANES), axis=0)
    bias_total = last[0]
    grad_norm = jnp.sqrt(last[1, 0])
    clipped = grad_own * (CLIP_NORM / jnp.maximum(grad_norm, CLIP_NORM))
    new_first = BETA_ONE * first + (1.0 - BETA_ONE) * clipped
    new_second = BETA_TWO * second + (1.0 - BETA_TWO) * clipped * clipped
    first_hat = new_first / (1.0 - BETA_ONE**ADAM_STEP)
    second_hat = new_second / (1.0 - BETA_TWO**ADAM_STEP)
    new_master = master - LEARN_RATE * (
        first_hat / (jnp.sqrt(second_hat) + ADAM_EPS) + WEIGHT_DECAY * master
    )
    return (
        node_out[None],
        pair_out[None],
        node_grad[None],
        pair_grad[None],
        grad_own,
        bias_total,
        grad_norm,
        new_master,
        new_first,
        new_second,
        low_of(new_master),
    )


def solution(mesh):
    layout = Layout(mesh.shape["crop"], mesh.shape["row"])
    return jax.shard_map(
        lambda *arrays: local(layout, *arrays),
        mesh=mesh,
        in_specs=(
            P("crop", "row", None),
            P("crop", "row", None, None),
            P("crop"),
            P("crop", None),
            P("crop", "row", None),
            P("crop", "row", None, None),
            P(("crop", "row")),
            P(("crop", "row")),
            P(("crop", "row")),
        ),
        out_specs=(
            P("crop", "row", None),
            P("crop", "row", None, None),
            P("crop", "row", None),
            P("crop", "row", None, None),
            P(("crop", "row")),
            P(),
            P(),
            P(("crop", "row")),
            P(("crop", "row")),
            P(("crop", "row")),
            P(("crop", "row")),
        ),
        check_vma=False,
    )
```

```python
import math
from functools import partial
from typing import Any, NamedTuple

import jax
import jax.numpy as jnp
import numpy as np
from jax import lax
from jax.experimental import pallas as pl
from jax.experimental.pallas import tpu as pltpu
from jax.sharding import PartitionSpec as P

NODE_DIM = 256
PAIR_DIM = 128
HEADS = 8
HEAD_DIM = 32
OUTER = 32
TRI_DIM = 128
FFN_NODE = 1024
FFN_PAIR = 512
RECYCLES = 4
ADAM_STEP = 3


EPS_NORM = 1e-05
ADAM_EPS = 1e-08
BETA_ONE = 0.9
BETA_TWO = 0.95
LEARN_RATE = 0.06
WEIGHT_DECAY = 0.1
CLIP_NORM = 1.0
MASK_FILL = 1000000000.0
HIGHEST = lax.Precision.HIGHEST


class Triangle(NamedTuple):
    gain_in: Any
    w_left: Any
    w_right: Any
    w_gate: Any
    gain_tri: Any
    w_tri_out: Any


class Params(NamedTuple):
    embed: Any
    gain_one: Any
    w_query: Any
    w_key: Any
    w_value: Any
    w_bias: Any
    w_attn_out: Any
    gain_two: Any
    w_node_up: Any
    w_node_down: Any
    gain_three: Any
    w_left_node: Any
    w_right_node: Any
    w_outer: Any
    outgoing: Triangle
    incoming: Triangle
    gain_pair: Any
    w_pair_up: Any
    w_pair_down: Any
    bias_pair: Any


LANES = 128
HEADS_WIDTH = HEADS * HEAD_DIM


def first_rows():
    square = PAIR_DIM * TRI_DIM
    triangle = Triangle(PAIR_DIM, square, square, PAIR_DIM * PAIR_DIM, TRI_DIM, square)
    sizes = Params(
        embed=RECYCLES * NODE_DIM,
        gain_one=NODE_DIM,
        w_query=NODE_DIM * HEADS_WIDTH,
        w_key=NODE_DIM * HEADS_WIDTH,
        w_value=NODE_DIM * HEADS_WIDTH,
        w_bias=PAIR_DIM * HEADS,
        w_attn_out=HEADS_WIDTH * NODE_DIM,
        gain_two=NODE_DIM,
        w_node_up=NODE_DIM * FFN_NODE,
        w_node_down=FFN_NODE * NODE_DIM,
        gain_three=NODE_DIM,
        w_left_node=NODE_DIM * OUTER,
        w_right_node=NODE_DIM * OUTER,
        w_outer=OUTER * OUTER * PAIR_DIM,
        outgoing=triangle,
        incoming=triangle,
        gain_pair=PAIR_DIM,
        w_pair_up=PAIR_DIM * FFN_PAIR,
        w_pair_down=FFN_PAIR * PAIR_DIM,
        bias_pair=PAIR_DIM,
    )
    leaves, tree = jax.tree.flatten(sizes)
    ends = np.cumsum(leaves) // LANES
    starts = [0] + [int(end) for end in ends[:-1]]
    return jax.tree.unflatten(tree, starts), int(ends[-1])


LOW = jnp.bfloat16
WIDE = jnp.float32
BOTH = ("crop", "row")
TILE = 16
VMEM_LIMIT = 56 * 2**20
SMALL_LIMIT = 28 * 2**20
INV_SQRT2 = 1.0 / math.sqrt(2.0)
INV_SQRT2PI = 1.0 / math.sqrt(2.0 * math.pi)


class Layout:
    def __init__(self, crops, rows):
        self.crops, self.rows = crops, rows
        self.devices = crops * rows
        self.wide = 2 ** (int(math.log2(rows)) // 2)
        self.high = rows // self.wide
        half = crops // 2
        self.moves = [
            (here, self.work_place(here))
            for here in range(self.devices)
            if here != self.work_place(here)
        ]
        high_of = lambda here: here % rows // self.wide
        self.near = [
            (here, there) for here, there in self.moves if abs(high_of(here) - high_of(there)) == 1
        ]
        self.far = [move for move in self.moves if move not in self.near]
        self.groups = [
            [self.work_place(c * rows + r) for r in range(rows)] for c in range(crops)
        ]
        self.cores = [
            [(2 * x + k) * rows + r for k in range(2)] for x in range(half) for r in range(rows)
        ]
        self.slabs = [[2 * x * rows + k for k in range(2 * rows)] for x in range(half)]
        self.chips = [
            [(2 * x + k) * rows + r for x in range(half)] for k in range(2) for r in range(rows)
        ]

    def work_place(self, here):
        crop, row = here // self.rows, here % self.rows
        high, wide = row // self.wide, row % self.wide
        core = crop % 2
        away = (high // (self.high // 2) + core) % 2
        crop = crop + away * (1 - 2 * core)
        high = high + away * (self.high - 1 - 2 * high)
        return crop * self.rows + high * self.wide + wide


def exchange(blocks, axes, groups=None):
    return lax.all_to_all(blocks, axes, 0, 0, axis_index_groups=groups, tiled=True)


def spread(part, count, axes, groups=None):
    return exchange(jnp.broadcast_to(part[None], (count,) + part.shape), axes, groups)


def dot_nn(a, b):
    return lax.dot_general(a, b, (((1,), (0,)), ((), ())), preferred_element_type=WIDE)


def dot_nt(a, b):
    return lax.dot_general(a, b, (((1,), (1,)), ((), ())), preferred_element_type=WIDE)


def dot_tn(a, b):
    return lax.dot_general(a, b, (((0,), (0,)), ((), ())), preferred_element_type=WIDE)


def norm_parts(x):
    hat, _, scale = norm_all(x)
    return hat, scale


def norm_all(x):
    mean = jnp.mean(x, axis=0, keepdims=True)
    centered = x - mean
    scale = lax.rsqrt(jnp.mean(centered * centered, axis=0, keepdims=True) + EPS_NORM)
    return centered * scale, mean, scale


def norm_back(grad, hat, scale, gain):
    grad_gain = jnp.sum(grad * hat, axis=1, keepdims=True)
    wide = grad * gain
    inner = jnp.mean(wide * hat, axis=0, keepdims=True)
    return scale * (wide - jnp.mean(wide, axis=0, keepdims=True) - hat * inner), grad_gain


def sigmoid(x):
    return 0.5 * jnp.tanh(0.5 * x) + 0.5


EMBED = slice(0, 8)
GAIN_ONE, GAIN_TWO, GAIN_THREE = slice(8, 10), slice(10, 12), slice(12, 14)
OUT_GAIN, OUT_TRI, IN_GAIN, IN_TRI = (slice(k, k + 1) for k in range(14, 18))
PAIR_GAIN, PAIR_BIAS = slice(18, 19), slice(19, 20)


def column(row):
    return jnp.broadcast_to(row, (LANES, row.shape[1])).T[:, :1]


def row_of(values):
    return jnp.broadcast_to(values, (values.shape[0], LANES)).T[:1]


def cat(ref):
    return jnp.concatenate([ref[t] for t in range(ref.shape[0])], axis=1)


def put(ref, value):
    count = ref.shape[0]
    width = value.shape[1] // count
    for t in range(count):
        ref[t] = value[:, t * width : (t + 1) * width].astype(ref.dtype)


def swapped(value):
    if value.shape[0] % TILE or value.shape[1] % TILE:
        return jnp.swapaxes(value.astype(WIDE), 0, 1).astype(LOW)
    return jnp.swapaxes(value, 0, 1)


def send_pair(scratch, out_ref):
    parts, share = out_ref.shape[0], out_ref.shape[1] // 2
    channels = parts * share
    for side in range(2):
        value = swapped(scratch[:, side * channels : (side + 1) * channels, :])
        out_ref[:, side * share : (side + 1) * share] = value.reshape(
            (parts, share) + value.shape[1:]
        )


def take_pair(in_ref, scratch):
    parts, share = in_ref.shape[0], in_ref.shape[1] // 2
    channels = parts * share
    for side in range(2):
        value = in_ref[:, side * share : (side + 1) * share]
        value = value.reshape((channels,) + value.shape[2:])
        scratch[:, side * channels : (side + 1) * channels, :] = swapped(value)


def front(x, gain, w_all, mask, x_out, mean_out, scale_out, gate_out, sides):
    hat, mean, scale = norm_all(x)
    all_three = dot_nn(w_all, (hat * gain).astype(LOW))
    channels = 2 * TRI_DIM
    put(sides, all_three[:channels] * mask)
    put(x_out, x)
    put(mean_out, mean)
    put(scale_out, scale)
    put(gate_out, sigmoid(all_three[channels:]))


def triangle_update(mixed, gain, w_out):
    hat, scale = norm_parts(mixed)
    normed = (hat * gain).astype(LOW)
    return hat, scale, normed, dot_nn(w_out, normed)


def post_back(grad, gate, hat, scale, normed, update, gain, w_out_back):
    update_grad = (grad * gate).astype(LOW)
    gate_grad = (grad * update * (gate * (1.0 - gate))).astype(LOW)
    grad_out = dot_nt(normed, update_grad)
    mixed_grad, grad_gain = norm_back(dot_nn(w_out_back, update_grad), hat, scale, gain)
    return mixed_grad, gate_grad, grad_out, grad_gain


def front_back(grad, x, mean, scale, sides_grad, gate_grad, mask, gain, w_all_back):
    hat = (x - mean) * scale
    normed = (hat * gain).astype(LOW)
    sides = jnp.concatenate([sides_grad * mask.astype(LOW), gate_grad], axis=0)
    grad_w = dot_nt(normed, sides)
    x_grad, grad_gain = norm_back(dot_nn(w_all_back, sides), hat, scale, gain)
    return grad + x_grad, grad_w, grad_gain


def gelu_parts(x):
    cumulative = 0.5 * lax.erf(x * INV_SQRT2) + 0.5
    density = INV_SQRT2PI * jnp.exp(-0.5 * x * x)
    return x * cumulative, cumulative + x * density


def zero_first(*refs):
    @pl.when((pl.program_id(0) == 0) & (pl.program_id(1) == 0))
    def _():
        for ref in refs:
            ref[...] = jnp.zeros_like(ref)


def run(body, step, extent, in_arrays, in_kinds, outs, scratch, flops, skip=0, aliases={}):
    def spec(kind, shape):
        lead = (0,) * len(shape)
        if kind == "m":
            return pl.BlockSpec(memory_space=pltpu.SMEM)
        if kind == "x":
            return pl.BlockSpec(memory_space=pl.ANY)
        block, at = {
            "R": (step[:1] + shape[1:-1] + step[1:], lambda c, r: (r + skip,) + lead[2:] + (c,)),
            "N": (step + shape[2:], lambda c, r: (r + skip, c) + lead[2:]),
            "r": (step[:1] + shape[1:-1] + step[1:], lambda c, r: (r,) + lead[2:] + (c,)),
            "n": (step + shape[2:], lambda c, r: (r, c) + lead[2:]),
            "s": (shape[:-2] + step, lambda c, r: lead[2:] + (r, c)),
            "c": (shape[:-1] + step[1:], lambda c, r: lead[1:] + (c,)),
            "t": (step[:1] + shape[1:], lambda c, r: (r,) + lead[1:]),
            "p": ((1,) + step[:1] + shape[2:], lambda c, r: (c, r) + lead[2:]),
            "q": (step[1:] + shape[1:], lambda c, r: (c,) + lead[1:]),
            "w": (shape, lambda c, r: lead),
        }[kind]
        return pl.BlockSpec(block, at)

    moved = sum(a.size * a.dtype.itemsize for a in in_arrays)
    return pl.pallas_call(
        body,
        grid=(extent[1] // step[1], extent[0] // step[0]),
        in_specs=[spec(kind, a.shape) for kind, a in zip(in_kinds, in_arrays)],
        out_specs=[spec(kind, shape) for kind, shape, _ in outs],
        out_shape=[jax.ShapeDtypeStruct(shape, dtype) for _, shape, dtype in outs],
        scratch_shapes=scratch,
        input_output_aliases=aliases,
        compiler_params=pltpu.CompilerParams(vmem_limit_bytes=VMEM_LIMIT),
        cost_estimate=pl.CostEstimate(flops=flops, bytes_accessed=moved, transcendentals=0),
    )(*in_arrays)


def all_low(w):
    return jnp.concatenate([w[k * PAIR_DIM : (k + 1) * PAIR_DIM].T for k in range(3)], axis=0)


def all_back(w):
    return jnp.concatenate([w[k * PAIR_DIM : (k + 1) * PAIR_DIM] for k in range(3)], axis=1)


def kernel_open(
    stays, pair, pair_home, table, right, mask, vectors, w_all, x_out, mean_out, scale_out, gate_out, sides_out, sides
):
    right_low = right[...]
    at_home = stays[0] == 1
    x = jnp.concatenate(
        [
            jnp.where(at_home, pair_home[t], pair[t]).T.astype(WIDE) + dot_tn(table[t], right_low)
            for t in range(pair.shape[0])
        ],
        axis=1,
    )
    front(
        x, column(vectors[OUT_GAIN]), all_low(w_all), cat(mask), x_out, mean_out, scale_out, gate_out,
        sides,
    )
    send_pair(sides, sides_out)


def kernel_middle(
    mixed, x_in, gate_in, mask, vectors, w_out, w_all,
    x_out, mean_out, scale_out, gate_out, sides_out, arrived, sides,
):
    arrived[...] = swapped(mixed[...])
    *_, update = triangle_update(cat(arrived).astype(WIDE), column(vectors[OUT_TRI]), w_out[...].T)
    x = cat(x_in).astype(WIDE) + cat(gate_in).astype(WIDE) * update
    front(
        x, column(vectors[IN_GAIN]), all_low(w_all), cat(mask),
        x_out, mean_out, scale_out, gate_out, sides,
    )
    send_pair(sides, sides_out)


def kernel_turn(sums, mixed, x_in, gate_in, cot, vectors, w_out, w_up, w_down, *rest):
    if sums:
        g_out, g_tri, g_up, g_down, g_pair, g_bias, arrived = rest
        zero_first(g_out, g_tri, g_up, g_down, g_pair, g_bias)
    else:
        pair_out, x_grad, gate_grad, mixed_grad, arrived, leaving = rest[-6:]
    rows = x_in.shape[0]
    arrived[...] = swapped(mixed[...])
    up_low, up_back = w_up[...].T, w_up[...]
    down_low, down_back = w_down[...].T, w_down[...]
    tri_col, pair_col = column(vectors[IN_TRI]), column(vectors[PAIR_GAIN])
    chunk = PAIR_DIM

    gate = cat(gate_in).astype(WIDE)
    mix_parts = triangle_update(cat(arrived).astype(WIDE), tri_col, w_out[...].T)
    x = cat(x_in).astype(WIDE) + gate * mix_parts[-1]
    hat, scale = norm_parts(x)
    normed = (hat * pair_col).astype(LOW)
    cot_low = jnp.concatenate([cot[t].T for t in range(rows)], axis=1)
    total = x + column(vectors[PAIR_BIAS])
    normed_grad = jnp.zeros_like(x)
    for c in range(FFN_PAIR // chunk):
        part = slice(c * chunk, (c + 1) * chunk)
        act, slope = gelu_parts(dot_nn(up_low[part], normed))
        act_low = act.astype(LOW)
        hidden_grad = (dot_nn(down_back[part], cot_low) * slope).astype(LOW)
        normed_grad = normed_grad + dot_nn(up_back[:, part], hidden_grad)
        if sums:
            g_up[:, part] += dot_nt(normed, hidden_grad)
            g_down[part] += dot_nt(act_low, cot_low)
        else:
            total = total + dot_nn(down_low[:, part], act_low)
    cot_wide = cot_low.astype(WIDE)
    back, grad_pair = norm_back(normed_grad, hat, scale, pair_col)
    grad = cot_wide + back
    mix_grad, gates, grad_out, grad_tri = post_back(grad, gate, *mix_parts, tri_col, w_out[...])
    if sums:
        g_bias[...] += jnp.sum(cot_wide, axis=1, keepdims=True)
        g_pair[...] += grad_pair
        g_out[...] += grad_out
        g_tri[...] += grad_tri
        return
    total_low = total.astype(LOW)
    width = total.shape[1] // rows
    for t in range(rows):
        pair_out[t] = total_low[:, t * width : (t + 1) * width].T
    put(x_grad, grad)
    put(leaving, mix_grad)
    put(gate_grad, gates)
    mixed_grad[...] = swapped(leaving[...])


def kernel_return(
    sums, sides_grad, x_after, mean_after, scale_after, gate_after, grad_in, mask, vectors, w_after,
    mixed, gate_in, w_out, *rest,
):
    if sums:
        g_after, g_gain, g_out, g_tri, sides, arrived = rest
        zero_first(g_after, g_gain, g_out, g_tri)
    else:
        x_grad, gate_grad, mixed_grad, sides, arrived, leaving = rest
    take_pair(sides_grad, sides)
    arrived[...] = swapped(mixed[...])
    tri_col = column(vectors[OUT_TRI])
    grad, grad_w, grad_gain = front_back(
        cat(grad_in).astype(WIDE), cat(x_after).astype(WIDE), cat(mean_after), cat(scale_after),
        cat(sides), cat(gate_after),
        cat(mask), column(vectors[IN_GAIN]), all_back(w_after),
    )
    mix_parts = triangle_update(cat(arrived).astype(WIDE), tri_col, w_out[...].T)
    mix_grad, gates, grad_out, grad_tri = post_back(
        grad, cat(gate_in).astype(WIDE), *mix_parts, tri_col, w_out[...]
    )
    if sums:
        g_after[...] += grad_w
        g_gain[...] += grad_gain
        g_out[...] += grad_out
        g_tri[...] += grad_tri
        return
    put(x_grad, grad)
    put(leaving, mix_grad)
    put(gate_grad, gates)
    mixed_grad[...] = swapped(leaving[...])


def kernel_close(
    sides_grad, x_after, mean_after, scale_after, gate_after, grad_in, mask, vectors, w_after,
    table, right,
    pair_grad, table_grad, right_grad, g_after, g_gain, sides,
):
    take_pair(sides_grad, sides)
    zero_first(g_after, g_gain)

    @pl.when(pl.program_id(1) == 0)
    def _():
        right_grad[...] = jnp.zeros_like(right_grad)

    grad, grad_w, grad_gain = front_back(
        cat(grad_in).astype(WIDE), cat(x_after).astype(WIDE), cat(mean_after), cat(scale_after),
        cat(sides), cat(gate_after),
        cat(mask), column(vectors[OUT_GAIN]), all_back(w_after),
    )
    g_after[...] += grad_w
    g_gain[...] += grad_gain
    low = grad.astype(LOW)
    rows = table.shape[0]
    width = low.shape[1] // rows
    for t in range(rows):
        own = low[:, t * width : (t + 1) * width]
        pair_grad[t] = own.T
        table_grad[0, t] = dot_nt(right[...], own)
        right_grad[...] += dot_nn(table[t], own)


CHANNELS = 8


def kernel_mix(incoming, left, right, *outs):
    parts, count, rows, length = left.shape
    part = rows // len(outs)
    for c in range(count):
        a = left[:, c].reshape(length, length)
        b = right[:, c].reshape(length, length)
        mixed = dot_tn(a, b) if incoming else dot_nt(a, b)
        mixed = mixed.astype(LOW).reshape(parts, rows, length)
        for k, out in enumerate(outs):
            out[:, c] = mixed[:, k * part : (k + 1) * part]


def kernel_mix_back(incoming, *refs):
    *grads, left, right, out = refs
    parts, count, rows, length = left.shape
    for c in range(count):
        g = jnp.concatenate([grad[:, c] for grad in grads], axis=1).reshape(length, length)
        a = left[:, c].reshape(length, length)
        b = right[:, c].reshape(length, length)
        a_grad = dot_nt(b, g) if incoming else dot_nn(g, b)
        b_grad = dot_nn(a, g) if incoming else dot_tn(g, a)
        out[:, 0, c] = a_grad.astype(LOW).reshape(parts, rows, length)
        out[:, 1, c] = b_grad.astype(LOW).reshape(parts, rows, length)


def mix(sides, incoming, pieces=1):
    parts, double, rows, length = sides.shape
    share = double // 2
    count = min(CHANNELS, share)
    steps = share // count
    block = (parts, count, rows, length)
    part = (parts, count, rows // pieces, length)
    return pl.pallas_call(
        lambda *refs: kernel_mix(incoming, *refs),
        grid=(steps,),
        in_specs=[
            pl.BlockSpec(block, lambda c: (0, c, 0, 0)),
            pl.BlockSpec(block, lambda c: (0, c + steps, 0, 0)),
        ],
        out_specs=[pl.BlockSpec(part, lambda c: (0, c, 0, 0))] * pieces,
        out_shape=[jax.ShapeDtypeStruct((parts, share) + part[2:], LOW)] * pieces,
        compiler_params=pltpu.CompilerParams(vmem_limit_bytes=VMEM_LIMIT),
        cost_estimate=pl.CostEstimate(
            flops=2 * share * length**3, bytes_accessed=3 * share * length * length * 2,
            transcendentals=0,
        ),
    )(sides, sides)


def mix_back(grads, sides, incoming):
    parts, double, rows, length = sides.shape
    share = double // 2
    count = min(CHANNELS, share)
    steps = share // count
    block = (parts, count, rows, length)
    part = (parts, count, rows // len(grads), length)
    out = pl.pallas_call(
        lambda *refs: kernel_mix_back(incoming, *refs),
        grid=(steps,),
        in_specs=[pl.BlockSpec(part, lambda c: (0, c, 0, 0))] * len(grads)
        + [
            pl.BlockSpec(block, lambda c: (0, c, 0, 0)),
            pl.BlockSpec(block, lambda c: (0, c + steps, 0, 0)),
        ],
        out_specs=pl.BlockSpec((parts, 2, count, rows, length), lambda c: (0, 0, c, 0, 0)),
        out_shape=jax.ShapeDtypeStruct((parts, 2, share, rows, length), LOW),
        compiler_params=pltpu.CompilerParams(vmem_limit_bytes=VMEM_LIMIT),
        cost_estimate=pl.CostEstimate(
            flops=4 * share * length**3, bytes_accessed=5 * share * length * length * 2,
            transcendentals=0,
        ),
    )(*grads, sides, sides)
    return out.reshape(sides.shape)


def share_rows(share):
    return -(-(share + 2 * LANES) // (TILE * LANES)) * TILE


def whole(shape):
    return pl.BlockSpec(shape, lambda *_: (0,) * len(shape))


def one_call(body, scalars, in_arrays, outs, scratch=(), limit=VMEM_LIMIT):
    return pl.pallas_call(
        body,
        in_specs=[pl.BlockSpec(memory_space=pltpu.SMEM)] * len(scalars)
        + [whole(a.shape) for a in in_arrays],
        out_specs=[whole(shape) for shape, _ in outs],
        out_shape=[jax.ShapeDtypeStruct(shape, dtype) for shape, dtype in outs],
        scratch_shapes=list(scratch),
        grid=(1,),
        compiler_params=pltpu.CompilerParams(vmem_limit_bytes=limit),
    )(*scalars, *in_arrays)


def lane_in(shape, start, width):
    lane = lax.broadcasted_iota(jnp.int32, shape, 1)
    return (lane >= start) & (lane < start + width)


def rolled(value, shift):
    shift %= LANES
    return pltpu.roll(value, shift, 1) if shift else value


def share_order(layout):
    return [((d // layout.rows) % 2, d // (2 * layout.rows), d % layout.rows) for d in range(layout.devices)]


def unpack(layout, shares, share):
    at, _ = first_rows()
    height = shares.shape[3]
    first = [share * d // LANES for d in range(layout.devices)]
    order = share_order(layout)
    matrices = [
        (at.w_query, NODE_DIM, 3, 3 * HEADS_WIDTH),
        (at.w_attn_out, HEADS_WIDTH, 1, NODE_DIM),
        (at.w_node_up, NODE_DIM, 1, FFN_NODE),
        (at.w_node_down, FFN_NODE, 1, NODE_DIM),
        (at.w_outer, OUTER * OUTER, 1, PAIR_DIM),
        (at.outgoing.w_left, 3 * PAIR_DIM, 1, TRI_DIM),
        (at.outgoing.w_tri_out, TRI_DIM, 1, PAIR_DIM),
        (at.incoming.w_left, 3 * PAIR_DIM, 1, TRI_DIM),
        (at.incoming.w_tri_out, TRI_DIM, 1, PAIR_DIM),
        (at.w_pair_up, PAIR_DIM, 1, FFN_PAIR),
        (at.w_pair_down, FFN_PAIR, 1, PAIR_DIM),
    ]
    small = [(at.embed, 8), (at.gain_one, 2), (at.gain_two, 2), (at.gain_three, 2)]
    small += [
        (start, 1)
        for start in (
            at.outgoing.gain_in, at.outgoing.gain_tri, at.incoming.gain_in, at.incoming.gain_tri,
            at.gain_pair, at.bias_pair,
        )
    ]

    def body(shares_ref, vectors, bias_out, factors_out, *rest):
        outs, flat, narrow = rest[:-2], rest[-2], rest[-1]
        for d, place in enumerate(order):
            block = shares_ref[place].astype(WIDE)
            if d:
                tail = flat[first[d] : first[d] + 1]
                flat[first[d] : first[d] + height] = block
                flat[first[d] : first[d] + 1] = block[:1] + tail
            else:
                flat[:height] = block
        row = 0
        vectors[...] = jnp.zeros_like(vectors)
        for start, count in small:
            vectors[row : row + count] = flat[start : start + count]
            row += count
        for out, (place, rows, count, width) in zip(outs, matrices):
            pieces = width // count // LANES
            for m in range(count):
                for a in range(pieces):
                    start = place + m * rows * pieces + a
                    value = (
                        flat[pl.ds(start, rows, stride=pieces), :]
                        if pieces > 1
                        else flat[start : start + rows]
                    )
                    lane = (m * pieces + a) * LANES
                    out[:, lane : lane + LANES] = value.astype(LOW)
        per_row = LANES // HEADS
        shape = (HEADS, LANES)
        value = flat[at.w_bias : at.w_bias + HEADS]
        for a in range(per_row):
            kept = jnp.where(lane_in(shape, 0, HEADS), rolled(value, -HEADS * a), 0.0)
            narrow[pl.ds(a, HEADS, stride=per_row), :] = kept
        bias_out[...] = narrow[:PAIR_DIM].astype(LOW)
        per_row = LANES // OUTER
        count = NODE_DIM // per_row
        shape = (count, LANES)
        left, right = (flat[start : start + count] for start in (at.w_left_node, at.w_right_node))
        for a in range(per_row):
            kept = jnp.where(lane_in(shape, 0, OUTER), rolled(left, -OUTER * a), 0.0)
            kept += jnp.where(lane_in(shape, OUTER, OUTER), rolled(right, OUTER - OUTER * a), 0.0)
            narrow[pl.ds(a, count, stride=per_row), :] = kept
        factors_out[...] = narrow[...].astype(LOW)

    return one_call(
        body,
        (),
        (shares,),
        [((24, LANES), WIDE), ((PAIR_DIM, LANES), LOW), ((NODE_DIM, LANES), LOW)]
        + [((rows, width), LOW) for _, rows, _, width in matrices],
        [pltpu.VMEM((first[-1] + height + TILE, LANES), WIDE), pltpu.VMEM((NODE_DIM, LANES), WIDE)],
    )


def pack(layout, share, scalars, grads, node_parts):
    at, total = first_rows()
    height = share_rows(share)
    first = [share * d // LANES for d in range(layout.devices)]
    order = share_order(layout)
    many = len(grads)

    def body(scalar_ref, *refs):
        ins, rest = refs[:many], refs[many:]
        (
            key_value, query_low, start, normed_own, normed_all, after_grad, vectors, w_projections,
            act_low, final_low, normed_two, hidden_grad, attended, after_low, g_factors,
            out, node_parts_out, flat, narrow, steps,
        ) = rest

        def store(place, count, value):
            rows, pieces = value.shape[0], value.shape[1] // count // LANES
            for m in range(count):
                for a in range(pieces):
                    lane = (m * pieces + a) * LANES
                    begin = place + m * rows * pieces + a
                    part = value[:, lane : lane + LANES]
                    if pieces > 1 and rows > 1:
                        flat[pl.ds(begin, rows, stride=pieces), :] = part
                    else:
                        flat[begin : begin + rows] = part

        flat[total:] = jnp.zeros((flat.shape[0] - total, LANES), WIDE)
        for ref, (place, count, _) in zip(ins, grads):
            store(place, count, row_of(ref[...]) if ref.shape[1] == 1 else ref[...])
        store(at.w_node_down, 1, dot_tn(act_low[...], final_low[...]))
        store(at.w_node_up, 1, dot_tn(normed_two[...], hidden_grad[...]))
        store(at.w_attn_out, 1, dot_tn(attended[...], after_low[...]))
        per_row = LANES // OUTER
        count = NODE_DIM // per_row
        narrow[...] = g_factors[...]
        left = jnp.zeros((count, LANES), WIDE)
        right = left
        for a in range(per_row):
            piece = narrow[pl.ds(a, count, stride=per_row), :]
            inside = lane_in(piece.shape, OUTER * a, OUTER)
            left = jnp.where(inside, rolled(piece, OUTER * a), left)
            right = jnp.where(inside, rolled(piece, OUTER * a - OUTER), right)
        store(at.w_left_node, 1, left)
        store(at.w_right_node, 1, right)

        store(at.w_query, 1, dot_tn(normed_own[...], query_low[...]))
        store(at.w_key, 2, dot_tn(normed_all[...], key_value[...]))
        steps[...] = dot_nt(key_value[...], w_projections[:, HEADS_WIDTH:])
        local_rows = query_low.shape[0]
        own = pl.ds(pl.multiple_of(scalar_ref[1] * local_rows, local_rows), local_rows)
        steps[own, :] += dot_nt(query_low[...], w_projections[:, :HEADS_WIDTH])
        hat, scale = row_norm(start[...])
        part, grad_gain = row_norm_back(steps[...], hat, scale, vector(vectors, GAIN_ONE))
        for r in range(node_parts_out.shape[0]):
            for a in range(NODE_DIM // LANES):
                piece = part[r * local_rows : (r + 1) * local_rows, a * LANES : (a + 1) * LANES]
                node_parts_out[r, a * local_rows : (a + 1) * local_rows] = piece.astype(LOW)
        store(at.gain_one, 1, grad_gain)
        flat[at.embed : at.embed + 2 * RECYCLES] = jnp.zeros((2 * RECYCLES, LANES), WIDE)
        column_sum = jnp.sum(after_grad[...], axis=0, keepdims=True)
        column_sum += jnp.sum(part, axis=0, keepdims=True)
        for a in range(NODE_DIM // LANES):
            place = at.embed + (NODE_DIM // LANES) * scalar_ref[0] + a
            flat[pl.ds(place, 1), :] = column_sum[:, a * LANES : (a + 1) * LANES]
        for d, where in enumerate(order):
            out[where] = flat[first[d] : first[d] + height].astype(LOW)

    shape = (2, layout.crops // 2, layout.rows, height, LANES)
    return one_call(
        body,
        (scalars,),
        tuple(array for _, _, array in grads) + tuple(node_parts),
        [(shape, LOW), ((layout.rows, node_parts[1].shape[0] * NODE_DIM // LANES, LANES), LOW)],
        [
            pltpu.VMEM((first[-1] + height + TILE, LANES), WIDE),
            pltpu.VMEM((NODE_DIM, LANES), WIDE),
            pltpu.VMEM(node_parts[2].shape, WIDE),
        ],
        SMALL_LIMIT,
    )


def row_norm(x):
    centered = x - jnp.mean(x, axis=-1, keepdims=True)
    scale = lax.rsqrt(jnp.mean(centered * centered, axis=-1, keepdims=True) + EPS_NORM)
    return centered * scale, scale


def row_norm_back(grad, hat, scale, gain):
    grad_gain = jnp.sum(grad * hat, axis=0, keepdims=True)
    wide = grad * gain
    inner = jnp.mean(wide * hat, axis=-1, keepdims=True)
    return scale * (wide - jnp.mean(wide, axis=-1, keepdims=True) - hat * inner), grad_gain


def vector(ref, rows):
    return jnp.concatenate([ref[r : r + 1] for r in range(rows.start, rows.stop)], axis=1)


def by_head(value):
    return jnp.concatenate(
        [
            jnp.where(lane_in(value.shape, h * HEAD_DIM, HEAD_DIM), value, 0.0)
            for h in range(HEADS)
        ],
        axis=0,
    )


def head_sum(value):
    rows = value.shape[0] // HEADS
    parts = [value[h * rows : (h + 1) * rows] for h in range(HEADS)]
    return sum(
        jnp.where(lane_in(part.shape, h * HEAD_DIM, HEAD_DIM), part, 0.0)
        for h, part in enumerate(parts)
    )


SCORE_SCALE = HEAD_DIM ** (-0.5)
KEEP_LANE = 2 * OUTER


def node_forward(
    recycle, node_ref, all_ref, bias_ref, keep, keep_rows, vectors, w_projections, w_attn_out, w_up, w_down,
    w_factors,
    node_out, factors_out, start_out, normed_own, normed_out, soft_out, heads_out, key_out, value_out,
    attended_out, after_out, act_out, slope_out, final_out, flat,
):
    pieces = NODE_DIM // LANES
    length = all_ref.shape[0] // pieces
    embed = jnp.concatenate(
        [vectors[pl.ds(pieces * recycle[0] + a, 1), :] for a in range(pieces)], axis=1
    )
    flat[...] = all_ref[...].astype(WIDE)
    all_rows = jnp.concatenate(
        [flat[pl.ds(a, length, stride=pieces), :] for a in range(pieces)], axis=1
    )
    gain = vector(vectors, GAIN_ONE)
    start_all = all_rows + embed
    normed_all = (row_norm(start_all)[0] * gain).astype(LOW)
    start_out[...] = start_all
    normed_out[...] = normed_all
    start = node_ref[...].astype(WIDE) + embed
    normed = (row_norm(start)[0] * gain).astype(LOW)
    normed_own[...] = normed
    query = dot_nn(normed, w_projections[:, :HEADS_WIDTH]).astype(LOW).astype(WIDE)
    heads = by_head(query).astype(LOW)
    key_value = dot_nn(normed_all, w_projections[:, HEADS_WIDTH:]).astype(LOW)
    key, value = key_value[:, :HEADS_WIDTH], key_value[:, HEADS_WIDTH:]
    heads_out[...] = heads
    key_out[...] = key
    value_out[...] = value
    scores = dot_nt(heads, key) * SCORE_SCALE + bias_ref[...] + (keep[...] - 1.0) * MASK_FILL
    powers = jnp.exp(scores - jnp.max(scores, axis=-1, keepdims=True))
    soft = powers / jnp.sum(powers, axis=-1, keepdims=True)
    soft_out[...] = soft
    attended = head_sum(dot_nn(soft.astype(LOW), value)).astype(LOW)
    attended_out[...] = attended
    after = start + dot_nn(attended, w_attn_out[...])
    after_out[...] = after
    normed = (row_norm(after)[0] * vector(vectors, GAIN_TWO)).astype(LOW)
    act, slope = gelu_parts(dot_nn(normed, w_up[...]))
    act_out[...] = act.astype(LOW)
    slope_out[...] = slope
    final = after + dot_nn(act.astype(LOW), w_down[...])
    final_out[...] = final
    node_out[...] = final.astype(LOW)
    normed = (row_norm(final)[0] * vector(vectors, GAIN_THREE)).astype(LOW)
    factors = dot_nn(normed, w_factors[...])
    factors = jnp.where(lane_in(factors.shape, KEEP_LANE, 1), keep_rows[...], factors).astype(LOW)
    factors_out[...] = jnp.broadcast_to(factors[None], factors_out.shape)


def node_backward(
    sources, factor_ref, cot, vectors, soft_ref, heads, key, value, after_ref, slope, final_ref,
    w_attn_out, w_up, w_down, w_factors,
    key_value_out, query_out, score_out, after_grad_out, final_low_out, normed_two_out,
    hidden_out, after_low_out, g_factors, g_two, g_three,
):
    ranks = key_value_out.shape[0] // cot.shape[0]
    left = factor_ref[sources[0]].astype(WIDE)
    right = sum(factor_ref[sources[1 + r]].astype(WIDE) for r in range(ranks))
    rows = jnp.where(lane_in(left.shape, 0, OUTER), left, right).astype(LOW)
    hat, scale = row_norm(final_ref[...])
    gain = vector(vectors, GAIN_THREE)
    g_factors[...] = dot_tn((hat * gain).astype(LOW), rows)
    part, g_three[...] = row_norm_back(dot_nt(rows, w_factors[...]), hat, scale, gain)
    final_grad = cot[...].astype(WIDE) + part
    final_low = final_grad.astype(LOW)
    final_low_out[...] = final_low
    hidden_grad = (dot_nt(final_low, w_down[...]) * slope[...]).astype(LOW)
    hidden_out[...] = hidden_grad
    hat, scale = row_norm(after_ref[...])
    gain = vector(vectors, GAIN_TWO)
    normed_two_out[...] = (hat * gain).astype(LOW)
    part, g_two[...] = row_norm_back(dot_nt(hidden_grad, w_up[...]), hat, scale, gain)
    after_grad = final_grad + part
    after_grad_out[...] = after_grad
    after_low = after_grad.astype(LOW)
    after_low_out[...] = after_low
    attended_grad = dot_nt(after_low, w_attn_out[...]).astype(LOW).astype(WIDE)
    grad_heads = by_head(attended_grad).astype(LOW)
    soft = soft_ref[...]
    soft_grad = dot_nt(grad_heads, value[...])
    score_grad = soft * (soft_grad - jnp.sum(soft_grad * soft, axis=-1, keepdims=True))
    score_low = score_grad.astype(LOW)
    score_out[...] = score_low
    key_part = dot_tn(score_low, heads[...]) * SCORE_SCALE
    key_value_out[:, :HEADS_WIDTH] = key_part.astype(LOW)
    key_value_out[:, HEADS_WIDTH:] = dot_tn(soft.astype(LOW), grad_heads).astype(LOW)
    query_out[...] = (head_sum(dot_nn(score_low, key[...])) * SCORE_SCALE).astype(LOW)


def outer_tables(
    sources, factors, w_outer, table_out, right_out, left_out, mask_out, w_wide, steps
):
    local_rows = left_out.shape[0]
    ranks = right_out.shape[1] // local_rows
    left_low = factors[sources[0]][:, :OUTER]
    left_out[...] = left_low
    right = jnp.concatenate([factors[sources[1 + r]].astype(WIDE) for r in range(ranks)], axis=0)
    turned = right.T
    right_out[...] = turned[OUTER : 2 * OUTER].astype(LOW)
    own_keep = factors[sources[0]][:, KEEP_LANE : KEEP_LANE + 1].astype(WIDE)
    mask_out[:, 0, :] = own_keep * turned[KEEP_LANE : KEEP_LANE + 1]
    w_wide[...] = w_outer[...].astype(WIDE)
    for q in range(OUTER):
        w_q = w_wide[pl.ds(q, OUTER, stride=OUTER), :].astype(LOW)
        steps[q] = dot_nn(left_low, w_q)
    table_out[...] = jnp.swapaxes(steps[...], 0, 1).astype(LOW)


def outer_backward(table_grad, right_grad, left, w_outer, factors_out, g_outer, w_wide, steps):
    crops, ranks, local_rows, _ = factors_out.shape
    steps[...] = jnp.swapaxes(jnp.sum(table_grad[...], axis=0), 0, 1)
    w_wide[...] = w_outer[...].astype(WIDE)
    left_grad = jnp.zeros((local_rows, OUTER), WIDE)
    for q in range(OUTER):
        grad_q = steps[q].astype(LOW)
        w_q = w_wide[pl.ds(q, OUTER, stride=OUTER), :].astype(LOW)
        left_grad = left_grad + dot_nt(grad_q, w_q)
        g_outer[pl.ds(q, OUTER, stride=OUTER), :] = dot_tn(left[...], grad_q)
    right_rows = right_grad[...].T
    for r in range(ranks):
        block = jnp.concatenate(
            [
                left_grad,
                right_rows[r * local_rows : (r + 1) * local_rows],
                jnp.zeros((local_rows, LANES - 2 * OUTER), WIDE),
            ],
            axis=1,
        ).astype(LOW)
        for c in range(crops):
            factors_out[c, r] = block


def low_of(x):
    return x.astype(LOW)


def local(layout, node, pair, recycle, mask, node_cot, pair_cot, master, first, second):
    crops, ranks = layout.crops, layout.rows
    devices = crops * ranks
    local_rows, length = node.shape[1], pair.shape[2]
    share = TRI_DIM // ranks
    node, pair, node_cot, pair_cot = node[0], pair[0], node_cot[0], pair_cot[0]

    crop_at, row_at = lax.axis_index("crop"), lax.axis_index("row")
    here = crop_at * ranks + row_at
    partner = layout.work_place(here)
    stays = partner == here
    work_crop, work_row = partner // ranks, partner % ranks
    near = lambda array: lax.ppermute(array, BOTH, layout.near)
    far = lambda array: lax.ppermute(array, BOTH, layout.far)
    settled = lambda own, close, *pieces: jnp.where(stays, own, close + jnp.concatenate(pieces))

    at, _ = first_rows()

    amount = master.shape[0]
    height = share_rows(amount)
    offset = (here * (amount % LANES)) % LANES
    shard = lax.dynamic_update_slice(jnp.zeros(height * LANES, LOW), low_of(master), (offset,))
    node_rows = local_rows * NODE_DIM // LANES
    shards = jnp.concatenate([shard.reshape(height, LANES), node.reshape(-1, LANES)], axis=0)
    shards = spread(shards, ranks, "row").reshape(ranks, -1, LANES)
    shards, pair = lax.optimization_barrier((shards, pair))
    node_all = shards[:, height:].reshape(-1, LANES)
    shards = shards[:, :height].reshape(-1, LANES)
    shards = spread(shards, crops // 2, BOTH, layout.chips)
    shards = spread(shards, 2, BOTH, layout.cores)
    shards = shards.reshape(2, crops // 2, ranks, height, LANES)
    (
        vectors, w_bias, w_factors, w_projections, w_attn_out, w_node_up, w_node_down, w_outer,
        w_out_all, w_out_end, w_in_all, w_in_end, w_pair_up, w_pair_down,
    ) = unpack(layout, shards, amount)
    pair_plane = lax.ppermute(pair, BOTH, layout.moves)
    keep = mask.astype(WIDE)
    keep_rows = lax.dynamic_slice_in_dim(keep[0], row_at * local_rows, local_rows, 0)[:, None]

    pair_bias = jnp.einsum("ijd,dh->hij", pair, w_bias[:, :HEADS], preferred_element_type=WIDE)
    rows_low = lambda width: ((local_rows, width), LOW)
    rows_wide = lambda width: ((local_rows, width), WIDE)
    by_heads = (HEADS * local_rows, length)
    (
        node_out, factors, start_all, normed_own, normed_all, soft, heads, key, value, attended, after, act_low,
        slope, node_final,
    ) = one_call(
        node_forward,
        (recycle,),
        (node, node_all, pair_bias.reshape(by_heads), keep, keep_rows, vectors, w_projections, w_attn_out,
         w_node_up, w_node_down, w_factors),
        [rows_low(NODE_DIM), ((2 * ranks, local_rows, LANES), LOW), ((length, NODE_DIM), WIDE),
         rows_low(NODE_DIM), ((length, NODE_DIM), LOW), (by_heads, WIDE), (by_heads[:1] + (HEADS_WIDTH,), LOW),
         ((length, HEADS_WIDTH), LOW), ((length, HEADS_WIDTH), LOW), rows_low(HEADS_WIDTH),
         rows_wide(NODE_DIM), rows_low(FFN_NODE), rows_wide(FFN_NODE), rows_wide(NODE_DIM)],
        [pltpu.VMEM(node_all.shape, WIDE)],
    )

    factors = exchange(factors, BOTH, layout.slabs)
    cot_first, cot_last = jnp.split(pair_cot, 2)
    factors, cot_first, pair_plane = lax.optimization_barrier((factors, cot_first, pair_plane))
    everyone = jnp.arange(ranks, dtype=jnp.int32)
    slab = 2 * ranks
    sources = jnp.concatenate([partner[None], work_crop * ranks + everyone]).astype(jnp.int32) % slab
    table, right, left, mask_plane = one_call(
        outer_tables,
        (sources,),
        (factors, w_outer),
        [((local_rows, OUTER, PAIR_DIM), LOW), ((OUTER, length), LOW), ((local_rows, OUTER), LOW),
         ((local_rows, 1, length), WIDE)],
        [pltpu.VMEM((OUTER * OUTER, PAIR_DIM), WIDE), pltpu.VMEM((OUTER, local_rows, PAIR_DIM), WIDE)],
    )

    step = (min(TILE, local_rows), min(LANES, length))
    extent = (local_rows, length)
    pieces = length // step[1]
    state = (local_rows, TRI_DIM, length)
    line = (local_rows, 1, length)
    sides_shape = (ranks, 2 * share, local_rows, length)
    mixed_shape = (TRI_DIM, local_rows, length)
    natural = (local_rows, length, PAIR_DIM)
    buffer = lambda channels: pltpu.VMEM((step[0], channels, step[1]), LOW)
    trade = lambda blocks: exchange(blocks, BOTH, layout.groups)
    merge = lambda blocks: blocks.reshape((TRI_DIM,) + blocks.shape[2:])
    split = lambda blocks: blocks.reshape((ranks, share) + blocks.shape[1:])
    unit = 2 * local_rows * length * PAIR_DIM * PAIR_DIM
    front_outs = (
        ("r", state, LOW), ("r", line, WIDE), ("r", line, WIDE), ("r", state, LOW),
        ("s", sides_shape, LOW),
    )
    square = (TRI_DIM, PAIR_DIM)
    gain_shape = (PAIR_DIM, 1)
    after_shape = (PAIR_DIM, 2 * TRI_DIM + PAIR_DIM)

    x_one, mean_tri_out, scale_tri_out, gate_tri_out, sides = run(
        kernel_open, step, extent,
        (stays.astype(jnp.int32)[None], pair_plane, pair, table, right, mask_plane, vectors, w_out_all),
        "mnntcrww", front_outs, [buffer(2 * TRI_DIM)], 4 * unit,
    )
    sides, cot_first, pair_cot = lax.optimization_barrier((sides, far(cot_first), pair_cot))
    sides_out, cot_near = lax.optimization_barrier((trade(sides), near(pair_cot)))
    mixed_out = merge(trade(mix(sides_out, False)[0]))
    mixed_out, cot_last = lax.optimization_barrier((mixed_out, cot_last))
    x_two, mean_tri_in, scale_tri_in, gate_tri_in, sides = run(
        kernel_middle, step, extent,
        (mixed_out, x_one, gate_tri_out, mask_plane, vectors, w_out_end, w_in_all), "srrrwww", front_outs, [buffer(TRI_DIM), buffer(2 * TRI_DIM)], 5 * unit,
    )
    sides, cot_last = lax.optimization_barrier((sides, far(cot_last)))
    sides_in, cot_plane = lax.optimization_barrier(
        (trade(sides), settled(pair_cot, cot_near, cot_first, cot_last))
    )
    turns = 2 if local_rows % (2 * TILE) == 0 else 1
    turn_rows = local_rows // turns
    mixed_in = [merge(trade(piece)) for piece in mix(sides_in, True, turns)]
    turned, grads_in = [], []
    ends = (vectors, w_in_end, w_pair_up, w_pair_down)
    for k in range(turns):
        *turned, mixed_grad = run(
            partial(kernel_turn, False), step, (turn_rows, length),
            (mixed_in[k], x_two, gate_tri_in, cot_plane, *ends, *turned),
            "sRRNwwww" + "xxx" * (k > 0),
            (("N", natural, LOW), ("R", state, LOW), ("R", state, LOW),
             ("s", (TRI_DIM, turn_rows, length), LOW)),
            [buffer(TRI_DIM), buffer(TRI_DIM)], 24 * unit // turns,
            skip=k * turn_rows // step[0], aliases={8: 0, 9: 1, 10: 2} if k else {},
        )
        if k:
            grads_in[-1], mixed_grad = lax.optimization_barrier((grads_in[-1], mixed_grad))
        grads_in.append(trade(split(mixed_grad)))
    pair_final, x_grad, gate_grad = turned
    sides_grad = trade(mix_back(grads_in, sides_in, True))
    sums = run(
        partial(kernel_turn, True), step, extent,
        (jnp.concatenate(mixed_in, axis=1), x_two, gate_tri_in, cot_plane, *ends), "srrnwwww",
        (("w", square, WIDE), ("w", gain_shape, WIDE), ("w", (PAIR_DIM, FFN_PAIR), WIDE),
         ("w", (FFN_PAIR, PAIR_DIM), WIDE), ("w", gain_shape, WIDE), ("w", gain_shape, WIDE)),
        [buffer(TRI_DIM)], 28 * unit,
    )
    sides_grad, *sums = lax.optimization_barrier((sides_grad, *sums))
    g_in_out, g_in_tri, g_up, g_down, g_pair, g_bias = sums
    out_first, out_last = jnp.split(pair_final, 2)
    sides_grad, out_near, out_first = lax.optimization_barrier(
        (sides_grad, near(pair_final), out_first)
    )
    backs = (sides_grad, x_two, mean_tri_in, scale_tri_in, gate_grad, x_grad, mask_plane,
             vectors, w_in_all, mixed_out, gate_tri_out, w_out_end)
    x_grad, gate_grad, mixed_grad = run(
        partial(kernel_return, False), step, extent, backs, "srrrrrrwwsrw",
        (("r", state, LOW), ("r", state, LOW), ("s", mixed_shape, LOW)),
        [buffer(2 * TRI_DIM), buffer(TRI_DIM), buffer(TRI_DIM)], 8 * unit,
    )
    mixed_grad, out_first = lax.optimization_barrier((mixed_grad, far(out_first)))
    mixed_grad = trade(split(mixed_grad))
    sums = run(
        partial(kernel_return, True), step, extent, backs, "srrrrrrwwsrw",
        (("w", after_shape, WIDE), ("w", gain_shape, WIDE), ("w", square, WIDE),
         ("w", gain_shape, WIDE)),
        [buffer(2 * TRI_DIM), buffer(TRI_DIM)], 12 * unit,
    )
    mixed_grad, *sums = lax.optimization_barrier((mixed_grad, *sums))
    g_in_all, g_in_gain, g_out_out, g_out_tri = sums
    sides_grad = trade(mix_back([mixed_grad], sides_out, False))
    sides_grad, out_last = lax.optimization_barrier((sides_grad, out_last))
    pair_one_grad, table_grad, right_part, g_out_all, g_out_gain = run(
        kernel_close, step, extent,
        (sides_grad, x_one, mean_tri_out, scale_tri_out, gate_grad, x_grad, mask_plane,
         vectors, w_out_all, table, right),
        "srrrrrrwwtc",
        (("n", natural, LOW), ("p", (pieces, local_rows, OUTER, PAIR_DIM), WIDE),
         ("c", (OUTER, length), WIDE), ("w", after_shape, WIDE), ("w", gain_shape, WIDE)),
        [buffer(2 * TRI_DIM)], 8 * unit,
    )

    factor_grads, g_outer = one_call(
        outer_backward,
        (),
        (table_grad, right_part, left, w_outer),
        [((2, ranks, local_rows, LANES), LOW), ((OUTER * OUTER, PAIR_DIM), WIDE)],
        [pltpu.VMEM((OUTER * OUTER, PAIR_DIM), WIDE), pltpu.VMEM((OUTER, local_rows, PAIR_DIM), WIDE)],
    )
    factor_grads, out_last = lax.optimization_barrier((factor_grads, far(out_last)))
    pair_out = settled(pair_final, out_near, out_first, out_last)
    factor_grads = exchange(factor_grads.reshape(slab, local_rows, LANES), BOTH, layout.slabs)
    factor_grads, pair_one_grad = lax.optimization_barrier((factor_grads, pair_one_grad))

    workers = layout.work_place(crop_at * ranks + everyone)
    sources = jnp.concatenate([partner[None], workers]).astype(jnp.int32) % slab
    (
        key_value, query_low, score_low, after_grad, final_low, normed_two, hidden_grad, after_low,
        g_factors, g_two, g_three,
    ) = one_call(
        node_backward,
        (sources,),
        (factor_grads, node_cot, vectors, soft, heads, key, value, after, slope, node_final,
         w_attn_out, w_node_up, w_node_down, w_factors),
        [((length, 2 * HEADS_WIDTH), LOW), rows_low(HEADS_WIDTH), (by_heads, LOW),
         rows_wide(NODE_DIM), rows_low(NODE_DIM), rows_low(NODE_DIM), rows_low(FFN_NODE),
         rows_low(NODE_DIM), ((NODE_DIM, LANES), WIDE), ((1, NODE_DIM), WIDE), ((1, NODE_DIM), WIDE)],
    )
    score_low = score_low.reshape(HEADS, local_rows, length)
    g_bias_head = jnp.einsum("ijd,hij->dh", pair, score_low, preferred_element_type=WIDE)
    g_bias_head = lax.optimization_barrier(g_bias_head).reshape(-1, LANES)
    pair_one_away = lax.ppermute(pair_one_grad, BOTH, layout.moves)
    grads = [
        (at.w_bias, 1, g_bias_head),
        (at.gain_two, 1, g_two),
        (at.gain_three, 1, g_three),
        (at.w_outer, 1, g_outer),
        (at.gain_pair, 1, g_pair),
        (at.w_pair_up, 1, g_up),
        (at.w_pair_down, 1, g_down),
        (at.bias_pair, 1, g_bias),
    ]
    for tri, g_all, g_gain, g_tri, g_out in (
        (at.outgoing, g_out_all, g_out_gain, g_out_tri, g_out_out),
        (at.incoming, g_in_all, g_in_gain, g_in_tri, g_in_out),
    ):
        grads += [
            (tri.gain_in, 1, g_gain),
            (tri.w_left, 3, g_all),
            (tri.gain_tri, 1, g_tri),
            (tri.w_tri_out, 1, g_out),
        ]

    blocks, node_blocks = pack(
        layout, amount, jnp.concatenate([recycle, row_at.astype(jnp.int32)[None]]), grads,
        (key_value, query_low, start_all, normed_own, normed_all, after_grad, vectors,
         w_projections, act_low, final_low, normed_two, hidden_grad, attended, after_low, g_factors),
    )
    total = lambda got: low_of(jnp.sum(got.astype(WIDE), axis=0))
    blocks = total(exchange(blocks, BOTH, layout.cores))
    blocks, pair_out = lax.optimization_barrier((exchange(blocks, BOTH, layout.chips), pair_out))
    blocks = total(blocks)
    blocks = exchange(jnp.concatenate([blocks, node_blocks], axis=1), "row")
    pair_grad = jnp.where(stays, pair_one_grad, pair_one_away).astype(WIDE) + jnp.einsum(
        "hij,dh->ijd", score_low, w_bias[:, :HEADS], preferred_element_type=WIDE
    )
    blocks, pair_grad = lax.optimization_barrier((blocks, low_of(pair_grad)))
    blocks = jnp.sum(blocks.astype(WIDE), axis=0)
    node_parts = jnp.split(blocks[height:], NODE_DIM // LANES)
    node_grad = low_of(after_grad + jnp.concatenate(node_parts, axis=1))
    blocks = blocks[:height]
    grad_own = lax.dynamic_slice(blocks.reshape(-1), (offset,), (amount,))
    square_own = jnp.broadcast_to(jnp.sum(grad_own * grad_own), (1, LANES))
    last = jnp.concatenate([g_bias.reshape(1, LANES), square_own], axis=0)
    last = jnp.sum(spread(last, devices, BOTH).reshape(devices, 2, LANES), axis=0)
    bias_total = last[0]
    grad_norm = jnp.sqrt(last[1, 0])
    clipped = grad_own * (CLIP_NORM / jnp.maximum(grad_norm, CLIP_NORM))
    new_first = BETA_ONE * first + (1.0 - BETA_ONE) * clipped
    new_second = BETA_TWO * second + (1.0 - BETA_TWO) * clipped * clipped
    first_hat = new_first / (1.0 - BETA_ONE**ADAM_STEP)
    second_hat = new_second / (1.0 - BETA_TWO**ADAM_STEP)
    new_master = master - LEARN_RATE * (
        first_hat / (jnp.sqrt(second_hat) + ADAM_EPS) + WEIGHT_DECAY * master
    )
    return (
        node_out[None],
        pair_out[None],
        node_grad[None],
        pair_grad[None],
        grad_own,
        bias_total,
        grad_norm,
        new_master,
        new_first,
        new_second,
        low_of(new_master),
    )


def solution(mesh):
    layout = Layout(mesh.shape["crop"], mesh.shape["row"])
    return jax.shard_map(
        lambda *arrays: local(layout, *arrays),
        mesh=mesh,
        in_specs=(
            P("crop", "row", None),
            P("crop", "row", None, None),
            P("crop"),
            P("crop", None),
            P("crop", "row", None),
            P("crop", "row", None, None),
            P(("crop", "row")),
            P(("crop", "row")),
            P(("crop", "row")),
        ),
        out_specs=(
            P("crop", "row", None),
            P("crop", "row", None, None),
            P("crop", "row", None),
            P("crop", "row", None, None),
            P(("crop", "row")),
            P(),
            P(),
            P(("crop", "row")),
            P(("crop", "row")),
            P(("crop", "row")),
            P(("crop", "row")),
        ),
        check_vma=False,
    )
```

```python
import math
from functools import partial
from typing import Any, NamedTuple

import jax
import jax.numpy as jnp
import numpy as np
from jax import lax
from jax.experimental import pallas as pl
from jax.experimental.pallas import tpu as pltpu
from jax.sharding import PartitionSpec as P

NODE_DIM = 256
PAIR_DIM = 128
HEADS = 8
HEAD_DIM = 32
OUTER = 32
TRI_DIM = 128
FFN_NODE = 1024
FFN_PAIR = 512
RECYCLES = 4
ADAM_STEP = 3


EPS_NORM = 1e-05
ADAM_EPS = 1e-08
BETA_ONE = 0.9
BETA_TWO = 0.95
LEARN_RATE = 0.06
WEIGHT_DECAY = 0.1
CLIP_NORM = 1.0
MASK_FILL = 1000000000.0
HIGHEST = lax.Precision.HIGHEST


class Triangle(NamedTuple):
    gain_in: Any
    w_left: Any
    w_right: Any
    w_gate: Any
    gain_tri: Any
    w_tri_out: Any


class Params(NamedTuple):
    embed: Any
    gain_one: Any
    w_query: Any
    w_key: Any
    w_value: Any
    w_bias: Any
    w_attn_out: Any
    gain_two: Any
    w_node_up: Any
    w_node_down: Any
    gain_three: Any
    w_left_node: Any
    w_right_node: Any
    w_outer: Any
    outgoing: Triangle
    incoming: Triangle
    gain_pair: Any
    w_pair_up: Any
    w_pair_down: Any
    bias_pair: Any


LANES = 128
HEADS_WIDTH = HEADS * HEAD_DIM


def first_rows():
    square = PAIR_DIM * TRI_DIM
    triangle = Triangle(PAIR_DIM, square, square, PAIR_DIM * PAIR_DIM, TRI_DIM, square)
    sizes = Params(
        embed=RECYCLES * NODE_DIM,
        gain_one=NODE_DIM,
        w_query=NODE_DIM * HEADS_WIDTH,
        w_key=NODE_DIM * HEADS_WIDTH,
        w_value=NODE_DIM * HEADS_WIDTH,
        w_bias=PAIR_DIM * HEADS,
        w_attn_out=HEADS_WIDTH * NODE_DIM,
        gain_two=NODE_DIM,
        w_node_up=NODE_DIM * FFN_NODE,
        w_node_down=FFN_NODE * NODE_DIM,
        gain_three=NODE_DIM,
        w_left_node=NODE_DIM * OUTER,
        w_right_node=NODE_DIM * OUTER,
        w_outer=OUTER * OUTER * PAIR_DIM,
        outgoing=triangle,
        incoming=triangle,
        gain_pair=PAIR_DIM,
        w_pair_up=PAIR_DIM * FFN_PAIR,
        w_pair_down=FFN_PAIR * PAIR_DIM,
        bias_pair=PAIR_DIM,
    )
    leaves, tree = jax.tree.flatten(sizes)
    ends = np.cumsum(leaves) // LANES
    starts = [0] + [int(end) for end in ends[:-1]]
    return jax.tree.unflatten(tree, starts), int(ends[-1])


LOW = jnp.bfloat16
WIDE = jnp.float32
BOTH = ("crop", "row")
TILE = 16
VMEM_LIMIT = 56 * 2**20
SMALL_LIMIT = 28 * 2**20
INV_SQRT2 = 1.0 / math.sqrt(2.0)
INV_SQRT2PI = 1.0 / math.sqrt(2.0 * math.pi)


class Layout:
    def __init__(self, crops, rows):
        self.crops, self.rows = crops, rows
        self.devices = crops * rows
        self.wide = 2 ** (int(math.log2(rows)) // 2)
        self.high = rows // self.wide
        half = crops // 2
        self.moves = [
            (here, self.work_place(here))
            for here in range(self.devices)
            if here != self.work_place(here)
        ]
        high_of = lambda here: here % rows // self.wide
        self.near = [
            (here, there) for here, there in self.moves if abs(high_of(here) - high_of(there)) == 1
        ]
        self.far = [move for move in self.moves if move not in self.near]
        self.groups = [
            [self.work_place(c * rows + r) for r in range(rows)] for c in range(crops)
        ]
        self.cores = [
            [(2 * x + k) * rows + r for k in range(2)] for x in range(half) for r in range(rows)
        ]
        self.slabs = [[2 * x * rows + k for k in range(2 * rows)] for x in range(half)]
        self.chips = [
            [(2 * x + k) * rows + r for x in range(half)] for k in range(2) for r in range(rows)
        ]

    def work_place(self, here):
        crop, row = here // self.rows, here % self.rows
        high, wide = row // self.wide, row % self.wide
        core = crop % 2
        away = (high // (self.high // 2) + core) % 2
        crop = crop + away * (1 - 2 * core)
        high = high + away * (self.high - 1 - 2 * high)
        return crop * self.rows + high * self.wide + wide


def exchange(blocks, axes, groups=None):
    return lax.all_to_all(blocks, axes, 0, 0, axis_index_groups=groups, tiled=True)


def spread(part, count, axes, groups=None):
    return exchange(jnp.broadcast_to(part[None], (count,) + part.shape), axes, groups)


def dot_nn(a, b):
    return lax.dot_general(a, b, (((1,), (0,)), ((), ())), preferred_element_type=WIDE)


def dot_nt(a, b):
    return lax.dot_general(a, b, (((1,), (1,)), ((), ())), preferred_element_type=WIDE)


def dot_tn(a, b):
    return lax.dot_general(a, b, (((0,), (0,)), ((), ())), preferred_element_type=WIDE)


def norm_parts(x):
    hat, _, scale = norm_all(x)
    return hat, scale


def norm_all(x):
    mean = jnp.mean(x, axis=0, keepdims=True)
    centered = x - mean
    scale = lax.rsqrt(jnp.mean(centered * centered, axis=0, keepdims=True) + EPS_NORM)
    return centered * scale, mean, scale


def norm_back(grad, hat, scale, gain):
    grad_gain = jnp.sum(grad * hat, axis=1, keepdims=True)
    wide = grad * gain
    inner = jnp.mean(wide * hat, axis=0, keepdims=True)
    return scale * (wide - jnp.mean(wide, axis=0, keepdims=True) - hat * inner), grad_gain


def sigmoid(x):
    return 0.5 * jnp.tanh(0.5 * x) + 0.5


EMBED = slice(0, 8)
GAIN_ONE, GAIN_TWO, GAIN_THREE = slice(8, 10), slice(10, 12), slice(12, 14)
OUT_GAIN, OUT_TRI, IN_GAIN, IN_TRI = (slice(k, k + 1) for k in range(14, 18))
PAIR_GAIN, PAIR_BIAS = slice(18, 19), slice(19, 20)


def column(row):
    return jnp.broadcast_to(row, (LANES, row.shape[1])).T[:, :1]


def row_of(values):
    return jnp.broadcast_to(values, (values.shape[0], LANES)).T[:1]


def cat(ref):
    return jnp.concatenate([ref[t] for t in range(ref.shape[0])], axis=1)


def put(ref, value):
    count = ref.shape[0]
    width = value.shape[1] // count
    for t in range(count):
        ref[t] = value[:, t * width : (t + 1) * width].astype(ref.dtype)


def swapped(value):
    if value.shape[0] % TILE or value.shape[1] % TILE:
        return jnp.swapaxes(value.astype(WIDE), 0, 1).astype(LOW)
    return jnp.swapaxes(value, 0, 1)


def send_pair(scratch, out_ref):
    parts, share = out_ref.shape[0], out_ref.shape[1] // 2
    channels = parts * share
    for side in range(2):
        value = swapped(scratch[:, side * channels : (side + 1) * channels, :])
        out_ref[:, side * share : (side + 1) * share] = value.reshape(
            (parts, share) + value.shape[1:]
        )


def take_pair(in_ref, scratch):
    parts, share = in_ref.shape[0], in_ref.shape[1] // 2
    channels = parts * share
    for side in range(2):
        value = in_ref[:, side * share : (side + 1) * share]
        value = value.reshape((channels,) + value.shape[2:])
        scratch[:, side * channels : (side + 1) * channels, :] = swapped(value)


def front(x, gain, w_all, mask, x_out, mean_out, scale_out, gate_out, sides):
    hat, mean, scale = norm_all(x)
    all_three = dot_nn(w_all, (hat * gain).astype(LOW))
    channels = 2 * TRI_DIM
    put(sides, all_three[:channels] * mask)
    put(x_out, x)
    put(mean_out, mean)
    put(scale_out, scale)
    put(gate_out, sigmoid(all_three[channels:]))


def triangle_update(mixed, gain, w_out):
    hat, scale = norm_parts(mixed)
    normed = (hat * gain).astype(LOW)
    return hat, scale, normed, dot_nn(w_out, normed)


def post_back(grad, gate, hat, scale, normed, update, gain, w_out_back):
    update_grad = (grad * gate).astype(LOW)
    gate_grad = (grad * update * (gate * (1.0 - gate))).astype(LOW)
    grad_out = dot_nt(normed, update_grad)
    mixed_grad, grad_gain = norm_back(dot_nn(w_out_back, update_grad), hat, scale, gain)
    return mixed_grad, gate_grad, grad_out, grad_gain


def front_back(grad, x, mean, scale, sides_grad, gate_grad, mask, gain, w_all_back):
    hat = (x - mean) * scale
    normed = (hat * gain).astype(LOW)
    sides = jnp.concatenate([sides_grad * mask.astype(LOW), gate_grad], axis=0)
    grad_w = dot_nt(normed, sides)
    x_grad, grad_gain = norm_back(dot_nn(w_all_back, sides), hat, scale, gain)
    return grad + x_grad, grad_w, grad_gain


def gelu_parts(x):
    cumulative = 0.5 * lax.erf(x * INV_SQRT2) + 0.5
    density = INV_SQRT2PI * jnp.exp(-0.5 * x * x)
    return x * cumulative, cumulative + x * density


FEW = 4


def few_rows(piece, *refs):
    rows = refs[0].shape[0]
    few = min(FEW, rows)

    def step(t, carry):
        piece(*(ref.at[pl.ds(t * few, few)] for ref in refs))
        return carry

    lax.fori_loop(0, rows // few, step, 0)


def zero_first(*refs):
    @pl.when((pl.program_id(0) == 0) & (pl.program_id(1) == 0))
    def _():
        for ref in refs:
            ref[...] = jnp.zeros_like(ref)


def run(body, step, extent, in_arrays, in_kinds, outs, scratch, flops, skip=0, aliases={}):
    def spec(kind, shape):
        lead = (0,) * len(shape)
        if kind == "m":
            return pl.BlockSpec(memory_space=pltpu.SMEM)
        if kind == "x":
            return pl.BlockSpec(memory_space=pl.ANY)
        block, at = {
            "R": (step[:1] + shape[1:-1] + step[1:], lambda c, r: (r + skip,) + lead[2:] + (c,)),
            "N": (step + shape[2:], lambda c, r: (r + skip, c) + lead[2:]),
            "r": (step[:1] + shape[1:-1] + step[1:], lambda c, r: (r,) + lead[2:] + (c,)),
            "n": (step + shape[2:], lambda c, r: (r, c) + lead[2:]),
            "s": (shape[:-2] + step, lambda c, r: lead[2:] + (r, c)),
            "c": (shape[:-1] + step[1:], lambda c, r: lead[1:] + (c,)),
            "t": (step[:1] + shape[1:], lambda c, r: (r,) + lead[1:]),
            "p": ((1,) + step[:1] + shape[2:], lambda c, r: (c, r) + lead[2:]),
            "q": (step[1:] + shape[1:], lambda c, r: (c,) + lead[1:]),
            "w": (shape, lambda c, r: lead),
        }[kind]
        return pl.BlockSpec(block, at)

    moved = sum(a.size * a.dtype.itemsize for a in in_arrays)
    return pl.pallas_call(
        body,
        grid=(extent[1] // step[1], extent[0] // step[0]),
        in_specs=[spec(kind, a.shape) for kind, a in zip(in_kinds, in_arrays)],
        out_specs=[spec(kind, shape) for kind, shape, _ in outs],
        out_shape=[jax.ShapeDtypeStruct(shape, dtype) for _, shape, dtype in outs],
        scratch_shapes=scratch,
        input_output_aliases=aliases,
        compiler_params=pltpu.CompilerParams(vmem_limit_bytes=VMEM_LIMIT),
        cost_estimate=pl.CostEstimate(flops=flops, bytes_accessed=moved, transcendentals=0),
    )(*in_arrays)


def all_low(w):
    return jnp.concatenate([w[k * PAIR_DIM : (k + 1) * PAIR_DIM].T for k in range(3)], axis=0)


def all_back(w):
    return jnp.concatenate([w[k * PAIR_DIM : (k + 1) * PAIR_DIM] for k in range(3)], axis=1)


def kernel_open(
    stays, pair, pair_home, table, right, mask, vectors, w_all, x_out, mean_out, scale_out, gate_out, sides_out, sides
):
    right_low = right[...]
    at_home = stays[0] == 1
    x = jnp.concatenate(
        [
            jnp.where(at_home, pair_home[t], pair[t]).T.astype(WIDE) + dot_tn(table[t], right_low)
            for t in range(pair.shape[0])
        ],
        axis=1,
    )
    front(
        x, column(vectors[OUT_GAIN]), all_low(w_all), cat(mask), x_out, mean_out, scale_out, gate_out,
        sides,
    )
    send_pair(sides, sides_out)


def kernel_middle(
    mixed, x_in, gate_in, mask, vectors, w_out, w_all,
    x_out, mean_out, scale_out, gate_out, sides_out, arrived, sides,
):
    arrived[...] = swapped(mixed[...])
    *_, update = triangle_update(cat(arrived).astype(WIDE), column(vectors[OUT_TRI]), w_out[...].T)
    x = cat(x_in).astype(WIDE) + cat(gate_in).astype(WIDE) * update
    front(
        x, column(vectors[IN_GAIN]), all_low(w_all), cat(mask),
        x_out, mean_out, scale_out, gate_out, sides,
    )
    send_pair(sides, sides_out)


def kernel_turn(sums, mixed, x_in, gate_in, cot, vectors, w_out, w_up, w_down, *rest):
    if sums:
        g_out, g_tri, g_up, g_down, g_pair, g_bias, arrived = rest
        zero_first(g_out, g_tri, g_up, g_down, g_pair, g_bias)
    else:
        pair_out, x_grad, gate_grad, mixed_grad, arrived, leaving = rest[-6:]
    arrived[...] = swapped(mixed[...])
    up_low, up_back = w_up[...].T, w_up[...]
    down_low, down_back = w_down[...].T, w_down[...]
    tri_col, pair_col = column(vectors[IN_TRI]), column(vectors[PAIR_GAIN])
    chunk = PAIR_DIM

    def piece(x_in, gate_in, cot, arrived):
        rows = x_in.shape[0]
        gate = cat(gate_in).astype(WIDE)
        mix_parts = triangle_update(cat(arrived).astype(WIDE), tri_col, w_out[...].T)
        x = cat(x_in).astype(WIDE) + gate * mix_parts[-1]
        hat, scale = norm_parts(x)
        normed = (hat * pair_col).astype(LOW)
        cot_low = jnp.concatenate([cot[t].T for t in range(rows)], axis=1)
        total = x + column(vectors[PAIR_BIAS])
        normed_grad = jnp.zeros_like(x)
        for c in range(FFN_PAIR // chunk):
            part = slice(c * chunk, (c + 1) * chunk)
            act, slope = gelu_parts(dot_nn(up_low[part], normed))
            act_low = act.astype(LOW)
            hidden_grad = (dot_nn(down_back[part], cot_low) * slope).astype(LOW)
            normed_grad = normed_grad + dot_nn(up_back[:, part], hidden_grad)
            if sums:
                g_up[:, part] += dot_nt(normed, hidden_grad)
                g_down[part] += dot_nt(act_low, cot_low)
            else:
                total = total + dot_nn(down_low[:, part], act_low)
        cot_wide = cot_low.astype(WIDE)
        back, grad_pair = norm_back(normed_grad, hat, scale, pair_col)
        grad = cot_wide + back
        mix_grad, gates, grad_out, grad_tri = post_back(grad, gate, *mix_parts, tri_col, w_out[...])
        if sums:
            g_bias[...] += jnp.sum(cot_wide, axis=1, keepdims=True)
            g_pair[...] += grad_pair
            g_out[...] += grad_out
            g_tri[...] += grad_tri
            return
        total_low = total.astype(LOW)
        width = total.shape[1] // rows
        for t in range(rows):
            pair_out[t] = total_low[:, t * width : (t + 1) * width].T
        put(x_grad, grad)
        put(leaving, mix_grad)
        put(gate_grad, gates)

    if sums:
        few_rows(piece, x_in, gate_in, cot, arrived)
    else:
        piece(x_in, gate_in, cot, arrived)
        mixed_grad[...] = swapped(leaving[...])


def kernel_return(
    sums, sides_grad, x_after, mean_after, scale_after, gate_after, grad_in, mask, vectors, w_after,
    mixed, gate_in, w_out, *rest,
):
    if sums:
        g_after, g_gain, g_out, g_tri, sides, arrived = rest
        zero_first(g_after, g_gain, g_out, g_tri)
    else:
        x_grad, gate_grad, mixed_grad, sides, arrived, leaving = rest
    take_pair(sides_grad, sides)
    arrived[...] = swapped(mixed[...])
    tri_col = column(vectors[OUT_TRI])
    after_col, after_back = column(vectors[IN_GAIN]), all_back(w_after)

    def piece(
        grad_in, x_after, mean_after, scale_after, sides, gate_after, mask, arrived, gate_in
    ):
        grad, grad_w, grad_gain = front_back(
            cat(grad_in).astype(WIDE), cat(x_after).astype(WIDE), cat(mean_after), cat(scale_after),
            cat(sides), cat(gate_after),
            cat(mask), after_col, after_back,
        )
        mix_parts = triangle_update(cat(arrived).astype(WIDE), tri_col, w_out[...].T)
        mix_grad, gates, grad_out, grad_tri = post_back(
            grad, cat(gate_in).astype(WIDE), *mix_parts, tri_col, w_out[...]
        )
        if sums:
            g_after[...] += grad_w
            g_gain[...] += grad_gain
            g_out[...] += grad_out
            g_tri[...] += grad_tri
            return
        put(x_grad, grad)
        put(leaving, mix_grad)
        put(gate_grad, gates)

    parts = (grad_in, x_after, mean_after, scale_after, sides, gate_after, mask, arrived, gate_in)
    if sums:
        few_rows(piece, *parts)
    else:
        piece(*parts)
        mixed_grad[...] = swapped(leaving[...])


def kernel_close(
    sides_grad, x_after, mean_after, scale_after, gate_after, grad_in, mask, vectors, w_after,
    table, right,
    pair_grad, table_grad, right_grad, g_after, g_gain, sides,
):
    take_pair(sides_grad, sides)
    zero_first(g_after, g_gain)

    @pl.when(pl.program_id(1) == 0)
    def _():
        right_grad[...] = jnp.zeros_like(right_grad)

    grad, grad_w, grad_gain = front_back(
        cat(grad_in).astype(WIDE), cat(x_after).astype(WIDE), cat(mean_after), cat(scale_after),
        cat(sides), cat(gate_after),
        cat(mask), column(vectors[OUT_GAIN]), all_back(w_after),
    )
    g_after[...] += grad_w
    g_gain[...] += grad_gain
    low = grad.astype(LOW)
    rows = table.shape[0]
    width = low.shape[1] // rows
    for t in range(rows):
        own = low[:, t * width : (t + 1) * width]
        pair_grad[t] = own.T
        table_grad[0, t] = dot_nt(right[...], own)
        right_grad[...] += dot_nn(table[t], own)


CHANNELS = 8


def kernel_mix(incoming, left, right, *outs):
    parts, count, rows, length = left.shape
    part = rows // len(outs)
    for c in range(count):
        a = left[:, c].reshape(length, length)
        b = right[:, c].reshape(length, length)
        mixed = dot_tn(a, b) if incoming else dot_nt(a, b)
        mixed = mixed.astype(LOW).reshape(parts, rows, length)
        for k, out in enumerate(outs):
            out[:, c] = mixed[:, k * part : (k + 1) * part]


def kernel_mix_back(incoming, *refs):
    *grads, left, right, out = refs
    parts, count, rows, length = left.shape
    for c in range(count):
        g = jnp.concatenate([grad[:, c] for grad in grads], axis=1).reshape(length, length)
        a = left[:, c].reshape(length, length)
        b = right[:, c].reshape(length, length)
        a_grad = dot_nt(b, g) if incoming else dot_nn(g, b)
        b_grad = dot_nn(a, g) if incoming else dot_tn(g, a)
        out[:, 0, c] = a_grad.astype(LOW).reshape(parts, rows, length)
        out[:, 1, c] = b_grad.astype(LOW).reshape(parts, rows, length)


def mix(sides, incoming, pieces=1):
    parts, double, rows, length = sides.shape
    share = double // 2
    count = min(CHANNELS, share)
    steps = share // count
    block = (parts, count, rows, length)
    part = (parts, count, rows // pieces, length)
    return pl.pallas_call(
        lambda *refs: kernel_mix(incoming, *refs),
        grid=(steps,),
        in_specs=[
            pl.BlockSpec(block, lambda c: (0, c, 0, 0)),
            pl.BlockSpec(block, lambda c: (0, c + steps, 0, 0)),
        ],
        out_specs=[pl.BlockSpec(part, lambda c: (0, c, 0, 0))] * pieces,
        out_shape=[jax.ShapeDtypeStruct((parts, share) + part[2:], LOW)] * pieces,
        compiler_params=pltpu.CompilerParams(vmem_limit_bytes=VMEM_LIMIT),
        cost_estimate=pl.CostEstimate(
            flops=2 * share * length**3, bytes_accessed=3 * share * length * length * 2,
            transcendentals=0,
        ),
    )(sides, sides)


def mix_back(grads, sides, incoming):
    parts, double, rows, length = sides.shape
    share = double // 2
    count = min(CHANNELS, share)
    steps = share // count
    block = (parts, count, rows, length)
    part = (parts, count, rows // len(grads), length)
    out = pl.pallas_call(
        lambda *refs: kernel_mix_back(incoming, *refs),
        grid=(steps,),
        in_specs=[pl.BlockSpec(part, lambda c: (0, c, 0, 0))] * len(grads)
        + [
            pl.BlockSpec(block, lambda c: (0, c, 0, 0)),
            pl.BlockSpec(block, lambda c: (0, c + steps, 0, 0)),
        ],
        out_specs=pl.BlockSpec((parts, 2, count, rows, length), lambda c: (0, 0, c, 0, 0)),
        out_shape=jax.ShapeDtypeStruct((parts, 2, share, rows, length), LOW),
        compiler_params=pltpu.CompilerParams(vmem_limit_bytes=VMEM_LIMIT),
        cost_estimate=pl.CostEstimate(
            flops=4 * share * length**3, bytes_accessed=5 * share * length * length * 2,
            transcendentals=0,
        ),
    )(*grads, sides, sides)
    return out.reshape(sides.shape)


def share_rows(share):
    return -(-(share + 2 * LANES) // (TILE * LANES)) * TILE


def whole(shape):
    return pl.BlockSpec(shape, lambda *_: (0,) * len(shape))


def one_call(body, scalars, in_arrays, outs, scratch=(), limit=VMEM_LIMIT):
    return pl.pallas_call(
        body,
        in_specs=[pl.BlockSpec(memory_space=pltpu.SMEM)] * len(scalars)
        + [whole(a.shape) for a in in_arrays],
        out_specs=[whole(shape) for shape, _ in outs],
        out_shape=[jax.ShapeDtypeStruct(shape, dtype) for shape, dtype in outs],
        scratch_shapes=list(scratch),
        grid=(1,),
        compiler_params=pltpu.CompilerParams(vmem_limit_bytes=limit),
    )(*scalars, *in_arrays)


def lane_in(shape, start, width):
    lane = lax.broadcasted_iota(jnp.int32, shape, 1)
    return (lane >= start) & (lane < start + width)


def rolled(value, shift):
    shift %= LANES
    return pltpu.roll(value, shift, 1) if shift else value


def share_order(layout):
    return [((d // layout.rows) % 2, d // (2 * layout.rows), d % layout.rows) for d in range(layout.devices)]


def unpack(layout, shares, share):
    at, _ = first_rows()
    height = shares.shape[3]
    first = [share * d // LANES for d in range(layout.devices)]
    order = share_order(layout)
    matrices = [
        (at.w_query, NODE_DIM, 3, 3 * HEADS_WIDTH),
        (at.w_attn_out, HEADS_WIDTH, 1, NODE_DIM),
        (at.w_node_up, NODE_DIM, 1, FFN_NODE),
        (at.w_node_down, FFN_NODE, 1, NODE_DIM),
        (at.w_outer, OUTER * OUTER, 1, PAIR_DIM),
        (at.outgoing.w_left, 3 * PAIR_DIM, 1, TRI_DIM),
        (at.outgoing.w_tri_out, TRI_DIM, 1, PAIR_DIM),
        (at.incoming.w_left, 3 * PAIR_DIM, 1, TRI_DIM),
        (at.incoming.w_tri_out, TRI_DIM, 1, PAIR_DIM),
        (at.w_pair_up, PAIR_DIM, 1, FFN_PAIR),
        (at.w_pair_down, FFN_PAIR, 1, PAIR_DIM),
    ]
    small = [(at.embed, 8), (at.gain_one, 2), (at.gain_two, 2), (at.gain_three, 2)]
    small += [
        (start, 1)
        for start in (
            at.outgoing.gain_in, at.outgoing.gain_tri, at.incoming.gain_in, at.incoming.gain_tri,
            at.gain_pair, at.bias_pair,
        )
    ]

    def body(shares_ref, vectors, bias_out, factors_out, *rest):
        outs, flat, narrow = rest[:-2], rest[-2], rest[-1]
        for d, place in enumerate(order):
            block = shares_ref[place].astype(WIDE)
            if d:
                tail = flat[first[d] : first[d] + 1]
                flat[first[d] : first[d] + height] = block
                flat[first[d] : first[d] + 1] = block[:1] + tail
            else:
                flat[:height] = block
        row = 0
        vectors[...] = jnp.zeros_like(vectors)
        for start, count in small:
            vectors[row : row + count] = flat[start : start + count]
            row += count
        for out, (place, rows, count, width) in zip(outs, matrices):
            pieces = width // count // LANES
            for m in range(count):
                for a in range(pieces):
                    start = place + m * rows * pieces + a
                    value = (
                        flat[pl.ds(start, rows, stride=pieces), :]
                        if pieces > 1
                        else flat[start : start + rows]
                    )
                    lane = (m * pieces + a) * LANES
                    out[:, lane : lane + LANES] = value.astype(LOW)
        per_row = LANES // HEADS
        shape = (HEADS, LANES)
        value = flat[at.w_bias : at.w_bias + HEADS]
        for a in range(per_row):
            kept = jnp.where(lane_in(shape, 0, HEADS), rolled(value, -HEADS * a), 0.0)
            narrow[pl.ds(a, HEADS, stride=per_row), :] = kept
        bias_out[...] = narrow[:PAIR_DIM].astype(LOW)
        per_row = LANES // OUTER
        count = NODE_DIM // per_row
        shape = (count, LANES)
        left, right = (flat[start : start + count] for start in (at.w_left_node, at.w_right_node))
        for a in range(per_row):
            kept = jnp.where(lane_in(shape, 0, OUTER), rolled(left, -OUTER * a), 0.0)
            kept += jnp.where(lane_in(shape, OUTER, OUTER), rolled(right, OUTER - OUTER * a), 0.0)
            narrow[pl.ds(a, count, stride=per_row), :] = kept
        factors_out[...] = narrow[...].astype(LOW)

    return one_call(
        body,
        (),
        (shares,),
        [((24, LANES), WIDE), ((PAIR_DIM, LANES), LOW), ((NODE_DIM, LANES), LOW)]
        + [((rows, width), LOW) for _, rows, _, width in matrices],
        [pltpu.VMEM((first[-1] + height + TILE, LANES), WIDE), pltpu.VMEM((NODE_DIM, LANES), WIDE)],
    )


def pack(layout, share, scalars, grads, node_parts):
    at, total = first_rows()
    height = share_rows(share)
    first = [share * d // LANES for d in range(layout.devices)]
    order = share_order(layout)
    many = len(grads)

    def body(scalar_ref, *refs):
        ins, rest = refs[:many], refs[many:]
        (
            key_value, query_low, start, normed_own, normed_all, after_grad, vectors, w_projections,
            act_low, final_low, normed_two, hidden_grad, attended, after_low, g_factors,
            out, node_parts_out, flat, narrow, steps,
        ) = rest

        def store(place, count, value):
            rows, pieces = value.shape[0], value.shape[1] // count // LANES
            for m in range(count):
                for a in range(pieces):
                    lane = (m * pieces + a) * LANES
                    begin = place + m * rows * pieces + a
                    part = value[:, lane : lane + LANES]
                    if pieces > 1 and rows > 1:
                        flat[pl.ds(begin, rows, stride=pieces), :] = part
                    else:
                        flat[begin : begin + rows] = part

        flat[total:] = jnp.zeros((flat.shape[0] - total, LANES), WIDE)
        for ref, (place, count, _) in zip(ins, grads):
            store(place, count, row_of(ref[...]) if ref.shape[1] == 1 else ref[...])
        store(at.w_node_down, 1, dot_tn(act_low[...], final_low[...]))
        store(at.w_node_up, 1, dot_tn(normed_two[...], hidden_grad[...]))
        store(at.w_attn_out, 1, dot_tn(attended[...], after_low[...]))
        per_row = LANES // OUTER
        count = NODE_DIM // per_row
        narrow[...] = g_factors[...]
        left = jnp.zeros((count, LANES), WIDE)
        right = left
        for a in range(per_row):
            piece = narrow[pl.ds(a, count, stride=per_row), :]
            inside = lane_in(piece.shape, OUTER * a, OUTER)
            left = jnp.where(inside, rolled(piece, OUTER * a), left)
            right = jnp.where(inside, rolled(piece, OUTER * a - OUTER), right)
        store(at.w_left_node, 1, left)
        store(at.w_right_node, 1, right)

        store(at.w_query, 1, dot_tn(normed_own[...], query_low[...]))
        store(at.w_key, 2, dot_tn(normed_all[...], key_value[...]))
        steps[...] = dot_nt(key_value[...], w_projections[:, HEADS_WIDTH:])
        local_rows = query_low.shape[0]
        own = pl.ds(pl.multiple_of(scalar_ref[1] * local_rows, local_rows), local_rows)
        steps[own, :] += dot_nt(query_low[...], w_projections[:, :HEADS_WIDTH])
        hat, scale = row_norm(start[...])
        part, grad_gain = row_norm_back(steps[...], hat, scale, vector(vectors, GAIN_ONE))
        for r in range(node_parts_out.shape[0]):
            for a in range(NODE_DIM // LANES):
                piece = part[r * local_rows : (r + 1) * local_rows, a * LANES : (a + 1) * LANES]
                node_parts_out[r, a * local_rows : (a + 1) * local_rows] = piece.astype(LOW)
        store(at.gain_one, 1, grad_gain)
        flat[at.embed : at.embed + 2 * RECYCLES] = jnp.zeros((2 * RECYCLES, LANES), WIDE)
        column_sum = jnp.sum(after_grad[...], axis=0, keepdims=True)
        column_sum += jnp.sum(part, axis=0, keepdims=True)
        for a in range(NODE_DIM // LANES):
            place = at.embed + (NODE_DIM // LANES) * scalar_ref[0] + a
            flat[pl.ds(place, 1), :] = column_sum[:, a * LANES : (a + 1) * LANES]
        for d, where in enumerate(order):
            out[where] = flat[first[d] : first[d] + height].astype(LOW)

    shape = (2, layout.crops // 2, layout.rows, height, LANES)
    return one_call(
        body,
        (scalars,),
        tuple(array for _, _, array in grads) + tuple(node_parts),
        [(shape, LOW), ((layout.rows, node_parts[1].shape[0] * NODE_DIM // LANES, LANES), LOW)],
        [
            pltpu.VMEM((first[-1] + height + TILE, LANES), WIDE),
            pltpu.VMEM((NODE_DIM, LANES), WIDE),
            pltpu.VMEM(node_parts[2].shape, WIDE),
        ],
        SMALL_LIMIT,
    )


def row_norm(x):
    centered = x - jnp.mean(x, axis=-1, keepdims=True)
    scale = lax.rsqrt(jnp.mean(centered * centered, axis=-1, keepdims=True) + EPS_NORM)
    return centered * scale, scale


def row_norm_back(grad, hat, scale, gain):
    grad_gain = jnp.sum(grad * hat, axis=0, keepdims=True)
    wide = grad * gain
    inner = jnp.mean(wide * hat, axis=-1, keepdims=True)
    return scale * (wide - jnp.mean(wide, axis=-1, keepdims=True) - hat * inner), grad_gain


def vector(ref, rows):
    return jnp.concatenate([ref[r : r + 1] for r in range(rows.start, rows.stop)], axis=1)


def by_head(value):
    return jnp.concatenate(
        [
            jnp.where(lane_in(value.shape, h * HEAD_DIM, HEAD_DIM), value, 0.0)
            for h in range(HEADS)
        ],
        axis=0,
    )


def head_sum(value):
    rows = value.shape[0] // HEADS
    parts = [value[h * rows : (h + 1) * rows] for h in range(HEADS)]
    return sum(
        jnp.where(lane_in(part.shape, h * HEAD_DIM, HEAD_DIM), part, 0.0)
        for h, part in enumerate(parts)
    )


SCORE_SCALE = HEAD_DIM ** (-0.5)
KEEP_LANE = 2 * OUTER


def node_forward(
    recycle, node_ref, all_ref, bias_ref, keep, keep_rows, vectors, w_projections, w_attn_out, w_up, w_down,
    w_factors,
    node_out, factors_out, start_out, normed_own, normed_out, soft_out, heads_out, key_out, value_out,
    attended_out, after_out, act_out, slope_out, final_out, flat,
):
    pieces = NODE_DIM // LANES
    length = all_ref.shape[0] // pieces
    embed = jnp.concatenate(
        [vectors[pl.ds(pieces * recycle[0] + a, 1), :] for a in range(pieces)], axis=1
    )
    flat[...] = all_ref[...].astype(WIDE)
    all_rows = jnp.concatenate(
        [flat[pl.ds(a, length, stride=pieces), :] for a in range(pieces)], axis=1
    )
    gain = vector(vectors, GAIN_ONE)
    start_all = all_rows + embed
    normed_all = (row_norm(start_all)[0] * gain).astype(LOW)
    start_out[...] = start_all
    normed_out[...] = normed_all
    start = node_ref[...].astype(WIDE) + embed
    normed = (row_norm(start)[0] * gain).astype(LOW)
    normed_own[...] = normed
    query = dot_nn(normed, w_projections[:, :HEADS_WIDTH]).astype(LOW).astype(WIDE)
    heads = by_head(query).astype(LOW)
    key_value = dot_nn(normed_all, w_projections[:, HEADS_WIDTH:]).astype(LOW)
    key, value = key_value[:, :HEADS_WIDTH], key_value[:, HEADS_WIDTH:]
    heads_out[...] = heads
    key_out[...] = key
    value_out[...] = value
    scores = dot_nt(heads, key) * SCORE_SCALE + bias_ref[...] + (keep[...] - 1.0) * MASK_FILL
    powers = jnp.exp(scores - jnp.max(scores, axis=-1, keepdims=True))
    soft = powers / jnp.sum(powers, axis=-1, keepdims=True)
    soft_out[...] = soft
    attended = head_sum(dot_nn(soft.astype(LOW), value)).astype(LOW)
    attended_out[...] = attended
    after = start + dot_nn(attended, w_attn_out[...])
    after_out[...] = after
    normed = (row_norm(after)[0] * vector(vectors, GAIN_TWO)).astype(LOW)
    act, slope = gelu_parts(dot_nn(normed, w_up[...]))
    act_out[...] = act.astype(LOW)
    slope_out[...] = slope
    final = after + dot_nn(act.astype(LOW), w_down[...])
    final_out[...] = final
    node_out[...] = final.astype(LOW)
    normed = (row_norm(final)[0] * vector(vectors, GAIN_THREE)).astype(LOW)
    factors = dot_nn(normed, w_factors[...])
    factors = jnp.where(lane_in(factors.shape, KEEP_LANE, 1), keep_rows[...], factors).astype(LOW)
    factors_out[...] = jnp.broadcast_to(factors[None], factors_out.shape)


def node_backward(
    sources, factor_ref, cot, vectors, soft_ref, heads, key, value, after_ref, slope, final_ref,
    w_attn_out, w_up, w_down, w_factors,
    key_value_out, query_out, score_out, after_grad_out, final_low_out, normed_two_out,
    hidden_out, after_low_out, g_factors, g_two, g_three,
):
    ranks = key_value_out.shape[0] // cot.shape[0]
    left = factor_ref[sources[0]].astype(WIDE)
    right = sum(factor_ref[sources[1 + r]].astype(WIDE) for r in range(ranks))
    rows = jnp.where(lane_in(left.shape, 0, OUTER), left, right).astype(LOW)
    hat, scale = row_norm(final_ref[...])
    gain = vector(vectors, GAIN_THREE)
    g_factors[...] = dot_tn((hat * gain).astype(LOW), rows)
    part, g_three[...] = row_norm_back(dot_nt(rows, w_factors[...]), hat, scale, gain)
    final_grad = cot[...].astype(WIDE) + part
    final_low = final_grad.astype(LOW)
    final_low_out[...] = final_low
    hidden_grad = (dot_nt(final_low, w_down[...]) * slope[...]).astype(LOW)
    hidden_out[...] = hidden_grad
    hat, scale = row_norm(after_ref[...])
    gain = vector(vectors, GAIN_TWO)
    normed_two_out[...] = (hat * gain).astype(LOW)
    part, g_two[...] = row_norm_back(dot_nt(hidden_grad, w_up[...]), hat, scale, gain)
    after_grad = final_grad + part
    after_grad_out[...] = after_grad
    after_low = after_grad.astype(LOW)
    after_low_out[...] = after_low
    attended_grad = dot_nt(after_low, w_attn_out[...]).astype(LOW).astype(WIDE)
    grad_heads = by_head(attended_grad).astype(LOW)
    soft = soft_ref[...]
    soft_grad = dot_nt(grad_heads, value[...])
    score_grad = soft * (soft_grad - jnp.sum(soft_grad * soft, axis=-1, keepdims=True))
    score_low = score_grad.astype(LOW)
    score_out[...] = score_low
    key_part = dot_tn(score_low, heads[...]) * SCORE_SCALE
    key_value_out[:, :HEADS_WIDTH] = key_part.astype(LOW)
    key_value_out[:, HEADS_WIDTH:] = dot_tn(soft.astype(LOW), grad_heads).astype(LOW)
    query_out[...] = (head_sum(dot_nn(score_low, key[...])) * SCORE_SCALE).astype(LOW)


def outer_tables(
    sources, factors, w_outer, table_out, right_out, left_out, mask_out, w_wide, steps
):
    local_rows = left_out.shape[0]
    ranks = right_out.shape[1] // local_rows
    left_low = factors[sources[0]][:, :OUTER]
    left_out[...] = left_low
    right = jnp.concatenate([factors[sources[1 + r]].astype(WIDE) for r in range(ranks)], axis=0)
    turned = right.T
    right_out[...] = turned[OUTER : 2 * OUTER].astype(LOW)
    own_keep = factors[sources[0]][:, KEEP_LANE : KEEP_LANE + 1].astype(WIDE)
    mask_out[:, 0, :] = own_keep * turned[KEEP_LANE : KEEP_LANE + 1]
    w_wide[...] = w_outer[...].astype(WIDE)
    for q in range(OUTER):
        w_q = w_wide[pl.ds(q, OUTER, stride=OUTER), :].astype(LOW)
        steps[q] = dot_nn(left_low, w_q)
    table_out[...] = jnp.swapaxes(steps[...], 0, 1).astype(LOW)


def outer_backward(table_grad, right_grad, left, w_outer, factors_out, g_outer, w_wide, steps):
    crops, ranks, local_rows, _ = factors_out.shape
    steps[...] = jnp.swapaxes(jnp.sum(table_grad[...], axis=0), 0, 1)
    w_wide[...] = w_outer[...].astype(WIDE)
    left_grad = jnp.zeros((local_rows, OUTER), WIDE)
    for q in range(OUTER):
        grad_q = steps[q].astype(LOW)
        w_q = w_wide[pl.ds(q, OUTER, stride=OUTER), :].astype(LOW)
        left_grad = left_grad + dot_nt(grad_q, w_q)
        g_outer[pl.ds(q, OUTER, stride=OUTER), :] = dot_tn(left[...], grad_q)
    right_rows = right_grad[...].T
    for r in range(ranks):
        block = jnp.concatenate(
            [
                left_grad,
                right_rows[r * local_rows : (r + 1) * local_rows],
                jnp.zeros((local_rows, LANES - 2 * OUTER), WIDE),
            ],
            axis=1,
        ).astype(LOW)
        for c in range(crops):
            factors_out[c, r] = block


def low_of(x):
    return x.astype(LOW)


def local(layout, node, pair, recycle, mask, node_cot, pair_cot, master, first, second):
    crops, ranks = layout.crops, layout.rows
    devices = crops * ranks
    local_rows, length = node.shape[1], pair.shape[2]
    share = TRI_DIM // ranks
    node, pair, node_cot, pair_cot = node[0], pair[0], node_cot[0], pair_cot[0]

    crop_at, row_at = lax.axis_index("crop"), lax.axis_index("row")
    here = crop_at * ranks + row_at
    partner = layout.work_place(here)
    stays = partner == here
    work_crop, work_row = partner // ranks, partner % ranks
    near = lambda array: lax.ppermute(array, BOTH, layout.near)
    far = lambda array: lax.ppermute(array, BOTH, layout.far)
    settled = lambda own, close, *pieces: jnp.where(stays, own, close + jnp.concatenate(pieces))

    at, _ = first_rows()

    amount = master.shape[0]
    height = share_rows(amount)
    offset = (here * (amount % LANES)) % LANES
    shard = lax.dynamic_update_slice(jnp.zeros(height * LANES, LOW), low_of(master), (offset,))
    node_rows = local_rows * NODE_DIM // LANES
    shards = jnp.concatenate([shard.reshape(height, LANES), node.reshape(-1, LANES)], axis=0)
    shards = spread(shards, ranks, "row").reshape(ranks, -1, LANES)
    shards, pair = lax.optimization_barrier((shards, pair))
    node_all = shards[:, height:].reshape(-1, LANES)
    shards = shards[:, :height].reshape(-1, LANES)
    shards = spread(shards, crops // 2, BOTH, layout.chips)
    shards = spread(shards, 2, BOTH, layout.cores)
    shards = shards.reshape(2, crops // 2, ranks, height, LANES)
    (
        vectors, w_bias, w_factors, w_projections, w_attn_out, w_node_up, w_node_down, w_outer,
        w_out_all, w_out_end, w_in_all, w_in_end, w_pair_up, w_pair_down,
    ) = unpack(layout, shards, amount)
    pair_plane = lax.ppermute(pair, BOTH, layout.moves)
    keep = mask.astype(WIDE)
    keep_rows = lax.dynamic_slice_in_dim(keep[0], row_at * local_rows, local_rows, 0)[:, None]

    pair_bias = jnp.einsum("ijd,dh->hij", pair, w_bias[:, :HEADS], preferred_element_type=WIDE)
    rows_low = lambda width: ((local_rows, width), LOW)
    rows_wide = lambda width: ((local_rows, width), WIDE)
    by_heads = (HEADS * local_rows, length)
    (
        node_out, factors, start_all, normed_own, normed_all, soft, heads, key, value, attended, after, act_low,
        slope, node_final,
    ) = one_call(
        node_forward,
        (recycle,),
        (node, node_all, pair_bias.reshape(by_heads), keep, keep_rows, vectors, w_projections, w_attn_out,
         w_node_up, w_node_down, w_factors),
        [rows_low(NODE_DIM), ((2 * ranks, local_rows, LANES), LOW), ((length, NODE_DIM), WIDE),
         rows_low(NODE_DIM), ((length, NODE_DIM), LOW), (by_heads, WIDE), (by_heads[:1] + (HEADS_WIDTH,), LOW),
         ((length, HEADS_WIDTH), LOW), ((length, HEADS_WIDTH), LOW), rows_low(HEADS_WIDTH),
         rows_wide(NODE_DIM), rows_low(FFN_NODE), rows_wide(FFN_NODE), rows_wide(NODE_DIM)],
        [pltpu.VMEM(node_all.shape, WIDE)],
    )

    factors = exchange(factors, BOTH, layout.slabs)
    cot_first, cot_last = jnp.split(pair_cot, 2)
    factors, cot_first, pair_plane = lax.optimization_barrier((factors, cot_first, pair_plane))
    everyone = jnp.arange(ranks, dtype=jnp.int32)
    slab = 2 * ranks
    sources = jnp.concatenate([partner[None], work_crop * ranks + everyone]).astype(jnp.int32) % slab
    table, right, left, mask_plane = one_call(
        outer_tables,
        (sources,),
        (factors, w_outer),
        [((local_rows, OUTER, PAIR_DIM), LOW), ((OUTER, length), LOW), ((local_rows, OUTER), LOW),
         ((local_rows, 1, length), WIDE)],
        [pltpu.VMEM((OUTER * OUTER, PAIR_DIM), WIDE), pltpu.VMEM((OUTER, local_rows, PAIR_DIM), WIDE)],
    )

    step = (min(TILE, local_rows), min(LANES, length))
    extent = (local_rows, length)
    pieces = length // step[1]
    state = (local_rows, TRI_DIM, length)
    line = (local_rows, 1, length)
    sides_shape = (ranks, 2 * share, local_rows, length)
    mixed_shape = (TRI_DIM, local_rows, length)
    natural = (local_rows, length, PAIR_DIM)
    buffer = lambda channels: pltpu.VMEM((step[0], channels, step[1]), LOW)
    trade = lambda blocks: exchange(blocks, BOTH, layout.groups)
    merge = lambda blocks: blocks.reshape((TRI_DIM,) + blocks.shape[2:])
    split = lambda blocks: blocks.reshape((ranks, share) + blocks.shape[1:])
    unit = 2 * local_rows * length * PAIR_DIM * PAIR_DIM
    front_outs = (
        ("r", state, LOW), ("r", line, WIDE), ("r", line, WIDE), ("r", state, LOW),
        ("s", sides_shape, LOW),
    )
    square = (TRI_DIM, PAIR_DIM)
    gain_shape = (PAIR_DIM, 1)
    after_shape = (PAIR_DIM, 2 * TRI_DIM + PAIR_DIM)

    x_one, mean_tri_out, scale_tri_out, gate_tri_out, sides = run(
        kernel_open, step, extent,
        (stays.astype(jnp.int32)[None], pair_plane, pair, table, right, mask_plane, vectors, w_out_all),
        "mnntcrww", front_outs, [buffer(2 * TRI_DIM)], 4 * unit,
    )
    sides, cot_first, pair_cot = lax.optimization_barrier((sides, far(cot_first), pair_cot))
    sides_out, cot_near = lax.optimization_barrier((trade(sides), near(pair_cot)))
    mixed_out = merge(trade(mix(sides_out, False)[0]))
    mixed_out, cot_last = lax.optimization_barrier((mixed_out, cot_last))
    x_two, mean_tri_in, scale_tri_in, gate_tri_in, sides = run(
        kernel_middle, step, extent,
        (mixed_out, x_one, gate_tri_out, mask_plane, vectors, w_out_end, w_in_all), "srrrwww", front_outs, [buffer(TRI_DIM), buffer(2 * TRI_DIM)], 5 * unit,
    )
    sides, cot_last = lax.optimization_barrier((sides, far(cot_last)))
    sides_in, cot_plane = lax.optimization_barrier(
        (trade(sides), settled(pair_cot, cot_near, cot_first, cot_last))
    )
    turns = 2 if local_rows % (2 * TILE) == 0 else 1
    turn_rows = local_rows // turns
    mixed_in = [merge(trade(piece)) for piece in mix(sides_in, True, turns)]
    turned, grads_in = [], []
    ends = (vectors, w_in_end, w_pair_up, w_pair_down)
    for k in range(turns):
        *turned, mixed_grad = run(
            partial(kernel_turn, False), step, (turn_rows, length),
            (mixed_in[k], x_two, gate_tri_in, cot_plane, *ends, *turned),
            "sRRNwwww" + "xxx" * (k > 0),
            (("N", natural, LOW), ("R", state, LOW), ("R", state, LOW),
             ("s", (TRI_DIM, turn_rows, length), LOW)),
            [buffer(TRI_DIM), buffer(TRI_DIM)], 24 * unit // turns,
            skip=k * turn_rows // step[0], aliases={8: 0, 9: 1, 10: 2} if k else {},
        )
        if k:
            grads_in[-1], mixed_grad = lax.optimization_barrier((grads_in[-1], mixed_grad))
        grads_in.append(trade(split(mixed_grad)))
    pair_final, x_grad, gate_grad = turned
    sides_grad = trade(mix_back(grads_in, sides_in, True))
    sums = run(
        partial(kernel_turn, True), step, extent,
        (jnp.concatenate(mixed_in, axis=1), x_two, gate_tri_in, cot_plane, *ends), "srrnwwww",
        (("w", square, WIDE), ("w", gain_shape, WIDE), ("w", (PAIR_DIM, FFN_PAIR), WIDE),
         ("w", (FFN_PAIR, PAIR_DIM), WIDE), ("w", gain_shape, WIDE), ("w", gain_shape, WIDE)),
        [buffer(TRI_DIM)], 28 * unit,
    )
    sides_grad, *sums = lax.optimization_barrier((sides_grad, *sums))
    g_in_out, g_in_tri, g_up, g_down, g_pair, g_bias = sums
    out_first, out_last = jnp.split(pair_final, 2)
    sides_grad, out_near, out_first = lax.optimization_barrier(
        (sides_grad, near(pair_final), out_first)
    )
    backs = (sides_grad, x_two, mean_tri_in, scale_tri_in, gate_grad, x_grad, mask_plane,
             vectors, w_in_all, mixed_out, gate_tri_out, w_out_end)
    x_grad, gate_grad, mixed_grad = run(
        partial(kernel_return, False), step, extent, backs, "srrrrrrwwsrw",
        (("r", state, LOW), ("r", state, LOW), ("s", mixed_shape, LOW)),
        [buffer(2 * TRI_DIM), buffer(TRI_DIM), buffer(TRI_DIM)], 8 * unit,
    )
    mixed_grad, out_first = lax.optimization_barrier((mixed_grad, far(out_first)))
    mixed_grad = trade(split(mixed_grad))
    sums = run(
        partial(kernel_return, True), step, extent, backs, "srrrrrrwwsrw",
        (("w", after_shape, WIDE), ("w", gain_shape, WIDE), ("w", square, WIDE),
         ("w", gain_shape, WIDE)),
        [buffer(2 * TRI_DIM), buffer(TRI_DIM)], 12 * unit,
    )
    mixed_grad, *sums = lax.optimization_barrier((mixed_grad, *sums))
    g_in_all, g_in_gain, g_out_out, g_out_tri = sums
    sides_grad = trade(mix_back([mixed_grad], sides_out, False))
    sides_grad, out_last = lax.optimization_barrier((sides_grad, out_last))
    pair_one_grad, table_grad, right_part, g_out_all, g_out_gain = run(
        kernel_close, step, extent,
        (sides_grad, x_one, mean_tri_out, scale_tri_out, gate_grad, x_grad, mask_plane,
         vectors, w_out_all, table, right),
        "srrrrrrwwtc",
        (("n", natural, LOW), ("p", (pieces, local_rows, OUTER, PAIR_DIM), WIDE),
         ("c", (OUTER, length), WIDE), ("w", after_shape, WIDE), ("w", gain_shape, WIDE)),
        [buffer(2 * TRI_DIM)], 8 * unit,
    )

    factor_grads, g_outer = one_call(
        outer_backward,
        (),
        (table_grad, right_part, left, w_outer),
        [((2, ranks, local_rows, LANES), LOW), ((OUTER * OUTER, PAIR_DIM), WIDE)],
        [pltpu.VMEM((OUTER * OUTER, PAIR_DIM), WIDE), pltpu.VMEM((OUTER, local_rows, PAIR_DIM), WIDE)],
    )
    factor_grads, out_last = lax.optimization_barrier((factor_grads, far(out_last)))
    pair_out = settled(pair_final, out_near, out_first, out_last)
    factor_grads = exchange(factor_grads.reshape(slab, local_rows, LANES), BOTH, layout.slabs)
    factor_grads, pair_one_grad = lax.optimization_barrier((factor_grads, pair_one_grad))

    workers = layout.work_place(crop_at * ranks + everyone)
    sources = jnp.concatenate([partner[None], workers]).astype(jnp.int32) % slab
    (
        key_value, query_low, score_low, after_grad, final_low, normed_two, hidden_grad, after_low,
        g_factors, g_two, g_three,
    ) = one_call(
        node_backward,
        (sources,),
        (factor_grads, node_cot, vectors, soft, heads, key, value, after, slope, node_final,
         w_attn_out, w_node_up, w_node_down, w_factors),
        [((length, 2 * HEADS_WIDTH), LOW), rows_low(HEADS_WIDTH), (by_heads, LOW),
         rows_wide(NODE_DIM), rows_low(NODE_DIM), rows_low(NODE_DIM), rows_low(FFN_NODE),
         rows_low(NODE_DIM), ((NODE_DIM, LANES), WIDE), ((1, NODE_DIM), WIDE), ((1, NODE_DIM), WIDE)],
    )
    score_low = score_low.reshape(HEADS, local_rows, length)
    g_bias_head = jnp.einsum("ijd,hij->dh", pair, score_low, preferred_element_type=WIDE)
    g_bias_head = lax.optimization_barrier(g_bias_head).reshape(-1, LANES)
    pair_one_away = lax.ppermute(pair_one_grad, BOTH, layout.moves)
    grads = [
        (at.w_bias, 1, g_bias_head),
        (at.gain_two, 1, g_two),
        (at.gain_three, 1, g_three),
        (at.w_outer, 1, g_outer),
        (at.gain_pair, 1, g_pair),
        (at.w_pair_up, 1, g_up),
        (at.w_pair_down, 1, g_down),
        (at.bias_pair, 1, g_bias),
    ]
    for tri, g_all, g_gain, g_tri, g_out in (
        (at.outgoing, g_out_all, g_out_gain, g_out_tri, g_out_out),
        (at.incoming, g_in_all, g_in_gain, g_in_tri, g_in_out),
    ):
        grads += [
            (tri.gain_in, 1, g_gain),
            (tri.w_left, 3, g_all),
            (tri.gain_tri, 1, g_tri),
            (tri.w_tri_out, 1, g_out),
        ]

    blocks, node_blocks = pack(
        layout, amount, jnp.concatenate([recycle, row_at.astype(jnp.int32)[None]]), grads,
        (key_value, query_low, start_all, normed_own, normed_all, after_grad, vectors,
         w_projections, act_low, final_low, normed_two, hidden_grad, attended, after_low, g_factors),
    )
    total = lambda got: low_of(jnp.sum(got.astype(WIDE), axis=0))
    blocks = total(exchange(blocks, BOTH, layout.cores))
    blocks, pair_out = lax.optimization_barrier((exchange(blocks, BOTH, layout.chips), pair_out))
    blocks = total(blocks)
    blocks = exchange(jnp.concatenate([blocks, node_blocks], axis=1), "row")
    pair_grad = jnp.where(stays, pair_one_grad, pair_one_away).astype(WIDE) + jnp.einsum(
        "hij,dh->ijd", score_low, w_bias[:, :HEADS], preferred_element_type=WIDE
    )
    blocks, pair_grad = lax.optimization_barrier((blocks, low_of(pair_grad)))
    blocks = jnp.sum(blocks.astype(WIDE), axis=0)
    node_parts = jnp.split(blocks[height:], NODE_DIM // LANES)
    node_grad = low_of(after_grad + jnp.concatenate(node_parts, axis=1))
    blocks = blocks[:height]
    grad_own = lax.dynamic_slice(blocks.reshape(-1), (offset,), (amount,))
    square_own = jnp.broadcast_to(jnp.sum(grad_own * grad_own), (1, LANES))
    last = jnp.concatenate([g_bias.reshape(1, LANES), square_own], axis=0)
    last = jnp.sum(spread(last, devices, BOTH).reshape(devices, 2, LANES), axis=0)
    bias_total = last[0]
    grad_norm = jnp.sqrt(last[1, 0])
    clipped = grad_own * (CLIP_NORM / jnp.maximum(grad_norm, CLIP_NORM))
    new_first = BETA_ONE * first + (1.0 - BETA_ONE) * clipped
    new_second = BETA_TWO * second + (1.0 - BETA_TWO) * clipped * clipped
    first_hat = new_first / (1.0 - BETA_ONE**ADAM_STEP)
    second_hat = new_second / (1.0 - BETA_TWO**ADAM_STEP)
    new_master = master - LEARN_RATE * (
        first_hat / (jnp.sqrt(second_hat) + ADAM_EPS) + WEIGHT_DECAY * master
    )
    return (
        node_out[None],
        pair_out[None],
        node_grad[None],
        pair_grad[None],
        grad_own,
        bias_total,
        grad_norm,
        new_master,
        new_first,
        new_second,
        low_of(new_master),
    )


def solution(mesh):
    layout = Layout(mesh.shape["crop"], mesh.shape["row"])
    return jax.shard_map(
        lambda *arrays: local(layout, *arrays),
        mesh=mesh,
        in_specs=(
            P("crop", "row", None),
            P("crop", "row", None, None),
            P("crop"),
            P("crop", None),
            P("crop", "row", None),
            P("crop", "row", None, None),
            P(("crop", "row")),
            P(("crop", "row")),
            P(("crop", "row")),
        ),
        out_specs=(
            P("crop", "row", None),
            P("crop", "row", None, None),
            P("crop", "row", None),
            P("crop", "row", None, None),
            P(("crop", "row")),
            P(),
            P(),
            P(("crop", "row")),
            P(("crop", "row")),
            P(("crop", "row")),
            P(("crop", "row")),
        ),
        check_vma=False,
    )
```

```python
import math
from functools import partial
from typing import Any, NamedTuple

import jax
import jax.numpy as jnp
import numpy as np
from jax import lax
from jax.experimental import pallas as pl
from jax.experimental.pallas import tpu as pltpu
from jax.sharding import PartitionSpec as P

NODE_DIM = 256
PAIR_DIM = 128
HEADS = 8
HEAD_DIM = 32
OUTER = 32
TRI_DIM = 128
FFN_NODE = 1024
FFN_PAIR = 512
RECYCLES = 4
ADAM_STEP = 3


EPS_NORM = 1e-05
ADAM_EPS = 1e-08
BETA_ONE = 0.9
BETA_TWO = 0.95
LEARN_RATE = 0.06
WEIGHT_DECAY = 0.1
CLIP_NORM = 1.0
MASK_FILL = 1000000000.0
HIGHEST = lax.Precision.HIGHEST


class Triangle(NamedTuple):
    gain_in: Any
    w_left: Any
    w_right: Any
    w_gate: Any
    gain_tri: Any
    w_tri_out: Any


class Params(NamedTuple):
    embed: Any
    gain_one: Any
    w_query: Any
    w_key: Any
    w_value: Any
    w_bias: Any
    w_attn_out: Any
    gain_two: Any
    w_node_up: Any
    w_node_down: Any
    gain_three: Any
    w_left_node: Any
    w_right_node: Any
    w_outer: Any
    outgoing: Triangle
    incoming: Triangle
    gain_pair: Any
    w_pair_up: Any
    w_pair_down: Any
    bias_pair: Any


LANES = 128
HEADS_WIDTH = HEADS * HEAD_DIM


def first_rows():
    square = PAIR_DIM * TRI_DIM
    triangle = Triangle(PAIR_DIM, square, square, PAIR_DIM * PAIR_DIM, TRI_DIM, square)
    sizes = Params(
        embed=RECYCLES * NODE_DIM,
        gain_one=NODE_DIM,
        w_query=NODE_DIM * HEADS_WIDTH,
        w_key=NODE_DIM * HEADS_WIDTH,
        w_value=NODE_DIM * HEADS_WIDTH,
        w_bias=PAIR_DIM * HEADS,
        w_attn_out=HEADS_WIDTH * NODE_DIM,
        gain_two=NODE_DIM,
        w_node_up=NODE_DIM * FFN_NODE,
        w_node_down=FFN_NODE * NODE_DIM,
        gain_three=NODE_DIM,
        w_left_node=NODE_DIM * OUTER,
        w_right_node=NODE_DIM * OUTER,
        w_outer=OUTER * OUTER * PAIR_DIM,
        outgoing=triangle,
        incoming=triangle,
        gain_pair=PAIR_DIM,
        w_pair_up=PAIR_DIM * FFN_PAIR,
        w_pair_down=FFN_PAIR * PAIR_DIM,
        bias_pair=PAIR_DIM,
    )
    leaves, tree = jax.tree.flatten(sizes)
    ends = np.cumsum(leaves) // LANES
    starts = [0] + [int(end) for end in ends[:-1]]
    return jax.tree.unflatten(tree, starts), int(ends[-1])


LOW = jnp.bfloat16
WIDE = jnp.float32
BOTH = ("crop", "row")
TILE = 16
VMEM_LIMIT = 56 * 2**20
SMALL_LIMIT = 28 * 2**20
INV_SQRT2 = 1.0 / math.sqrt(2.0)
INV_SQRT2PI = 1.0 / math.sqrt(2.0 * math.pi)


class Layout:
    def __init__(self, crops, rows):
        self.crops, self.rows = crops, rows
        self.devices = crops * rows
        self.wide = 2 ** (int(math.log2(rows)) // 2)
        self.high = rows // self.wide
        half = crops // 2
        self.moves = [
            (here, self.work_place(here))
            for here in range(self.devices)
            if here != self.work_place(here)
        ]
        high_of = lambda here: here % rows // self.wide
        self.near = [
            (here, there) for here, there in self.moves if abs(high_of(here) - high_of(there)) == 1
        ]
        self.far = [move for move in self.moves if move not in self.near]
        self.groups = [
            [self.work_place(c * rows + r) for r in range(rows)] for c in range(crops)
        ]
        self.cores = [
            [(2 * x + k) * rows + r for k in range(2)] for x in range(half) for r in range(rows)
        ]
        self.slabs = [[2 * x * rows + k for k in range(2 * rows)] for x in range(half)]
        self.chips = [
            [(2 * x + k) * rows + r for x in range(half)] for k in range(2) for r in range(rows)
        ]

    def work_place(self, here):
        crop, row = here // self.rows, here % self.rows
        high, wide = row // self.wide, row % self.wide
        core = crop % 2
        away = (high // (self.high // 2) + core) % 2
        crop = crop + away * (1 - 2 * core)
        high = high + away * (self.high - 1 - 2 * high)
        return crop * self.rows + high * self.wide + wide


def exchange(blocks, axes, groups=None):
    return lax.all_to_all(blocks, axes, 0, 0, axis_index_groups=groups, tiled=True)


def spread(part, count, axes, groups=None):
    return exchange(jnp.broadcast_to(part[None], (count,) + part.shape), axes, groups)


def dot_nn(a, b):
    return lax.dot_general(a, b, (((1,), (0,)), ((), ())), preferred_element_type=WIDE)


def dot_nt(a, b):
    return lax.dot_general(a, b, (((1,), (1,)), ((), ())), preferred_element_type=WIDE)


def dot_tn(a, b):
    return lax.dot_general(a, b, (((0,), (0,)), ((), ())), preferred_element_type=WIDE)


def norm_parts(x):
    hat, _, scale = norm_all(x)
    return hat, scale


def norm_all(x):
    mean = jnp.mean(x, axis=0, keepdims=True)
    centered = x - mean
    scale = lax.rsqrt(jnp.mean(centered * centered, axis=0, keepdims=True) + EPS_NORM)
    return centered * scale, mean, scale


def norm_back(grad, hat, scale, gain):
    grad_gain = jnp.sum(grad * hat, axis=1, keepdims=True)
    wide = grad * gain
    inner = jnp.mean(wide * hat, axis=0, keepdims=True)
    return scale * (wide - jnp.mean(wide, axis=0, keepdims=True) - hat * inner), grad_gain


def sigmoid(x):
    return 0.5 * jnp.tanh(0.5 * x) + 0.5


EMBED = slice(0, 8)
GAIN_ONE, GAIN_TWO, GAIN_THREE = slice(8, 10), slice(10, 12), slice(12, 14)
OUT_GAIN, OUT_TRI, IN_GAIN, IN_TRI = (slice(k, k + 1) for k in range(14, 18))
PAIR_GAIN, PAIR_BIAS = slice(18, 19), slice(19, 20)


def column(row):
    return jnp.broadcast_to(row, (LANES, row.shape[1])).T[:, :1]


def row_of(values):
    return jnp.broadcast_to(values, (values.shape[0], LANES)).T[:1]


def cat(ref):
    return jnp.concatenate([ref[t] for t in range(ref.shape[0])], axis=1)


def put(ref, value):
    count = ref.shape[0]
    width = value.shape[1] // count
    for t in range(count):
        ref[t] = value[:, t * width : (t + 1) * width].astype(ref.dtype)


def swapped(value):
    if value.shape[0] % TILE or value.shape[1] % TILE:
        return jnp.swapaxes(value.astype(WIDE), 0, 1).astype(LOW)
    return jnp.swapaxes(value, 0, 1)


def send_pair(scratch, out_ref):
    parts, share = out_ref.shape[0], out_ref.shape[1] // 2
    channels = parts * share
    for side in range(2):
        value = swapped(scratch[:, side * channels : (side + 1) * channels, :])
        out_ref[:, side * share : (side + 1) * share] = value.reshape(
            (parts, share) + value.shape[1:]
        )


def take_pair(in_ref, scratch):
    parts, share = in_ref.shape[0], in_ref.shape[1] // 2
    channels = parts * share
    for side in range(2):
        value = in_ref[:, side * share : (side + 1) * share]
        value = value.reshape((channels,) + value.shape[2:])
        scratch[:, side * channels : (side + 1) * channels, :] = swapped(value)


def front(x, gain, w_all, mask, x_out, mean_out, scale_out, gate_out, sides):
    hat, mean, scale = norm_all(x)
    all_three = dot_nn(w_all, (hat * gain).astype(LOW))
    channels = 2 * TRI_DIM
    put(sides, all_three[:channels] * mask)
    put(x_out, x)
    put(mean_out, mean)
    put(scale_out, scale)
    put(gate_out, sigmoid(all_three[channels:]))


def triangle_update(mixed, gain, w_out):
    hat, scale = norm_parts(mixed)
    normed = (hat * gain).astype(LOW)
    return hat, scale, normed, dot_nn(w_out, normed)


def post_back(grad, gate, hat, scale, normed, update, gain, w_out_back):
    update_grad = (grad * gate).astype(LOW)
    gate_grad = (grad * update * (gate * (1.0 - gate))).astype(LOW)
    grad_out = dot_nt(normed, update_grad)
    mixed_grad, grad_gain = norm_back(dot_nn(w_out_back, update_grad), hat, scale, gain)
    return mixed_grad, gate_grad, grad_out, grad_gain


def front_back(grad, x, mean, scale, sides_grad, gate_grad, mask, gain, w_all_back):
    hat = (x - mean) * scale
    normed = (hat * gain).astype(LOW)
    sides = jnp.concatenate([sides_grad * mask.astype(LOW), gate_grad], axis=0)
    grad_w = dot_nt(normed, sides)
    x_grad, grad_gain = norm_back(dot_nn(w_all_back, sides), hat, scale, gain)
    return grad + x_grad, grad_w, grad_gain


def gelu_parts(x):
    cumulative = 0.5 * lax.erf(x * INV_SQRT2) + 0.5
    density = INV_SQRT2PI * jnp.exp(-0.5 * x * x)
    return x * cumulative, cumulative + x * density


FEW = 4


def few_rows(piece, *refs):
    rows = refs[0].shape[0]
    few = min(FEW, rows)

    def step(t, carry):
        piece(*(ref.at[pl.ds(t * few, few)] for ref in refs))
        return carry

    lax.fori_loop(0, rows // few, step, 0)


def zero_first(*refs):
    @pl.when((pl.program_id(0) == 0) & (pl.program_id(1) == 0))
    def _():
        for ref in refs:
            ref[...] = jnp.zeros_like(ref)


def run(body, step, extent, in_arrays, in_kinds, outs, scratch, flops, skip=0, aliases={}):
    def spec(kind, shape):
        lead = (0,) * len(shape)
        if kind == "m":
            return pl.BlockSpec(memory_space=pltpu.SMEM)
        if kind == "x":
            return pl.BlockSpec(memory_space=pl.ANY)
        block, at = {
            "R": (step[:1] + shape[1:-1] + step[1:], lambda c, r: (r + skip,) + lead[2:] + (c,)),
            "N": (step + shape[2:], lambda c, r: (r + skip, c) + lead[2:]),
            "r": (step[:1] + shape[1:-1] + step[1:], lambda c, r: (r,) + lead[2:] + (c,)),
            "n": (step + shape[2:], lambda c, r: (r, c) + lead[2:]),
            "s": (shape[:-2] + step, lambda c, r: lead[2:] + (r, c)),
            "c": (shape[:-1] + step[1:], lambda c, r: lead[1:] + (c,)),
            "t": (step[:1] + shape[1:], lambda c, r: (r,) + lead[1:]),
            "p": ((1,) + step[:1] + shape[2:], lambda c, r: (c, r) + lead[2:]),
            "q": (step[1:] + shape[1:], lambda c, r: (c,) + lead[1:]),
            "w": (shape, lambda c, r: lead),
        }[kind]
        return pl.BlockSpec(block, at)

    moved = sum(a.size * a.dtype.itemsize for a in in_arrays)
    return pl.pallas_call(
        body,
        grid=(extent[1] // step[1], extent[0] // step[0]),
        in_specs=[spec(kind, a.shape) for kind, a in zip(in_kinds, in_arrays)],
        out_specs=[spec(kind, shape) for kind, shape, _ in outs],
        out_shape=[jax.ShapeDtypeStruct(shape, dtype) for _, shape, dtype in outs],
        scratch_shapes=scratch,
        input_output_aliases=aliases,
        compiler_params=pltpu.CompilerParams(vmem_limit_bytes=VMEM_LIMIT),
        cost_estimate=pl.CostEstimate(flops=flops, bytes_accessed=moved, transcendentals=0),
    )(*in_arrays)


def all_low(w):
    return jnp.concatenate([w[k * PAIR_DIM : (k + 1) * PAIR_DIM].T for k in range(3)], axis=0)


def all_back(w):
    return jnp.concatenate([w[k * PAIR_DIM : (k + 1) * PAIR_DIM] for k in range(3)], axis=1)


def kernel_open(
    stays, pair, pair_home, table, right, mask, vectors, w_all, x_out, mean_out, scale_out, gate_out, sides_out, sides
):
    right_low = right[...]
    at_home = stays[0] == 1
    x = jnp.concatenate(
        [
            jnp.where(at_home, pair_home[t], pair[t]).T.astype(WIDE) + dot_tn(table[t], right_low)
            for t in range(pair.shape[0])
        ],
        axis=1,
    )
    front(
        x, column(vectors[OUT_GAIN]), all_low(w_all), cat(mask), x_out, mean_out, scale_out, gate_out,
        sides,
    )
    send_pair(sides, sides_out)


def kernel_middle(
    mixed, x_in, gate_in, mask, vectors, w_out, w_all,
    x_out, mean_out, scale_out, gate_out, sides_out, arrived, sides,
):
    arrived[...] = swapped(mixed[...])
    *_, update = triangle_update(cat(arrived).astype(WIDE), column(vectors[OUT_TRI]), w_out[...].T)
    x = cat(x_in).astype(WIDE) + cat(gate_in).astype(WIDE) * update
    front(
        x, column(vectors[IN_GAIN]), all_low(w_all), cat(mask),
        x_out, mean_out, scale_out, gate_out, sides,
    )
    send_pair(sides, sides_out)


def kernel_turn(sums, mixed, x_in, gate_in, cot, vectors, w_out, w_up, w_down, *rest):
    if sums:
        g_out, g_tri, g_up, g_down, g_pair, g_bias, arrived = rest
        zero_first(g_out, g_tri, g_up, g_down, g_pair, g_bias)
    else:
        pair_out, x_grad, gate_grad, mixed_grad, arrived, leaving = rest[-6:]
    arrived[...] = swapped(mixed[...])
    up_low, up_back = w_up[...].T, w_up[...]
    down_low, down_back = w_down[...].T, w_down[...]
    tri_col, pair_col = column(vectors[IN_TRI]), column(vectors[PAIR_GAIN])
    chunk = PAIR_DIM

    def piece(x_in, gate_in, cot, arrived):
        rows = x_in.shape[0]
        gate = cat(gate_in).astype(WIDE)
        mix_parts = triangle_update(cat(arrived).astype(WIDE), tri_col, w_out[...].T)
        x = cat(x_in).astype(WIDE) + gate * mix_parts[-1]
        hat, scale = norm_parts(x)
        normed = (hat * pair_col).astype(LOW)
        cot_low = jnp.concatenate([cot[t].T for t in range(rows)], axis=1)
        total = x + column(vectors[PAIR_BIAS])
        normed_grad = jnp.zeros_like(x)
        for c in range(FFN_PAIR // chunk):
            part = slice(c * chunk, (c + 1) * chunk)
            act, slope = gelu_parts(dot_nn(up_low[part], normed))
            act_low = act.astype(LOW)
            hidden_grad = (dot_nn(down_back[part], cot_low) * slope).astype(LOW)
            normed_grad = normed_grad + dot_nn(up_back[:, part], hidden_grad)
            if sums:
                g_up[:, part] += dot_nt(normed, hidden_grad)
                g_down[part] += dot_nt(act_low, cot_low)
            else:
                total = total + dot_nn(down_low[:, part], act_low)
        cot_wide = cot_low.astype(WIDE)
        back, grad_pair = norm_back(normed_grad, hat, scale, pair_col)
        grad = cot_wide + back
        mix_grad, gates, grad_out, grad_tri = post_back(grad, gate, *mix_parts, tri_col, w_out[...])
        if sums:
            g_bias[...] += jnp.sum(cot_wide, axis=1, keepdims=True)
            g_pair[...] += grad_pair
            g_out[...] += grad_out
            g_tri[...] += grad_tri
            return
        total_low = total.astype(LOW)
        width = total.shape[1] // rows
        for t in range(rows):
            pair_out[t] = total_low[:, t * width : (t + 1) * width].T
        put(x_grad, grad)
        put(leaving, mix_grad)
        put(gate_grad, gates)

    if sums:
        few_rows(piece, x_in, gate_in, cot, arrived)
    else:
        piece(x_in, gate_in, cot, arrived)
        mixed_grad[...] = swapped(leaving[...])


def kernel_return(
    sums, sides_grad, x_after, mean_after, scale_after, gate_after, grad_in, mask, vectors, w_after,
    mixed, gate_in, w_out, *rest,
):
    if sums:
        g_after, g_gain, g_out, g_tri, sides, arrived = rest
        zero_first(g_after, g_gain, g_out, g_tri)
    else:
        x_grad, gate_grad, mixed_grad, sides, arrived, leaving = rest
    take_pair(sides_grad, sides)
    arrived[...] = swapped(mixed[...])
    tri_col = column(vectors[OUT_TRI])
    after_col, after_back = column(vectors[IN_GAIN]), all_back(w_after)

    def piece(
        grad_in, x_after, mean_after, scale_after, sides, gate_after, mask, arrived, gate_in
    ):
        grad, grad_w, grad_gain = front_back(
            cat(grad_in).astype(WIDE), cat(x_after).astype(WIDE), cat(mean_after), cat(scale_after),
            cat(sides), cat(gate_after),
            cat(mask), after_col, after_back,
        )
        mix_parts = triangle_update(cat(arrived).astype(WIDE), tri_col, w_out[...].T)
        mix_grad, gates, grad_out, grad_tri = post_back(
            grad, cat(gate_in).astype(WIDE), *mix_parts, tri_col, w_out[...]
        )
        if sums:
            g_after[...] += grad_w
            g_gain[...] += grad_gain
            g_out[...] += grad_out
            g_tri[...] += grad_tri
            return
        put(x_grad, grad)
        put(leaving, mix_grad)
        put(gate_grad, gates)

    parts = (grad_in, x_after, mean_after, scale_after, sides, gate_after, mask, arrived, gate_in)
    if sums:
        few_rows(piece, *parts)
    else:
        piece(*parts)
        mixed_grad[...] = swapped(leaving[...])


def kernel_close(
    sides_grad, x_after, mean_after, scale_after, gate_after, grad_in, mask, vectors, w_after,
    table, right,
    pair_grad, table_grad, right_grad, g_after, g_gain, sides,
):
    take_pair(sides_grad, sides)
    zero_first(g_after, g_gain)

    @pl.when(pl.program_id(1) == 0)
    def _():
        right_grad[...] = jnp.zeros_like(right_grad)

    grad, grad_w, grad_gain = front_back(
        cat(grad_in).astype(WIDE), cat(x_after).astype(WIDE), cat(mean_after), cat(scale_after),
        cat(sides), cat(gate_after),
        cat(mask), column(vectors[OUT_GAIN]), all_back(w_after),
    )
    g_after[...] += grad_w
    g_gain[...] += grad_gain
    low = grad.astype(LOW)
    rows = table.shape[0]
    width = low.shape[1] // rows
    for t in range(rows):
        own = low[:, t * width : (t + 1) * width]
        pair_grad[t] = own.T
        table_grad[0, t] = dot_nt(right[...], own)
        right_grad[...] += dot_nn(table[t], own)


CHANNELS = 8


def kernel_mix(incoming, left, right, *outs):
    parts, count, rows, length = left.shape
    part = rows // len(outs)
    for c in range(count):
        a = left[:, c].reshape(length, length)
        b = right[:, c].reshape(length, length)
        mixed = dot_tn(a, b) if incoming else dot_nt(a, b)
        mixed = mixed.astype(LOW).reshape(parts, rows, length)
        for k, out in enumerate(outs):
            out[:, c] = mixed[:, k * part : (k + 1) * part]


def kernel_mix_back(incoming, *refs):
    *grads, left, right, out = refs
    parts, count, rows, length = left.shape
    for c in range(count):
        g = jnp.concatenate([grad[:, c] for grad in grads], axis=1).reshape(length, length)
        a = left[:, c].reshape(length, length)
        b = right[:, c].reshape(length, length)
        a_grad = dot_nt(b, g) if incoming else dot_nn(g, b)
        b_grad = dot_nn(a, g) if incoming else dot_tn(g, a)
        out[:, 0, c] = a_grad.astype(LOW).reshape(parts, rows, length)
        out[:, 1, c] = b_grad.astype(LOW).reshape(parts, rows, length)


def mix(sides, incoming, pieces=1):
    parts, double, rows, length = sides.shape
    share = double // 2
    count = min(CHANNELS, share)
    steps = share // count
    block = (parts, count, rows, length)
    part = (parts, count, rows // pieces, length)
    return pl.pallas_call(
        lambda *refs: kernel_mix(incoming, *refs),
        grid=(steps,),
        in_specs=[
            pl.BlockSpec(block, lambda c: (0, c, 0, 0)),
            pl.BlockSpec(block, lambda c: (0, c + steps, 0, 0)),
        ],
        out_specs=[pl.BlockSpec(part, lambda c: (0, c, 0, 0))] * pieces,
        out_shape=[jax.ShapeDtypeStruct((parts, share) + part[2:], LOW)] * pieces,
        compiler_params=pltpu.CompilerParams(vmem_limit_bytes=VMEM_LIMIT),
        cost_estimate=pl.CostEstimate(
            flops=2 * share * length**3, bytes_accessed=3 * share * length * length * 2,
            transcendentals=0,
        ),
    )(sides, sides)


def mix_back(grads, sides, incoming):
    parts, double, rows, length = sides.shape
    share = double // 2
    count = min(CHANNELS, share)
    steps = share // count
    block = (parts, count, rows, length)
    part = (parts, count, rows // len(grads), length)
    out = pl.pallas_call(
        lambda *refs: kernel_mix_back(incoming, *refs),
        grid=(steps,),
        in_specs=[pl.BlockSpec(part, lambda c: (0, c, 0, 0))] * len(grads)
        + [
            pl.BlockSpec(block, lambda c: (0, c, 0, 0)),
            pl.BlockSpec(block, lambda c: (0, c + steps, 0, 0)),
        ],
        out_specs=pl.BlockSpec((parts, 2, count, rows, length), lambda c: (0, 0, c, 0, 0)),
        out_shape=jax.ShapeDtypeStruct((parts, 2, share, rows, length), LOW),
        compiler_params=pltpu.CompilerParams(vmem_limit_bytes=VMEM_LIMIT),
        cost_estimate=pl.CostEstimate(
            flops=4 * share * length**3, bytes_accessed=5 * share * length * length * 2,
            transcendentals=0,
        ),
    )(*grads, sides, sides)
    return out.reshape(sides.shape)


def share_rows(share):
    return -(-(share + 2 * LANES) // (TILE * LANES)) * TILE


def whole(shape):
    return pl.BlockSpec(shape, lambda *_: (0,) * len(shape))


def one_call(body, scalars, in_arrays, outs, scratch=(), limit=VMEM_LIMIT):
    return pl.pallas_call(
        body,
        in_specs=[pl.BlockSpec(memory_space=pltpu.SMEM)] * len(scalars)
        + [whole(a.shape) for a in in_arrays],
        out_specs=[whole(shape) for shape, _ in outs],
        out_shape=[jax.ShapeDtypeStruct(shape, dtype) for shape, dtype in outs],
        scratch_shapes=list(scratch),
        grid=(1,),
        compiler_params=pltpu.CompilerParams(vmem_limit_bytes=limit),
    )(*scalars, *in_arrays)


def lane_in(shape, start, width):
    lane = lax.broadcasted_iota(jnp.int32, shape, 1)
    return (lane >= start) & (lane < start + width)


def rolled(value, shift):
    shift %= LANES
    return pltpu.roll(value, shift, 1) if shift else value


def share_order(layout):
    return [((d // layout.rows) % 2, d // (2 * layout.rows), d % layout.rows) for d in range(layout.devices)]


def unpack(layout, shares, share):
    at, _ = first_rows()
    height = shares.shape[3]
    first = [share * d // LANES for d in range(layout.devices)]
    order = share_order(layout)
    matrices = [
        (at.w_query, NODE_DIM, 3, 3 * HEADS_WIDTH),
        (at.w_attn_out, HEADS_WIDTH, 1, NODE_DIM),
        (at.w_node_up, NODE_DIM, 1, FFN_NODE),
        (at.w_node_down, FFN_NODE, 1, NODE_DIM),
        (at.w_outer, OUTER * OUTER, 1, PAIR_DIM),
        (at.outgoing.w_left, 3 * PAIR_DIM, 1, TRI_DIM),
        (at.outgoing.w_tri_out, TRI_DIM, 1, PAIR_DIM),
        (at.incoming.w_left, 3 * PAIR_DIM, 1, TRI_DIM),
        (at.incoming.w_tri_out, TRI_DIM, 1, PAIR_DIM),
        (at.w_pair_up, PAIR_DIM, 1, FFN_PAIR),
        (at.w_pair_down, FFN_PAIR, 1, PAIR_DIM),
    ]
    small = [(at.embed, 8), (at.gain_one, 2), (at.gain_two, 2), (at.gain_three, 2)]
    small += [
        (start, 1)
        for start in (
            at.outgoing.gain_in, at.outgoing.gain_tri, at.incoming.gain_in, at.incoming.gain_tri,
            at.gain_pair, at.bias_pair,
        )
    ]

    def body(shares_ref, vectors, bias_out, factors_out, *rest):
        outs, flat, narrow = rest[:-2], rest[-2], rest[-1]
        for d, place in enumerate(order):
            block = shares_ref[place].astype(WIDE)
            if d:
                tail = flat[first[d] : first[d] + 1]
                flat[first[d] : first[d] + height] = block
                flat[first[d] : first[d] + 1] = block[:1] + tail
            else:
                flat[:height] = block
        row = 0
        vectors[...] = jnp.zeros_like(vectors)
        for start, count in small:
            vectors[row : row + count] = flat[start : start + count]
            row += count
        for out, (place, rows, count, width) in zip(outs, matrices):
            pieces = width // count // LANES
            for m in range(count):
                for a in range(pieces):
                    start = place + m * rows * pieces + a
                    value = (
                        flat[pl.ds(start, rows, stride=pieces), :]
                        if pieces > 1
                        else flat[start : start + rows]
                    )
                    lane = (m * pieces + a) * LANES
                    out[:, lane : lane + LANES] = value.astype(LOW)
        per_row = LANES // HEADS
        shape = (HEADS, LANES)
        value = flat[at.w_bias : at.w_bias + HEADS]
        for a in range(per_row):
            kept = jnp.where(lane_in(shape, 0, HEADS), rolled(value, -HEADS * a), 0.0)
            narrow[pl.ds(a, HEADS, stride=per_row), :] = kept
        bias_out[...] = narrow[:PAIR_DIM].astype(LOW)
        per_row = LANES // OUTER
        count = NODE_DIM // per_row
        shape = (count, LANES)
        left, right = (flat[start : start + count] for start in (at.w_left_node, at.w_right_node))
        for a in range(per_row):
            kept = jnp.where(lane_in(shape, 0, OUTER), rolled(left, -OUTER * a), 0.0)
            kept += jnp.where(lane_in(shape, OUTER, OUTER), rolled(right, OUTER - OUTER * a), 0.0)
            narrow[pl.ds(a, count, stride=per_row), :] = kept
        factors_out[...] = narrow[...].astype(LOW)

    return one_call(
        body,
        (),
        (shares,),
        [((24, LANES), WIDE), ((PAIR_DIM, LANES), LOW), ((NODE_DIM, LANES), LOW)]
        + [((rows, width), LOW) for _, rows, _, width in matrices],
        [pltpu.VMEM((first[-1] + height + TILE, LANES), WIDE), pltpu.VMEM((NODE_DIM, LANES), WIDE)],
    )


def pack(layout, share, scalars, grads, node_parts):
    at, total = first_rows()
    height = share_rows(share)
    first = [share * d // LANES for d in range(layout.devices)]
    order = share_order(layout)
    many = len(grads)

    def body(scalar_ref, *refs):
        ins, rest = refs[:many], refs[many:]
        (
            key_value, query_low, start, normed_own, normed_all, after_grad, vectors, w_projections,
            act_low, final_low, normed_two, hidden_grad, attended, after_low, g_factors,
            out, node_parts_out, flat, narrow, steps,
        ) = rest

        def store(place, count, value):
            rows, pieces = value.shape[0], value.shape[1] // count // LANES
            for m in range(count):
                for a in range(pieces):
                    lane = (m * pieces + a) * LANES
                    begin = place + m * rows * pieces + a
                    part = value[:, lane : lane + LANES]
                    if pieces > 1 and rows > 1:
                        flat[pl.ds(begin, rows, stride=pieces), :] = part
                    else:
                        flat[begin : begin + rows] = part

        flat[total:] = jnp.zeros((flat.shape[0] - total, LANES), WIDE)
        for ref, (place, count, _) in zip(ins, grads):
            store(place, count, row_of(ref[...]) if ref.shape[1] == 1 else ref[...])
        store(at.w_node_down, 1, dot_tn(act_low[...], final_low[...]))
        store(at.w_node_up, 1, dot_tn(normed_two[...], hidden_grad[...]))
        store(at.w_attn_out, 1, dot_tn(attended[...], after_low[...]))
        per_row = LANES // OUTER
        count = NODE_DIM // per_row
        narrow[...] = g_factors[...]
        left = jnp.zeros((count, LANES), WIDE)
        right = left
        for a in range(per_row):
            piece = narrow[pl.ds(a, count, stride=per_row), :]
            inside = lane_in(piece.shape, OUTER * a, OUTER)
            left = jnp.where(inside, rolled(piece, OUTER * a), left)
            right = jnp.where(inside, rolled(piece, OUTER * a - OUTER), right)
        store(at.w_left_node, 1, left)
        store(at.w_right_node, 1, right)

        store(at.w_query, 1, dot_tn(normed_own[...], query_low[...]))
        store(at.w_key, 2, dot_tn(normed_all[...], key_value[...]))
        steps[...] = dot_nt(key_value[...], w_projections[:, HEADS_WIDTH:])
        local_rows = query_low.shape[0]
        own = pl.ds(pl.multiple_of(scalar_ref[1] * local_rows, local_rows), local_rows)
        steps[own, :] += dot_nt(query_low[...], w_projections[:, :HEADS_WIDTH])
        hat, scale = row_norm(start[...])
        part, grad_gain = row_norm_back(steps[...], hat, scale, vector(vectors, GAIN_ONE))
        for r in range(node_parts_out.shape[0]):
            for a in range(NODE_DIM // LANES):
                piece = part[r * local_rows : (r + 1) * local_rows, a * LANES : (a + 1) * LANES]
                node_parts_out[r, a * local_rows : (a + 1) * local_rows] = piece.astype(LOW)
        store(at.gain_one, 1, grad_gain)
        flat[at.embed : at.embed + 2 * RECYCLES] = jnp.zeros((2 * RECYCLES, LANES), WIDE)
        column_sum = jnp.sum(after_grad[...], axis=0, keepdims=True)
        column_sum += jnp.sum(part, axis=0, keepdims=True)
        for a in range(NODE_DIM // LANES):
            place = at.embed + (NODE_DIM // LANES) * scalar_ref[0] + a
            flat[pl.ds(place, 1), :] = column_sum[:, a * LANES : (a + 1) * LANES]
        for d, where in enumerate(order):
            out[where] = flat[first[d] : first[d] + height].astype(LOW)

    shape = (2, layout.crops // 2, layout.rows, height, LANES)
    return one_call(
        body,
        (scalars,),
        tuple(array for _, _, array in grads) + tuple(node_parts),
        [(shape, LOW), ((layout.rows, node_parts[1].shape[0] * NODE_DIM // LANES, LANES), LOW)],
        [
            pltpu.VMEM((first[-1] + height + TILE, LANES), WIDE),
            pltpu.VMEM((NODE_DIM, LANES), WIDE),
            pltpu.VMEM(node_parts[2].shape, WIDE),
        ],
        SMALL_LIMIT,
    )


def row_norm(x):
    centered = x - jnp.mean(x, axis=-1, keepdims=True)
    scale = lax.rsqrt(jnp.mean(centered * centered, axis=-1, keepdims=True) + EPS_NORM)
    return centered * scale, scale


def row_norm_back(grad, hat, scale, gain):
    grad_gain = jnp.sum(grad * hat, axis=0, keepdims=True)
    wide = grad * gain
    inner = jnp.mean(wide * hat, axis=-1, keepdims=True)
    return scale * (wide - jnp.mean(wide, axis=-1, keepdims=True) - hat * inner), grad_gain


def vector(ref, rows):
    return jnp.concatenate([ref[r : r + 1] for r in range(rows.start, rows.stop)], axis=1)


def by_head(value):
    return jnp.concatenate(
        [
            jnp.where(lane_in(value.shape, h * HEAD_DIM, HEAD_DIM), value, 0.0)
            for h in range(HEADS)
        ],
        axis=0,
    )


def head_sum(value):
    rows = value.shape[0] // HEADS
    parts = [value[h * rows : (h + 1) * rows] for h in range(HEADS)]
    return sum(
        jnp.where(lane_in(part.shape, h * HEAD_DIM, HEAD_DIM), part, 0.0)
        for h, part in enumerate(parts)
    )


SCORE_SCALE = HEAD_DIM ** (-0.5)
KEEP_LANE = 2 * OUTER


def node_forward(
    recycle, node_ref, all_ref, bias_ref, keep, keep_rows, vectors, w_projections, w_attn_out, w_up, w_down,
    w_factors,
    node_out, factors_out, start_out, normed_own, normed_out, soft_out, heads_out, key_out, value_out,
    attended_out, after_out, act_out, slope_out, final_out, flat,
):
    pieces = NODE_DIM // LANES
    length = all_ref.shape[0] // pieces
    embed = jnp.concatenate(
        [vectors[pl.ds(pieces * recycle[0] + a, 1), :] for a in range(pieces)], axis=1
    )
    flat[...] = all_ref[...].astype(WIDE)
    all_rows = jnp.concatenate(
        [flat[pl.ds(a, length, stride=pieces), :] for a in range(pieces)], axis=1
    )
    gain = vector(vectors, GAIN_ONE)
    start_all = all_rows + embed
    normed_all = (row_norm(start_all)[0] * gain).astype(LOW)
    start_out[...] = start_all
    normed_out[...] = normed_all
    start = node_ref[...].astype(WIDE) + embed
    normed = (row_norm(start)[0] * gain).astype(LOW)
    normed_own[...] = normed
    query = dot_nn(normed, w_projections[:, :HEADS_WIDTH]).astype(LOW).astype(WIDE)
    heads = by_head(query).astype(LOW)
    key_value = dot_nn(normed_all, w_projections[:, HEADS_WIDTH:]).astype(LOW)
    key, value = key_value[:, :HEADS_WIDTH], key_value[:, HEADS_WIDTH:]
    heads_out[...] = heads
    key_out[...] = key
    value_out[...] = value
    scores = dot_nt(heads, key) * SCORE_SCALE + bias_ref[...] + (keep[...] - 1.0) * MASK_FILL
    powers = jnp.exp(scores - jnp.max(scores, axis=-1, keepdims=True))
    soft = powers / jnp.sum(powers, axis=-1, keepdims=True)
    soft_out[...] = soft
    attended = head_sum(dot_nn(soft.astype(LOW), value)).astype(LOW)
    attended_out[...] = attended
    after = start + dot_nn(attended, w_attn_out[...])
    after_out[...] = after
    normed = (row_norm(after)[0] * vector(vectors, GAIN_TWO)).astype(LOW)
    act, slope = gelu_parts(dot_nn(normed, w_up[...]))
    act_out[...] = act.astype(LOW)
    slope_out[...] = slope
    final = after + dot_nn(act.astype(LOW), w_down[...])
    final_out[...] = final
    node_out[...] = final.astype(LOW)
    normed = (row_norm(final)[0] * vector(vectors, GAIN_THREE)).astype(LOW)
    factors = dot_nn(normed, w_factors[...])
    factors = jnp.where(lane_in(factors.shape, KEEP_LANE, 1), keep_rows[...], factors).astype(LOW)
    factors_out[...] = jnp.broadcast_to(factors[None], factors_out.shape)


def node_backward(
    sources, factor_ref, cot, vectors, soft_ref, heads, key, value, after_ref, slope, final_ref,
    w_attn_out, w_up, w_down, w_factors,
    key_value_out, query_out, score_out, after_grad_out, final_low_out, normed_two_out,
    hidden_out, after_low_out, g_factors, g_two, g_three,
):
    ranks = key_value_out.shape[0] // cot.shape[0]
    left = factor_ref[sources[0]].astype(WIDE)
    right = sum(factor_ref[sources[1 + r]].astype(WIDE) for r in range(ranks))
    rows = jnp.where(lane_in(left.shape, 0, OUTER), left, right).astype(LOW)
    hat, scale = row_norm(final_ref[...])
    gain = vector(vectors, GAIN_THREE)
    g_factors[...] = dot_tn((hat * gain).astype(LOW), rows)
    part, g_three[...] = row_norm_back(dot_nt(rows, w_factors[...]), hat, scale, gain)
    final_grad = cot[...].astype(WIDE) + part
    final_low = final_grad.astype(LOW)
    final_low_out[...] = final_low
    hidden_grad = (dot_nt(final_low, w_down[...]) * slope[...]).astype(LOW)
    hidden_out[...] = hidden_grad
    hat, scale = row_norm(after_ref[...])
    gain = vector(vectors, GAIN_TWO)
    normed_two_out[...] = (hat * gain).astype(LOW)
    part, g_two[...] = row_norm_back(dot_nt(hidden_grad, w_up[...]), hat, scale, gain)
    after_grad = final_grad + part
    after_grad_out[...] = after_grad
    after_low = after_grad.astype(LOW)
    after_low_out[...] = after_low
    attended_grad = dot_nt(after_low, w_attn_out[...]).astype(LOW).astype(WIDE)
    grad_heads = by_head(attended_grad).astype(LOW)
    soft = soft_ref[...]
    soft_grad = dot_nt(grad_heads, value[...])
    score_grad = soft * (soft_grad - jnp.sum(soft_grad * soft, axis=-1, keepdims=True))
    score_low = score_grad.astype(LOW)
    score_out[...] = score_low
    key_part = dot_tn(score_low, heads[...]) * SCORE_SCALE
    key_value_out[:, :HEADS_WIDTH] = key_part.astype(LOW)
    key_value_out[:, HEADS_WIDTH:] = dot_tn(soft.astype(LOW), grad_heads).astype(LOW)
    query_out[...] = (head_sum(dot_nn(score_low, key[...])) * SCORE_SCALE).astype(LOW)


def outer_tables(
    sources, factors, w_outer, table_out, right_out, left_out, mask_out, w_wide, steps
):
    local_rows = left_out.shape[0]
    ranks = right_out.shape[1] // local_rows
    left_low = factors[sources[0]][:, :OUTER]
    left_out[...] = left_low
    right = jnp.concatenate([factors[sources[1 + r]].astype(WIDE) for r in range(ranks)], axis=0)
    turned = right.T
    right_out[...] = turned[OUTER : 2 * OUTER].astype(LOW)
    own_keep = factors[sources[0]][:, KEEP_LANE : KEEP_LANE + 1].astype(WIDE)
    mask_out[:, 0, :] = own_keep * turned[KEEP_LANE : KEEP_LANE + 1]
    w_wide[...] = w_outer[...].astype(WIDE)
    for q in range(OUTER):
        w_q = w_wide[pl.ds(q, OUTER, stride=OUTER), :].astype(LOW)
        steps[q] = dot_nn(left_low, w_q)
    table_out[...] = jnp.swapaxes(steps[...], 0, 1).astype(LOW)


def outer_backward(table_grad, right_grad, left, w_outer, factors_out, g_outer, w_wide, steps):
    crops, ranks, local_rows, _ = factors_out.shape
    steps[...] = jnp.swapaxes(jnp.sum(table_grad[...], axis=0), 0, 1)
    w_wide[...] = w_outer[...].astype(WIDE)
    left_grad = jnp.zeros((local_rows, OUTER), WIDE)
    for q in range(OUTER):
        grad_q = steps[q].astype(LOW)
        w_q = w_wide[pl.ds(q, OUTER, stride=OUTER), :].astype(LOW)
        left_grad = left_grad + dot_nt(grad_q, w_q)
        g_outer[pl.ds(q, OUTER, stride=OUTER), :] = dot_tn(left[...], grad_q)
    right_rows = right_grad[...].T
    for r in range(ranks):
        block = jnp.concatenate(
            [
                left_grad,
                right_rows[r * local_rows : (r + 1) * local_rows],
                jnp.zeros((local_rows, LANES - 2 * OUTER), WIDE),
            ],
            axis=1,
        ).astype(LOW)
        for c in range(crops):
            factors_out[c, r] = block


def low_of(x):
    return x.astype(LOW)


def local(layout, node, pair, recycle, mask, node_cot, pair_cot, master, first, second):
    crops, ranks = layout.crops, layout.rows
    devices = crops * ranks
    local_rows, length = node.shape[1], pair.shape[2]
    share = TRI_DIM // ranks
    node, pair, node_cot, pair_cot = node[0], pair[0], node_cot[0], pair_cot[0]

    crop_at, row_at = lax.axis_index("crop"), lax.axis_index("row")
    here = crop_at * ranks + row_at
    partner = layout.work_place(here)
    stays = partner == here
    work_crop, work_row = partner // ranks, partner % ranks
    near = lambda array: lax.ppermute(array, BOTH, layout.near)
    far = lambda array: lax.ppermute(array, BOTH, layout.far)
    settled = lambda own, close, *pieces: jnp.where(stays, own, close + jnp.concatenate(pieces))

    at, _ = first_rows()

    amount = master.shape[0]
    height = share_rows(amount)
    offset = (here * (amount % LANES)) % LANES
    shard = lax.dynamic_update_slice(jnp.zeros(height * LANES, LOW), low_of(master), (offset,))
    node_rows = local_rows * NODE_DIM // LANES
    shards = jnp.concatenate([shard.reshape(height, LANES), node.reshape(-1, LANES)], axis=0)
    shards = spread(shards, ranks, "row").reshape(ranks, -1, LANES)
    shards, pair = lax.optimization_barrier((shards, pair))
    node_all = shards[:, height:].reshape(-1, LANES)
    shards = shards[:, :height].reshape(-1, LANES)
    shards = spread(shards, crops // 2, BOTH, layout.chips)
    shards = spread(shards, 2, BOTH, layout.cores)
    shards = shards.reshape(2, crops // 2, ranks, height, LANES)
    (
        vectors, w_bias, w_factors, w_projections, w_attn_out, w_node_up, w_node_down, w_outer,
        w_out_all, w_out_end, w_in_all, w_in_end, w_pair_up, w_pair_down,
    ) = unpack(layout, shards, amount)
    pair_plane = lax.ppermute(pair, BOTH, layout.moves)
    keep = mask.astype(WIDE)
    keep_rows = lax.dynamic_slice_in_dim(keep[0], row_at * local_rows, local_rows, 0)[:, None]

    pair_bias = jnp.einsum("ijd,dh->hij", pair, w_bias[:, :HEADS], preferred_element_type=WIDE)
    rows_low = lambda width: ((local_rows, width), LOW)
    rows_wide = lambda width: ((local_rows, width), WIDE)
    by_heads = (HEADS * local_rows, length)
    (
        node_out, factors, start_all, normed_own, normed_all, soft, heads, key, value, attended, after, act_low,
        slope, node_final,
    ) = one_call(
        node_forward,
        (recycle,),
        (node, node_all, pair_bias.reshape(by_heads), keep, keep_rows, vectors, w_projections, w_attn_out,
         w_node_up, w_node_down, w_factors),
        [rows_low(NODE_DIM), ((2 * ranks, local_rows, LANES), LOW), ((length, NODE_DIM), WIDE),
         rows_low(NODE_DIM), ((length, NODE_DIM), LOW), (by_heads, WIDE), (by_heads[:1] + (HEADS_WIDTH,), LOW),
         ((length, HEADS_WIDTH), LOW), ((length, HEADS_WIDTH), LOW), rows_low(HEADS_WIDTH),
         rows_wide(NODE_DIM), rows_low(FFN_NODE), rows_wide(FFN_NODE), rows_wide(NODE_DIM)],
        [pltpu.VMEM(node_all.shape, WIDE)],
    )

    factors = exchange(factors, BOTH, layout.slabs)
    cot_first, cot_last = jnp.split(pair_cot, 2)
    factors, cot_first, pair_plane = lax.optimization_barrier((factors, cot_first, pair_plane))
    everyone = jnp.arange(ranks, dtype=jnp.int32)
    slab = 2 * ranks
    sources = jnp.concatenate([partner[None], work_crop * ranks + everyone]).astype(jnp.int32) % slab
    table, right, left, mask_plane = one_call(
        outer_tables,
        (sources,),
        (factors, w_outer),
        [((local_rows, OUTER, PAIR_DIM), LOW), ((OUTER, length), LOW), ((local_rows, OUTER), LOW),
         ((local_rows, 1, length), WIDE)],
        [pltpu.VMEM((OUTER * OUTER, PAIR_DIM), WIDE), pltpu.VMEM((OUTER, local_rows, PAIR_DIM), WIDE)],
    )

    step = (min(TILE, local_rows), min(LANES, length))
    extent = (local_rows, length)
    pieces = length // step[1]
    state = (local_rows, TRI_DIM, length)
    line = (local_rows, 1, length)
    sides_shape = (ranks, 2 * share, local_rows, length)
    mixed_shape = (TRI_DIM, local_rows, length)
    natural = (local_rows, length, PAIR_DIM)
    buffer = lambda channels: pltpu.VMEM((step[0], channels, step[1]), LOW)
    trade = lambda blocks: exchange(blocks, BOTH, layout.groups)
    merge = lambda blocks: blocks.reshape((TRI_DIM,) + blocks.shape[2:])
    split = lambda blocks: blocks.reshape((ranks, share) + blocks.shape[1:])
    unit = 2 * local_rows * length * PAIR_DIM * PAIR_DIM
    front_outs = (
        ("r", state, LOW), ("r", line, WIDE), ("r", line, WIDE), ("r", state, LOW),
        ("s", sides_shape, LOW),
    )
    square = (TRI_DIM, PAIR_DIM)
    gain_shape = (PAIR_DIM, 1)
    after_shape = (PAIR_DIM, 2 * TRI_DIM + PAIR_DIM)

    x_one, mean_tri_out, scale_tri_out, gate_tri_out, sides = run(
        kernel_open, step, extent,
        (stays.astype(jnp.int32)[None], pair_plane, pair, table, right, mask_plane, vectors, w_out_all),
        "mnntcrww", front_outs, [buffer(2 * TRI_DIM)], 4 * unit,
    )
    sides, cot_first, pair_cot = lax.optimization_barrier((sides, far(cot_first), pair_cot))
    sides_out, cot_near = lax.optimization_barrier((trade(sides), near(pair_cot)))
    mixed_out = merge(trade(mix(sides_out, False)[0]))
    mixed_out, cot_last = lax.optimization_barrier((mixed_out, cot_last))
    x_two, mean_tri_in, scale_tri_in, gate_tri_in, sides = run(
        kernel_middle, step, extent,
        (mixed_out, x_one, gate_tri_out, mask_plane, vectors, w_out_end, w_in_all), "srrrwww", front_outs, [buffer(TRI_DIM), buffer(2 * TRI_DIM)], 5 * unit,
    )
    sides, cot_last = lax.optimization_barrier((sides, far(cot_last)))
    sides_in, cot_plane = lax.optimization_barrier(
        (trade(sides), settled(pair_cot, cot_near, cot_first, cot_last))
    )
    turns = 2 if local_rows % (2 * TILE) == 0 else 1
    turn_rows = local_rows // turns
    mixed_in = [merge(trade(piece)) for piece in mix(sides_in, True, turns)]
    turned, grads_in = [], []
    ends = (vectors, w_in_end, w_pair_up, w_pair_down)
    for k in range(turns):
        *turned, mixed_grad = run(
            partial(kernel_turn, False), step, (turn_rows, length),
            (mixed_in[k], x_two, gate_tri_in, cot_plane, *ends, *turned),
            "sRRNwwww" + "xxx" * (k > 0),
            (("N", natural, LOW), ("R", state, LOW), ("R", state, LOW),
             ("s", (TRI_DIM, turn_rows, length), LOW)),
            [buffer(TRI_DIM), buffer(TRI_DIM)], 24 * unit // turns,
            skip=k * turn_rows // step[0], aliases={8: 0, 9: 1, 10: 2} if k else {},
        )
        if k:
            grads_in[-1], mixed_grad = lax.optimization_barrier((grads_in[-1], mixed_grad))
        grads_in.append(trade(split(mixed_grad)))
    pair_final, x_grad, gate_grad = turned
    sides_grad = trade(mix_back(grads_in, sides_in, True))
    sums = run(
        partial(kernel_turn, True), step, extent,
        (jnp.concatenate(mixed_in, axis=1), x_two, gate_tri_in, cot_plane, *ends), "srrnwwww",
        (("w", square, WIDE), ("w", gain_shape, WIDE), ("w", (PAIR_DIM, FFN_PAIR), WIDE),
         ("w", (FFN_PAIR, PAIR_DIM), WIDE), ("w", gain_shape, WIDE), ("w", gain_shape, WIDE)),
        [buffer(TRI_DIM)], 28 * unit,
    )
    sides_grad, *sums = lax.optimization_barrier((sides_grad, *sums))
    g_in_out, g_in_tri, g_up, g_down, g_pair, g_bias = sums
    out_first, out_last = jnp.split(pair_final, 2)
    sides_grad, out_near, out_first = lax.optimization_barrier(
        (sides_grad, near(pair_final), out_first)
    )
    backs = (sides_grad, x_two, mean_tri_in, scale_tri_in, gate_grad, x_grad, mask_plane,
             vectors, w_in_all, mixed_out, gate_tri_out, w_out_end)
    x_grad, gate_grad, mixed_grad = run(
        partial(kernel_return, False), step, extent, backs, "srrrrrrwwsrw",
        (("r", state, LOW), ("r", state, LOW), ("s", mixed_shape, LOW)),
        [buffer(2 * TRI_DIM), buffer(TRI_DIM), buffer(TRI_DIM)], 8 * unit,
    )
    mixed_grad, out_first = lax.optimization_barrier((mixed_grad, far(out_first)))
    mixed_grad = trade(split(mixed_grad))
    sums = run(
        partial(kernel_return, True), step, extent, backs, "srrrrrrwwsrw",
        (("w", after_shape, WIDE), ("w", gain_shape, WIDE), ("w", square, WIDE),
         ("w", gain_shape, WIDE)),
        [buffer(2 * TRI_DIM), buffer(TRI_DIM)], 12 * unit,
    )
    mixed_grad, *sums = lax.optimization_barrier((mixed_grad, *sums))
    g_in_all, g_in_gain, g_out_out, g_out_tri = sums
    sides_grad = trade(mix_back([mixed_grad], sides_out, False))
    sides_grad, out_last = lax.optimization_barrier((sides_grad, out_last))
    pair_one_grad, table_grad, right_part, g_out_all, g_out_gain = run(
        kernel_close, step, extent,
        (sides_grad, x_one, mean_tri_out, scale_tri_out, gate_grad, x_grad, mask_plane,
         vectors, w_out_all, table, right),
        "srrrrrrwwtc",
        (("n", natural, LOW), ("p", (pieces, local_rows, OUTER, PAIR_DIM), WIDE),
         ("c", (OUTER, length), WIDE), ("w", after_shape, WIDE), ("w", gain_shape, WIDE)),
        [buffer(2 * TRI_DIM)], 8 * unit,
    )

    factor_grads, g_outer = one_call(
        outer_backward,
        (),
        (table_grad, right_part, left, w_outer),
        [((2, ranks, local_rows, LANES), LOW), ((OUTER * OUTER, PAIR_DIM), WIDE)],
        [pltpu.VMEM((OUTER * OUTER, PAIR_DIM), WIDE), pltpu.VMEM((OUTER, local_rows, PAIR_DIM), WIDE)],
    )
    factor_grads, out_last = lax.optimization_barrier((factor_grads, far(out_last)))
    pair_out = settled(pair_final, out_near, out_first, out_last)
    factor_grads = exchange(factor_grads.reshape(slab, local_rows, LANES), BOTH, layout.slabs)
    factor_grads, pair_one_grad, pair_out = lax.optimization_barrier(
        (factor_grads, pair_one_grad, pair_out)
    )

    workers = layout.work_place(crop_at * ranks + everyone)
    sources = jnp.concatenate([partner[None], workers]).astype(jnp.int32) % slab
    (
        key_value, query_low, score_low, after_grad, final_low, normed_two, hidden_grad, after_low,
        g_factors, g_two, g_three,
    ) = one_call(
        node_backward,
        (sources,),
        (factor_grads, node_cot, vectors, soft, heads, key, value, after, slope, node_final,
         w_attn_out, w_node_up, w_node_down, w_factors),
        [((length, 2 * HEADS_WIDTH), LOW), rows_low(HEADS_WIDTH), (by_heads, LOW),
         rows_wide(NODE_DIM), rows_low(NODE_DIM), rows_low(NODE_DIM), rows_low(FFN_NODE),
         rows_low(NODE_DIM), ((NODE_DIM, LANES), WIDE), ((1, NODE_DIM), WIDE), ((1, NODE_DIM), WIDE)],
    )
    score_low = score_low.reshape(HEADS, local_rows, length)
    g_bias_head = jnp.einsum("ijd,hij->dh", pair, score_low, preferred_element_type=WIDE)
    g_bias_head = lax.optimization_barrier(g_bias_head).reshape(-1, LANES)
    pair_one_away = lax.ppermute(pair_one_grad, BOTH, layout.moves)
    grads = [
        (at.w_bias, 1, g_bias_head),
        (at.gain_two, 1, g_two),
        (at.gain_three, 1, g_three),
        (at.w_outer, 1, g_outer),
        (at.gain_pair, 1, g_pair),
        (at.w_pair_up, 1, g_up),
        (at.w_pair_down, 1, g_down),
        (at.bias_pair, 1, g_bias),
    ]
    for tri, g_all, g_gain, g_tri, g_out in (
        (at.outgoing, g_out_all, g_out_gain, g_out_tri, g_out_out),
        (at.incoming, g_in_all, g_in_gain, g_in_tri, g_in_out),
    ):
        grads += [
            (tri.gain_in, 1, g_gain),
            (tri.w_left, 3, g_all),
            (tri.gain_tri, 1, g_tri),
            (tri.w_tri_out, 1, g_out),
        ]

    blocks, node_blocks = pack(
        layout, amount, jnp.concatenate([recycle, row_at.astype(jnp.int32)[None]]), grads,
        (key_value, query_low, start_all, normed_own, normed_all, after_grad, vectors,
         w_projections, act_low, final_low, normed_two, hidden_grad, attended, after_low, g_factors),
    )
    total = lambda got: low_of(jnp.sum(got.astype(WIDE), axis=0))
    blocks = total(exchange(blocks, BOTH, layout.cores))
    blocks = exchange(blocks, BOTH, layout.chips)
    blocks = total(blocks)
    blocks = exchange(jnp.concatenate([blocks, node_blocks], axis=1), "row")
    pair_grad = jnp.where(stays, pair_one_grad, pair_one_away).astype(WIDE) + jnp.einsum(
        "hij,dh->ijd", score_low, w_bias[:, :HEADS], preferred_element_type=WIDE
    )
    blocks, pair_grad = lax.optimization_barrier((blocks, low_of(pair_grad)))
    blocks = jnp.sum(blocks.astype(WIDE), axis=0)
    node_parts = jnp.split(blocks[height:], NODE_DIM // LANES)
    node_grad = low_of(after_grad + jnp.concatenate(node_parts, axis=1))
    blocks = blocks[:height]
    grad_own = lax.dynamic_slice(blocks.reshape(-1), (offset,), (amount,))
    square_own = jnp.broadcast_to(jnp.sum(grad_own * grad_own), (1, LANES))
    last = jnp.concatenate([g_bias.reshape(1, LANES), square_own], axis=0)
    last = jnp.sum(spread(last, devices, BOTH).reshape(devices, 2, LANES), axis=0)
    bias_total = last[0]
    grad_norm = jnp.sqrt(last[1, 0])
    clipped = grad_own * (CLIP_NORM / jnp.maximum(grad_norm, CLIP_NORM))
    new_first = BETA_ONE * first + (1.0 - BETA_ONE) * clipped
    new_second = BETA_TWO * second + (1.0 - BETA_TWO) * clipped * clipped
    first_hat = new_first / (1.0 - BETA_ONE**ADAM_STEP)
    second_hat = new_second / (1.0 - BETA_TWO**ADAM_STEP)
    new_master = master - LEARN_RATE * (
        first_hat / (jnp.sqrt(second_hat) + ADAM_EPS) + WEIGHT_DECAY * master
    )
    return (
        node_out[None],
        pair_out[None],
        node_grad[None],
        pair_grad[None],
        grad_own,
        bias_total,
        grad_norm,
        new_master,
        new_first,
        new_second,
        low_of(new_master),
    )


def solution(mesh):
    layout = Layout(mesh.shape["crop"], mesh.shape["row"])
    return jax.shard_map(
        lambda *arrays: local(layout, *arrays),
        mesh=mesh,
        in_specs=(
            P("crop", "row", None),
            P("crop", "row", None, None),
            P("crop"),
            P("crop", None),
            P("crop", "row", None),
            P("crop", "row", None, None),
            P(("crop", "row")),
            P(("crop", "row")),
            P(("crop", "row")),
        ),
        out_specs=(
            P("crop", "row", None),
            P("crop", "row", None, None),
            P("crop", "row", None),
            P("crop", "row", None, None),
            P(("crop", "row")),
            P(),
            P(),
            P(("crop", "row")),
            P(("crop", "row")),
            P(("crop", "row")),
            P(("crop", "row")),
        ),
        check_vma=False,
    )
```
